32 devices in a mesh: dp: 8 (over y, x, core), seq: 4 (over z).
Axes of the slice: x: 2, y: 2, z: 4, core: 2. Of those that a mesh axis runs over, the one named last changes fastest.
Arguments:
- tokens: float32 [8, 896, 1024], P('dp', 'seq'), may hold values from -6 to 6
- ln1_gain: float32 [1024], P(('dp', 'seq')), may hold values from 0.5 to 1.5
- ln1_bias: float32 [1024], P(('dp', 'seq')), may hold values from -2 to 2
- w_qkv: float32 [1024, 3072], P('dp', 'seq'), may hold values from -0.1875 to 0.1875
- w_out: float32 [1024, 1024], P('dp', 'seq'), may hold values from -0.75 to 0.75
- ln2_gain: float32 [1024], P(('dp', 'seq')), may hold values from 0.5 to 1.5
- ln2_bias: float32 [1024], P(('dp', 'seq')), may hold values from -2 to 2
- w_up: float32 [1024, 4096], P('dp', 'seq'), may hold values from -0.1875 to 0.1875
- w_down: float32 [4096, 1024], P(('dp', 'seq')), may hold values from -0.09375 to 0.09375
- w_unpatch: float32 [1024, 2048], P('dp', 'seq'), may hold values from -0.1875 to 0.1875
- dec_w1: float32 [96, 64], replicated, may hold values from -0.625 to 0.625
- dec_b1: float32 [64], replicated, may hold values from -3 to 3
- dec_w2: float32 [64, 4], replicated, may hold values from -0.75 to 0.75
- dec_b2: float32 [4], replicated, may hold values from -3 to 3
- counts: int32 [8], P('dp'), may hold values from 32 to 128, as said below
- sample_texels: int32 [8, 3, 8192], P('dp', None, 'seq'), may hold values from 0 to 16383
- d_density: float32 [8, 8192], P('dp', 'seq'), may hold values from -6 to 6
- d_color: float32 [8, 3, 8192], P('dp', None, 'seq'), may hold values from -6 to 6
Outputs:
- density: float32 [8, 8192], P('dp', 'seq')
- color: float32 [8, 3, 8192], P('dp', None, 'seq')
- g_tokens: float32 [8, 896, 1024], P('dp', 'seq')
- g_ln1_gain: float32 [1024], P(('dp', 'seq'))
- g_ln1_bias: float32 [1024], P(('dp', 'seq'))
- g_w_qkv: float32 [1024, 3072], P('dp', 'seq')
- g_w_out: float32 [1024, 1024], P('dp', 'seq')
- g_ln2_gain: float32 [1024], P(('dp', 'seq'))
- g_ln2_bias: float32 [1024], P(('dp', 'seq'))
- g_w_up: float32 [1024, 4096], P('dp', 'seq')
- g_w_down: float32 [4096, 1024], P(('dp', 'seq'))
- g_w_unpatch: float32 [1024, 2048], P('dp', 'seq')
- g_dec_w1: float32 [96, 64], replicated
- g_dec_b1: float32 [64], replicated
- g_dec_w2: float32 [64, 4], replicated
- g_dec_b2: float32 [4], replicated
The draws below stay inside these ranges and needn't reach their ends.
Inputs may be any that keep to these rules, and one draw needn't show every extreme that they name: A scene's image tokens fill its first counts slots in part order; some scene has all 128 slots filled.
All inputs are finite; a program needn't handle non-finite values.
Results may differ from the reference program's by a relative error of at most 0.023.
Values may be sent and summed in bfloat16 or wider, within the bound.
A program may use at most 192 MiB of HBM per device.

```python
import jax
import jax.numpy as jnp
from jax import lax

D = 1024
HEADS = 16
FF = 4096
PATCH = 8
CH = 32
DH = 64
PRES = 16
IMG_DEV = 32
HEAD_DIM = 64
UNPATCH = 2048
PLANE_DEV = 192
TOK_DEV = 224
SCENES = 8
SCENE_TOK = 896
SAMPLES = 8192
TEXELS = 16384
N_SEQ = 4


def draw_counts(key, part):
    key = jax.random.fold_in(key, 7)
    kind_key, size_key, pick_key = jax.random.split(key, 3)
    large = jax.random.randint(kind_key, (SCENES,), 0, 10) < 3
    smaller = jax.random.randint(size_key, (SCENES,), IMG_DEV, 2 * IMG_DEV + 1)
    chosen = jax.random.randint(pick_key, (), 0, SCENES)
    filled = large | (jnp.arange(SCENES, dtype=jnp.int32) == chosen)
    return jnp.where(filled, N_SEQ * IMG_DEV, smaller).astype(jnp.int32)


def with_ends(entries, rng, least, largest):
    longest = entries.shape.index(max(entries.shape))
    spots = []
    for shift in (0, 1):
        where = [jax.random.randint(jax.random.fold_in(rng, axis), (), 0, length) for axis, length in enumerate(entries.shape)]
        where[longest] = (where[longest] + shift) % entries.shape[longest]
        spots.append(tuple(where))
    return entries.at[spots[0]].set(least).at[spots[1]].set(largest)


def level_of(stream_key, shape, cuts, least, top_value):
    level, own = 1.0, jax.random.fold_in(stream_key, 6)
    for dim, shards_of in cuts:
        draws = jnp.exp(jax.random.uniform(jax.random.fold_in(own, dim), (shards_of,), jnp.float32, least / len(cuts), top_value / len(cuts)))
        level = level * jnp.repeat(draws, shape[dim] // shards_of).reshape([-1 if axis == dim else 1 for axis in range(len(shape))])
    return level


def gaussian(key, extent, scale, limit, shards=(), kind=jnp.bfloat16):
    drawn = jax.random.normal(key, extent, jnp.float32) * scale
    if len(shards) > 0:
        drawn = level_of(key, extent, shards, -0.22, 0.18) * drawn
    return jnp.clip(drawn, min=-limit, max=limit).astype(kind)


def setup_inputs(seed: int = 0) -> dict:
    streams_of = jax.random.split(jax.random.key(seed), 19)
    tokens = gaussian(streams_of[0], (SCENES, SCENE_TOK, D), 1.0, 6.0, ((0, 8), (1, 4)), jnp.float32)
    ln1_gain = jnp.clip(1.0 + 0.1 * jax.random.normal(streams_of[1], (D,), jnp.float32), 0.5, 1.5)
    ln1_bias = gaussian(streams_of[2], (D,), 0.3, 2.0, ((0, 32),), jnp.float32)
    w_qkv = gaussian(streams_of[3], (D, 3 * D), D ** -0.5, 0.1875, ((0, 8), (1, 4)), jnp.float32)
    w_out = gaussian(streams_of[4], (D, D), (max(1, D // 16)) ** -0.5, 0.75, ((0, 8), (1, 4)), jnp.float32)
    ln2_gain = jnp.clip(1.0 + 0.1 * jax.random.normal(streams_of[5], (D,), jnp.float32), 0.5, 1.5)
    ln2_bias = gaussian(streams_of[6], (D,), 0.3, 2.0, ((0, 32),), jnp.float32)
    w_up = gaussian(streams_of[7], (D, FF), D ** -0.5, 0.1875, ((0, 8), (1, 4)), jnp.float32)
    w_down = gaussian(streams_of[8], (FF, D), FF ** -0.5, 0.09375, ((0, 32),), jnp.float32)
    w_unpatch = gaussian(streams_of[9], (D, UNPATCH), D ** -0.5, 0.1875, ((0, 8), (1, 4)), jnp.float32)
    dec_w1 = gaussian(streams_of[10], (3 * CH, DH), (3 * CH) ** -0.5, 0.625, (), jnp.float32)
    dec_b1 = gaussian(streams_of[11], (DH,), 0.5, 3.0, (), jnp.float32)
    dec_w2 = gaussian(streams_of[12], (DH, 4), DH ** -0.5, 0.75, (), jnp.float32)
    dec_b2 = gaussian(streams_of[13], (4,), 0.5, 3.0, (), jnp.float32)
    counts = draw_counts(jax.random.fold_in(streams_of[18], 71), 0)
    sample_texels = with_ends(jax.random.randint(streams_of[15], (SCENES, 3, SAMPLES), 0, TEXELS), jax.random.fold_in(streams_of[15], 1), 0, TEXELS - 1).astype(jnp.int32)
    d_density = gaussian(streams_of[16], (SCENES, SAMPLES), 1.0, 6.0, ((0, 8), (1, 4)), jnp.float32)
    d_color = gaussian(streams_of[17], (SCENES, 3, SAMPLES), 1.0, 6.0, ((0, 8), (2, 4)), jnp.float32)
    return {"tokens": tokens, "ln1_gain": ln1_gain, "ln1_bias": ln1_bias, "w_qkv": w_qkv, "w_out": w_out, "ln2_gain": ln2_gain, "ln2_bias": ln2_bias, "w_up": w_up, "w_down": w_down, "w_unpatch": w_unpatch, "dec_w1": dec_w1, "dec_b1": dec_b1, "dec_w2": dec_w2, "dec_b2": dec_b2, "counts": counts, "sample_texels": sample_texels, "d_density": d_density, "d_color": d_color}


@jax.custom_vjp
def low(v):
    return lax.optimization_barrier(v.astype(jnp.bfloat16)).astype(jnp.float32)

@jax.custom_vjp
def low_back(v):
    return v

def low_keep(v):
    return (low(v), None)

def low_pass(kept, grad):
    return (grad,)

def back_keep(v):
    return (v, None)

def back_low(kept, grad):
    return (low(grad),)
low.defvjp(low_keep, low_pass)
low_back.defvjp(back_keep, back_low)
EPSILON = 1e-05
NEGATIVE = -1e+30

def highest(left, right):
    return jnp.dot(left, right, precision=lax.Precision.HIGHEST, preferred_element_type=jnp.float32)

def layer_norm(values, gain, shift):
    center = values - lax.optimization_barrier(jnp.mean(values, axis=-1, keepdims=True))
    spread = lax.optimization_barrier(jnp.mean(center * center, axis=-1, keepdims=True))
    return center * lax.rsqrt(spread + EPSILON) * gain + shift

def gelu_exact(values):
    return jax.nn.gelu(values, approximate=False)

def key_mask(count):
    position = jnp.arange(SCENE_TOK, dtype=jnp.int32)
    owner = position // TOK_DEV
    offset = position % TOK_DEV
    return (offset < PLANE_DEV) | (owner * IMG_DEV + offset - PLANE_DEV < count)

def table_rows(texel):
    side = PRES * PATCH
    quarter = PRES * PRES // N_SEQ
    row_pos = texel // side
    col_pos = texel % side
    token = row_pos // PATCH * PRES + col_pos // PATCH
    sub_pos = row_pos % PATCH * PATCH + col_pos % PATCH
    plane = jnp.arange(3, dtype=jnp.int32)[:, None]
    grid_row = token // quarter * PLANE_DEV + plane * quarter + token % quarter
    return (grid_row * (PATCH * PATCH) + sub_pos).astype(jnp.int32)

def scene_forward(ln1_gain, ln1_bias, w_qkv, w_out, ln2_gain, ln2_bias, w_up, w_down, w_unpatch, dec_w1, dec_b1, dec_w2, dec_b2, scene_rows, valid, rows):
    scale = HEAD_DIM ** (-0.5)
    hidden_one = low(layer_norm(scene_rows, low(ln1_gain), low(ln1_bias)))
    qkv = low_back(low(highest(hidden_one, low(w_qkv))))
    queries = qkv[:, :D].reshape(SCENE_TOK, HEADS, HEAD_DIM).transpose(1, 0, 2)
    keys = qkv[:, D:2 * D].reshape(SCENE_TOK, HEADS, HEAD_DIM).transpose(1, 0, 2)
    values = qkv[:, 2 * D:].reshape(SCENE_TOK, HEADS, HEAD_DIM).transpose(1, 0, 2)

    def one_head(parts):
        query_h, key_h, value_h = parts
        scores = low_back(highest(query_h, key_h.T) * scale)
        scores = jnp.where(valid[None, :], scores, NEGATIVE)
        probs = jax.nn.softmax(scores, axis=-1)
        return low_back(low(highest(low(probs), value_h)))
    head_out = lax.map(jax.checkpoint(one_head), (queries, keys, values))
    mixed = head_out.transpose(1, 0, 2).reshape(SCENE_TOK, D)
    after_attn = scene_rows + low_back(highest(mixed, low(w_out)))
    hidden_two = low(layer_norm(after_attn, low(ln2_gain), low(ln2_bias)))
    pre_act = low_back(highest(hidden_two, low(w_up)))
    activated = low(gelu_exact(pre_act))
    layer_out = after_attn + low_back(highest(activated, low(w_down)))
    plane_rows = low(layer_out.reshape(N_SEQ, TOK_DEV, D)[:, :PLANE_DEV].reshape(N_SEQ * PLANE_DEV, D))
    texels = low_back(low(highest(plane_rows, low(w_unpatch))))
    table = texels.reshape(-1, CH)
    features = table[rows.reshape(-1)].reshape(3, SAMPLES, CH).transpose(1, 0, 2).reshape(SAMPLES, 3 * CH)
    dec_pre = highest(features, dec_w1) + dec_b1
    dec_out = highest(gelu_exact(dec_pre), dec_w2) + dec_b2
    density = jax.nn.softplus(dec_out[:, 0])
    color = jax.nn.sigmoid(dec_out[:, 1:]).T
    return (density, color)

def reference(tokens, ln1_gain, ln1_bias, w_qkv, w_out, ln2_gain, ln2_bias, w_up, w_down, w_unpatch, dec_w1, dec_b1, dec_w2, dec_b2, counts, sample_texels, d_density, d_color):
    params = (ln1_gain, ln1_bias, w_qkv, w_out, ln2_gain, ln2_bias, w_up, w_down, w_unpatch, dec_w1, dec_b1, dec_w2, dec_b2)

    def one_scene(totals, scene):
        scene_rows, count, texel, grad_density, grad_color = scene
        valid = key_mask(count)
        rows = table_rows(texel)

        def forward(*inputs):
            return scene_forward(*inputs, valid, rows)
        outputs, pull = jax.vjp(forward, *params, scene_rows)
        grads = pull((grad_density, grad_color))
        totals = tuple((total + grad for total, grad in zip(totals, grads[:-1])))
        return (totals, (outputs[0], outputs[1], grads[-1]))
    start = tuple((jnp.zeros_like(param) for param in params))
    totals, (density, color, g_tokens) = lax.scan(one_scene, start, (tokens, counts, sample_texels, d_density, d_color))
    return (density, color, g_tokens) + totals
```

```python
import functools

import jax
import jax.numpy as jnp
from jax import lax
from jax.experimental import pallas as pl
from jax.experimental.pallas import tpu as pltpu
from jax.sharding import PartitionSpec as P

HEADS = 16
PATCH = 8
CH = 32
PRES = 16


EPSILON = 1e-05
NEGATIVE = -1e30
VMEM_LIMIT = 56 * 2**20
AHEAD = 3


MESH = pl.DeviceIdType.MESH


class Place:
    def __init__(self, n, seq_size):
        dp = lax.axis_index("dp")
        self.n, self.seq_size = n, seq_size
        self.seq = lax.axis_index("seq")
        self.i = (lax.div(dp, n * n), lax.rem(lax.div(dp, n), n), lax.rem(dp, n))
        self.dp = dp

    def size(self, axis):
        return self.seq_size if axis == 3 else self.n

    def me(self, axis):
        return self.seq if axis == 3 else self.i[axis]

    def peer(self, axis, step):
        to = lax.rem(self.me(axis) + step, self.size(axis))
        if axis == 3:
            return to, (self.dp, to)
        where = [to if a == axis else self.i[a] for a in range(3)]
        return to, ((where[0] * self.n + where[1]) * self.n + where[2], self.seq)

    def source(self, axis, step):
        size = self.size(axis)
        return lax.rem(self.me(axis) + (size - step), size)

    def enter(self):
        barrier = pltpu.get_barrier_semaphore()
        count = 0
        for axis in range(4):
            for step in range(1, self.size(axis)):
                pl.semaphore_signal(
                    barrier, inc=1, device_id=self.peer(axis, step)[1], device_id_type=MESH
                )
                count += 1
        pl.semaphore_wait(barrier, count)


def remote(src, dst, send, recv, device):
    return pltpu.make_async_remote_copy(
        src_ref=src, dst_ref=dst, send_sem=send, recv_sem=recv, device_id=device, device_id_type=MESH
    )


class Matrix:
    def __init__(self, name, rows, cols, by_rows, parts):
        self.name, self.rows, self.cols, self.by_rows = name, rows, cols, by_rows
        self.parts = parts if rows % (16 * parts) == 0 else 1

    def shape(self, n, seq_size):
        if self.by_rows:
            return (n, n, n, seq_size, self.rows, self.cols)
        return (n, n, n, self.rows, seq_size * self.cols)

    def tail(self, part, first, count):
        size = self.rows // self.parts
        rows = pl.ds(part * size, size)
        if self.by_rows:
            return (pl.ds(first, count), rows, slice(None))
        if isinstance(first, int):
            return (rows, pl.ds(first * self.cols, count * self.cols))
        return (rows, pl.ds(pl.multiple_of(first * self.cols, 128), count * self.cols))

    def tail_shape(self, count):
        size = self.rows // self.parts
        return (count, size, self.cols) if self.by_rows else (size, count * self.cols)


def small_sum(place, value, slots, send, recv):
    for stage, axis in enumerate((2, 1, 0, 3)):
        me = place.me(axis)
        slots[stage, me] = value
        copies = []
        for step in range(1, place.size(axis)):
            ref = slots.at[stage, me]
            copy = remote(
                ref, ref, send.at[stage, step - 1], recv.at[stage, step - 1], place.peer(axis, step)[1]
            )
            copy.start()
            copies.append(copy)
        for copy in copies:
            copy.wait()
        value = slots[stage, 0]
        for other in range(1, place.size(axis)):
            value = value + slots[stage, other]
    return value


class Gather:
    def __init__(self, place, matrices, refs, sems):
        self.place, self.refs = place, refs
        self.chunks = [(w, m, p) for w, m in enumerate(matrices) for p in range(m.parts)]
        self.seq_send, self.seq_recv, self.hop_send, self.hop_recv, self.far_send, self.far_recv = sems
        self.copies = {}

    def _send(self, key, axis, region, send, recv):
        made = []
        for step in range(1, self.place.size(axis)):
            copy = remote(region, region, send.at[step - 1], recv.at[step - 1], self.place.peer(axis, step)[1])
            copy.start()
            made.append(copy)
        self.copies[key] = made

    def _take(self, key):
        for copy in self.copies[key]:
            copy.wait_recv()

    def region(self, k, index, first, count):
        w, matrix, part = self.chunks[k]
        return self.refs[w].at[index + matrix.tail(part, first, count)]

    def along_seq(self, k):
        p = self.place
        self._send((k, 0), 3, self.region(k, p.i, p.seq, 1), self.seq_send.at[k], self.seq_recv.at[k])

    def hop(self, k, number):
        p, half = self.place, self.place.seq_size // 2
        if number == 0:
            self._take((k, 0))
        else:
            self._take((k, 1, 0))
            self._take((k, 1, 1))
        for h in (0, 1):
            axis = 1 - h if number == 0 else h
            index = [p.i[0], p.i[1], p.i[2]]
            if number == 1:
                index[1 - axis] = slice(None)
            at = 2 * number + h
            region = self.region(k, tuple(index), h * half, half)
            self._send((k, 1 + number, h), axis, region, self.hop_send.at[k, at], self.hop_recv.at[k, at])

    def third(self, k):
        p = self.place
        self._take((k, 2, 0))
        self._take((k, 2, 1))
        region = self.region(k, (slice(None), slice(None), p.i[2]), 0, p.seq_size)
        self._send((k, 3), 2, region, self.far_send.at[k], self.far_recv.at[k])

    def arrived(self, k):
        self._take((k, 3))

    def finish(self):
        for made in self.copies.values():
            for copy in made:
                copy.wait_send()


def gather_sems(n, seq_size, chunks):
    sem = pltpu.SemaphoreType.DMA
    return [sem((chunks, seq_size - 1))] * 2 + [sem((chunks, 4, n - 1))] * 2 + [sem((chunks, n - 1))] * 2


def gather_kernel(n, seq_size, matrices, *refs):
    count = len(matrices)
    shards, gains, wholes, gains_out = refs[:count], refs[count], refs[count + 1 : 2 * count + 1], refs[2 * count + 1]
    rest = refs[2 * count + 2 :]
    bufs, (slots, small_send, small_recv, out_sem), sems = rest[:count], rest[count : count + 4], rest[count + 4 :]
    place = Place(n, seq_size)
    for matrix, shard, buf in zip(matrices, shards, bufs):
        if matrix.by_rows:
            buf[place.i + (place.seq,)] = shard[...].astype(jnp.bfloat16)
        else:
            at = pl.ds(pl.multiple_of(place.seq * matrix.cols, 128), matrix.cols)
            buf[place.i + (slice(None), at)] = shard[...].astype(jnp.bfloat16)
    place.enter()
    gather = Gather(place, matrices, bufs, sems)
    total = len(gather.chunks)
    for k in range(AHEAD):
        gather.along_seq(k)
    gains_out[...] = small_sum(place, gains[...], slots, small_send, small_recv)
    outs = []
    for t in range(total + 6):
        if t < total:
            gather.hop(t, 0)
            if t + AHEAD < total:
                gather.along_seq(t + AHEAD)
        if 0 <= t - 2 < total:
            gather.hop(t - 2, 1)
        if 0 <= t - 4 < total:
            gather.third(t - 4)
        if 0 <= t - 6 < total:
            gather.arrived(t - 6)
            w, matrix, part = gather.chunks[t - 6]
            index = (slice(None),) * 3 + matrix.tail(part, 0, seq_size)
            copy = pltpu.make_async_copy(bufs[w].at[index], wholes[w].at[index], out_sem.at[t - 6])
            copy.start()
            outs.append(copy)
    gather.finish()
    for copy in outs:
        copy.wait()


def gather_weights(n, seq_size, matrices, shards, gains):
    chunks = sum(m.parts for m in matrices)
    vmem, any_space = pl.BlockSpec(memory_space=pltpu.VMEM), pl.BlockSpec(memory_space=pl.ANY)
    shapes = [m.shape(n, seq_size) for m in matrices]
    largest = max(n, seq_size)
    return pl.pallas_call(
        functools.partial(gather_kernel, n, seq_size, matrices),
        out_shape=[jax.ShapeDtypeStruct(s, jnp.bfloat16) for s in shapes]
        + [jax.ShapeDtypeStruct(gains.shape, jnp.float32)],
        in_specs=[vmem] * (len(matrices) + 1),
        out_specs=[any_space] * len(matrices) + [vmem],
        scratch_shapes=[pltpu.VMEM(s, jnp.bfloat16) for s in shapes]
        + [
            pltpu.VMEM((4, largest) + gains.shape, jnp.float32),
            pltpu.SemaphoreType.DMA((4, largest - 1)),
            pltpu.SemaphoreType.DMA((4, largest - 1)),
            pltpu.SemaphoreType.DMA((chunks,)),
        ]
        + gather_sems(n, seq_size, chunks),
        compiler_params=pltpu.CompilerParams(
            collective_id=0, has_side_effects=True, vmem_limit_bytes=VMEM_LIMIT
        ),
    )(*shards, gains)


class Scatter:
    def __init__(self, place, matrices, wholes, refs, far, hops, near, outs, sems):
        self.place, self.wholes, self.refs = place, wholes, refs
        self.far, self.hops, self.near, self.outs = far, hops, near, outs
        self.chunks = [(w, m, p) for w, m in enumerate(matrices) for p in range(m.parts)]
        self.seq_send, self.seq_recv, self.hop_send, self.hop_recv, self.far_send, self.far_recv = sems
        self.copies = {}

    def _send(self, key, axis, region_to, slot, send, recv):
        made = []
        for step in range(1, self.place.size(axis)):
            to, device = self.place.peer(axis, step)
            copy = remote(region_to(to), slot(step - 1), send.at[step - 1], recv.at[step - 1], device)
            copy.start()
            made.append(copy)
        self.copies[key] = made

    def _take(self, key):
        for copy in self.copies[key]:
            copy.wait_recv()

    def _index(self, k, index, first, count):
        w, matrix, part = self.chunks[k]
        return index + matrix.tail(part, first, count)

    def third(self, k):
        w, matrix, part = self.chunks[k]
        p, every = self.place, slice(None)
        tail = matrix.tail(part, 0, p.seq_size)
        self._send(
            (k, 3),
            2,
            lambda to: self.wholes[w].at[(every, every, to) + tail],
            lambda s: self.far[w].at[(s, every, every) + tail],
            self.far_send.at[k],
            self.far_recv.at[k],
        )

    def hop(self, k, number):
        w, matrix, part = self.chunks[k]
        p, half, n = self.place, self.place.seq_size // 2, self.place.n
        ref = self.refs[w]
        if number == 0:
            self._take((k, 3))
            tail = matrix.tail(part, 0, p.seq_size)

            @pl.loop(0, n * n)
            def _(at):
                a, b = lax.div(at, n), lax.rem(at, n)
                value = ref[(a, b) + tail].astype(jnp.float32)
                for s in range(n - 1):
                    value = value + self.far[w][(s, a, b) + tail].astype(jnp.float32)
                ref[(a, b) + tail] = value.astype(jnp.bfloat16)

        else:
            for h in (0, 1):
                self._take((k, 1, h))
                tail, local = matrix.tail(part, h * half, half), matrix.tail(part, 0, half)
                for a in range(n):
                    index = (p.i[0], a) if h == 0 else (a, p.i[1])
                    value = ref[index + tail].astype(jnp.float32)
                    for s in range(n - 1):
                        value = value + self.hops[w][(h, s, a) + local].astype(jnp.float32)
                    ref[index + tail] = value.astype(jnp.bfloat16)
        for h in (0, 1):
            axis = h if number == 0 else 1 - h
            tail, local = matrix.tail(part, h * half, half), matrix.tail(part, 0, half)
            other = slice(None) if number == 0 else p.i[1 - axis]
            at = 2 * number + h

            def region_to(to, axis=axis, other=other, tail=tail):
                index = (to, other) if axis == 0 else (other, to)
                return ref.at[index + tail]

            def slot(s, h=h, local=local):
                return self.hops[w].at[(h, s, pl.ds(0, n) if number == 0 else n) + local]

            self._send((k, 1 + number, h), axis, region_to, slot, self.hop_send.at[k, at], self.hop_recv.at[k, at])

    def along_seq(self, k):
        w, matrix, part = self.chunks[k]
        p, half, n = self.place, self.place.seq_size // 2, self.place.n
        ref = self.refs[w]
        for h in (0, 1):
            self._take((k, 2, h))
            tail, local = matrix.tail(part, h * half, half), matrix.tail(part, 0, half)
            value = ref[p.i[:2] + tail].astype(jnp.float32)
            for s in range(n - 1):
                value = value + self.hops[w][(h, s, n) + local].astype(jnp.float32)
            ref[p.i[:2] + tail] = value.astype(jnp.bfloat16)
        size = matrix.rows // matrix.parts
        self._send(
            (k, 0),
            3,
            lambda to: ref.at[p.i[:2] + matrix.tail(part, to, 1)],
            lambda s: self.near[w].at[(s,) + matrix.tail(part, 0, 1)],
            self.seq_send.at[k],
            self.seq_recv.at[k],
        )

    def arrived(self, k):
        w, matrix, part = self.chunks[k]
        p = self.place
        self._take((k, 0))
        value = self.refs[w][p.i[:2] + matrix.tail(part, p.seq, 1)].astype(jnp.float32)
        for s in range(p.seq_size - 1):
            value = value + self.near[w][(s,) + matrix.tail(part, 0, 1)].astype(jnp.float32)
        size = matrix.rows // matrix.parts
        self.outs[w][pl.ds(part * size, size)] = value.reshape(size, matrix.cols)

    def finish(self):
        for made in self.copies.values():
            for copy in made:
                copy.wait_send()


def scatter_kernel(n, seq_size, matrices, *refs):
    count = len(matrices)
    grads, small, outs, small_out = refs[:count], refs[count], refs[count + 1 : 2 * count + 1], refs[2 * count + 1]
    rest = refs[2 * count + 2 :]
    bufs, far, hops, near = [rest[i * count : (i + 1) * count] for i in range(4)]
    slots, small_send, small_recv, in_sem = rest[4 * count : 4 * count + 4]
    sems = rest[4 * count + 4 :]
    place = Place(n, seq_size)
    scatter = Scatter(place, matrices, grads, bufs, far, hops, near, outs, sems)
    total = len(scatter.chunks)
    loads = []
    for k, (w, matrix, part) in enumerate(scatter.chunks):
        tail, every = matrix.tail(part, 0, seq_size), (slice(None),) * 2
        copy = pltpu.make_async_copy(
            grads[w].at[every + (place.i[2],) + tail], bufs[w].at[every + tail], in_sem.at[k]
        )
        copy.start()
        loads.append(copy)
    place.enter()
    for t in range(total + 8):
        if t < total:
            scatter.third(t)
        if 0 <= t - 2 < total:
            loads[t - 2].wait()
            scatter.hop(t - 2, 0)
        if 0 <= t - 4 < total:
            scatter.hop(t - 4, 1)
        if 0 <= t - 6 < total:
            scatter.along_seq(t - 6)
        if 0 <= t - 8 < total:
            scatter.arrived(t - 8)
        if t == 8:
            small_out[...] = small_sum(place, small[...], slots, small_send, small_recv)
    scatter.finish()


def scatter_grads(n, seq_size, matrices, grads, small):
    chunks = sum(m.parts for m in matrices)
    vmem, any_space = pl.BlockSpec(memory_space=pltpu.VMEM), pl.BlockSpec(memory_space=pl.ANY)
    shapes = [m.shape(n, seq_size) for m in matrices]
    largest = max(n, seq_size)
    bfloat = jnp.bfloat16
    return pl.pallas_call(
        functools.partial(scatter_kernel, n, seq_size, matrices),
        out_shape=[jax.ShapeDtypeStruct((m.rows, m.cols), jnp.float32) for m in matrices]
        + [jax.ShapeDtypeStruct(small.shape, jnp.float32)],
        in_specs=[any_space] * len(matrices) + [vmem],
        out_specs=[vmem] * (len(matrices) + 1),
        scratch_shapes=[pltpu.VMEM((n, n) + s[3:], bfloat) for s in shapes]
        + [pltpu.VMEM((n - 1, n, n) + s[3:], bfloat) for s in shapes]
        + [
            pltpu.VMEM(
                (2, n - 1, n + 1)
                + ((seq_size // 2, m.rows, m.cols) if m.by_rows else (m.rows, seq_size // 2 * m.cols)),
                bfloat,
            )
            for m in matrices
        ]
        + [
            pltpu.VMEM((seq_size - 1,) + ((1, m.rows, m.cols) if m.by_rows else (m.rows, m.cols)), bfloat)
            for m in matrices
        ]
        + [
            pltpu.VMEM((4, largest) + small.shape, jnp.float32),
            pltpu.SemaphoreType.DMA((4, largest - 1)),
            pltpu.SemaphoreType.DMA((4, largest - 1)),
            pltpu.SemaphoreType.DMA((chunks,)),
        ]
        + gather_sems(n, seq_size, chunks),
        compiler_params=pltpu.CompilerParams(
            collective_id=1, has_side_effects=True, vmem_limit_bytes=VMEM_LIMIT
        ),
    )(*grads, small)


def weight_list(shards):
    names = ("qkv", "out", "up", "down", "unpatch")
    parts = (4, 1, 4, 4, 2)
    return tuple(
        Matrix(name, shard.shape[0], shard.shape[1], name == "down", part)
        for name, shard, part in zip(names, shards, parts)
    )


def matmul(left, right):
    return jnp.dot(left, right, preferred_element_type=jnp.float32)


def matmul_tn(left, right):
    return lax.dot_general(
        left, right, (((0,), (0,)), ((), ())), preferred_element_type=jnp.float32
    )


def matmul_nt(left, right):
    return lax.dot_general(
        left, right, (((1,), (1,)), ((), ())), preferred_element_type=jnp.float32
    )


def exact(left, right):
    return jnp.dot(left, right, precision=lax.Precision.HIGHEST, preferred_element_type=jnp.float32)


def exact_tn(left, right):
    return lax.dot_general(
        left,
        right,
        (((0,), (0,)), ((), ())),
        precision=lax.Precision.HIGHEST,
        preferred_element_type=jnp.float32,
    )


def exact_nt(left, right):
    return lax.dot_general(
        left,
        right,
        (((1,), (1,)), ((), ())),
        precision=lax.Precision.HIGHEST,
        preferred_element_type=jnp.float32,
    )


def gelu_exact(values):
    return jax.nn.gelu(values, approximate=False)


def norm_forward(values, gain, shift):
    center = values - jnp.mean(values, axis=-1, keepdims=True)
    inverse = lax.rsqrt(jnp.mean(center * center, axis=-1, keepdims=True) + EPSILON)
    normed = center * inverse
    return (normed * gain + shift, normed, inverse)


def norm_backward(grad, normed, inverse, gain):
    scaled = grad * gain
    inner = scaled - jnp.mean(scaled, axis=-1, keepdims=True)
    inner = inner - normed * jnp.mean(scaled * normed, axis=-1, keepdims=True)
    return (inner * inverse, jnp.sum(grad * normed, axis=0), jnp.sum(grad, axis=0))


def split_heads(matrix, heads):
    return matrix.reshape(matrix.shape[0], heads, matrix.shape[1] // heads).transpose(1, 0, 2)


def join_heads(stacked):
    return stacked.transpose(1, 0, 2).reshape(stacked.shape[1], stacked.shape[0] * stacked.shape[2])


def shards(
    tokens,
    ln1_gain,
    ln1_bias,
    w_qkv,
    w_out,
    ln2_gain,
    ln2_bias,
    w_up,
    w_down,
    w_unpatch,
    dec_w1,
    dec_b1,
    dec_w2,
    dec_b2,
    counts,
    sample_texels,
    d_density,
    d_color,
):
    seq_size = lax.axis_size("seq")
    dp_size = lax.axis_size("dp")
    quarter = PRES * PRES // seq_size
    plane_dev = 3 * quarter
    rows_in = tokens[0]
    tok_dev = rows_in.shape[0]
    width = rows_in.shape[1]
    head_dim = width // HEADS
    scale = head_dim ** (-0.5)
    bfloat = jnp.bfloat16
    n = round(dp_size ** (1 / 3))
    shards_of = (w_qkv, w_out, w_up, w_down, w_unpatch)
    matrices = weight_list(shards_of)
    device = lax.axis_index("dp") * seq_size + lax.axis_index("seq")
    gains = jnp.stack([ln1_gain, ln1_bias, ln2_gain, ln2_bias])
    spread = jnp.zeros((8, width), jnp.float32)
    spread = lax.dynamic_update_slice(spread, gains, (0, device * gains.shape[1]))
    *wholes, gains_all = gather_weights(n, seq_size, matrices, shards_of, spread)
    qkv_weight, out_weight, up_weight, down_weight, unpatch_weight = [
        w.reshape(-1, w.shape[-1]) for w in wholes
    ]
    gain_one, shift_one, gain_two, shift_two = [
        lax.reduce_precision(gains_all[i], 8, 7) for i in range(4)
    ]
    norm_one, normed_one, inverse_one = norm_forward(rows_in, gain_one, shift_one)
    hidden_one = norm_one.astype(bfloat)
    qkv = matmul(hidden_one, qkv_weight).astype(bfloat)
    keys_all, values_all = (
        lax.all_gather(qkv[:, width : 2 * width], "seq", axis=0, tiled=True),
        lax.all_gather(qkv[:, 2 * width :], "seq", axis=0, tiled=True),
    )
    position = jnp.arange(seq_size * tok_dev, dtype=jnp.int32)
    owner = position // tok_dev
    offset = position % tok_dev
    key_valid = (offset < plane_dev) | (
        owner * (tok_dev - plane_dev) + offset - plane_dev < counts[0]
    )
    query_heads = split_heads(qkv[:, :width], HEADS)
    key_heads = split_heads(keys_all, HEADS)
    value_heads = split_heads(values_all, HEADS)

    def head_forward(parts):
        query_h, key_h, value_h = parts
        scores = jnp.where(key_valid[None, :], matmul_nt(query_h, key_h) * scale, NEGATIVE)
        peak = jnp.max(scores, axis=-1, keepdims=True)
        expo = jnp.exp(scores - peak)
        total = jnp.sum(expo, axis=-1, keepdims=True)
        probs = (expo / total).astype(bfloat)
        return (matmul(probs, value_h), peak[:, 0] + jnp.log(total[:, 0]))

    head_out, log_norm = lax.map(head_forward, (query_heads, key_heads, value_heads))
    mixed = join_heads(head_out).astype(bfloat)
    after_attn = rows_in + matmul(mixed, out_weight)
    norm_two, normed_two, inverse_two = norm_forward(after_attn, gain_two, shift_two)
    hidden_two = norm_two.astype(bfloat)
    pre_act = matmul(hidden_two, up_weight)
    act_value, act_pull = jax.vjp(gelu_exact, pre_act)
    activated = act_value.astype(bfloat)
    layer_out = after_attn + matmul(activated, down_weight)
    plane_rows = layer_out[:plane_dev].astype(bfloat)
    own_texels = matmul(plane_rows, unpatch_weight).astype(bfloat)
    texels = lax.all_gather(own_texels, "seq", axis=0, tiled=True)
    table = texels.reshape(-1, CH)
    texel = sample_texels[0]
    samples = texel.shape[1]
    side = PRES * PATCH
    row_pos = texel // side
    col_pos = texel % side
    token = row_pos // PATCH * PRES + col_pos // PATCH
    sub_pos = row_pos % PATCH * PATCH + col_pos % PATCH
    plane = jnp.arange(3, dtype=jnp.int32)[:, None]
    grid_row = token // quarter * plane_dev + plane * quarter + token % quarter
    flat_rows = (grid_row * (PATCH * PATCH) + sub_pos).reshape(-1)
    picked = jnp.take(table, flat_rows, axis=0).astype(jnp.float32)
    features = picked.reshape(3, samples, CH).transpose(1, 0, 2).reshape(samples, 3 * CH)
    dec_pre = exact(features, dec_w1) + dec_b1
    dec_hidden, dec_pull = jax.vjp(gelu_exact, dec_pre)
    dec_out = exact(dec_hidden, dec_w2) + dec_b2
    density = jax.nn.softplus(dec_out[:, 0])
    color_value = jax.nn.sigmoid(dec_out[:, 1:])
    grad_dec_out = jnp.concatenate(
        [
            (d_density[0] * jax.nn.sigmoid(dec_out[:, 0]))[:, None],
            d_color[0].T * color_value * (1.0 - color_value),
        ],
        axis=1,
    )
    grad_w_two = exact_tn(dec_hidden, grad_dec_out)
    grad_b_two = jnp.sum(grad_dec_out, axis=0)
    grad_dec_pre = dec_pull(exact_nt(grad_dec_out, dec_w2))[0]
    grad_w_one = exact_tn(features, grad_dec_pre)
    grad_b_one = jnp.sum(grad_dec_pre, axis=0)
    grad_features = exact_nt(grad_dec_pre, dec_w1)
    spread_grads = grad_features.reshape(samples, 3, CH).transpose(1, 0, 2).reshape(-1, CH)
    grad_table = jnp.zeros(table.shape, jnp.float32).at[flat_rows].add(spread_grads)
    own_grad_texels = (
        lax.psum_scatter(
            grad_table.reshape(texels.shape).astype(jnp.bfloat16),
            "seq",
            scatter_dimension=0,
            tiled=True,
        )
        .astype(jnp.float32)
        .astype(bfloat)
    )
    grad_planes = matmul_nt(own_grad_texels, unpatch_weight)
    grad_unpatch = matmul_tn(plane_rows, own_grad_texels)
    grad_layer = jnp.concatenate(
        [grad_planes, jnp.zeros((tok_dev - plane_dev, width), jnp.float32)], axis=0
    )
    grad_layer_low = grad_layer.astype(bfloat)
    grad_down = matmul_tn(activated, grad_layer_low)
    grad_pre = act_pull(matmul_nt(grad_layer_low, down_weight))[0].astype(bfloat)
    grad_up = matmul_tn(hidden_two, grad_pre)
    grad_norm_two, grad_gain_two, grad_shift_two = norm_backward(
        matmul_nt(grad_pre, up_weight), normed_two, inverse_two, gain_two
    )
    grad_after = grad_layer + grad_norm_two
    grad_after_low = grad_after.astype(bfloat)
    grad_out_weight = matmul_tn(mixed, grad_after_low)
    grad_mixed = matmul_nt(grad_after_low, out_weight).astype(bfloat)
    grad_heads = split_heads(grad_mixed, HEADS)

    def head_backward(parts):
        query_h, key_h, value_h, norm_h, grad_h = parts
        scores = matmul_nt(query_h, key_h) * scale
        probs = jnp.where(key_valid[None, :], jnp.exp(scores - norm_h[:, None]), 0.0)
        grad_value = matmul_tn(probs.astype(bfloat), grad_h)
        grad_probs = matmul_nt(grad_h, value_h)
        grad_scores = (
            probs * (grad_probs - jnp.sum(probs * grad_probs, axis=-1, keepdims=True))
        ).astype(bfloat)
        grad_query = matmul(grad_scores, key_h) * scale
        grad_key = matmul_tn(grad_scores, query_h) * scale
        return (grad_query, grad_key, grad_value)

    grad_query, grad_key, grad_value = lax.map(
        head_backward, (query_heads, key_heads, value_heads, log_norm, grad_heads)
    )
    own_key_grad, own_value_grad = (
        lax.psum_scatter(
            join_heads(grad_key).astype(jnp.bfloat16), "seq", scatter_dimension=0, tiled=True
        ).astype(jnp.float32),
        lax.psum_scatter(
            join_heads(grad_value).astype(jnp.bfloat16), "seq", scatter_dimension=0, tiled=True
        ).astype(jnp.float32),
    )
    grad_qkv = jnp.concatenate(
        [join_heads(grad_query), own_key_grad, own_value_grad], axis=1
    ).astype(bfloat)
    grad_qkv_weight = matmul_tn(hidden_one, grad_qkv)
    grad_norm_one, grad_gain_one, grad_shift_one = norm_backward(
        matmul_nt(grad_qkv, qkv_weight), normed_one, inverse_one, gain_one
    )
    grad_tokens = grad_after + grad_norm_one
    whole_grads = [
        grad.astype(bfloat).reshape(m.shape(n, seq_size))
        for m, grad in zip(matrices, (grad_qkv_weight, grad_out_weight, grad_up, grad_down, grad_unpatch))
    ]
    small_parts = [grad_gain_one, grad_shift_one, grad_gain_two, grad_shift_two]
    small_parts += [grad_w_one, grad_b_one, grad_w_two, grad_b_two]
    flat = jnp.concatenate([part.reshape(-1) for part in small_parts])
    lanes = 128
    padded = -(-flat.shape[0] // (8 * lanes)) * 8 * lanes
    small = jnp.pad(flat, (0, padded - flat.shape[0])).reshape(-1, lanes)
    *block_sums, small_sums = scatter_grads(n, seq_size, matrices, whole_grads, small)
    flat_sums, at, sums = small_sums.reshape(-1), 0, []
    for part in small_parts:
        sums.append(flat_sums[at : at + part.size].reshape(part.shape))
        at += part.size
    own = width // (dp_size * seq_size)
    sum_qkv, sum_out, sum_up, sum_down, sum_unpatch = block_sums
    sum_gain_one, sum_shift_one, sum_gain_two, sum_shift_two = [
        lax.dynamic_slice(part, (device * own,), (own,)) for part in sums[:4]
    ]
    decoder_sums = sums[4:]
    return (
        density[None],
        color_value.T[None],
        grad_tokens[None],
        sum_gain_one,
        sum_shift_one,
        sum_qkv,
        sum_out,
        sum_gain_two,
        sum_shift_two,
        sum_up,
        sum_down,
        sum_unpatch,
        decoder_sums[0],
        decoder_sums[1],
        decoder_sums[2],
        decoder_sums[3],
    )


def solution(mesh):
    in_specs = (
        P("dp", "seq", None),
        P(("dp", "seq")),
        P(("dp", "seq")),
        P("dp", "seq"),
        P("dp", "seq"),
        P(("dp", "seq")),
        P(("dp", "seq")),
        P("dp", "seq"),
        P(("dp", "seq"), None),
        P("dp", "seq"),
        P(),
        P(),
        P(),
        P(),
        P("dp"),
        P("dp", None, "seq"),
        P("dp", "seq"),
        P("dp", None, "seq"),
    )
    out_specs = (
        P("dp", "seq"),
        P("dp", None, "seq"),
        P("dp", "seq", None),
        P(("dp", "seq")),
        P(("dp", "seq")),
        P("dp", "seq"),
        P("dp", "seq"),
        P(("dp", "seq")),
        P(("dp", "seq")),
        P("dp", "seq"),
        P(("dp", "seq"), None),
        P("dp", "seq"),
        P(),
        P(),
        P(),
        P(),
    )
    return jax.shard_map(shards, mesh=mesh, in_specs=in_specs, out_specs=out_specs, check_vma=False)
```

```python
import functools
import math

import jax
import jax.numpy as jnp
from jax import lax
from jax.experimental import pallas as pl
from jax.experimental.pallas import tpu as pltpu
from jax.sharding import PartitionSpec as P

HEADS = 16
PATCH = 8
CH = 32
PRES = 16


EPSILON = 1e-05
NEGATIVE = -1e30
VMEM_LIMIT = 56 * 2**20
AHEAD = 3
LAG = 2


MESH = pl.DeviceIdType.MESH


class Place:
    def __init__(self, n, seq_size):
        dp = lax.axis_index("dp")
        self.n, self.seq_size = n, seq_size
        self.seq = lax.axis_index("seq")
        self.i = (lax.div(dp, n * n), lax.rem(lax.div(dp, n), n), lax.rem(dp, n))
        self.dp = dp

    def size(self, axis):
        return self.seq_size if axis == 3 else self.n

    def me(self, axis):
        return self.seq if axis == 3 else self.i[axis]

    def peer(self, axis, step):
        to = lax.rem(self.me(axis) + step, self.size(axis))
        if axis == 3:
            return to, (self.dp, to)
        where = [to if a == axis else self.i[a] for a in range(3)]
        return to, ((where[0] * self.n + where[1]) * self.n + where[2], self.seq)

    def source(self, axis, step):
        size = self.size(axis)
        return lax.rem(self.me(axis) + (size - step), size)

    def enter(self, axes=(0, 1, 2, 3)):
        barrier = pltpu.get_barrier_semaphore()
        count = 0
        for axis in axes:
            for step in range(1, self.size(axis)):
                pl.semaphore_signal(
                    barrier, inc=1, device_id=self.peer(axis, step)[1], device_id_type=MESH
                )
                count += 1
        pl.semaphore_wait(barrier, count)


def remote(src, dst, send, recv, device):
    return pltpu.make_async_remote_copy(
        src_ref=src, dst_ref=dst, send_sem=send, recv_sem=recv, device_id=device, device_id_type=MESH
    )


class Matrix:
    def __init__(self, name, rows, cols, by_rows, parts):
        self.name, self.rows, self.cols, self.by_rows = name, rows, cols, by_rows
        self.parts = parts if rows % (16 * parts) == 0 else 1

    def shape(self, n, seq_size):
        if self.by_rows:
            return (n, n, n, seq_size, self.rows, self.cols)
        return (n, n, n, self.rows, seq_size * self.cols)

    def tail(self, part, first, count):
        size = self.rows // self.parts
        rows = pl.ds(part * size, size)
        if self.by_rows:
            return (pl.ds(first, count), rows, slice(None))
        if isinstance(first, int):
            return (rows, pl.ds(first * self.cols, count * self.cols))
        return (rows, pl.ds(pl.multiple_of(first * self.cols, 128), count * self.cols))

    def tail_shape(self, count):
        size = self.rows // self.parts
        return (count, size, self.cols) if self.by_rows else (size, count * self.cols)


def small_stage(place, value, slots, send, recv, stage, axis):
    me = place.me(axis)
    slots[stage, me] = value
    copies = []
    for step in range(1, place.size(axis)):
        ref = slots.at[stage, me]
        copy = remote(
            ref, ref, send.at[stage, step - 1], recv.at[stage, step - 1], place.peer(axis, step)[1]
        )
        copy.start()
        copies.append(copy)

    def end():
        for copy in copies:
            copy.wait()
        total = slots[stage, 0]
        for other in range(1, place.size(axis)):
            total = total + slots[stage, other]
        return total

    return end


def small_sum(place, value, slots, send, recv, between=None):
    for stage, axis in enumerate((2, 1, 0, 3)):
        end = small_stage(place, value, slots, send, recv, stage, axis)
        if between is not None:
            between()
        value = end()
    return value


class Gather:
    def __init__(self, place, matrices, refs, sems):
        self.place, self.refs = place, refs
        self.chunks = [(w, m, p) for w, m in enumerate(matrices) for p in range(m.parts)]
        self.seq_send, self.seq_recv, self.hop_send, self.hop_recv, self.far_send, self.far_recv = sems
        self.copies = {}

    def _send(self, key, axis, region, send, recv):
        made = []
        for step in range(1, self.place.size(axis)):
            copy = remote(region, region, send.at[step - 1], recv.at[step - 1], self.place.peer(axis, step)[1])
            copy.start()
            made.append(copy)
        self.copies[key] = made

    def _take(self, key):
        for copy in self.copies[key]:
            copy.wait_recv()

    def region(self, k, index, first, count):
        w, matrix, part = self.chunks[k]
        return self.refs[w].at[index + matrix.tail(part, first, count)]

    def along_seq(self, k):
        p = self.place
        self._send((k, 0), 3, self.region(k, p.i, p.seq, 1), self.seq_send.at[k], self.seq_recv.at[k])

    def hop(self, k, number):
        p, half = self.place, self.place.seq_size // 2
        if number == 0:
            self._take((k, 0))
        else:
            self._take((k, 1, 0))
            self._take((k, 1, 1))
        for h in (0, 1):
            axis = 1 - h if number == 0 else h
            index = [p.i[0], p.i[1], p.i[2]]
            if number == 1:
                index[1 - axis] = slice(None)
            at = 2 * number + h
            region = self.region(k, tuple(index), h * half, half)
            self._send((k, 1 + number, h), axis, region, self.hop_send.at[k, at], self.hop_recv.at[k, at])

    def third(self, k):
        p = self.place
        self._take((k, 2, 0))
        self._take((k, 2, 1))
        region = self.region(k, (slice(None), slice(None), p.i[2]), 0, p.seq_size)
        self._send((k, 3), 2, region, self.far_send.at[k], self.far_recv.at[k])

    def arrived(self, k):
        self._take((k, 3))

    def finish(self):
        for made in self.copies.values():
            for copy in made:
                copy.wait_send()


def gather_sems(n, seq_size, chunks):
    sem = pltpu.SemaphoreType.DMA
    return [sem((chunks, seq_size - 1))] * 2 + [sem((chunks, 4, n - 1))] * 2 + [sem((chunks, n - 1))] * 2


class Scatter:
    def __init__(self, place, matrices, wholes, refs, far, hops, near, outs, sems):
        self.place, self.wholes, self.refs = place, wholes, refs
        self.far, self.hops, self.near, self.outs = far, hops, near, outs
        self.chunks = [(w, m, p) for w, m in enumerate(matrices) for p in range(m.parts)]
        self.seq_send, self.seq_recv, self.hop_send, self.hop_recv, self.far_send, self.far_recv = sems
        self.copies = {}

    def _send(self, key, axis, region_to, slot, send, recv):
        made = []
        for step in range(1, self.place.size(axis)):
            to, device = self.place.peer(axis, step)
            copy = remote(region_to(to), slot(step - 1), send.at[step - 1], recv.at[step - 1], device)
            copy.start()
            made.append(copy)
        self.copies[key] = made

    def _take(self, key):
        for copy in self.copies[key]:
            copy.wait_recv()

    def _index(self, k, index, first, count):
        w, matrix, part = self.chunks[k]
        return index + matrix.tail(part, first, count)

    def third(self, k):
        w, matrix, part = self.chunks[k]
        p, every = self.place, slice(None)
        tail = matrix.tail(part, 0, p.seq_size)
        self._send(
            (k, 3),
            2,
            lambda to: self.wholes[w].at[(every, every, to) + tail],
            lambda s: self.far[w].at[(s, every, every) + tail],
            self.far_send.at[k],
            self.far_recv.at[k],
        )

    def hop(self, k, number):
        w, matrix, part = self.chunks[k]
        p, half, n = self.place, self.place.seq_size // 2, self.place.n
        ref = self.refs[w]
        if number == 0:
            self._take((k, 3))
            tail = matrix.tail(part, 0, p.seq_size)

            @pl.loop(0, n * n)
            def _(at):
                a, b = lax.div(at, n), lax.rem(at, n)
                value = ref[(a, b) + tail].astype(jnp.float32)
                for s in range(n - 1):
                    value = value + self.far[w][(s, a, b) + tail].astype(jnp.float32)
                ref[(a, b) + tail] = value.astype(jnp.bfloat16)

        else:
            for h in (0, 1):
                self._take((k, 1, h))
                tail, local = matrix.tail(part, h * half, half), matrix.tail(part, 0, half)
                for a in range(n):
                    index = (p.i[0], a) if h == 0 else (a, p.i[1])
                    value = ref[index + tail].astype(jnp.float32)
                    for s in range(n - 1):
                        value = value + self.hops[w][(h, s, a) + local].astype(jnp.float32)
                    ref[index + tail] = value.astype(jnp.bfloat16)
        for h in (0, 1):
            axis = h if number == 0 else 1 - h
            tail, local = matrix.tail(part, h * half, half), matrix.tail(part, 0, half)
            other = slice(None) if number == 0 else p.i[1 - axis]
            at = 2 * number + h

            def region_to(to, axis=axis, other=other, tail=tail):
                index = (to, other) if axis == 0 else (other, to)
                return ref.at[index + tail]

            def slot(s, h=h, local=local):
                return self.hops[w].at[(h, s, pl.ds(0, n) if number == 0 else n) + local]

            self._send((k, 1 + number, h), axis, region_to, slot, self.hop_send.at[k, at], self.hop_recv.at[k, at])

    def along_seq(self, k):
        w, matrix, part = self.chunks[k]
        p, half, n = self.place, self.place.seq_size // 2, self.place.n
        ref = self.refs[w]
        for h in (0, 1):
            self._take((k, 2, h))
            tail, local = matrix.tail(part, h * half, half), matrix.tail(part, 0, half)
            value = ref[p.i[:2] + tail].astype(jnp.float32)
            for s in range(n - 1):
                value = value + self.hops[w][(h, s, n) + local].astype(jnp.float32)
            ref[p.i[:2] + tail] = value.astype(jnp.bfloat16)
        size = matrix.rows // matrix.parts
        self._send(
            (k, 0),
            3,
            lambda to: ref.at[p.i[:2] + matrix.tail(part, to, 1)],
            lambda s: self.near[w].at[(s,) + matrix.tail(part, 0, 1)],
            self.seq_send.at[k],
            self.seq_recv.at[k],
        )

    def arrived(self, k):
        w, matrix, part = self.chunks[k]
        p = self.place
        self._take((k, 0))
        value = self.refs[w][p.i[:2] + matrix.tail(part, p.seq, 1)].astype(jnp.float32)
        for s in range(p.seq_size - 1):
            value = value + self.near[w][(s,) + matrix.tail(part, 0, 1)].astype(jnp.float32)
        size = matrix.rows // matrix.parts
        self.outs[w][pl.ds(part * size, size)] = value.reshape(size, matrix.cols)

    def finish(self):
        for made in self.copies.values():
            for copy in made:
                copy.wait_send()


def scatter_kernel(n, seq_size, matrices, *refs):
    count = len(matrices)
    grads, small, outs, small_out = refs[:count], refs[count], refs[count + 1 : 2 * count + 1], refs[2 * count + 1]
    rest = refs[2 * count + 2 :]
    bufs, far, hops, near = [rest[i * count : (i + 1) * count] for i in range(4)]
    slots, small_send, small_recv, in_sem = rest[4 * count : 4 * count + 4]
    sems = rest[4 * count + 4 :]
    place = Place(n, seq_size)
    scatter = Scatter(place, matrices, grads, bufs, far, hops, near, outs, sems)
    total = len(scatter.chunks)
    loads = []
    for k, (w, matrix, part) in enumerate(scatter.chunks):
        tail, every = matrix.tail(part, 0, seq_size), (slice(None),) * 2
        copy = pltpu.make_async_copy(
            grads[w].at[every + (place.i[2],) + tail], bufs[w].at[every + tail], in_sem.at[k]
        )
        copy.start()
        loads.append(copy)
    place.enter()
    for t in range(total + 8):
        if t < total:
            scatter.third(t)
        if 0 <= t - 2 < total:
            loads[t - 2].wait()
            scatter.hop(t - 2, 0)
        if 0 <= t - 4 < total:
            scatter.hop(t - 4, 1)
        if 0 <= t - 6 < total:
            scatter.along_seq(t - 6)
        if 0 <= t - 8 < total:
            scatter.arrived(t - 8)
        if t == 8:
            small_out[...] = small_sum(place, small[...], slots, small_send, small_recv)
    scatter.finish()


def scatter_grads(n, seq_size, matrices, grads, small):
    chunks = sum(m.parts for m in matrices)
    vmem, any_space = pl.BlockSpec(memory_space=pltpu.VMEM), pl.BlockSpec(memory_space=pl.ANY)
    shapes = [m.shape(n, seq_size) for m in matrices]
    largest = max(n, seq_size)
    bfloat = jnp.bfloat16
    return pl.pallas_call(
        functools.partial(scatter_kernel, n, seq_size, matrices),
        out_shape=[jax.ShapeDtypeStruct((m.rows, m.cols), jnp.float32) for m in matrices]
        + [jax.ShapeDtypeStruct(small.shape, jnp.float32)],
        in_specs=[any_space] * len(matrices) + [vmem],
        out_specs=[vmem] * (len(matrices) + 1),
        scratch_shapes=[pltpu.VMEM((n, n) + s[3:], bfloat) for s in shapes]
        + [pltpu.VMEM((n - 1, n, n) + s[3:], bfloat) for s in shapes]
        + [
            pltpu.VMEM(
                (2, n - 1, n + 1)
                + ((seq_size // 2, m.rows, m.cols) if m.by_rows else (m.rows, seq_size // 2 * m.cols)),
                bfloat,
            )
            for m in matrices
        ]
        + [
            pltpu.VMEM((seq_size - 1,) + ((1, m.rows, m.cols) if m.by_rows else (m.rows, m.cols)), bfloat)
            for m in matrices
        ]
        + [
            pltpu.VMEM((4, largest) + small.shape, jnp.float32),
            pltpu.SemaphoreType.DMA((4, largest - 1)),
            pltpu.SemaphoreType.DMA((4, largest - 1)),
            pltpu.SemaphoreType.DMA((chunks,)),
        ]
        + gather_sems(n, seq_size, chunks),
        compiler_params=pltpu.CompilerParams(
            collective_id=1, has_side_effects=True, vmem_limit_bytes=VMEM_LIMIT
        ),
    )(*grads, small)


def gelu_parts(x):
    cdf = 0.5 + 0.5 * lax.erf(x * (0.5**0.5))
    return x * cdf, cdf + x * (jnp.exp(-0.5 * x * x) * (2.0 * math.pi) ** -0.5)


def split_low(x):
    high = x.astype(jnp.bfloat16)
    return high, (x - high.astype(jnp.float32)).astype(jnp.bfloat16)


def texel_place(texel, seq_size, me):
    side, quarter = PRES * PATCH, PRES * PRES // seq_size
    row, col = texel // side, texel % side
    token = row // PATCH * PRES + col // PATCH
    a, b = row % PATCH, col % PATCH
    fold = PATCH // 2
    mine = token // quarter == me
    key = jnp.where(mine, a // 2 * quarter + token % quarter, -1)
    return key, a % 2 * PATCH + b, fold


def decode_kernel(
    n,
    seq_size,
    tile,
    texels,
    index,
    w1,
    b1,
    w2,
    b2,
    d_density,
    d_color,
    density,
    color,
    grad_texels,
    g_w1,
    g_b1,
    g_w2,
    g_b2,
    tables,
    grad_tables,
    features,
    part_out,
    part_in,
    own_part,
    grad_all,
    sems,
):
    send_sem, recv_sem, back_send, back_recv = sems
    place = Place(n, seq_size)
    bfloat, f32 = jnp.bfloat16, jnp.float32
    samples = index.shape[2]
    quarter = PRES * PRES // seq_size
    width = texels.shape[1]
    groups = 2 * PATCH
    cols = groups * CH
    depth = width // cols * quarter
    hidden = w1.shape[1]
    place.enter((3,))
    for p in range(3):
        own = texels[p * quarter : (p + 1) * quarter].astype(f32)
        stacked = jnp.concatenate([own[:, i * cols : (i + 1) * cols] for i in range(width // cols)], axis=0)
        tables[p] = stacked.T.astype(bfloat)
    w1_high, w1_low = split_low(w1[...])
    w1_stack = jnp.concatenate([w1_high, w1_low], axis=1)
    tiles = samples // tile

    def one_hot(source, at, p):
        texel = index[source, pl.ds(p, 1), at]
        key, group, _ = texel_place(texel, seq_size, place.seq)
        rows = lax.broadcasted_iota(jnp.int32, (depth, tile), 0)
        return (rows == key).astype(f32).astype(bfloat), group

    def forward(source):
        @pl.loop(0, tiles)
        def _(t):
            at = pl.ds(pl.multiple_of(t * tile, tile), tile)
            picked = []
            for p in range(3):
                hot, group = one_hot(source, at, p)
                spread = matmul(tables[p], hot)
                total = jnp.where(group == 0, spread[:CH], 0.0)
                for g in range(1, groups):
                    total = total + jnp.where(group == g, spread[g * CH : (g + 1) * CH], 0.0)
                picked.append(total)
            feature = jnp.concatenate(picked, axis=0).astype(bfloat)
            features[source, :, at] = feature
            both = matmul_tn(w1_stack, feature)
            part = both[:hidden] + both[hidden:]
            own_part[:, at] = part
            part_out[source, :, at] = part.astype(bfloat)

    copies = []
    for step in range(1, seq_size):
        to, device = place.peer(3, step)
        forward(to)
        copy = remote(part_out.at[to], part_in.at[step - 1], send_sem.at[step - 1], recv_sem.at[step - 1], device)
        copy.start()
        copies.append(copy)
    forward(place.seq)
    pre = own_part[...] + b1[...]
    for step, copy in enumerate(copies):
        copy.wait_recv()
        pre = pre + part_in[step].astype(f32)
    act, slope = gelu_parts(pre)
    highest = lax.Precision.HIGHEST
    out = lax.dot_general(
        w2[...], act, (((0,), (0,)), ((), ())), precision=highest, preferred_element_type=f32
    ) + b2[...]
    gate = 1.0 / (1.0 + jnp.exp(-out))
    first = out[:1]
    density[...] = jnp.maximum(first, 0.0) + jnp.log1p(jnp.exp(-jnp.abs(first)))
    color[...] = gate[1:4]
    grad_out = jnp.concatenate(
        [
            d_density[...] * gate[:1],
            d_color[...] * gate[1:4] * (1.0 - gate[1:4]),
            jnp.zeros((w2.shape[1] - 4, samples), f32),
        ],
        axis=0,
    )
    grad_pre = jnp.dot(w2[...], grad_out, precision=highest, preferred_element_type=f32) * slope
    me = place.seq
    grad_all[me] = grad_pre.astype(bfloat)
    backs = []
    for step in range(1, seq_size):
        ref = grad_all.at[me]
        copy = remote(ref, ref, back_send.at[step - 1], back_recv.at[step - 1], place.peer(3, step)[1])
        copy.start()
        backs.append(copy)
    g_w2[...] = lax.dot_general(
        grad_out, act, (((1,), (1,)), ((), ())), precision=highest, preferred_element_type=f32
    )
    g_b2[...] = jnp.sum(grad_out, axis=1, keepdims=True)
    g_b1[...] = jnp.sum(grad_pre, axis=1, keepdims=True)
    g_w1[...] = jnp.zeros(g_w1.shape, f32)
    grad_tables[...] = jnp.zeros(grad_tables.shape, f32)

    def backward(source):
        @pl.loop(0, tiles)
        def _(t):
            at = pl.ds(pl.multiple_of(t * tile, tile), tile)
            grad = grad_all[source, :, at]
            g_w1[...] += matmul_nt(features[source, :, at], grad)
            grad_feature = matmul(w1_high, grad) + matmul(w1_low, grad)
            for p in range(3):
                hot, group = one_hot(source, at, p)
                mine = grad_feature[p * CH : (p + 1) * CH]
                spread = jnp.concatenate(
                    [jnp.where(group == g, mine, 0.0) for g in range(groups)], axis=0
                ).astype(bfloat)
                grad_tables[p] += matmul_nt(spread, hot)

    backward(me)
    for step, copy in enumerate(backs):
        copy.wait_recv()
        backward(place.source(3, step + 1))
    for p in range(3):
        back = grad_tables[p].T
        for i in range(width // cols):
            grad_texels[p * quarter : (p + 1) * quarter, i * cols : (i + 1) * cols] = back[
                i * quarter : (i + 1) * quarter
            ].astype(bfloat)
    for copy in copies + backs:
        copy.wait_send()


def decode(n, seq_size, texels, index, dec_w1, dec_b1, dec_w2, dec_b2, d_density, d_color):
    bfloat, f32 = jnp.bfloat16, jnp.float32
    samples, hidden = index.shape[2], dec_w1.shape[1]
    rows = 8
    w2 = jnp.pad(dec_w2, ((0, 0), (0, rows - dec_w2.shape[1])))
    b2 = jnp.pad(dec_b2, (0, rows - dec_b2.shape[0]))[:, None]
    quarter = PRES * PRES // seq_size
    cols = 2 * PATCH * CH
    depth = texels.shape[1] // cols * quarter
    vmem = pl.BlockSpec(memory_space=pltpu.VMEM)
    sem = pltpu.SemaphoreType.DMA((seq_size - 1,))

    def kernel(*refs):
        decode_kernel(n, seq_size, min(512, samples), *refs[:-4], refs[-4:])

    return pl.pallas_call(
        kernel,
        out_shape=[
            jax.ShapeDtypeStruct((1, samples), f32),
            jax.ShapeDtypeStruct((3, samples), f32),
            jax.ShapeDtypeStruct(texels.shape, bfloat),
            jax.ShapeDtypeStruct(dec_w1.shape, f32),
            jax.ShapeDtypeStruct((hidden, 1), f32),
            jax.ShapeDtypeStruct((rows, hidden), f32),
            jax.ShapeDtypeStruct((rows, 1), f32),
        ],
        in_specs=[vmem] * 8,
        out_specs=[vmem] * 7,
        scratch_shapes=[
            pltpu.VMEM((3, cols, depth), bfloat),
            pltpu.VMEM((3, cols, depth), f32),
            pltpu.VMEM((seq_size, 3 * CH, samples), bfloat),
            pltpu.VMEM((seq_size, hidden, samples), bfloat),
            pltpu.VMEM((seq_size - 1, hidden, samples), bfloat),
            pltpu.VMEM((hidden, samples), f32),
            pltpu.VMEM((seq_size, hidden, samples), bfloat),
            sem,
            sem,
            sem,
            sem,
        ],
        compiler_params=pltpu.CompilerParams(
            collective_id=2, has_side_effects=True, vmem_limit_bytes=VMEM_LIMIT
        ),
        cost_estimate=pl.CostEstimate(flops=16 * 10**9, bytes_accessed=4 * 10**6, transcendentals=0),
    )(texels, index, dec_w1, dec_b1[:, None], w2, b2, d_density, d_color)


def columns(ref, first, count):
    block = ref[..., pl.ds(first, count)]
    return block.reshape(-1, count)


def normalize(values):
    center = values - jnp.mean(values, axis=-1, keepdims=True)
    inverse = lax.rsqrt(jnp.mean(center * center, axis=-1, keepdims=True) + EPSILON)
    return center * inverse, inverse


def forward_kernel(n, seq_size, matrices, *refs):
    count = len(matrices)
    refs = list(refs)

    def take(k):
        taken = refs[:k]
        del refs[:k]
        return taken

    shards = take(count)
    tokens, gains, index, valid = take(4)
    wholes = take(count)
    gains_out, index_out, hidden_all, query, keys, values, mixed = take(7)
    normed_one, inverse_one, normed_two, inverse_two, hidden_two, act, slope, planes, texels = take(9)
    bufs = take(count)
    after, index_send, index_recv, hidden_send, hidden_recv, slots, small_send, small_recv, out_sem = take(9)
    bfloat, f32 = jnp.bfloat16, jnp.float32
    place = Place(n, seq_size)
    for matrix, shard, buf in zip(matrices, shards, bufs):
        if matrix.by_rows:
            buf[place.i + (place.seq,)] = shard[...].astype(bfloat)
        else:
            at = pl.ds(pl.multiple_of(place.seq * matrix.cols, 128), matrix.cols)
            buf[place.i + (slice(None), at)] = shard[...].astype(bfloat)
    index_out[place.seq] = index[...]
    place.enter()
    gather = Gather(place, matrices, bufs, refs)
    total = len(gather.chunks)
    outs = []
    state = [0]

    def advance():
        t = state[0]
        state[0] += 1
        if t < total:
            gather.hop(t, 0)
            if t + AHEAD < total:
                gather.along_seq(t + AHEAD)
        if 0 <= t - LAG < total:
            gather.hop(t - LAG, 1)
        if 0 <= t - 2 * LAG < total:
            gather.third(t - 2 * LAG)
        k = t - 3 * LAG
        if 0 <= k < total:
            gather.arrived(k)
            w, matrix, part = gather.chunks[k]
            at = (slice(None),) * 3 + matrix.tail(part, 0, seq_size)
            copy = pltpu.make_async_copy(bufs[w].at[at], wholes[w].at[at], out_sem.at[k])
            copy.start()
            outs.append(copy)

    def advance_to(weight):
        last = max(k for k, (w, _, _) in enumerate(gather.chunks) if w == weight)
        while state[0] <= last + 3 * LAG:
            advance()

    def spread(ref, send, recv):
        copies = []
        for step in range(1, seq_size):
            copy = remote(ref, ref, send.at[step - 1], recv.at[step - 1], place.peer(3, step)[1])
            copy.start()
            copies.append(copy)
        return copies

    for k in range(AHEAD):
        gather.along_seq(k)
    later = spread(index_out.at[place.seq], index_send, index_recv)
    normed, inverse = normalize(tokens[...])
    normed_one[...] = normed
    inverse_one[...] = inverse
    gain_sum = small_sum(place, gains[...], slots, small_send, small_recv, advance)
    gains_out[...] = gain_sum.astype(bfloat).astype(f32)
    hidden_all[place.seq] = (normed_one[...] * gains_out[0:1] + gains_out[1:2]).astype(bfloat)
    hidden_copies = spread(hidden_all.at[place.seq], hidden_send, hidden_recv)
    w_qkv, w_out, w_up, w_down, w_unpatch = bufs
    width = tokens.shape[1]
    tile = 512
    advance_to(0)
    for at in range(0, width, tile):
        query[:, at : at + tile] = matmul(hidden_all[place.seq], columns(w_qkv, at, tile)).astype(bfloat)
    for copy in hidden_copies:
        copy.wait_recv()
    hidden = hidden_all[...].reshape(-1, width)

    @pl.loop(0, width // tile)
    def _(t):
        at = pl.multiple_of(t * tile, tile)
        keys[:, pl.ds(at, tile)] = matmul(hidden, columns(w_qkv, at + width, tile)).astype(bfloat)
        values[:, pl.ds(at, tile)] = matmul(hidden, columns(w_qkv, at + 2 * width, tile)).astype(bfloat)

    advance()
    pair = 2 * width // HEADS
    scale = (width // HEADS) ** (-0.5)
    rows = tokens.shape[0]
    first = lax.broadcasted_iota(jnp.int32, (rows, pair), 1) < pair // 2
    pairs, segments = HEADS // 2, 4
    for segment in range(segments):

        @pl.loop(segment * pairs // segments, (segment + 1) * pairs // segments)
        def _(p):
            at = pl.ds(pl.multiple_of(p * pair, pair), pair)
            query_two, key_two, value_two = query[:, at].astype(f32) * scale, keys[:, at], values[:, at]
            made = []
            for mine in (first, ~first):
                scores = matmul_nt(jnp.where(mine, query_two, 0.0).astype(bfloat), key_two)
                scores = jnp.where(valid[...] > 0.0, scores, NEGATIVE)
                expo = jnp.exp(scores - jnp.max(scores, axis=-1, keepdims=True))
                probs = expo * (1.0 / jnp.sum(expo, axis=-1, keepdims=True))
                made.append(matmul(probs.astype(bfloat), value_two))
            mixed[:, at] = jnp.where(first, made[0], made[1]).astype(bfloat)

        advance()
    advance_to(1)
    for at in range(0, width, tile):
        after[:, at : at + tile] = tokens[:, at : at + tile] + matmul(mixed[...], columns(w_out, at, tile))
    normed, inverse = normalize(after[...])
    normed_two[...] = normed
    inverse_two[...] = inverse
    hidden_two[...] = (normed * gains_out[2:3] + gains_out[3:4]).astype(bfloat)
    advance_to(2)

    @pl.loop(0, act.shape[1] // tile)
    def _(t):
        at = pl.multiple_of(t * tile, tile)
        value, rate = gelu_parts(matmul(hidden_two[...], columns(w_up, at, tile)))
        act[:, pl.ds(at, tile)] = value.astype(bfloat)
        slope[:, pl.ds(at, tile)] = rate.astype(bfloat)

    advance_to(3)
    deep = act.shape[1] // n
    for i in range(n):
        block = w_down[i].reshape(deep, width)
        for at in range(0, width, tile):
            after[:, at : at + tile] += matmul(act[:, i * deep : (i + 1) * deep], block[:, at : at + tile])
    planes[...] = after[: planes.shape[0]].astype(bfloat)
    advance_to(4)
    while state[0] < total + 3 * LAG:
        advance()
    for at in range(0, texels.shape[1], tile):
        texels[:, at : at + tile] = matmul(planes[...], columns(w_unpatch, at, tile)).astype(bfloat)
    gather.finish()
    for copy in later:
        copy.wait()
    for copy in hidden_copies:
        copy.wait_send()
    for copy in outs:
        copy.wait()


def forward_layer(n, seq_size, matrices, shards, tokens, gains, index, valid):
    chunks = sum(m.parts for m in matrices)
    vmem, any_space = pl.BlockSpec(memory_space=pltpu.VMEM), pl.BlockSpec(memory_space=pl.ANY)
    shapes = [m.shape(n, seq_size) for m in matrices]
    largest = max(n, seq_size)
    bfloat, f32 = jnp.bfloat16, jnp.float32
    rows, width = tokens.shape
    plane_rows = 3 * PRES * PRES // seq_size
    ff = matrices[2].cols * seq_size
    results = [
        ((8, width), f32),
        ((seq_size,) + index.shape, jnp.int32),
        ((seq_size, rows, width), bfloat),
        ((rows, width), bfloat),
        ((seq_size * rows, width), bfloat),
        ((seq_size * rows, width), bfloat),
        ((rows, width), bfloat),
        ((rows, width), f32),
        ((rows, 1), f32),
        ((rows, width), f32),
        ((rows, 1), f32),
        ((rows, width), bfloat),
        ((rows, ff), bfloat),
        ((rows, ff), bfloat),
        ((plane_rows, width), bfloat),
        ((plane_rows, matrices[4].cols * seq_size), bfloat),
    ]
    sem = pltpu.SemaphoreType.DMA
    made = pl.pallas_call(
        functools.partial(forward_kernel, n, seq_size, matrices),
        out_shape=[jax.ShapeDtypeStruct(s, bfloat) for s in shapes]
        + [jax.ShapeDtypeStruct(s, t) for s, t in results],
        in_specs=[vmem] * (len(matrices) + 4),
        out_specs=[any_space] * len(matrices) + [vmem] * len(results),
        scratch_shapes=[pltpu.VMEM(s, bfloat) for s in shapes]
        + [pltpu.VMEM((rows, width), f32)]
        + [sem((seq_size - 1,))] * 4
        + [pltpu.VMEM((4, largest) + gains.shape, f32)]
        + [sem((4, largest - 1))] * 2
        + [sem((chunks,))]
        + gather_sems(n, seq_size, chunks),
        compiler_params=pltpu.CompilerParams(
            collective_id=0, has_side_effects=True, vmem_limit_bytes=VMEM_LIMIT
        ),
    )(*shards, tokens, gains, index, valid)
    return made[: len(matrices)], made[len(matrices) :]


def weight_list(shards):
    names = ("qkv", "out", "up", "down", "unpatch")
    parts = (4, 1, 4, 4, 2)
    return tuple(
        Matrix(name, shard.shape[0], shard.shape[1], name == "down", part)
        for name, shard, part in zip(names, shards, parts)
    )


def matmul(left, right):
    return jnp.dot(left, right, preferred_element_type=jnp.float32)


def matmul_tn(left, right):
    return lax.dot_general(
        left, right, (((0,), (0,)), ((), ())), preferred_element_type=jnp.float32
    )


def matmul_nt(left, right):
    return lax.dot_general(
        left, right, (((1,), (1,)), ((), ())), preferred_element_type=jnp.float32
    )


def gelu_exact(values):
    return jax.nn.gelu(values, approximate=False)


def norm_forward(values, gain, shift):
    center = values - jnp.mean(values, axis=-1, keepdims=True)
    inverse = lax.rsqrt(jnp.mean(center * center, axis=-1, keepdims=True) + EPSILON)
    normed = center * inverse
    return (normed * gain + shift, normed, inverse)


def norm_backward(grad, normed, inverse, gain):
    scaled = grad * gain
    inner = scaled - jnp.mean(scaled, axis=-1, keepdims=True)
    inner = inner - normed * jnp.mean(scaled * normed, axis=-1, keepdims=True)
    return (inner * inverse, jnp.sum(grad * normed, axis=0), jnp.sum(grad, axis=0))


def split_heads(matrix, heads):
    return matrix.reshape(matrix.shape[0], heads, matrix.shape[1] // heads).transpose(1, 0, 2)


def join_heads(stacked):
    return stacked.transpose(1, 0, 2).reshape(stacked.shape[1], stacked.shape[0] * stacked.shape[2])


def shards(
    tokens,
    ln1_gain,
    ln1_bias,
    w_qkv,
    w_out,
    ln2_gain,
    ln2_bias,
    w_up,
    w_down,
    w_unpatch,
    dec_w1,
    dec_b1,
    dec_w2,
    dec_b2,
    counts,
    sample_texels,
    d_density,
    d_color,
):
    seq_size = lax.axis_size("seq")
    dp_size = lax.axis_size("dp")
    quarter = PRES * PRES // seq_size
    plane_dev = 3 * quarter
    rows_in = tokens[0]
    tok_dev = rows_in.shape[0]
    width = rows_in.shape[1]
    head_dim = width // HEADS
    scale = head_dim ** (-0.5)
    bfloat = jnp.bfloat16
    n = round(dp_size ** (1 / 3))
    shards_of = (w_qkv, w_out, w_up, w_down, w_unpatch)
    matrices = weight_list(shards_of)
    device = lax.axis_index("dp") * seq_size + lax.axis_index("seq")
    gains = jnp.stack([ln1_gain, ln1_bias, ln2_gain, ln2_bias])
    spread = jnp.zeros((8, width), jnp.float32)
    spread = lax.dynamic_update_slice(spread, gains, (0, device * gains.shape[1]))
    position = jnp.arange(seq_size * tok_dev, dtype=jnp.int32)
    owner = position // tok_dev
    offset = position % tok_dev
    key_valid = (offset < plane_dev) | (
        owner * (tok_dev - plane_dev) + offset - plane_dev < counts[0]
    )
    wholes, made = forward_layer(
        n, seq_size, matrices, shards_of, rows_in, spread, sample_texels[0], key_valid.astype(jnp.float32)[None]
    )
    gains_all, index_all, hidden_all, query, keys_all, values_all, mixed = made[:7]
    normed_one, inverse_one, normed_two, inverse_two, hidden_two, activated, slope, plane_rows, own_texels = made[7:]
    qkv_weight, out_weight, up_weight, down_weight, unpatch_weight = [
        w.reshape(-1, w.shape[-1]) for w in wholes
    ]
    gain_one, gain_two = gains_all[0], gains_all[2]
    hidden_one = lax.dynamic_index_in_dim(hidden_all, lax.axis_index("seq"), 0, keepdims=False)
    density, color_value, own_grad_texels, grad_w_one, grad_b_one, grad_w_two, grad_b_two = decode(
        n, seq_size, own_texels, index_all, dec_w1, dec_b1, dec_w2, dec_b2, d_density, d_color[0]
    )
    grad_b_one, grad_w_two, grad_b_two = grad_b_one[:, 0], grad_w_two[:4].T, grad_b_two[:4, 0]
    query_heads = split_heads(query, HEADS)
    key_heads = split_heads(keys_all, HEADS)
    value_heads = split_heads(values_all, HEADS)
    grad_planes = matmul_nt(own_grad_texels, unpatch_weight)
    grad_unpatch = matmul_tn(plane_rows, own_grad_texels)
    grad_layer = jnp.concatenate(
        [grad_planes, jnp.zeros((tok_dev - plane_dev, width), jnp.float32)], axis=0
    )
    grad_layer_low = grad_layer.astype(bfloat)
    grad_down = matmul_tn(activated, grad_layer_low)
    grad_pre = (matmul_nt(grad_layer_low, down_weight) * slope.astype(jnp.float32)).astype(bfloat)
    grad_up = matmul_tn(hidden_two, grad_pre)
    grad_norm_two, grad_gain_two, grad_shift_two = norm_backward(
        matmul_nt(grad_pre, up_weight), normed_two, inverse_two, gain_two
    )
    grad_after = grad_layer + grad_norm_two
    grad_after_low = grad_after.astype(bfloat)
    grad_out_weight = matmul_tn(mixed, grad_after_low)
    grad_mixed = matmul_nt(grad_after_low, out_weight).astype(bfloat)
    grad_heads = split_heads(grad_mixed, HEADS)

    def head_backward(parts):
        query_h, key_h, value_h, grad_h = parts
        scores = jnp.where(key_valid[None, :], matmul_nt(query_h, key_h) * scale, NEGATIVE)
        probs = jax.nn.softmax(scores, axis=-1)
        grad_value = matmul_tn(probs.astype(bfloat), grad_h)
        grad_probs = matmul_nt(grad_h, value_h)
        grad_scores = (
            probs * (grad_probs - jnp.sum(probs * grad_probs, axis=-1, keepdims=True))
        ).astype(bfloat)
        grad_query = matmul(grad_scores, key_h) * scale
        grad_key = matmul_tn(grad_scores, query_h) * scale
        return (grad_query, grad_key, grad_value)

    grad_query, grad_key, grad_value = lax.map(
        head_backward, (query_heads, key_heads, value_heads, grad_heads)
    )
    own_key_grad, own_value_grad = (
        lax.psum_scatter(
            join_heads(grad_key).astype(jnp.bfloat16), "seq", scatter_dimension=0, tiled=True
        ).astype(jnp.float32),
        lax.psum_scatter(
            join_heads(grad_value).astype(jnp.bfloat16), "seq", scatter_dimension=0, tiled=True
        ).astype(jnp.float32),
    )
    grad_qkv = jnp.concatenate(
        [join_heads(grad_query), own_key_grad, own_value_grad], axis=1
    ).astype(bfloat)
    grad_qkv_weight = matmul_tn(hidden_one, grad_qkv)
    grad_norm_one, grad_gain_one, grad_shift_one = norm_backward(
        matmul_nt(grad_qkv, qkv_weight), normed_one, inverse_one, gain_one
    )
    grad_tokens = grad_after + grad_norm_one
    whole_grads = [
        grad.astype(bfloat).reshape(m.shape(n, seq_size))
        for m, grad in zip(matrices, (grad_qkv_weight, grad_out_weight, grad_up, grad_down, grad_unpatch))
    ]
    small_parts = [grad_gain_one, grad_shift_one, grad_gain_two, grad_shift_two]
    small_parts += [grad_w_one, grad_b_one, grad_w_two, grad_b_two]
    flat = jnp.concatenate([part.reshape(-1) for part in small_parts])
    lanes = 128
    padded = -(-flat.shape[0] // (8 * lanes)) * 8 * lanes
    small = jnp.pad(flat, (0, padded - flat.shape[0])).reshape(-1, lanes)
    *block_sums, small_sums = scatter_grads(n, seq_size, matrices, whole_grads, small)
    flat_sums, at, sums = small_sums.reshape(-1), 0, []
    for part in small_parts:
        sums.append(flat_sums[at : at + part.size].reshape(part.shape))
        at += part.size
    own = width // (dp_size * seq_size)
    sum_qkv, sum_out, sum_up, sum_down, sum_unpatch = block_sums
    sum_gain_one, sum_shift_one, sum_gain_two, sum_shift_two = [
        lax.dynamic_slice(part, (device * own,), (own,)) for part in sums[:4]
    ]
    decoder_sums = sums[4:]
    return (
        density,
        color_value[None],
        grad_tokens[None],
        sum_gain_one,
        sum_shift_one,
        sum_qkv,
        sum_out,
        sum_gain_two,
        sum_shift_two,
        sum_up,
        sum_down,
        sum_unpatch,
        decoder_sums[0],
        decoder_sums[1],
        decoder_sums[2],
        decoder_sums[3],
    )


def solution(mesh):
    in_specs = (
        P("dp", "seq", None),
        P(("dp", "seq")),
        P(("dp", "seq")),
        P("dp", "seq"),
        P("dp", "seq"),
        P(("dp", "seq")),
        P(("dp", "seq")),
        P("dp", "seq"),
        P(("dp", "seq"), None),
        P("dp", "seq"),
        P(),
        P(),
        P(),
        P(),
        P("dp"),
        P("dp", None, "seq"),
        P("dp", "seq"),
        P("dp", None, "seq"),
    )
    out_specs = (
        P("dp", "seq"),
        P("dp", None, "seq"),
        P("dp", "seq", None),
        P(("dp", "seq")),
        P(("dp", "seq")),
        P("dp", "seq"),
        P("dp", "seq"),
        P(("dp", "seq")),
        P(("dp", "seq")),
        P("dp", "seq"),
        P(("dp", "seq"), None),
        P("dp", "seq"),
        P(),
        P(),
        P(),
        P(),
    )
    return jax.shard_map(shards, mesh=mesh, in_specs=in_specs, out_specs=out_specs, check_vma=False)
```

```python
import functools
import math

import jax
import jax.numpy as jnp
from jax import lax
from jax.experimental import pallas as pl
from jax.experimental.pallas import tpu as pltpu
from jax.sharding import PartitionSpec as P

HEADS = 16
PATCH = 8
CH = 32
PRES = 16


EPSILON = 1e-05
NEGATIVE = -1e30
VMEM_LIMIT = 58 * 2**20
AHEAD = 3
LAG = 2


MESH = pl.DeviceIdType.MESH


class Place:
    def __init__(self, n, seq_size):
        dp = lax.axis_index("dp")
        self.n, self.seq_size = n, seq_size
        self.seq = lax.axis_index("seq")
        self.i = (lax.div(dp, n * n), lax.rem(lax.div(dp, n), n), lax.rem(dp, n))
        self.dp = dp

    def size(self, axis):
        return self.seq_size if axis == 3 else self.n

    def me(self, axis):
        return self.seq if axis == 3 else self.i[axis]

    def peer(self, axis, step):
        to = lax.rem(self.me(axis) + step, self.size(axis))
        if axis == 3:
            return to, (self.dp, to)
        where = [to if a == axis else self.i[a] for a in range(3)]
        return to, ((where[0] * self.n + where[1]) * self.n + where[2], self.seq)

    def source(self, axis, step):
        size = self.size(axis)
        return lax.rem(self.me(axis) + (size - step), size)

    def enter(self, axes=(0, 1, 2, 3)):
        barrier = pltpu.get_barrier_semaphore()
        count = 0
        for axis in axes:
            for step in range(1, self.size(axis)):
                pl.semaphore_signal(
                    barrier, inc=1, device_id=self.peer(axis, step)[1], device_id_type=MESH
                )
                count += 1
        pl.semaphore_wait(barrier, count)


def remote(src, dst, send, recv, device):
    return pltpu.make_async_remote_copy(
        src_ref=src, dst_ref=dst, send_sem=send, recv_sem=recv, device_id=device, device_id_type=MESH
    )


class Matrix:
    def __init__(self, name, rows, cols, by_rows, parts):
        self.name, self.rows, self.cols, self.by_rows = name, rows, cols, by_rows
        self.parts = parts if rows % (16 * parts) == 0 else 1

    def shape(self, n, seq_size):
        if self.by_rows:
            return (n, n, n, seq_size, self.rows, self.cols)
        return (n, n, n, self.rows, seq_size * self.cols)

    def tail(self, part, first, count):
        size = self.rows // self.parts
        rows = pl.ds(part * size, size)
        if self.by_rows:
            return (pl.ds(first, count), rows, slice(None))
        if isinstance(first, int):
            return (rows, pl.ds(first * self.cols, count * self.cols))
        return (rows, pl.ds(pl.multiple_of(first * self.cols, 128), count * self.cols))

    def tail_shape(self, count):
        size = self.rows // self.parts
        return (count, size, self.cols) if self.by_rows else (size, count * self.cols)


def small_stage(place, value, slots, send, recv, stage, axis):
    me = place.me(axis)
    slots[stage, me] = value
    copies = []
    for step in range(1, place.size(axis)):
        ref = slots.at[stage, me]
        copy = remote(
            ref, ref, send.at[stage, step - 1], recv.at[stage, step - 1], place.peer(axis, step)[1]
        )
        copy.start()
        copies.append(copy)

    def end():
        for copy in copies:
            copy.wait()
        total = slots[stage, 0]
        for other in range(1, place.size(axis)):
            total = total + slots[stage, other]
        return total

    return end


def small_sum(place, value, slots, send, recv, between=None):
    for stage, axis in enumerate((2, 1, 0, 3)):
        end = small_stage(place, value, slots, send, recv, stage, axis)
        if between is not None:
            between()
        value = end()
    return value


class Gather:
    def __init__(self, place, matrices, refs, sems):
        self.place, self.refs = place, refs
        self.chunks = [(w, m, p) for w, m in enumerate(matrices) for p in range(m.parts)]
        self.seq_send, self.seq_recv, self.hop_send, self.hop_recv, self.far_send, self.far_recv = sems
        self.copies = {}

    def _send(self, key, axis, region, send, recv):
        made = []
        for step in range(1, self.place.size(axis)):
            copy = remote(region, region, send.at[step - 1], recv.at[step - 1], self.place.peer(axis, step)[1])
            copy.start()
            made.append(copy)
        self.copies[key] = made

    def _take(self, key):
        for copy in self.copies[key]:
            copy.wait_recv()

    def region(self, k, index, first, count):
        w, matrix, part = self.chunks[k]
        return self.refs[w].at[index + matrix.tail(part, first, count)]

    def along_seq(self, k):
        p = self.place
        self._send((k, 0), 3, self.region(k, p.i, p.seq, 1), self.seq_send.at[k], self.seq_recv.at[k])

    def hop(self, k, number):
        p, half = self.place, self.place.seq_size // 2
        if number == 0:
            self._take((k, 0))
        else:
            self._take((k, 1, 0))
            self._take((k, 1, 1))
        for h in (0, 1):
            axis = 1 - h if number == 0 else h
            index = [p.i[0], p.i[1], p.i[2]]
            if number == 1:
                index[1 - axis] = slice(None)
            at = 2 * number + h
            region = self.region(k, tuple(index), h * half, half)
            self._send((k, 1 + number, h), axis, region, self.hop_send.at[k, at], self.hop_recv.at[k, at])

    def third(self, k):
        p = self.place
        self._take((k, 2, 0))
        self._take((k, 2, 1))
        region = self.region(k, (slice(None), slice(None), p.i[2]), 0, p.seq_size)
        self._send((k, 3), 2, region, self.far_send.at[k], self.far_recv.at[k])

    def arrived(self, k):
        self._take((k, 3))

    def finish(self):
        for made in self.copies.values():
            for copy in made:
                copy.wait_send()


def gather_sems(n, seq_size, chunks):
    sem = pltpu.SemaphoreType.DMA
    return [sem((chunks, seq_size - 1))] * 2 + [sem((chunks, 4, n - 1))] * 2 + [sem((chunks, n - 1))] * 2


def gelu_parts(x):
    cdf = 0.5 + 0.5 * lax.erf(x * (0.5**0.5))
    return x * cdf, cdf + x * (jnp.exp(-0.5 * x * x) * (2.0 * math.pi) ** -0.5)


def split_low(x):
    high = x.astype(jnp.bfloat16)
    return high, (x - high.astype(jnp.float32)).astype(jnp.bfloat16)


def texel_place(texel, seq_size, me):
    side, quarter = PRES * PATCH, PRES * PRES // seq_size
    row, col = texel // side, texel % side
    token = row // PATCH * PRES + col // PATCH
    a, b = row % PATCH, col % PATCH
    fold = PATCH // 2
    mine = token // quarter == me
    key = jnp.where(mine, a // 2 * quarter + token % quarter, -1)
    return key, a % 2 * PATCH + b, fold


def decode_both(
    place,
    grad_texels,
    tile,
    texels,
    index,
    w1,
    b1,
    w2,
    b2,
    d_density,
    d_color,
    density,
    color,
    g_w1,
    g_b1,
    g_w2,
    g_b2,
    tables,
    grad_tables,
    features,
    part_out,
    part_in,
    own_part,
    grad_all,
    send_sem,
    recv_sem,
    back_send,
    back_recv,
):
    seq_size = place.seq_size
    bfloat, f32 = jnp.bfloat16, jnp.float32
    samples = index.shape[2]
    quarter = PRES * PRES // seq_size
    width = texels.shape[1]
    groups = 2 * PATCH
    cols = groups * CH
    depth = width // cols * quarter
    hidden = w1.shape[1]
    for p in range(3):
        own = texels[p * quarter : (p + 1) * quarter].astype(f32)
        stacked = jnp.concatenate([own[:, i * cols : (i + 1) * cols] for i in range(width // cols)], axis=0)
        tables[p] = stacked.T.astype(bfloat)
    w1_high, w1_low = split_low(w1[...])
    w1_stack = jnp.concatenate([w1_high, w1_low], axis=1)
    tiles = samples // tile

    def one_hot(source, at, p):
        texel = index[source, pl.ds(p, 1), at]
        key, group, _ = texel_place(texel, seq_size, place.seq)
        rows = lax.broadcasted_iota(jnp.int32, (depth, tile), 0)
        return (rows == key).astype(f32).astype(bfloat), group

    def forward(source):
        @pl.loop(0, tiles)
        def _(t):
            at = pl.ds(pl.multiple_of(t * tile, tile), tile)
            picked = []
            for p in range(3):
                hot, group = one_hot(source, at, p)
                spread = matmul(tables[p], hot)
                total = jnp.where(group == 0, spread[:CH], 0.0)
                for g in range(1, groups):
                    total = total + jnp.where(group == g, spread[g * CH : (g + 1) * CH], 0.0)
                picked.append(total)
            feature = jnp.concatenate(picked, axis=0).astype(bfloat)
            features[source, :, at] = feature
            both = matmul_tn(w1_stack, feature)
            part = both[:hidden] + both[hidden:]
            own_part[:, at] = part
            part_out[source, :, at] = part.astype(bfloat)

    copies = []
    for step in range(1, seq_size):
        to, device = place.peer(3, step)
        forward(to)
        copy = remote(part_out.at[to], part_in.at[step - 1], send_sem.at[step - 1], recv_sem.at[step - 1], device)
        copy.start()
        copies.append(copy)
    forward(place.seq)
    pre = own_part[...] + b1[...]
    for step, copy in enumerate(copies):
        copy.wait_recv()
        pre = pre + part_in[step].astype(f32)
    act, slope = gelu_parts(pre)
    highest = lax.Precision.HIGHEST
    out = lax.dot_general(
        w2[...], act, (((0,), (0,)), ((), ())), precision=highest, preferred_element_type=f32
    ) + b2[...]
    gate = 1.0 / (1.0 + jnp.exp(-out))
    first = out[:1]
    density[...] = jnp.maximum(first, 0.0) + jnp.log1p(jnp.exp(-jnp.abs(first)))
    color[...] = gate[1:4]
    grad_out = jnp.concatenate(
        [
            d_density[...] * gate[:1],
            d_color[...] * gate[1:4] * (1.0 - gate[1:4]),
            jnp.zeros((w2.shape[1] - 4, samples), f32),
        ],
        axis=0,
    )
    grad_pre = jnp.dot(w2[...], grad_out, precision=highest, preferred_element_type=f32) * slope
    me = place.seq
    grad_all[me] = grad_pre.astype(bfloat)
    backs = []
    for step in range(1, seq_size):
        ref = grad_all.at[me]
        copy = remote(ref, ref, back_send.at[step - 1], back_recv.at[step - 1], place.peer(3, step)[1])
        copy.start()
        backs.append(copy)
    g_w2[...] = lax.dot_general(
        grad_out, act, (((1,), (1,)), ((), ())), precision=highest, preferred_element_type=f32
    )
    g_b2[...] = jnp.sum(grad_out, axis=1, keepdims=True)
    g_b1[...] = jnp.sum(grad_pre, axis=1, keepdims=True)
    g_w1[...] = jnp.zeros(g_w1.shape, f32)
    grad_tables[...] = jnp.zeros(grad_tables.shape, f32)

    def backward(source):
        @pl.loop(0, tiles)
        def _(t):
            at = pl.ds(pl.multiple_of(t * tile, tile), tile)
            grad = grad_all[source, :, at]
            g_w1[...] += matmul_nt(features[source, :, at], grad)
            grad_feature = matmul(w1_high, grad) + matmul(w1_low, grad)
            for p in range(3):
                hot, group = one_hot(source, at, p)
                mine = grad_feature[p * CH : (p + 1) * CH]
                spread = jnp.concatenate(
                    [jnp.where(group == g, mine, 0.0) for g in range(groups)], axis=0
                ).astype(bfloat)
                grad_tables[p] += matmul_nt(spread, hot)

    backward(me)
    for step, copy in enumerate(backs):
        copy.wait_recv()
        backward(place.source(3, step + 1))
    for p in range(3):
        back = grad_tables[p].T
        for i in range(width // cols):
            block = back[i * quarter : (i + 1) * quarter].astype(bfloat)
            grad_texels[p * quarter : (p + 1) * quarter, i * cols : (i + 1) * cols] = block
    for copy in copies + backs:
        copy.wait_send()


def core_columns(ref, n, segment, to):
    width = ref.shape[1]
    parts = width // (n * segment)
    if segment % 128 == 0:
        places = [pl.multiple_of((q * n + to) * segment, 128) for q in range(parts)]
        return jnp.concatenate([ref[:, pl.ds(at, segment)] for at in places], axis=1).T
    place = lax.broadcasted_iota(jnp.int32, (width, width // n), 1)
    source = (lax.div(place, segment) * n + to) * segment + lax.rem(place, segment)
    pick = lax.broadcasted_iota(jnp.int32, (width, width // n), 0) == source
    return matmul(ref[...], pick.astype(jnp.float32).astype(jnp.bfloat16)).astype(jnp.bfloat16).T


class Exchange:
    def __init__(self, place, send, recv):
        self.place, self.send, self.recv = place, send, recv
        self.made, self.used = [], 0

    def _start(self, source_of, buf):
        copies, p = [], self.place
        for step in range(1, p.size(2)):
            to, device = p.peer(2, step)
            sems = (self.send.at[self.used, step - 1], self.recv.at[self.used, step - 1])
            copy = remote(source_of(step, to), buf.at[p.i[2]], *sems, device)
            copy.start()
            copies.append(copy)
        self.used += 1
        self.made += copies

        def wait():
            for copy in copies:
                copy.wait_recv()

        return wait

    def columns(self, ref, segment, split, buf):
        p = self.place
        for step in range(1, p.size(2)):
            split[step - 1] = core_columns(ref, p.n, segment, p.peer(2, step)[0])
        wait = self._start(lambda step, to: split.at[step - 1], buf)
        buf[p.i[2]] = core_columns(ref, p.n, segment, p.i[2])
        return wait

    def rows(self, buf):
        return self._start(lambda step, to: buf.at[self.place.i[2]], buf)

    def finish(self):
        for copy in self.made:
            copy.wait_send()


def weight_grad(left, right, grad, first=0, tile=512):
    shape, width = grad.shape[:-1], right.shape[-1]
    for at in range(0, width, tile):
        size = min(tile, width - at)
        block = matmul(left[0], right[0, :, at : at + size])
        for i in range(1, left.shape[0]):
            block = block + matmul(left[i], right[i, :, at : at + size])
        grad[..., first + at : first + at + size] = block.astype(jnp.bfloat16).reshape(shape + (size,))


def norm_back(grad, normed, inverse, gain):
    scaled = grad * gain
    inner = scaled - jnp.mean(scaled, axis=-1, keepdims=True)
    inner = inner - normed * jnp.mean(scaled * normed, axis=-1, keepdims=True)
    return inner * inverse


def feed_back(place, matrices, refs):
    (planes, act, slope, hidden_two, normed_two, inverse_two, gains, weights) = refs[:8]
    (grads_out, grad_after, norm_grads, bufs) = refs[8:12]
    (planes_split, planes_all, act_split, act_all, hidden_split, hidden_all) = refs[12:18]
    (texels_all, layer_all, pre_all, layer, load_sem, out_sem, send, recv) = refs[18:26]
    grads = [buf.at[0] for buf in bufs]
    n = place.n
    bfloat, f32 = jnp.bfloat16, jnp.float32
    up, down, unpatch = matrices
    w_up, w_down, w_unpatch = bufs
    exchange = Exchange(place, send, recv)
    me = place.i[2]
    loads, waits = [], []

    def start():
        for k in (2, 1, 0):
            copy = pltpu.make_async_copy(weights[k], bufs[k], load_sem.at[k])
            copy.start()
            loads.append(copy)

    def start_remote():
        waits.append(exchange.columns(planes, unpatch.rows, planes_split, planes_all))
        waits.append(exchange.columns(act, place.seq_size * down.rows, act_split, act_all))
        waits.append(exchange.columns(hidden_two, up.rows, hidden_split, hidden_all))

    outs = []

    def put(k):
        copy = pltpu.make_async_copy(grads[k], grads_out[k], out_sem.at[k])
        copy.start()
        outs.append(copy)

    def end():
        got_texels = exchange.rows(texels_all)
        loads[0].wait()
        grad_texels = texels_all[me]
        step = layer.shape[1] // n
        for i in range(n):
            block = w_unpatch[i].reshape(step, -1)
            layer[:, i * step : (i + 1) * step] = matmul_nt(grad_texels, block)
        layer_all[me] = layer[...].astype(bfloat)
        got_layer = exchange.rows(layer_all)
        loads[1].wait()
        step = act.shape[1] // (n * n)
        for i in range(n):
            for j in range(n):
                block = w_down[i, j].reshape(step, -1)
                at = (i * n + j) * step
                value = matmul_nt(layer_all[me], block) * slope[:, at : at + step].astype(f32)
                pre_all[me, :, at : at + step] = value.astype(bfloat)
        got_pre = exchange.rows(pre_all)
        waits[0]()
        got_texels()
        weight_grad(planes_all, texels_all, grads[2])
        put(2)
        loads[2].wait()
        step = layer.shape[1] // n
        pieces = []
        for i in range(n):
            block = w_up[i].reshape(step, -1)
            pieces.append(matmul_nt(pre_all[me], block))
        grad = jnp.concatenate(pieces, axis=1)
        normed = normed_two[...]
        norm_grads[0:1] = jnp.sum(grad * normed, axis=0, keepdims=True)
        norm_grads[1:2] = jnp.sum(grad, axis=0, keepdims=True)
        grad_after[...] = layer[...] + norm_back(grad, normed, inverse_two[...], gains[2:3])
        waits[1]()
        got_layer()
        weight_grad(act_all, layer_all, grads[1])
        put(1)
        waits[2]()
        got_pre()
        weight_grad(hidden_all, pre_all, grads[0])
        put(0)
        exchange.finish()
        for copy in outs:
            copy.wait()

    return start, start_remote, end


def middle_kernel(n, seq_size, matrices, *refs):
    refs = list(refs)

    def take(k):
        taken = refs[:k]
        del refs[:k]
        return taken

    decode_in, feed_in, weights = take(8), take(7), take(3)
    density, color, g_w1, g_b1, g_w2, g_b2, grad_after, norm_grads = take(8)
    grads_out, bufs, decode_scratch = take(3), take(3), take(11)
    place = Place(n, seq_size)
    feed = list(feed_in) + [weights, grads_out, grad_after, norm_grads, bufs] + refs
    texels_all = refs[6]
    start, start_remote, end = feed_back(place, matrices, feed)
    start()
    place.enter((2, 3))
    start_remote()
    tile = min(512, decode_in[1].shape[2])
    outs = (density, color, g_w1, g_b1, g_w2, g_b2)
    decode_both(place, texels_all.at[place.i[2]], tile, *decode_in, *outs, *decode_scratch)
    end()


def middle(n, seq_size, matrices, decode_in, feed_in, weights):
    texels, index, dec_w1, dec_b1, dec_w2, dec_b2, d_density, d_color = decode_in
    planes, act, slope, hidden_two, normed_two, inverse_two, gains = feed_in
    bfloat, f32 = jnp.bfloat16, jnp.float32
    samples, hidden = index.shape[2], dec_w1.shape[1]
    slots = 8
    w2 = jnp.pad(dec_w2, ((0, 0), (0, slots - dec_w2.shape[1])))
    b2 = jnp.pad(dec_b2, (0, slots - dec_b2.shape[0]))[:, None]
    quarter = PRES * PRES // seq_size
    cols = 2 * PATCH * CH
    depth = texels.shape[1] // cols * quarter
    vmem, any_space = pl.BlockSpec(memory_space=pltpu.VMEM), pl.BlockSpec(memory_space=pl.ANY)
    sem = pltpu.SemaphoreType.DMA
    rows, width = normed_two.shape
    ff, core_ff = act.shape[1], act.shape[1] // n
    shapes = [m.shape(n, seq_size) for m in matrices]
    halves = [(n, n) + s[3:] for s in shapes]
    return pl.pallas_call(
        functools.partial(middle_kernel, n, seq_size, matrices),
        out_shape=[
            jax.ShapeDtypeStruct((1, samples), f32),
            jax.ShapeDtypeStruct((3, samples), f32),
            jax.ShapeDtypeStruct(dec_w1.shape, f32),
            jax.ShapeDtypeStruct((hidden, 1), f32),
            jax.ShapeDtypeStruct((slots, hidden), f32),
            jax.ShapeDtypeStruct((slots, 1), f32),
            jax.ShapeDtypeStruct((rows, width), f32),
            jax.ShapeDtypeStruct((2, width), f32),
        ]
        + [jax.ShapeDtypeStruct(s, bfloat) for s in halves],
        in_specs=[vmem] * 15 + [any_space] * 3,
        out_specs=[vmem] * 8 + [any_space] * 3,
        scratch_shapes=[pltpu.VMEM(s, bfloat) for s in shapes]
        + [
            pltpu.VMEM((3, cols, depth), bfloat),
            pltpu.VMEM((3, cols, depth), f32),
            pltpu.VMEM((seq_size, 3 * CH, samples), bfloat),
            pltpu.VMEM((seq_size, hidden, samples), bfloat),
            pltpu.VMEM((seq_size - 1, hidden, samples), bfloat),
            pltpu.VMEM((hidden, samples), f32),
            pltpu.VMEM((seq_size, hidden, samples), bfloat),
        ]
        + [sem((seq_size - 1,))] * 4
        + [
            pltpu.VMEM((n - 1, width // n, rows), bfloat),
            pltpu.VMEM((n, width // n, rows), bfloat),
            pltpu.VMEM((n - 1, core_ff, rows), bfloat),
            pltpu.VMEM((n, core_ff, rows), bfloat),
            pltpu.VMEM((n - 1, width // n, rows), bfloat),
            pltpu.VMEM((n, width // n, rows), bfloat),
            pltpu.VMEM((n,) + texels.shape, bfloat),
            pltpu.VMEM((n, rows, width), bfloat),
            pltpu.VMEM((n, rows, ff), bfloat),
            pltpu.VMEM((rows, width), f32),
            sem((3,)),
            sem((3,)),
        ]
        + [sem((8, n - 1))] * 2,
        compiler_params=pltpu.CompilerParams(
            collective_id=2, has_side_effects=True, vmem_limit_bytes=VMEM_LIMIT
        ),
    )(texels, index, dec_w1, dec_b1[:, None], w2, b2, d_density, d_color, *feed_in, *weights)


class Scatter:
    def __init__(self, place, matrices, sources, kept, hops, near, outs, sems):
        self.place, self.sources, self.kept = place, sources, kept
        self.hops, self.near, self.outs = hops, near, outs
        self.chunks = [(w, m, p) for w, m in enumerate(matrices) for p in range(m.parts)]
        self.load_sem, self.seq_send, self.seq_recv, self.hop_send, self.hop_recv = sems
        self.copies, self.loads = {}, {}

    def _send(self, key, axis, region_to, slot, send, recv):
        made = []
        for step in range(1, self.place.size(axis)):
            to, device = self.place.peer(axis, step)
            copy = remote(region_to(to), slot(step - 1), send.at[step - 1], recv.at[step - 1], device)
            copy.start()
            made.append(copy)
        self.copies[key] = made

    def _take(self, key):
        for copy in self.copies[key]:
            copy.wait_recv()

    def hop(self, k, number):
        w, matrix, part = self.chunks[k]
        p, half, n = self.place, self.place.seq_size // 2, self.place.n
        kept, every = self.kept[w], slice(None)
        local = matrix.tail(part, 0, half)
        if number == 0:
            for h in (0, 1):
                index = (p.i[0], every) if h == 0 else (every, p.i[1])
                source = self.sources[w].at[index + matrix.tail(part, h * half, half)]
                copy = pltpu.make_async_copy(source, kept.at[(h, every) + local], self.load_sem.at[k, h])
                copy.start()
                self.loads[k, h] = copy
        else:
            for h in (0, 1):
                self.loads[k, h].wait()
                self._take((k, 1, h))
                for a in range(n):
                    value = kept[(h, a) + local].astype(jnp.float32)
                    for s in range(n - 1):
                        value = value + self.hops[w][(h, s, a) + local].astype(jnp.float32)
                    kept[(h, a) + local] = value.astype(jnp.bfloat16)
        for h in (0, 1):
            axis = h if number == 0 else 1 - h
            tail, at = matrix.tail(part, h * half, half), 2 * number + h

            def region_to(to, h=h, tail=tail):
                if number == 1:
                    return kept.at[(h, to) + local]
                return self.sources[w].at[((to, every) if h == 0 else (every, to)) + tail]

            def slot(s, h=h):
                return self.hops[w].at[(h, s, pl.ds(0, n) if number == 0 else n) + local]

            self._send((k, 1 + number, h), axis, region_to, slot, self.hop_send.at[k, at], self.hop_recv.at[k, at])

    def _block(self, matrix, part, j):
        p, half = self.place, self.place.seq_size // 2
        h = lax.div(j, half)
        return (h, p.i[1] + h * (p.i[0] - p.i[1])) + matrix.tail(part, lax.rem(j, half), 1)

    def along_seq(self, k):
        w, matrix, part = self.chunks[k]
        p, half, n = self.place, self.place.seq_size // 2, self.place.n
        kept = self.kept[w]
        local = matrix.tail(part, 0, half)
        for h in (0, 1):
            self._take((k, 2, h))
            value = kept[(h, p.i[1 - h]) + local].astype(jnp.float32)
            for s in range(n - 1):
                value = value + self.hops[w][(h, s, n) + local].astype(jnp.float32)
            kept[(h, p.i[1 - h]) + local] = value.astype(jnp.bfloat16)
        self._send(
            (k, 0),
            3,
            lambda to: kept.at[self._block(matrix, part, to)],
            lambda s: self.near[w].at[(s,) + matrix.tail(part, 0, 1)],
            self.seq_send.at[k],
            self.seq_recv.at[k],
        )

    def arrived(self, k):
        w, matrix, part = self.chunks[k]
        p = self.place
        self._take((k, 0))
        value = self.kept[w][self._block(matrix, part, p.seq)].astype(jnp.float32)
        for s in range(p.seq_size - 1):
            value = value + self.near[w][(s,) + matrix.tail(part, 0, 1)].astype(jnp.float32)
        size = matrix.rows // matrix.parts
        self.outs[w][pl.ds(part * size, size)] = value.reshape(size, matrix.cols)

    def finish(self):
        for made in self.copies.values():
            for copy in made:
                copy.wait_send()


def backward_kernel(n, seq_size, matrices, *refs):
    count = len(matrices)
    refs = list(refs)

    def take(k):
        taken = refs[:k]
        del refs[:k]
        return taken

    grad_after, mixed, query, normed_one, inverse_one, gains, valid, small = take(8)
    w_out_in, w_qkv_in, keys_in, values_in, hidden_all_in = take(5)
    early = take(count - 2)
    outs = take(count)
    g_tokens, small_out = take(2)
    w_out, w_qkv, work = take(3)
    g_out, g_qkv = w_out.at[0], w_qkv.at[0]
    kept, hops, near = take(count), take(count), take(count)
    mixed_split, mixed_all, after_all, hidden_split, hidden_core, own_split, own_core = take(7)
    query_all, grad_all, hidden_in = take(3)
    grad_mixed, load_sem, core_send, core_recv, hidden_send, hidden_recv = take(6)
    slots, small_send, small_recv = take(3)
    sems = refs
    bfloat, f32 = jnp.bfloat16, jnp.float32
    place = Place(n, seq_size)
    me = place.i[2]
    loads = []
    rows, width = query.shape
    token_rows = normed_one.shape[0]
    keys, values = grad_all.at[me, :, pl.ds(0, width)], grad_all.at[me, :, pl.ds(width, width)]
    for k, (source, target) in enumerate(
        ((hidden_all_in, work), (w_out_in, w_out), (keys_in, keys), (values_in, values), (w_qkv_in, w_qkv))
    ):
        copy = pltpu.make_async_copy(source, target, load_sem.at[k])
        copy.start()
        loads.append(copy)
    place.enter()
    scatter = Scatter(place, matrices, list(early) + [g_out, g_qkv], kept, hops, near, outs, sems)
    total = len(scatter.chunks)
    state = [0]

    def advance():
        t = state[0]
        state[0] += 1
        if t < total:
            scatter.hop(t, 0)
        if 0 <= t - LAG < total:
            scatter.hop(t - LAG, 1)
        if 0 <= t - 2 * LAG < total:
            scatter.along_seq(t - 2 * LAG)
        if 0 <= t - 3 * LAG < total:
            scatter.arrived(t - 3 * LAG)

    advance()
    advance()
    exchange = Exchange(place, core_send, core_recv)
    out_matrix, qkv_matrix = matrices[-2:]
    got_mixed = exchange.columns(mixed, out_matrix.rows, mixed_split, mixed_all)
    after_all[me] = grad_after[...].astype(bfloat)
    got_after = exchange.rows(after_all)
    loads[0].wait()
    own = work.at[pl.ds(pl.multiple_of(place.seq * token_rows, 16), rows)]
    got_own = exchange.columns(own, qkv_matrix.rows, own_split, own_core)
    got_hidden = exchange.columns(work, qkv_matrix.rows, hidden_split, hidden_core)
    loads[1].wait()
    step = width // n
    for i in range(n):
        block = w_out[i].reshape(step, width)
        grad_mixed[:, i * step : (i + 1) * step] = matmul_nt(after_all[me], block).astype(bfloat)
    got_mixed()
    got_after()
    weight_grad(mixed_all, after_all, g_out)
    loads[2].wait()
    loads[3].wait()
    pair = 2 * width // HEADS
    scale = (width // HEADS) ** (-0.5)
    first = lax.broadcasted_iota(jnp.int32, (rows, pair), 1) < pair // 2
    pairs, segments = HEADS // 2, 4
    for segment in range(segments):

        @pl.loop(segment * pairs // segments, (segment + 1) * pairs // segments)
        def _(p):
            at = pl.ds(pl.multiple_of(p * pair, pair), pair)
            query_two, grad_two = query[:, at].astype(f32) * scale, grad_mixed[:, at].astype(f32)
            later = pl.ds(pl.multiple_of(width + p * pair, pair), pair)
            key_two, value_two = grad_all[me, :, at], grad_all[me, :, later]
            key_turned = key_two.T
            grad_key, grad_value, turned = 0.0, 0.0, []
            for h, mine in enumerate((first, ~first)):
                query_h = jnp.where(mine, query_two, 0.0).astype(bfloat)
                grad_h = jnp.where(mine, grad_two, 0.0).astype(bfloat)
                scores = jnp.where(valid[...] > 0.0, matmul_nt(key_two, query_h), NEGATIVE)
                expo = jnp.exp(scores - jnp.max(scores, axis=0, keepdims=True))
                probs = expo * (1.0 / jnp.sum(expo, axis=0, keepdims=True))
                grad_value = grad_value + matmul(probs.astype(bfloat), grad_h)
                grad_probs = matmul_nt(value_two, grad_h)
                inner = jnp.sum(probs * grad_probs, axis=0, keepdims=True)
                grad_scores = (probs * (grad_probs - inner)).astype(bfloat)
                grad_key = grad_key + matmul(grad_scores, query_h)
                grad_query = matmul(key_turned, grad_scores)
                turned.append(grad_query[h * (pair // 2) : (h + 1) * (pair // 2)])
            query_all[me, :, at] = (jnp.concatenate(turned, axis=0) * scale).T.astype(bfloat)
            grad_all[me, :, at] = grad_key.astype(bfloat)
            grad_all[me, :, later] = grad_value.astype(bfloat)

        advance()
    got_grad = exchange.rows(grad_all)
    got_query = exchange.rows(query_all)
    loads[4].wait()
    for i in range(n):
        block = w_qkv[i].reshape(step, 3 * width)
        work[:, i * step : (i + 1) * step] = matmul_nt(grad_all[me], block[:, width:]).astype(bfloat)
    pieces = [matmul_nt(query_all[me], w_qkv[i].reshape(step, 3 * width)[:, :width]) for i in range(n)]
    from_query = jnp.concatenate(pieces, axis=1)
    hidden_copies = []
    for s in range(1, seq_size):
        to, device = place.peer(3, s)
        source = work.at[pl.ds(pl.multiple_of(to * token_rows, 16), token_rows)]
        copy = remote(source, hidden_in.at[s - 1], hidden_send.at[s - 1], hidden_recv.at[s - 1], device)
        copy.start()
        hidden_copies.append(copy)
    advance()
    got_grad()
    got_query()
    got_hidden()
    got_own()
    weight_grad(own_core, query_all, g_qkv)
    weight_grad(hidden_core, grad_all, g_qkv, width)
    advance()
    grad = work[pl.ds(pl.multiple_of(place.seq * token_rows, 16), token_rows)].astype(f32)
    rest = jnp.zeros((token_rows - rows, width), f32)
    grad = grad + jnp.concatenate([from_query, rest], axis=0)
    advance()
    for s, copy in enumerate(hidden_copies):
        copy.wait_recv()
        grad = grad + hidden_in[s].astype(f32)
    normed = normed_one[...]
    g_tokens[...] = norm_back(grad, normed, inverse_one[...], gains[0:1])
    g_tokens[0:rows] += grad_after[...]
    gain_row = jnp.sum(grad * normed, axis=0, keepdims=True)
    shift_row = jnp.sum(grad, axis=0, keepdims=True)
    slots_in = jnp.concatenate([gain_row, shift_row, small[2:]], axis=0)
    small_out[...] = small_sum(place, slots_in, slots, small_send, small_recv, advance)
    while state[0] < total + 3 * LAG:
        advance()
    scatter.finish()
    exchange.finish()
    for copy in hidden_copies:
        copy.wait_send()


def half_tail(matrix, seq_size):
    half = seq_size // 2
    if matrix.by_rows:
        return (half, matrix.rows, matrix.cols)
    return (matrix.rows, half * matrix.cols)


def backward_attention(n, seq_size, matrices, inputs, loaded, early):
    grad_after, mixed, query, normed_one, inverse_one, gains, valid, small = inputs
    bfloat, f32 = jnp.bfloat16, jnp.float32
    vmem, any_space = pl.BlockSpec(memory_space=pltpu.VMEM), pl.BlockSpec(memory_space=pl.ANY)
    shapes = [m.shape(n, seq_size) for m in matrices]
    chunks = sum(m.parts for m in matrices)
    rows, width = query.shape
    all_rows = loaded[2].shape[0]
    largest = max(n, seq_size)
    sem = pltpu.SemaphoreType.DMA
    return pl.pallas_call(
        functools.partial(backward_kernel, n, seq_size, matrices),
        out_shape=[jax.ShapeDtypeStruct((m.rows, m.cols), f32) for m in matrices]
        + [jax.ShapeDtypeStruct(normed_one.shape, f32), jax.ShapeDtypeStruct(small.shape, f32)],
        in_specs=[vmem] * len(inputs) + [any_space] * (len(loaded) + len(early)),
        out_specs=[vmem] * (len(matrices) + 2),
        scratch_shapes=[pltpu.VMEM(x.shape, bfloat) for x in loaded[:3]]
        + [pltpu.VMEM((2, n) + half_tail(m, seq_size), bfloat) for m in matrices]
        + [pltpu.VMEM((2, n - 1, n + 1) + half_tail(m, seq_size), bfloat) for m in matrices]
        + [pltpu.VMEM((seq_size - 1,) + ((1, m.rows, m.cols) if m.by_rows else (m.rows, m.cols)), bfloat) for m in matrices]
        + [
            pltpu.VMEM((n - 1, width // n, rows), bfloat),
            pltpu.VMEM((n, width // n, rows), bfloat),
            pltpu.VMEM((n, rows, width), bfloat),
            pltpu.VMEM((n - 1, width // n, all_rows), bfloat),
            pltpu.VMEM((n, width // n, all_rows), bfloat),
            pltpu.VMEM((n - 1, width // n, rows), bfloat),
            pltpu.VMEM((n, width // n, rows), bfloat),
            pltpu.VMEM((n, rows, width), bfloat),
            pltpu.VMEM((n, all_rows, 2 * width), bfloat),
            pltpu.VMEM((seq_size - 1,) + normed_one.shape, bfloat),
            pltpu.VMEM((rows, width), bfloat),
            sem((len(loaded),)),
        ]
        + [sem((8, n - 1))] * 2
        + [sem((seq_size - 1,))] * 2
        + [pltpu.VMEM((4, largest) + small.shape, f32)]
        + [sem((4, largest - 1))] * 2
        + [sem((chunks, 2))]
        + [sem((chunks, seq_size - 1))] * 2
        + [sem((chunks, 4, n - 1))] * 2,
        compiler_params=pltpu.CompilerParams(
            collective_id=1, has_side_effects=True, vmem_limit_bytes=VMEM_LIMIT
        ),
    )(*inputs, *loaded, *early)


def columns(ref, first, count):
    block = ref[..., pl.ds(first, count)]
    return block.reshape(-1, count)


def normalize(values):
    center = values - jnp.mean(values, axis=-1, keepdims=True)
    inverse = lax.rsqrt(jnp.mean(center * center, axis=-1, keepdims=True) + EPSILON)
    return center * inverse, inverse


def forward_kernel(n, seq_size, matrices, *refs):
    count = len(matrices)
    refs = list(refs)

    def take(k):
        taken = refs[:k]
        del refs[:k]
        return taken

    shards = take(count)
    tokens, gains, index, valid = take(4)
    wholes = take(count)
    gains_out, index_out, hidden_all, query, keys, values, mixed = take(7)
    normed_one, inverse_one, normed_two, inverse_two, hidden_two, act, slope, planes, texels = take(9)
    bufs = take(count)
    after, index_send, index_recv, hidden_send, hidden_recv, slots, small_send, small_recv, out_sem = take(9)
    bfloat, f32 = jnp.bfloat16, jnp.float32
    place = Place(n, seq_size)
    for matrix, shard, buf in zip(matrices, shards, bufs):
        if matrix.by_rows:
            buf[place.i + (place.seq,)] = shard[...].astype(bfloat)
        else:
            at = pl.ds(pl.multiple_of(place.seq * matrix.cols, 128), matrix.cols)
            buf[place.i + (slice(None), at)] = shard[...].astype(bfloat)
    index_out[place.seq] = index[...]
    place.enter()
    gather = Gather(place, matrices, bufs, refs)
    total = len(gather.chunks)
    outs = []
    state = [0]

    def advance():
        t = state[0]
        state[0] += 1
        if t < total:
            gather.hop(t, 0)
            if t + AHEAD < total:
                gather.along_seq(t + AHEAD)
        if 0 <= t - LAG < total:
            gather.hop(t - LAG, 1)
        if 0 <= t - 2 * LAG < total:
            gather.third(t - 2 * LAG)
        k = t - 3 * LAG
        if 0 <= k < total:
            gather.arrived(k)
            w, matrix, part = gather.chunks[k]
            at = (slice(None),) * 3 + matrix.tail(part, 0, seq_size)
            copy = pltpu.make_async_copy(bufs[w].at[at], wholes[w].at[at], out_sem.at[k])
            copy.start()
            outs.append(copy)

    def advance_to(weight):
        last = max(k for k, (w, _, _) in enumerate(gather.chunks) if w == weight)
        while state[0] <= last + 3 * LAG:
            advance()

    def spread(ref, send, recv):
        copies = []
        for step in range(1, seq_size):
            copy = remote(ref, ref, send.at[step - 1], recv.at[step - 1], place.peer(3, step)[1])
            copy.start()
            copies.append(copy)
        return copies

    for k in range(AHEAD):
        gather.along_seq(k)
    later = spread(index_out.at[place.seq], index_send, index_recv)
    normed, inverse = normalize(tokens[...])
    normed_one[...] = normed
    inverse_one[...] = inverse
    gain_sum = small_sum(place, gains[...], slots, small_send, small_recv, advance)
    gains_out[...] = gain_sum.astype(bfloat).astype(f32)
    hidden_all[place.seq] = (normed_one[...] * gains_out[0:1] + gains_out[1:2]).astype(bfloat)
    hidden_copies = spread(hidden_all.at[place.seq], hidden_send, hidden_recv)
    w_qkv, w_out, w_up, w_down, w_unpatch = bufs
    width = tokens.shape[1]
    tile = 512
    advance_to(0)
    for at in range(0, width, tile):
        own = hidden_all[place.seq, pl.ds(0, query.shape[0])]
        query[:, at : at + tile] = matmul(own, columns(w_qkv, at, tile)).astype(bfloat)
    for copy in hidden_copies:
        copy.wait_recv()

    @pl.loop(0, width // tile)
    def _(t):
        at = pl.multiple_of(t * tile, tile)
        hidden = hidden_all[...].reshape(-1, width)
        keys[:, pl.ds(at, tile)] = matmul(hidden, columns(w_qkv, at + width, tile)).astype(bfloat)
        values[:, pl.ds(at, tile)] = matmul(hidden, columns(w_qkv, at + 2 * width, tile)).astype(bfloat)

    advance()
    pair = 2 * width // HEADS
    scale = (width // HEADS) ** (-0.5)
    rows = query.shape[0]
    first = lax.broadcasted_iota(jnp.int32, (rows, pair), 1) < pair // 2
    pairs, segments = HEADS // 2, 4
    for segment in range(segments):

        @pl.loop(segment * pairs // segments, (segment + 1) * pairs // segments)
        def _(p):
            at = pl.ds(pl.multiple_of(p * pair, pair), pair)
            query_two, key_two, value_two = query[:, at].astype(f32) * scale, keys[:, at], values[:, at]
            made = []
            for mine in (first, ~first):
                scores = matmul_nt(jnp.where(mine, query_two, 0.0).astype(bfloat), key_two)
                scores = jnp.where(valid[...] > 0.0, scores, NEGATIVE)
                expo = jnp.exp(scores - jnp.max(scores, axis=-1, keepdims=True))
                probs = expo * (1.0 / jnp.sum(expo, axis=-1, keepdims=True))
                made.append(matmul(probs.astype(bfloat), value_two))
            mixed[:, at] = jnp.where(first, made[0], made[1]).astype(bfloat)

        advance()
    advance_to(1)
    for at in range(0, width, tile):
        after[:, at : at + tile] = tokens[:rows, at : at + tile] + matmul(mixed[...], columns(w_out, at, tile))
    normed, inverse = normalize(after[...])
    normed_two[...] = normed
    inverse_two[...] = inverse
    hidden_two[...] = (normed * gains_out[2:3] + gains_out[3:4]).astype(bfloat)
    advance_to(2)

    @pl.loop(0, act.shape[1] // tile)
    def _(t):
        at = pl.multiple_of(t * tile, tile)
        value, rate = gelu_parts(matmul(hidden_two[...], columns(w_up, at, tile)))
        act[:, pl.ds(at, tile)] = value.astype(bfloat)
        slope[:, pl.ds(at, tile)] = rate.astype(bfloat)

    advance_to(3)
    deep = act.shape[1] // n
    for i in range(n):
        block = w_down[i].reshape(deep, width)
        for at in range(0, width, tile):
            after[:, at : at + tile] += matmul(act[:, i * deep : (i + 1) * deep], block[:, at : at + tile])
    planes[...] = after[...].astype(bfloat)
    advance_to(4)
    while state[0] < total + 3 * LAG:
        advance()
    for at in range(0, texels.shape[1], tile):
        texels[:, at : at + tile] = matmul(planes[...], columns(w_unpatch, at, tile)).astype(bfloat)
    gather.finish()
    for copy in later:
        copy.wait()
    for copy in hidden_copies:
        copy.wait_send()
    for copy in outs:
        copy.wait()


def forward_layer(n, seq_size, matrices, shards, tokens, gains, index, valid):
    chunks = sum(m.parts for m in matrices)
    vmem, any_space = pl.BlockSpec(memory_space=pltpu.VMEM), pl.BlockSpec(memory_space=pl.ANY)
    shapes = [m.shape(n, seq_size) for m in matrices]
    largest = max(n, seq_size)
    bfloat, f32 = jnp.bfloat16, jnp.float32
    rows, width = tokens.shape
    plane_rows = 3 * PRES * PRES // seq_size
    ff = matrices[2].cols * seq_size
    results = [
        ((8, width), f32),
        ((seq_size,) + index.shape, jnp.int32),
        ((seq_size, rows, width), bfloat),
        ((plane_rows, width), bfloat),
        ((seq_size * rows, width), bfloat),
        ((seq_size * rows, width), bfloat),
        ((plane_rows, width), bfloat),
        ((rows, width), f32),
        ((rows, 1), f32),
        ((plane_rows, width), f32),
        ((plane_rows, 1), f32),
        ((plane_rows, width), bfloat),
        ((plane_rows, ff), bfloat),
        ((plane_rows, ff), bfloat),
        ((plane_rows, width), bfloat),
        ((plane_rows, matrices[4].cols * seq_size), bfloat),
    ]
    sem = pltpu.SemaphoreType.DMA
    made = pl.pallas_call(
        functools.partial(forward_kernel, n, seq_size, matrices),
        out_shape=[jax.ShapeDtypeStruct(s, bfloat) for s in shapes]
        + [jax.ShapeDtypeStruct(s, t) for s, t in results],
        in_specs=[vmem] * (len(matrices) + 4),
        out_specs=[any_space] * len(matrices) + [vmem] * len(results),
        scratch_shapes=[pltpu.VMEM(s, bfloat) for s in shapes]
        + [pltpu.VMEM((plane_rows, width), f32)]
        + [sem((seq_size - 1,))] * 4
        + [pltpu.VMEM((4, largest) + gains.shape, f32)]
        + [sem((4, largest - 1))] * 2
        + [sem((chunks,))]
        + gather_sems(n, seq_size, chunks),
        compiler_params=pltpu.CompilerParams(
            collective_id=0, has_side_effects=True, vmem_limit_bytes=VMEM_LIMIT
        ),
    )(*shards, tokens, gains, index, valid)
    return made[: len(matrices)], made[len(matrices) :]


def weight_list(shards):
    names = ("qkv", "out", "up", "down", "unpatch")
    parts = (4, 1, 4, 4, 2)
    return tuple(
        Matrix(name, shard.shape[0], shard.shape[1], name == "down", part)
        for name, shard, part in zip(names, shards, parts)
    )


def matmul(left, right):
    return jnp.dot(left, right, preferred_element_type=jnp.float32)


def matmul_tn(left, right):
    return lax.dot_general(
        left, right, (((0,), (0,)), ((), ())), preferred_element_type=jnp.float32
    )


def matmul_nt(left, right):
    return lax.dot_general(
        left, right, (((1,), (1,)), ((), ())), preferred_element_type=jnp.float32
    )


def gelu_exact(values):
    return jax.nn.gelu(values, approximate=False)


def norm_forward(values, gain, shift):
    center = values - jnp.mean(values, axis=-1, keepdims=True)
    inverse = lax.rsqrt(jnp.mean(center * center, axis=-1, keepdims=True) + EPSILON)
    normed = center * inverse
    return (normed * gain + shift, normed, inverse)


def norm_backward(grad, normed, inverse, gain):
    scaled = grad * gain
    inner = scaled - jnp.mean(scaled, axis=-1, keepdims=True)
    inner = inner - normed * jnp.mean(scaled * normed, axis=-1, keepdims=True)
    return (inner * inverse, jnp.sum(grad * normed, axis=0), jnp.sum(grad, axis=0))


def split_heads(matrix, heads):
    return matrix.reshape(matrix.shape[0], heads, matrix.shape[1] // heads).transpose(1, 0, 2)


def join_heads(stacked):
    return stacked.transpose(1, 0, 2).reshape(stacked.shape[1], stacked.shape[0] * stacked.shape[2])


def split_at(values, count):
    return values[:count], values[count:]


def shards(
    tokens,
    ln1_gain,
    ln1_bias,
    w_qkv,
    w_out,
    ln2_gain,
    ln2_bias,
    w_up,
    w_down,
    w_unpatch,
    dec_w1,
    dec_b1,
    dec_w2,
    dec_b2,
    counts,
    sample_texels,
    d_density,
    d_color,
):
    seq_size = lax.axis_size("seq")
    dp_size = lax.axis_size("dp")
    quarter = PRES * PRES // seq_size
    plane_dev = 3 * quarter
    rows_in = tokens[0]
    tok_dev = rows_in.shape[0]
    width = rows_in.shape[1]
    head_dim = width // HEADS
    scale = head_dim ** (-0.5)
    bfloat = jnp.bfloat16
    n = round(dp_size ** (1 / 3))
    shards_of = (w_qkv, w_out, w_up, w_down, w_unpatch)
    matrices = weight_list(shards_of)
    device = lax.axis_index("dp") * seq_size + lax.axis_index("seq")
    gains = jnp.stack([ln1_gain, ln1_bias, ln2_gain, ln2_bias])
    spread = jnp.zeros((8, width), jnp.float32)
    spread = lax.dynamic_update_slice(spread, gains, (0, device * gains.shape[1]))
    position = jnp.arange(seq_size * tok_dev, dtype=jnp.int32)
    owner = position // tok_dev
    offset = position % tok_dev
    key_valid = (offset < plane_dev) | (
        owner * (tok_dev - plane_dev) + offset - plane_dev < counts[0]
    )
    wholes, made = forward_layer(
        n, seq_size, matrices, shards_of, rows_in, spread, sample_texels[0], key_valid.astype(jnp.float32)[None]
    )
    gains_all, index_all, hidden_all, query, keys_all, values_all, mixed = made[:7]
    normed_one, inverse_one, normed_two, inverse_two, hidden_two, activated, slope, plane_rows, own_texels = made[7:]
    qkv, out, up, down, unpatch = matrices
    (density, color_value, grad_w_one, grad_b_one, grad_w_two, grad_b_two, grad_after, norm_grads), grads = split_at(
        middle(
            n,
            seq_size,
            (up, down, unpatch),
            (own_texels, index_all, dec_w1, dec_b1, dec_w2, dec_b2, d_density, d_color[0]),
            (plane_rows, activated, slope, hidden_two, normed_two, inverse_two, gains_all),
            wholes[2:],
        ),
        8,
    )
    decoder = (grad_w_one, grad_b_one[:, 0], grad_w_two[:4].T, grad_b_two[:4, 0])
    flat = jnp.concatenate([part.reshape(-1) for part in decoder])
    lines = -(-(flat.shape[0] + 4 * width) // (8 * width)) * 8
    flat = jnp.pad(flat, (0, (lines - 4) * width - flat.shape[0])).reshape(-1, width)
    small = jnp.concatenate([jnp.zeros((2, width), jnp.float32), norm_grads, flat], axis=0)
    valid = key_valid.astype(jnp.float32)[:, None]
    block_sums, (grad_tokens, small_sums) = split_at(
        backward_attention(
            n,
            seq_size,
            (unpatch, down, up, out, qkv),
            (grad_after, mixed, query, normed_one, inverse_one, gains_all, valid, small),
            (wholes[1], wholes[0], keys_all, values_all, hidden_all.reshape(-1, width)),
            (grads[2], grads[1], grads[0]),
        ),
        5,
    )
    flat_sums, at, decoder_sums = small_sums[4:].reshape(-1), 0, []
    for part in decoder:
        decoder_sums.append(flat_sums[at : at + part.size].reshape(part.shape))
        at += part.size
    own = width // (dp_size * seq_size)
    sum_unpatch, sum_down, sum_up, sum_out, sum_qkv = block_sums
    norm_sums = lax.dynamic_slice(small_sums, (0, device * own), (4, own))
    sum_gain_one, sum_shift_one, sum_gain_two, sum_shift_two = [norm_sums[i] for i in range(4)]
    return (
        density,
        color_value[None],
        grad_tokens[None],
        sum_gain_one,
        sum_shift_one,
        sum_qkv,
        sum_out,
        sum_gain_two,
        sum_shift_two,
        sum_up,
        sum_down,
        sum_unpatch,
        decoder_sums[0],
        decoder_sums[1],
        decoder_sums[2],
        decoder_sums[3],
    )


def solution(mesh):
    in_specs = (
        P("dp", "seq", None),
        P(("dp", "seq")),
        P(("dp", "seq")),
        P("dp", "seq"),
        P("dp", "seq"),
        P(("dp", "seq")),
        P(("dp", "seq")),
        P("dp", "seq"),
        P(("dp", "seq"), None),
        P("dp", "seq"),
        P(),
        P(),
        P(),
        P(),
        P("dp"),
        P("dp", None, "seq"),
        P("dp", "seq"),
        P("dp", None, "seq"),
    )
    out_specs = (
        P("dp", "seq"),
        P("dp", None, "seq"),
        P("dp", "seq", None),
        P(("dp", "seq")),
        P(("dp", "seq")),
        P("dp", "seq"),
        P("dp", "seq"),
        P(("dp", "seq")),
        P(("dp", "seq")),
        P("dp", "seq"),
        P(("dp", "seq"), None),
        P("dp", "seq"),
        P(),
        P(),
        P(),
        P(),
    )
    return jax.shard_map(shards, mesh=mesh, in_specs=in_specs, out_specs=out_specs, check_vma=False)
```

```python
import functools
import math

import jax
import jax.numpy as jnp
from jax import lax
from jax.experimental import pallas as pl
from jax.experimental.pallas import tpu as pltpu
from jax.sharding import PartitionSpec as P

HEADS = 16
PATCH = 8
CH = 32
PRES = 16


EPSILON = 1e-05
NEGATIVE = -1e30
VMEM_LIMIT = 58 * 2**20
AHEAD = 4
LAG = 2


MESH = pl.DeviceIdType.MESH


class Place:
    def __init__(self, n, seq_size):
        dp = lax.axis_index("dp")
        self.n, self.seq_size = n, seq_size
        self.seq = lax.axis_index("seq")
        self.i = (lax.div(dp, n * n), lax.rem(lax.div(dp, n), n), lax.rem(dp, n))
        self.dp = dp

    def size(self, axis):
        return self.seq_size if axis == 3 else self.n

    def me(self, axis):
        return self.seq if axis == 3 else self.i[axis]

    def peer(self, axis, step):
        to = lax.rem(self.me(axis) + step, self.size(axis))
        if axis == 3:
            return to, (self.dp, to)
        where = [to if a == axis else self.i[a] for a in range(3)]
        return to, ((where[0] * self.n + where[1]) * self.n + where[2], self.seq)

    def source(self, axis, step):
        size = self.size(axis)
        return lax.rem(self.me(axis) + (size - step), size)

    def enter(self, axes=(0, 1, 2, 3)):
        barrier = pltpu.get_barrier_semaphore()
        count = 0
        for axis in axes:
            for step in range(1, self.size(axis)):
                pl.semaphore_signal(
                    barrier, inc=1, device_id=self.peer(axis, step)[1], device_id_type=MESH
                )
                count += 1
        pl.semaphore_wait(barrier, count)


def remote(src, dst, send, recv, device):
    return pltpu.make_async_remote_copy(
        src_ref=src, dst_ref=dst, send_sem=send, recv_sem=recv, device_id=device, device_id_type=MESH
    )


class Line:
    def __init__(self, place):
        z = place.seq
        assert place.seq_size == 4
        self.dp, self.me = place.dp, z
        self.pair, self.far, self.opposite = z + 1 - 2 * lax.rem(z, 2), lax.rem(z + 2, 4), 3 - z
        self.middle = z * (3 - z) == 2
        self.end = z * (3 - z) == 0

    def _copy(self, source, target, send, recv, to):
        return remote(source, target, send, recv, (self.dp, to))

    def gather_start(self, region, send, recv):
        own = region(self.me)
        self._copy(own, own, send.at[0], recv.at[0], self.pair).start()
        self._copy(own, own, send.at[1], recv.at[1], self.far).start()

        @pl.when(self.middle)
        def _():
            self._copy(own, own, send.at[2], recv.at[2], self.opposite).start()

    def gather_relay(self, region, send, recv):
        block = region(self.far)
        self._copy(block, block, send.at[1], recv.at[1], self.far).wait_recv()

        @pl.when(self.middle)
        def _():
            self._copy(block, block, send.at[3], recv.at[2], self.pair).start()

    def gather_take(self, region, send, recv, which=("pair", "opposite")):
        for i, name, j in ((0, "pair", self.pair), (2, "opposite", self.opposite)):
            if name in which:
                self._copy(region(j), region(j), send.at[i], recv.at[i], self.pair).wait_recv()

    def gather_finish(self, region, send, recv):
        own = region(self.me)
        for i in (0, 1):
            self._copy(own, own, send.at[i], recv.at[i], self.pair).wait_send()

        @pl.when(self.middle)
        def _():
            for i in (2, 3):
                self._copy(own, own, send.at[i], recv.at[2], self.pair).wait_send()

    def sum_start(self, region, slot, send, recv, which=("opposite", "far", "pair")):
        if "opposite" in which:
            block = region(self.opposite)

            @pl.when(self.middle)
            def _():
                self._copy(block, slot(2), send.at[2], recv.at[2], self.opposite).start()

            @pl.when(self.end)
            def _():
                self._copy(block, slot(3), send.at[2], recv.at[3], self.pair).start()

        if "far" in which:

            @pl.when(self.end)
            def _():
                self._copy(region(self.far), slot(1), send.at[1], recv.at[1], self.far).start()

        if "pair" in which:
            self._copy(region(self.pair), slot(0), send.at[0], recv.at[0], self.pair).start()

    def sum_relay(self, region, slot, send, recv, add):
        @pl.when(self.middle)
        def _():
            block = region(self.far)
            self._copy(block, slot(3), send.at[2], recv.at[3], self.pair).wait_recv()
            add(self.far)
            self._copy(block, slot(1), send.at[1], recv.at[1], self.far).start()

    def sum_take(self, region, slot, send, recv):
        for i in (0, 1):
            self._copy(region(self.me), slot(i), send.at[i], recv.at[i], self.pair).wait_recv()

        @pl.when(self.middle)
        def _():
            self._copy(region(self.me), slot(2), send.at[2], recv.at[2], self.pair).wait_recv()

    def sum_of(self, own, slots):
        total = own.astype(jnp.float32) + slots(0).astype(jnp.float32) + slots(1).astype(jnp.float32)
        return total + jnp.where(self.middle, slots(2).astype(jnp.float32), 0.0)

    def sum_finish(self, region, slot, send, recv):
        for i in (0, 1, 2):
            self._copy(region(self.me), slot(0), send.at[i], recv.at[0], self.pair).wait_send()


class Matrix:
    def __init__(self, name, rows, cols, by_rows, parts):
        self.name, self.rows, self.cols, self.by_rows = name, rows, cols, by_rows
        self.parts = parts if rows % (16 * parts) == 0 else 1

    def shape(self, n, seq_size):
        if self.by_rows:
            return (n, n, n, seq_size, self.rows, self.cols)
        return (n, n, n, self.rows, seq_size * self.cols)

    def tail(self, part, first, count):
        size = self.rows // self.parts
        rows = pl.ds(part * size, size)
        if self.by_rows:
            return (pl.ds(first, count), rows, slice(None))
        if isinstance(first, int):
            return (rows, pl.ds(first * self.cols, count * self.cols))
        return (rows, pl.ds(pl.multiple_of(first * self.cols, 128), count * self.cols))

    def tail_shape(self, count):
        size = self.rows // self.parts
        return (count, size, self.cols) if self.by_rows else (size, count * self.cols)


def small_stage(place, value, slots, send, recv, stage, axis):
    me = place.me(axis)
    slots[stage, me] = value
    copies = []
    for step in range(1, place.size(axis)):
        ref = slots.at[stage, me]
        copy = remote(
            ref, ref, send.at[stage, step - 1], recv.at[stage, step - 1], place.peer(axis, step)[1]
        )
        copy.start()
        copies.append(copy)

    def end():
        for copy in copies:
            copy.wait()
        total = slots[stage, 0]
        for other in range(1, place.size(axis)):
            total = total + slots[stage, other]
        return total

    return end


def small_sum(place, parts, between=None):
    values = [part[0] for part in parts]
    for stage, axis in enumerate((2, 1, 0, 3)):
        ends = [small_stage(place, v, *part[1:], stage, axis) for v, part in zip(values, parts)]
        if between is not None:
            between()
        values = [end() for end in ends]
    return values


class Gather:
    def __init__(self, place, matrices, refs, sems):
        self.place, self.refs, self.line = place, refs, Line(place)
        self.chunks = [(w, m, p) for w, m in enumerate(matrices) for p in range(m.parts)]
        self.seq_send, self.seq_recv, self.hop_send, self.hop_recv, self.far_send, self.far_recv = sems
        self.copies = {}

    def _send(self, key, axis, region, send, recv):
        made = []
        for step in range(1, self.place.size(axis)):
            copy = remote(region, region, send.at[step - 1], recv.at[step - 1], self.place.peer(axis, step)[1])
            copy.start()
            made.append(copy)
        self.copies[key] = made

    def _take(self, key):
        for copy in self.copies[key]:
            copy.wait_recv()

    def region(self, k, index, first, count):
        w, matrix, part = self.chunks[k]
        return self.refs[w].at[index + matrix.tail(part, first, count)]

    def _along(self, k):
        return lambda j: self.region(k, self.place.i, j, 1), self.seq_send.at[k], self.seq_recv.at[k]

    def along_seq(self, k):
        self.line.gather_start(*self._along(k))

    def relay(self, k):
        self.line.gather_relay(*self._along(k))

    def hop(self, k, number):
        p, half = self.place, self.place.seq_size // 2
        if number == 0:
            self.line.gather_take(*self._along(k))
        else:
            self._take((k, 1, 0))
            self._take((k, 1, 1))
        for h in (0, 1):
            axis = 1 - h if number == 0 else h
            index = [p.i[0], p.i[1], p.i[2]]
            if number == 1:
                index[1 - axis] = slice(None)
            at = 2 * number + h
            region = self.region(k, tuple(index), h * half, half)
            self._send((k, 1 + number, h), axis, region, self.hop_send.at[k, at], self.hop_recv.at[k, at])

    def third(self, k):
        p = self.place
        self._take((k, 2, 0))
        self._take((k, 2, 1))
        region = self.region(k, (slice(None), slice(None), p.i[2]), 0, p.seq_size)
        self._send((k, 3), 2, region, self.far_send.at[k], self.far_recv.at[k])

    def arrived(self, k):
        self._take((k, 3))

    def finish(self):
        for k in range(len(self.chunks)):
            self.line.gather_finish(*self._along(k))
        for made in self.copies.values():
            for copy in made:
                copy.wait_send()


def gather_sems(n, seq_size, chunks):
    sem = pltpu.SemaphoreType.DMA
    return [sem((chunks, 4)), sem((chunks, 3))] + [sem((chunks, 4, n - 1))] * 2 + [sem((chunks, n - 1))] * 2


def gelu_parts(x):
    cdf = 0.5 + 0.5 * lax.erf(x * (0.5**0.5))
    return x * cdf, cdf + x * (jnp.exp(-0.5 * x * x) * (2.0 * math.pi) ** -0.5)


def split_low(x):
    high = x.astype(jnp.bfloat16)
    return high, (x - high.astype(jnp.float32)).astype(jnp.bfloat16)


def texel_place(texel, seq_size, me):
    side, quarter = PRES * PATCH, PRES * PRES // seq_size
    row, col = texel // side, texel % side
    token = row // PATCH * PRES + col // PATCH
    a, b = row % PATCH, col % PATCH
    fold = PATCH // 2
    mine = token // quarter == me
    key = jnp.where(mine, a // 2 * quarter + token % quarter, -1)
    return key, a % 2 * PATCH + b, fold


def decode_both(
    place,
    grad_texels,
    tile,
    texels,
    index,
    w1,
    b1,
    w2,
    b2,
    d_density,
    d_color,
    density,
    color,
    grads,
    tables,
    grad_tables,
    features,
    part_out,
    part_in,
    own_part,
    grad_all,
    send_sem,
    recv_sem,
    back_send,
    back_recv,
):
    seq_size = place.seq_size
    bfloat, f32 = jnp.bfloat16, jnp.float32
    samples = index.shape[3]
    quarter = PRES * PRES // seq_size
    width = texels.shape[1]
    groups = 2 * PATCH
    cols = groups * CH
    depth = width // cols * quarter
    hidden, inputs = w1.shape
    line = Line(place)
    for p in range(3):
        own = texels[p * quarter : (p + 1) * quarter].astype(f32)
        stacked = jnp.concatenate([own[:, i * cols : (i + 1) * cols] for i in range(width // cols)], axis=0)
        tables[p] = stacked.T.astype(bfloat)
    w1_high, w1_low = split_low(w1[...])
    w1_stack = jnp.concatenate([w1_high, w1_low], axis=0)
    tiles = samples // tile

    def one_hot(source, at, p):
        texel = index[source, p, :, at]
        key, group, _ = texel_place(texel, seq_size, place.seq)
        rows = lax.broadcasted_iota(jnp.int32, (depth, tile), 0)
        return (rows == key).astype(f32).astype(bfloat), group

    def forward(source):
        @pl.loop(0, tiles)
        def _(t):
            at = pl.ds(pl.multiple_of(t * tile, tile), tile)
            picked = []
            for p in range(3):
                hot, group = one_hot(source, at, p)
                spread = matmul(tables[p], hot)
                total = jnp.where(group == 0, spread[:CH], 0.0)
                for g in range(1, groups):
                    total = total + jnp.where(group == g, spread[g * CH : (g + 1) * CH], 0.0)
                picked.append(total)
            feature = jnp.concatenate(picked, axis=0).astype(bfloat)
            features[source, :, at] = feature
            both = matmul(w1_stack, feature)
            part = both[:hidden] + both[hidden:]
            own_part[:, at] = part
            part_out[source, :, at] = part.astype(bfloat)

    forward_line = (lambda j: part_out.at[j], lambda i: part_in.at[i], send_sem, recv_sem)
    for name, j in (("opposite", line.opposite), ("far", line.far), ("pair", line.pair)):
        forward(j)
        line.sum_start(*forward_line, which=(name,))

    def add(j):
        part_out[j] = (part_out[j].astype(f32) + part_in[3].astype(f32)).astype(bfloat)

    line.sum_relay(*forward_line, add)
    forward(place.seq)
    highest = lax.Precision.HIGHEST
    tn, nt = (((0,), (0,)), ((), ())), (((1,), (1,)), ((), ()))
    ones = jnp.ones((8, samples), f32)

    def eight(x):
        return jnp.concatenate([x, jnp.zeros((8 - x.shape[0], x.shape[1]), f32)], axis=0)

    def dot(left, right, dims):
        return lax.dot_general(left, right, dims, precision=highest, preferred_element_type=f32)

    shift = dot(eight(b1[...]), ones, tn)
    line.sum_take(*forward_line)
    pre = line.sum_of(own_part[...], lambda i: part_in[i]) + shift
    act, slope = gelu_parts(pre)
    out = jnp.dot(w2[...], act, precision=highest, preferred_element_type=f32) + dot(eight(b2[...]), ones, tn)
    gate = 1.0 / (1.0 + jnp.exp(-out))
    first = out[:1]
    density[...] = jnp.maximum(first, 0.0) + jnp.log1p(jnp.exp(-jnp.abs(first)))
    rows = [d_density[...] * gate[:1]]
    for p in range(3):
        own = gate[p + 1 : p + 2]
        color[p] = own
        rows.append(d_color[p] * own * (1.0 - own))
    grad_out = jnp.concatenate(rows, axis=0)
    grad_pre = dot(eight(w2[...]), eight(grad_out), tn) * slope
    me = place.seq
    grad_all[me] = grad_pre.astype(bfloat)
    back_line = (lambda j: grad_all.at[j], back_send, back_recv)
    line.gather_start(*back_line)
    grads[...] = jnp.zeros(grads.shape, f32)
    outs = w2.shape[0]
    grads[hidden : hidden + outs, :hidden] = dot(grad_out, act, nt)
    grads[hidden + 8 : hidden + 9, :hidden] = dot(ones, grad_pre, nt)[:1]
    grads[hidden + 16 : hidden + 17, :outs] = dot(ones, grad_out, nt)[:1]
    grad_tables[...] = jnp.zeros(grad_tables.shape, f32)

    def backward(source):
        @pl.loop(0, tiles)
        def _(t):
            at = pl.ds(pl.multiple_of(t * tile, tile), tile)
            grad = grad_all[source, :, at]
            grads[:hidden, :inputs] += matmul_nt(grad, features[source, :, at])
            grad_feature = matmul_tn(w1_high, grad) + matmul_tn(w1_low, grad)
            for p in range(3):
                hot, group = one_hot(source, at, p)
                mine = grad_feature[p * CH : (p + 1) * CH]
                spread = jnp.concatenate(
                    [jnp.where(group == g, mine, 0.0) for g in range(groups)], axis=0
                ).astype(bfloat)
                grad_tables[p] += matmul_nt(spread, hot)

    backward(me)
    line.gather_relay(*back_line)
    backward(line.far)
    line.gather_take(*back_line, which=("pair",))
    backward(line.pair)
    line.gather_take(*back_line, which=("opposite",))
    backward(line.opposite)
    for p in range(3):
        back = grad_tables[p].T
        for i in range(width // cols):
            block = back[i * quarter : (i + 1) * quarter].astype(bfloat)
            grad_texels[p * quarter : (p + 1) * quarter, i * cols : (i + 1) * cols] = block
    line.sum_finish(*forward_line)
    line.gather_finish(*back_line)


def core_columns(ref, n, segment, to):
    width = ref.shape[1]
    parts = width // (n * segment)
    if segment % 128 == 0:
        places = [pl.multiple_of((q * n + to) * segment, 128) for q in range(parts)]
        return jnp.concatenate([ref[:, pl.ds(at, segment)] for at in places], axis=1).T
    place = lax.broadcasted_iota(jnp.int32, (width, width // n), 1)
    source = (lax.div(place, segment) * n + to) * segment + lax.rem(place, segment)
    pick = lax.broadcasted_iota(jnp.int32, (width, width // n), 0) == source
    return matmul(ref[...], pick.astype(jnp.float32).astype(jnp.bfloat16)).astype(jnp.bfloat16).T


class Exchange:
    def __init__(self, place, send, recv):
        self.place, self.send, self.recv = place, send, recv
        self.made, self.used = [], 0

    def _start(self, source_of, buf):
        copies, p = [], self.place
        for step in range(1, p.size(2)):
            to, device = p.peer(2, step)
            sems = (self.send.at[self.used, step - 1], self.recv.at[self.used, step - 1])
            copy = remote(source_of(step, to), buf.at[p.i[2]], *sems, device)
            copy.start()
            copies.append(copy)
        self.used += 1
        self.made += copies

        def wait():
            for copy in copies:
                copy.wait_recv()

        return wait

    def columns(self, ref, segment, split, buf):
        p = self.place
        for step in range(1, p.size(2)):
            split[step - 1] = core_columns(ref, p.n, segment, p.peer(2, step)[0])
        wait = self._start(lambda step, to: split.at[step - 1], buf)
        buf[p.i[2]] = core_columns(ref, p.n, segment, p.i[2])
        return wait

    def rows(self, buf):
        return self._start(lambda step, to: buf.at[self.place.i[2]], buf)

    def finish(self):
        for copy in self.made:
            copy.wait_send()


def weight_grad(left, right, grad, first=0, tile=512):
    shape, width = grad.shape[:-1], right.shape[-1]
    for at in range(0, width, tile):
        size = min(tile, width - at)
        block = matmul(left[0], right[0, :, at : at + size])
        for i in range(1, left.shape[0]):
            block = block + matmul(left[i], right[i, :, at : at + size])
        grad[..., first + at : first + at + size] = block.astype(jnp.bfloat16).reshape(shape + (size,))


def norm_back(grad, normed, inverse, gain):
    scaled = grad * gain
    inner = scaled - jnp.mean(scaled, axis=-1, keepdims=True)
    inner = inner - normed * jnp.mean(scaled * normed, axis=-1, keepdims=True)
    return inner * inverse


def feed_back(place, matrices, refs):
    (planes, hidden_two, inverse_two, gains, act_in, slope_in, normed_in, weights) = refs[:8]
    (grads_out, grad_after, norm_grads, bufs) = refs[8:12]
    (planes_split, planes_all, act_split, act_all, hidden_split, hidden_all) = refs[12:18]
    (texels_all, layer_all, pre_all, layer, act, slope, normed_two, load_sem, out_sem, send, recv) = refs[18:29]
    grads = [buf.at[0] for buf in bufs]
    n = place.n
    bfloat, f32 = jnp.bfloat16, jnp.float32
    up, down, unpatch = matrices
    w_up, w_down, w_unpatch = bufs
    exchange = Exchange(place, send, recv)
    me = place.i[2]
    loads, waits = [], []

    def start():
        pairs = [(act_in, act)] + [(weights[k], bufs[k]) for k in (2, 1, 0)] + [(slope_in, slope), (normed_in, normed_two)]
        for k, (source, target) in enumerate(pairs):
            copy = pltpu.make_async_copy(source, target, load_sem.at[k])
            copy.start()
            loads.append(copy)

    def start_remote():
        waits.append(exchange.columns(planes, unpatch.rows, planes_split, planes_all))
        loads[0].wait()
        waits.append(exchange.columns(act, place.seq_size * down.rows, act_split, act_all))
        waits.append(exchange.columns(hidden_two, up.rows, hidden_split, hidden_all))

    outs = []

    def put(k):
        copy = pltpu.make_async_copy(grads[k], grads_out[k], out_sem.at[k])
        copy.start()
        outs.append(copy)

    def end():
        got_texels = exchange.rows(texels_all)
        loads[1].wait()
        grad_texels = texels_all[me]
        step = layer.shape[1] // n
        for i in range(n):
            block = w_unpatch[i].reshape(step, -1)
            layer[:, i * step : (i + 1) * step] = matmul_nt(grad_texels, block)
        layer_all[me] = layer[...].astype(bfloat)
        got_layer = exchange.rows(layer_all)
        loads[2].wait()
        loads[4].wait()
        step = act.shape[1] // (n * n)
        for i in range(n):
            for j in range(n):
                block = w_down[i, j].reshape(step, -1)
                at = (i * n + j) * step
                value = matmul_nt(layer_all[me], block) * slope[:, at : at + step].astype(f32)
                pre_all[me, :, at : at + step] = value.astype(bfloat)
        got_pre = exchange.rows(pre_all)
        waits[0]()
        got_texels()
        weight_grad(planes_all, texels_all, grads[2])
        put(2)
        loads[3].wait()
        loads[5].wait()
        step = layer.shape[1] // n
        pieces = []
        for i in range(n):
            block = w_up[i].reshape(step, -1)
            pieces.append(matmul_nt(pre_all[me], block))
        grad = jnp.concatenate(pieces, axis=1)
        normed = normed_two[...]
        norm_grads[0:1] = jnp.sum(grad * normed, axis=0, keepdims=True)
        norm_grads[1:2] = jnp.sum(grad, axis=0, keepdims=True)
        grad_after[...] = layer[...] + norm_back(grad, normed, inverse_two[...], gains[2:3])
        waits[1]()
        got_layer()
        weight_grad(act_all, layer_all, grads[1])
        put(1)
        waits[2]()
        got_pre()
        weight_grad(hidden_all, pre_all, grads[0])
        put(0)
        exchange.finish()
        for copy in outs:
            copy.wait()

    return start, start_remote, end


def middle_kernel(n, seq_size, matrices, *refs):
    refs = list(refs)

    def take(k):
        taken = refs[:k]
        del refs[:k]
        return taken

    decode_in, feed_in, weights = take(8), take(7), take(3)
    density, color, decoder_grads, grad_after, norm_grads = take(5)
    grads_out, bufs, decode_scratch = take(3), take(3), take(11)
    place = Place(n, seq_size)
    feed = list(feed_in) + [weights, grads_out, grad_after, norm_grads, bufs] + refs
    texels_all = refs[6]
    start, start_remote, end = feed_back(place, matrices, feed)
    start()
    place.enter((2, 3))
    start_remote()
    tile = min(512, decode_in[1].shape[3])
    outs = (density, color, decoder_grads)
    decode_both(place, texels_all.at[place.i[2]], tile, *decode_in, *outs, *decode_scratch)
    end()


def middle(n, seq_size, matrices, decode_in, feed_in, weights):
    texels, index, w1, b1, w2, b2, d_density, d_color = decode_in
    planes, hidden_two, inverse_two, gains, act, slope, normed_two = feed_in
    bfloat, f32 = jnp.bfloat16, jnp.float32
    samples, hidden = index.shape[3], w1.shape[0]
    quarter = PRES * PRES // seq_size
    cols = 2 * PATCH * CH
    depth = texels.shape[1] // cols * quarter
    vmem, any_space = pl.BlockSpec(memory_space=pltpu.VMEM), pl.BlockSpec(memory_space=pl.ANY)
    sem = pltpu.SemaphoreType.DMA
    rows, width = normed_two.shape
    ff, core_ff = act.shape[1], act.shape[1] // n
    shapes = [m.shape(n, seq_size) for m in matrices]
    halves = [(n, n) + s[3:] for s in shapes]
    return pl.pallas_call(
        functools.partial(middle_kernel, n, seq_size, matrices),
        out_shape=[
            jax.ShapeDtypeStruct((1, samples), f32),
            jax.ShapeDtypeStruct((3, 1, samples), f32),
            jax.ShapeDtypeStruct((hidden + 24, 128), f32),
            jax.ShapeDtypeStruct((rows, width), f32),
            jax.ShapeDtypeStruct((2, width), f32),
        ]
        + [jax.ShapeDtypeStruct(s, bfloat) for s in halves],
        in_specs=[vmem] * 12 + [any_space] * 6,
        out_specs=[vmem] * 5 + [any_space] * 3,
        scratch_shapes=[pltpu.VMEM(s, bfloat) for s in shapes]
        + [
            pltpu.VMEM((3, cols, depth), bfloat),
            pltpu.VMEM((3, cols, depth), f32),
            pltpu.VMEM((seq_size, 3 * CH, samples), bfloat),
            pltpu.VMEM((seq_size, hidden, samples), bfloat),
            pltpu.VMEM((4, hidden, samples), bfloat),
            pltpu.VMEM((hidden, samples), f32),
            pltpu.VMEM((seq_size, hidden, samples), bfloat),
        ]
        + [sem((3,)), sem((4,)), sem((4,)), sem((3,))]
        + [
            pltpu.VMEM((n - 1, width // n, rows), bfloat),
            pltpu.VMEM((n, width // n, rows), bfloat),
            pltpu.VMEM((n - 1, core_ff, rows), bfloat),
            pltpu.VMEM((n, core_ff, rows), bfloat),
            pltpu.VMEM((n - 1, width // n, rows), bfloat),
            pltpu.VMEM((n, width // n, rows), bfloat),
            pltpu.VMEM((n,) + texels.shape, bfloat),
            pltpu.VMEM((n, rows, width), bfloat),
            pltpu.VMEM((n, rows, ff), bfloat),
            pltpu.VMEM((rows, width), f32),
            pltpu.VMEM((rows, ff), bfloat),
            pltpu.VMEM((rows, ff), bfloat),
            pltpu.VMEM((rows, width), f32),
            sem((6,)),
            sem((3,)),
        ]
        + [sem((8, n - 1))] * 2,
        compiler_params=pltpu.CompilerParams(
            collective_id=2, has_side_effects=True, vmem_limit_bytes=VMEM_LIMIT
        ),
    )(*decode_in, *feed_in, *weights)


class Scatter:
    def __init__(self, place, matrices, sources, kept, hops, near, outs, sems):
        self.place, self.sources, self.kept = place, sources, kept
        self.hops, self.near, self.outs, self.line = hops, near, outs, Line(place)
        self.chunks = [(w, m, p) for w, m in enumerate(matrices) for p in range(m.parts)]
        self.load_sem, self.seq_send, self.seq_recv, self.hop_send, self.hop_recv = sems
        self.copies, self.loads = {}, {}

    def _send(self, key, axis, region_to, slot, send, recv):
        made = []
        for step in range(1, self.place.size(axis)):
            to, device = self.place.peer(axis, step)
            copy = remote(region_to(to), slot(step - 1), send.at[step - 1], recv.at[step - 1], device)
            copy.start()
            made.append(copy)
        self.copies[key] = made

    def _take(self, key):
        for copy in self.copies[key]:
            copy.wait_recv()

    def hop(self, k, number):
        w, matrix, part = self.chunks[k]
        p, half, n = self.place, self.place.seq_size // 2, self.place.n
        kept, every = self.kept[w], slice(None)
        local = matrix.tail(part, 0, half)
        if number == 0:
            for h in (0, 1):
                index = (p.i[0], every) if h == 0 else (every, p.i[1])
                source = self.sources[w].at[index + matrix.tail(part, h * half, half)]
                copy = pltpu.make_async_copy(source, kept.at[(h, every) + local], self.load_sem.at[k, h])
                copy.start()
                self.loads[k, h] = copy
        else:
            for h in (0, 1):
                self.loads[k, h].wait()
                self._take((k, 1, h))
                for a in range(n):
                    value = kept[(h, a) + local].astype(jnp.float32)
                    for s in range(n - 1):
                        value = value + self.hops[w][(h, s, a) + local].astype(jnp.float32)
                    kept[(h, a) + local] = value.astype(jnp.bfloat16)
        for h in (0, 1):
            axis = h if number == 0 else 1 - h
            tail, at = matrix.tail(part, h * half, half), 2 * number + h

            def region_to(to, h=h, tail=tail):
                if number == 1:
                    return kept.at[(h, to) + local]
                return self.sources[w].at[((to, every) if h == 0 else (every, to)) + tail]

            def slot(s, h=h):
                return self.hops[w].at[(h, s, pl.ds(0, n) if number == 0 else n) + local]

            self._send((k, 1 + number, h), axis, region_to, slot, self.hop_send.at[k, at], self.hop_recv.at[k, at])

    def _block(self, matrix, part, j):
        p, half = self.place, self.place.seq_size // 2
        h = lax.div(j, half)
        return (h, p.i[1] + h * (p.i[0] - p.i[1])) + matrix.tail(part, lax.rem(j, half), 1)

    def along_seq(self, k):
        w, matrix, part = self.chunks[k]
        p, half, n = self.place, self.place.seq_size // 2, self.place.n
        kept = self.kept[w]
        local = matrix.tail(part, 0, half)
        for h in (0, 1):
            self._take((k, 2, h))
            value = kept[(h, p.i[1 - h]) + local].astype(jnp.float32)
            for s in range(n - 1):
                value = value + self.hops[w][(h, s, n) + local].astype(jnp.float32)
            kept[(h, p.i[1 - h]) + local] = value.astype(jnp.bfloat16)
        self.line.sum_start(*self._along(k))

    def _along(self, k):
        w, matrix, part = self.chunks[k]
        kept, near, own = self.kept[w], self.near[w], matrix.tail(part, 0, 1)
        region, slot = lambda j: kept.at[self._block(matrix, part, j)], lambda i: near.at[(i,) + own]
        return region, slot, self.seq_send.at[k], self.seq_recv.at[k]

    def relay(self, k):
        w, matrix, part = self.chunks[k]
        kept, own = self.kept[w], matrix.tail(part, 0, 1)

        def add(j):
            at = self._block(matrix, part, j)
            kept[at] = (kept[at].astype(jnp.float32) + self.near[w][(3,) + own].astype(jnp.float32)).astype(jnp.bfloat16)

        self.line.sum_relay(*self._along(k), add)

    def arrived(self, k):
        w, matrix, part = self.chunks[k]
        own = matrix.tail(part, 0, 1)
        self.line.sum_take(*self._along(k))
        value = self.kept[w][self._block(matrix, part, self.place.seq)]
        value = self.line.sum_of(value, lambda i: self.near[w][(i,) + own])
        size = matrix.rows // matrix.parts
        self.outs[w][pl.ds(part * size, size)] = value.reshape(size, matrix.cols)

    def finish(self):
        for k in range(len(self.chunks)):
            self.line.sum_finish(*self._along(k))
        for made in self.copies.values():
            for copy in made:
                copy.wait_send()


def backward_kernel(n, seq_size, matrices, *refs):
    count = len(matrices)
    refs = list(refs)

    def take(k):
        taken = refs[:k]
        del refs[:k]
        return taken

    grad_after, mixed, query, normed_one, inverse_one, gains, norm_grads, decoder_grads, scene_count = take(9)
    w_out_in, w_qkv_in, keys_in, values_in, hidden_all_in = take(5)
    early = take(count - 2)
    outs = take(count)
    g_tokens, *norm_outs = take(5)
    g_w1, g_b1, g_w2, g_b2 = take(4)
    w_out, w_qkv, work = take(3)
    g_out, g_qkv = w_out.at[0], w_qkv.at[0]
    kept, hops, near = take(count), take(count), take(count)
    mixed_split, mixed_all, after_all, hidden_split, hidden_core, own_split, own_core = take(7)
    query_all, grad_all, hidden_in = take(3)
    grad_mixed, load_sem, core_send, core_recv, hidden_send, hidden_recv = take(6)
    norm_part, decoder_part = take(3), take(3)
    sems = refs
    bfloat, f32 = jnp.bfloat16, jnp.float32
    place = Place(n, seq_size)
    me = place.i[2]
    loads = []
    rows, width = query.shape
    token_rows = normed_one.shape[0]
    keys, values = grad_all.at[me, :, pl.ds(0, width)], grad_all.at[me, :, pl.ds(width, width)]
    for k, (source, target) in enumerate(
        ((hidden_all_in, work), (w_out_in, w_out), (keys_in, keys), (values_in, values), (w_qkv_in, w_qkv))
    ):
        copy = pltpu.make_async_copy(source, target, load_sem.at[k])
        copy.start()
        loads.append(copy)
    place.enter()
    scatter = Scatter(place, matrices, list(early) + [g_out, g_qkv], kept, hops, near, outs, sems)
    total = len(scatter.chunks)
    state = [0]

    def advance():
        t = state[0]
        state[0] += 1
        if t < total:
            scatter.hop(t, 0)
        if 0 <= t - LAG < total:
            scatter.hop(t - LAG, 1)
        if 0 <= t - 2 * LAG < total:
            scatter.along_seq(t - 2 * LAG)
        if 0 <= t - 2 * LAG - 1 < total:
            scatter.relay(t - 2 * LAG - 1)
        if 0 <= t - 3 * LAG - 1 < total:
            scatter.arrived(t - 3 * LAG - 1)

    line = Line(place)
    advance()
    advance()
    exchange = Exchange(place, core_send, core_recv)
    out_matrix, qkv_matrix = matrices[-2:]
    got_mixed = exchange.columns(mixed, out_matrix.rows, mixed_split, mixed_all)
    after_all[me] = grad_after[...].astype(bfloat)
    got_after = exchange.rows(after_all)
    loads[0].wait()
    own = work.at[pl.ds(pl.multiple_of(place.seq * token_rows, 16), rows)]
    got_own = exchange.columns(own, qkv_matrix.rows, own_split, own_core)
    got_hidden = exchange.columns(work, qkv_matrix.rows, hidden_split, hidden_core)
    loads[1].wait()
    step = width // n
    for i in range(n):
        block = w_out[i].reshape(step, width)
        grad_mixed[:, i * step : (i + 1) * step] = matmul_nt(after_all[me], block).astype(bfloat)
    got_mixed()
    got_after()
    weight_grad(mixed_all, after_all, g_out)
    loads[2].wait()
    loads[3].wait()
    valid = key_valid(scene_count, seq_size, rows, token_rows, 0)
    pair = 2 * width // HEADS
    scale = (width // HEADS) ** (-0.5)
    first = lax.broadcasted_iota(jnp.int32, (rows, pair), 1) < pair // 2
    pairs, segments = HEADS // 2, 4
    for segment in range(segments):

        @pl.loop(segment * pairs // segments, (segment + 1) * pairs // segments)
        def _(p):
            at = pl.ds(pl.multiple_of(p * pair, pair), pair)
            query_two, grad_two = query[:, at].astype(f32) * scale, grad_mixed[:, at].astype(f32)
            later = pl.ds(pl.multiple_of(width + p * pair, pair), pair)
            key_two, value_two = grad_all[me, :, at], grad_all[me, :, later]
            key_turned = key_two.T
            grad_key, grad_value, turned = 0.0, 0.0, []
            for h, mine in enumerate((first, ~first)):
                query_h = jnp.where(mine, query_two, 0.0).astype(bfloat)
                grad_h = jnp.where(mine, grad_two, 0.0).astype(bfloat)
                scores = jnp.where(valid, matmul_nt(key_two, query_h), NEGATIVE)
                expo = jnp.exp(scores - jnp.max(scores, axis=0, keepdims=True))
                probs = expo * (1.0 / jnp.sum(expo, axis=0, keepdims=True))
                grad_value = grad_value + matmul(probs.astype(bfloat), grad_h)
                grad_probs = matmul_nt(value_two, grad_h)
                inner = jnp.sum(probs * grad_probs, axis=0, keepdims=True)
                grad_scores = (probs * (grad_probs - inner)).astype(bfloat)
                grad_key = grad_key + matmul(grad_scores, query_h)
                grad_query = matmul(key_turned, grad_scores)
                turned.append(grad_query[h * (pair // 2) : (h + 1) * (pair // 2)])
            query_all[me, :, at] = (jnp.concatenate(turned, axis=0) * scale).T.astype(bfloat)
            grad_all[me, :, at] = grad_key.astype(bfloat)
            grad_all[me, :, later] = grad_value.astype(bfloat)

        advance()
    got_grad = exchange.rows(grad_all)
    got_query = exchange.rows(query_all)
    loads[4].wait()
    for i in range(n):
        block = w_qkv[i].reshape(step, 3 * width)
        work[:, i * step : (i + 1) * step] = matmul_nt(grad_all[me], block[:, width:]).astype(bfloat)
    pieces = [matmul_nt(query_all[me], w_qkv[i].reshape(step, 3 * width)[:, :width]) for i in range(n)]
    from_query = jnp.concatenate(pieces, axis=1)
    hidden_line = (
        lambda j: work.at[pl.ds(pl.multiple_of(j * token_rows, 16), token_rows)],
        lambda i: hidden_in.at[i],
        hidden_send,
        hidden_recv,
    )
    line.sum_start(*hidden_line)
    advance()
    got_grad()
    got_query()
    got_hidden()
    got_own()
    weight_grad(own_core, query_all, g_qkv)

    def add(j):
        at = pl.ds(pl.multiple_of(j * token_rows, 16), token_rows)
        work[at] = (work[at].astype(f32) + hidden_in[3].astype(f32)).astype(bfloat)

    line.sum_relay(*hidden_line, add)
    weight_grad(hidden_core, grad_all, g_qkv, width)
    advance()
    advance()
    line.sum_take(*hidden_line)
    grad = line.sum_of(work[pl.ds(pl.multiple_of(place.seq * token_rows, 16), token_rows)], lambda i: hidden_in[i])
    rest = jnp.zeros((token_rows - rows, width), f32)
    grad = grad + jnp.concatenate([from_query, rest], axis=0)
    normed = normed_one[...]
    g_tokens[...] = norm_back(grad, normed, inverse_one[...], gains[0:1])
    g_tokens[0:rows] += grad_after[...]
    gain_row = jnp.sum(grad * normed, axis=0, keepdims=True)
    shift_row = jnp.sum(grad, axis=0, keepdims=True)
    norm_rows = jnp.concatenate([gain_row, shift_row, norm_grads[...], jnp.zeros((4, width), f32)], axis=0)
    parts = [(norm_rows, *norm_part), (decoder_grads[...], *decoder_part)]
    norm_sums, decoder_sums = small_sum(place, parts, advance)
    own = norm_outs[0].shape[1]
    spot = lax.broadcasted_iota(jnp.int32, (width, own), 0) - lax.broadcasted_iota(jnp.int32, (width, own), 1)
    pick = (spot == (place.dp * seq_size + place.seq) * own).astype(f32)
    picked = jnp.dot(norm_sums, pick, precision=lax.Precision.HIGHEST, preferred_element_type=f32)
    for i, ref in enumerate(norm_outs):
        ref[...] = picked[i : i + 1]
    hidden, inputs = g_w1.shape
    g_w1[...] = decoder_sums[:hidden, :inputs]
    g_w2[...] = decoder_sums[hidden : hidden + g_w2.shape[0], :hidden]
    g_b1[...] = decoder_sums[hidden + 8 : hidden + 9, :hidden]
    g_b2[...] = decoder_sums[hidden + 16 : hidden + 17, : g_b2.shape[1]]
    while state[0] < total + 3 * LAG + 1:
        advance()
    scatter.finish()
    exchange.finish()
    line.sum_finish(*hidden_line)


def half_tail(matrix, seq_size):
    half = seq_size // 2
    if matrix.by_rows:
        return (half, matrix.rows, matrix.cols)
    return (matrix.rows, half * matrix.cols)


def backward_attention(n, seq_size, matrices, inputs, loaded, early):
    grad_after, mixed, query, normed_one, inverse_one, gains, norm_grads, decoder_grads, scene_count = inputs
    own = query.shape[1] // (lax.axis_size("dp") * seq_size)
    hidden, features, outs = decoder_grads.shape[0] - 24, 3 * CH, 4
    bfloat, f32 = jnp.bfloat16, jnp.float32
    vmem, any_space = pl.BlockSpec(memory_space=pltpu.VMEM), pl.BlockSpec(memory_space=pl.ANY)
    shapes = [m.shape(n, seq_size) for m in matrices]
    chunks = sum(m.parts for m in matrices)
    rows, width = query.shape
    all_rows = loaded[2].shape[0]
    largest = max(n, seq_size)
    sem = pltpu.SemaphoreType.DMA
    return pl.pallas_call(
        functools.partial(backward_kernel, n, seq_size, matrices),
        out_shape=[jax.ShapeDtypeStruct((m.rows, m.cols), f32) for m in matrices]
        + [jax.ShapeDtypeStruct(normed_one.shape, f32)]
        + [jax.ShapeDtypeStruct((1, own), f32)] * 4
        + [jax.ShapeDtypeStruct(s, f32) for s in ((hidden, features), (1, hidden), (outs, hidden), (1, outs))],
        in_specs=[vmem] * (len(inputs) - 1) + [pl.BlockSpec(memory_space=pltpu.SMEM)] + [any_space] * (len(loaded) + len(early)),
        out_specs=[vmem] * (len(matrices) + 9),
        scratch_shapes=[pltpu.VMEM(x.shape, bfloat) for x in loaded[:3]]
        + [pltpu.VMEM((2, n) + half_tail(m, seq_size), bfloat) for m in matrices]
        + [pltpu.VMEM((2, n - 1, n + 1) + half_tail(m, seq_size), bfloat) for m in matrices]
        + [pltpu.VMEM((4,) + ((1, m.rows, m.cols) if m.by_rows else (m.rows, m.cols)), bfloat) for m in matrices]
        + [
            pltpu.VMEM((n - 1, width // n, rows), bfloat),
            pltpu.VMEM((n, width // n, rows), bfloat),
            pltpu.VMEM((n, rows, width), bfloat),
            pltpu.VMEM((n - 1, width // n, all_rows), bfloat),
            pltpu.VMEM((n, width // n, all_rows), bfloat),
            pltpu.VMEM((n - 1, width // n, rows), bfloat),
            pltpu.VMEM((n, width // n, rows), bfloat),
            pltpu.VMEM((n, rows, width), bfloat),
            pltpu.VMEM((n, all_rows, 2 * width), bfloat),
            pltpu.VMEM((4,) + normed_one.shape, bfloat),
            pltpu.VMEM((rows, width), bfloat),
            sem((len(loaded),)),
        ]
        + [sem((8, n - 1))] * 2
        + [sem((3,)), sem((4,))]
        + [pltpu.VMEM((4, largest, 8, width), f32)]
        + [sem((4, largest - 1))] * 2
        + [pltpu.VMEM((4, largest) + decoder_grads.shape, f32)]
        + [sem((4, largest - 1))] * 2
        + [sem((chunks, 2))]
        + [sem((chunks, 3)), sem((chunks, 4))]
        + [sem((chunks, 4, n - 1))] * 2,
        compiler_params=pltpu.CompilerParams(
            collective_id=1, has_side_effects=True, vmem_limit_bytes=VMEM_LIMIT
        ),
    )(*inputs, *loaded, *early)


def columns(ref, first, count):
    block = ref[..., pl.ds(first, count)]
    return block.reshape(-1, count)


def normalize(values):
    center = values - jnp.mean(values, axis=-1, keepdims=True)
    inverse = lax.rsqrt(jnp.mean(center * center, axis=-1, keepdims=True) + EPSILON)
    return center * inverse, inverse


def forward_kernel(n, seq_size, matrices, *refs):
    count = len(matrices)
    refs = list(refs)

    def take(k):
        taken = refs[:k]
        del refs[:k]
        return taken

    shards = take(count)
    tokens, gain_one, shift_one, gain_two, shift_two, index, scene_count = take(7)
    wholes = take(count)
    gains_out, index_out, inverse_one, inverse_two = take(4)
    kept = take(12)
    bufs = take(count)
    made = take(12)
    hidden_all, query, keys, values, mixed, normed_one, normed_two, hidden_two, act, slope, planes, texels = made
    after, index_send, index_recv, hidden_send, hidden_recv, slots, small_send, small_recv, out_sem, kept_sem = take(10)
    bfloat, f32 = jnp.bfloat16, jnp.float32
    place = Place(n, seq_size)
    line = Line(place)
    for matrix, shard, buf in zip(matrices, shards, bufs):
        if matrix.by_rows:
            buf[place.i + (place.seq,)] = shard[...].astype(bfloat)
        else:
            at = pl.ds(pl.multiple_of(place.seq * matrix.cols, 128), matrix.cols)
            buf[place.i + (slice(None), at)] = shard[...].astype(bfloat)
    index_out[place.seq] = index[...]
    rows_all, width = tokens.shape
    rows = query.shape[0]
    own = gain_one.shape[1]
    first_own = (place.dp * seq_size + place.seq) * own
    spot = lax.broadcasted_iota(jnp.int32, (own, width), 1) - lax.broadcasted_iota(jnp.int32, (own, width), 0)
    spread_out = (spot == first_own).astype(f32).astype(bfloat)
    gains = [ref[...] for ref in (gain_one, shift_one, gain_two, shift_two)]
    gains = jnp.concatenate(gains + [jnp.zeros((4, own), f32)], axis=0).astype(bfloat)
    gains = matmul(gains, spread_out)
    place.enter()
    gather = Gather(place, matrices, bufs, refs)
    total = len(gather.chunks)
    outs = []
    state = [0]

    def put(*which):
        for k in which:
            copy = pltpu.make_async_copy(made[k], kept[k], kept_sem.at[k])
            copy.start()
            outs.append(copy)

    def advance():
        t = state[0]
        state[0] += 1
        if t + AHEAD < total:
            gather.along_seq(t + AHEAD)
        if t + 1 < total:
            gather.relay(t + 1)
        if t < total:
            gather.hop(t, 0)
        if 0 <= t - LAG < total:
            gather.hop(t - LAG, 1)
        if 0 <= t - 2 * LAG < total:
            gather.third(t - 2 * LAG)
        k = t - 3 * LAG
        if 0 <= k < total:
            gather.arrived(k)
            w, matrix, part = gather.chunks[k]
            at = (slice(None),) * 3 + matrix.tail(part, 0, seq_size)
            copy = pltpu.make_async_copy(bufs[w].at[at], wholes[w].at[at], out_sem.at[k])
            copy.start()
            outs.append(copy)

    def advance_to(weight):
        last = max(k for k, (w, _, _) in enumerate(gather.chunks) if w == weight)
        while state[0] <= last + 3 * LAG:
            advance()

    for k in range(AHEAD):
        gather.along_seq(k)
    index_line = (lambda j: index_out.at[j], index_send, index_recv)
    hidden_line = (lambda j: hidden_all.at[j], hidden_send, hidden_recv)
    line.gather_start(*index_line)
    normed, inverse = normalize(tokens[...])
    normed_one[...] = normed
    inverse_one[...] = inverse
    put(5)
    gather.relay(0)
    (gains_out[...],) = small_sum(place, [(gains, slots, small_send, small_recv)], advance)
    hidden_all[place.seq] = (normed_one[...] * gains_out[0:1] + gains_out[1:2]).astype(bfloat)
    line.gather_start(*hidden_line)
    line.gather_relay(*index_line)
    w_qkv, w_out, w_up, w_down, w_unpatch = bufs
    tile = 512
    advance()
    advance()
    advance()
    line.gather_relay(*hidden_line)
    advance_to(0)
    for at in range(0, width, tile):
        block = hidden_all[place.seq, pl.ds(0, rows)]
        query[:, at : at + tile] = matmul(block, columns(w_qkv, at, tile)).astype(bfloat)
    line.gather_take(*hidden_line)
    put(0, 1)

    @pl.loop(0, width // tile)
    def _(t):
        at = pl.multiple_of(t * tile, tile)
        hidden = hidden_all[...].reshape(-1, width)
        keys[:, pl.ds(at, tile)] = matmul(hidden, columns(w_qkv, at + width, tile)).astype(bfloat)
        values[:, pl.ds(at, tile)] = matmul(hidden, columns(w_qkv, at + 2 * width, tile)).astype(bfloat)

    put(2, 3)
    advance()
    valid = key_valid(scene_count, seq_size, rows, rows_all, 1)
    pair = 2 * width // HEADS
    scale = (width // HEADS) ** (-0.5)
    first = lax.broadcasted_iota(jnp.int32, (rows, pair), 1) < pair // 2
    pairs, segments = HEADS // 2, 4
    for segment in range(segments):

        @pl.loop(segment * pairs // segments, (segment + 1) * pairs // segments)
        def _(p):
            at = pl.ds(pl.multiple_of(p * pair, pair), pair)
            query_two, key_two, value_two = query[:, at].astype(f32) * scale, keys[:, at], values[:, at]
            both = []
            for mine in (first, ~first):
                scores = matmul_nt(jnp.where(mine, query_two, 0.0).astype(bfloat), key_two)
                scores = jnp.where(valid, scores, NEGATIVE)
                expo = jnp.exp(scores - jnp.max(scores, axis=-1, keepdims=True))
                probs = expo * (1.0 / jnp.sum(expo, axis=-1, keepdims=True))
                both.append(matmul(probs.astype(bfloat), value_two))
            mixed[:, at] = jnp.where(first, both[0], both[1]).astype(bfloat)

        advance()
    put(4)
    advance_to(1)
    for at in range(0, width, tile):
        after[:, at : at + tile] = tokens[:rows, at : at + tile] + matmul(mixed[...], columns(w_out, at, tile))
    normed, inverse = normalize(after[...])
    normed_two[...] = normed
    inverse_two[...] = inverse
    hidden_two[...] = (normed * gains_out[2:3] + gains_out[3:4]).astype(bfloat)
    put(6, 7)
    advance_to(2)

    @pl.loop(0, act.shape[1] // tile)
    def _(t):
        at = pl.multiple_of(t * tile, tile)
        value, rate = gelu_parts(matmul(hidden_two[...], columns(w_up, at, tile)))
        act[:, pl.ds(at, tile)] = value.astype(bfloat)
        slope[:, pl.ds(at, tile)] = rate.astype(bfloat)

    put(8, 9)
    advance_to(3)
    deep = act.shape[1] // n
    for i in range(n):
        block = w_down[i].reshape(deep, width)
        for at in range(0, width, tile):
            after[:, at : at + tile] += matmul(act[:, i * deep : (i + 1) * deep], block[:, at : at + tile])
    planes[...] = after[...].astype(bfloat)
    put(10)
    advance_to(4)
    for at in range(0, texels.shape[1], tile):
        texels[:, at : at + tile] = matmul(planes[...], columns(w_unpatch, at, tile)).astype(bfloat)
    put(11)
    gather.finish()
    line.gather_take(*index_line)
    line.gather_finish(*index_line)
    line.gather_finish(*hidden_line)
    for copy in outs:
        copy.wait()


def key_valid(scene_count, seq_size, plane_rows, rows, axis):
    shape = (1, seq_size * rows) if axis == 1 else (seq_size * rows, 1)
    position = lax.broadcasted_iota(jnp.int32, shape, axis)
    owner = lax.div(position, rows)
    offset = position - owner * rows
    return (offset < plane_rows) | (owner * (rows - plane_rows) + offset - plane_rows < scene_count[0, 0])


def forward_layer(n, seq_size, matrices, shards, tokens, gains, index, scene_count):
    chunks = sum(m.parts for m in matrices)
    vmem, any_space = pl.BlockSpec(memory_space=pltpu.VMEM), pl.BlockSpec(memory_space=pl.ANY)
    shapes = [m.shape(n, seq_size) for m in matrices]
    largest = max(n, seq_size)
    bfloat, f32 = jnp.bfloat16, jnp.float32
    rows, width = tokens.shape
    plane_rows = 3 * PRES * PRES // seq_size
    ff = matrices[2].cols * seq_size
    results = [
        ((8, width), f32),
        ((seq_size,) + index.shape, jnp.int32),
        ((rows, 1), f32),
        ((plane_rows, 1), f32),
    ]
    kept = [
        ((seq_size, rows, width), bfloat),
        ((plane_rows, width), bfloat),
        ((seq_size * rows, width), bfloat),
        ((seq_size * rows, width), bfloat),
        ((plane_rows, width), bfloat),
        ((rows, width), f32),
        ((plane_rows, width), f32),
        ((plane_rows, width), bfloat),
        ((plane_rows, ff), bfloat),
        ((plane_rows, ff), bfloat),
        ((plane_rows, width), bfloat),
        ((plane_rows, matrices[4].cols * seq_size), bfloat),
    ]
    sem = pltpu.SemaphoreType.DMA
    made = pl.pallas_call(
        functools.partial(forward_kernel, n, seq_size, matrices),
        out_shape=[jax.ShapeDtypeStruct(s, bfloat) for s in shapes]
        + [jax.ShapeDtypeStruct(s, t) for s, t in results + kept],
        in_specs=[vmem] * (len(matrices) + 6) + [pl.BlockSpec(memory_space=pltpu.SMEM)],
        out_specs=[any_space] * len(matrices) + [vmem] * len(results) + [any_space] * len(kept),
        scratch_shapes=[pltpu.VMEM(s, bfloat) for s in shapes]
        + [pltpu.VMEM(s, t) for s, t in kept]
        + [pltpu.VMEM((plane_rows, width), f32)]
        + [sem((4,)), sem((3,))] * 2
        + [pltpu.VMEM((4, largest, 8, width), f32)]
        + [sem((4, largest - 1))] * 2
        + [sem((chunks,)), sem((len(kept),))]
        + gather_sems(n, seq_size, chunks),
        compiler_params=pltpu.CompilerParams(
            collective_id=0, has_side_effects=True, vmem_limit_bytes=VMEM_LIMIT
        ),
    )(*shards, tokens, *gains, index, scene_count)
    return made[: len(matrices)], made[len(matrices) :]


def weight_list(shards):
    names = ("qkv", "out", "up", "down", "unpatch")
    parts = (4, 1, 4, 4, 2)
    return tuple(
        Matrix(name, shard.shape[0], shard.shape[1], name == "down", part)
        for name, shard, part in zip(names, shards, parts)
    )


def matmul(left, right):
    return jnp.dot(left, right, preferred_element_type=jnp.float32)


def matmul_tn(left, right):
    return lax.dot_general(
        left, right, (((0,), (0,)), ((), ())), preferred_element_type=jnp.float32
    )


def matmul_nt(left, right):
    return lax.dot_general(
        left, right, (((1,), (1,)), ((), ())), preferred_element_type=jnp.float32
    )


def split_at(values, count):
    return values[:count], values[count:]


def shards(
    tokens,
    ln1_gain,
    ln1_bias,
    w_qkv,
    w_out,
    ln2_gain,
    ln2_bias,
    w_up,
    w_down,
    w_unpatch,
    dec_w1,
    dec_b1,
    dec_w2,
    dec_b2,
    counts,
    sample_texels,
    d_density,
    d_color,
):
    seq_size = lax.axis_size("seq")
    dp_size = lax.axis_size("dp")
    n = round(dp_size ** (1 / 3))
    shards_of = (w_qkv, w_out, w_up, w_down, w_unpatch)
    matrices = weight_list(shards_of)
    qkv, out, up, down, unpatch = matrices
    gains = [part[None] for part in (ln1_gain, ln1_bias, ln2_gain, ln2_bias)]
    scene_count = counts[None]
    index = sample_texels.transpose(1, 0, 2)
    wholes, made = forward_layer(n, seq_size, matrices, shards_of, tokens[0], gains, index, scene_count)
    gains_all, index_all, inverse_one, inverse_two = made[:4]
    hidden_all, query, keys, values, mixed, normed_one = made[4:10]
    normed_two, hidden_two, act, slope, planes, texels = made[10:]
    decoder = (dec_w1.T, dec_b1[None], dec_w2.T, dec_b2[None])
    (density, color, decoder_grads, grad_after, norm_grads), grads = split_at(
        middle(
            n,
            seq_size,
            (up, down, unpatch),
            (texels, index_all) + decoder + (d_density, d_color.transpose(1, 0, 2)),
            (planes, hidden_two, inverse_two, gains_all, act, slope, normed_two),
            wholes[2:],
        ),
        5,
    )
    block_sums, (g_tokens, *small_sums) = split_at(
        backward_attention(
            n,
            seq_size,
            (unpatch, down, up, out, qkv),
            (grad_after, mixed, query, normed_one, inverse_one, gains_all, norm_grads, decoder_grads, scene_count),
            (wholes[1], wholes[0], keys, values, hidden_all.reshape(-1, hidden_all.shape[2])),
            (grads[2], grads[1], grads[0]),
        ),
        5,
    )
    g_unpatch, g_down, g_up, g_out, g_qkv = block_sums
    gain_one, shift_one, gain_two, shift_two = [part[0] for part in small_sums[:4]]
    g_w1, g_b1, g_w2, g_b2 = small_sums[4:]
    return (
        density,
        color.transpose(1, 0, 2),
        g_tokens[None],
        gain_one,
        shift_one,
        g_qkv,
        g_out,
        gain_two,
        shift_two,
        g_up,
        g_down,
        g_unpatch,
        g_w1.T,
        g_b1[0],
        g_w2.T,
        g_b2[0],
    )


def solution(mesh):
    in_specs = (
        P("dp", "seq", None),
        P(("dp", "seq")),
        P(("dp", "seq")),
        P("dp", "seq"),
        P("dp", "seq"),
        P(("dp", "seq")),
        P(("dp", "seq")),
        P("dp", "seq"),
        P(("dp", "seq"), None),
        P("dp", "seq"),
        P(),
        P(),
        P(),
        P(),
        P("dp"),
        P("dp", None, "seq"),
        P("dp", "seq"),
        P("dp", None, "seq"),
    )
    out_specs = (
        P("dp", "seq"),
        P("dp", None, "seq"),
        P("dp", "seq", None),
        P(("dp", "seq")),
        P(("dp", "seq")),
        P("dp", "seq"),
        P("dp", "seq"),
        P(("dp", "seq")),
        P(("dp", "seq")),
        P("dp", "seq"),
        P(("dp", "seq"), None),
        P("dp", "seq"),
        P(),
        P(),
        P(),
        P(),
    )
    return jax.shard_map(shards, mesh=mesh, in_specs=in_specs, out_specs=out_specs, check_vma=False)
```

```python
import functools
import math

import jax
import jax.numpy as jnp
from jax import lax
from jax.experimental import pallas as pl
from jax.experimental.pallas import tpu as pltpu
from jax.sharding import PartitionSpec as P

HEADS = 16
PATCH = 8
CH = 32
PRES = 16


EPSILON = 1e-05
NEGATIVE = -1e30
VMEM_LIMIT = 58 * 2**20
AHEAD = 2
FIRST = 1
PIECE = 32
HIDDEN_LAG = 1
HIDDEN_FIRST = -1
HIDDEN_EVERY = 2
SUM_AT = 4
HALVES = 2
LAG = 2


MESH = pl.DeviceIdType.MESH


class Place:
    def __init__(self, n, seq_size):
        dp = lax.axis_index("dp")
        self.n, self.seq_size = n, seq_size
        self.seq = lax.axis_index("seq")
        self.i = (lax.div(dp, n * n), lax.rem(lax.div(dp, n), n), lax.rem(dp, n))
        self.dp = dp

    def size(self, axis):
        return self.seq_size if axis == 3 else self.n

    def me(self, axis):
        return self.seq if axis == 3 else self.i[axis]

    def peer(self, axis, step):
        to = lax.rem(self.me(axis) + step, self.size(axis))
        if axis == 3:
            return to, (self.dp, to)
        where = [to if a == axis else self.i[a] for a in range(3)]
        return to, ((where[0] * self.n + where[1]) * self.n + where[2], self.seq)

    def source(self, axis, step):
        size = self.size(axis)
        return lax.rem(self.me(axis) + (size - step), size)

    def enter(self, axes=(0, 1, 2, 3)):
        barrier = pltpu.get_barrier_semaphore()
        count = 0
        for axis in axes:
            for step in range(1, self.size(axis)):
                pl.semaphore_signal(
                    barrier, inc=1, device_id=self.peer(axis, step)[1], device_id_type=MESH
                )
                count += 1
        pl.semaphore_wait(barrier, count)


def remote(src, dst, send, recv, device):
    return pltpu.make_async_remote_copy(
        src_ref=src, dst_ref=dst, send_sem=send, recv_sem=recv, device_id=device, device_id_type=MESH
    )


class Line:
    def __init__(self, place):
        z = place.seq
        assert place.seq_size == 4
        self.dp, self.me = place.dp, z
        self.pair, self.far, self.opposite = z + 1 - 2 * lax.rem(z, 2), lax.rem(z + 2, 4), 3 - z
        self.middle = z * (3 - z) == 2
        self.end = z * (3 - z) == 0

    def _copy(self, source, target, send, recv, to):
        return remote(source, target, send, recv, (self.dp, to))

    def gather_start(self, region, send, recv):
        own = region(self.me)
        self._copy(own, own, send.at[0], recv.at[0], self.pair).start()
        self._copy(own, own, send.at[1], recv.at[1], self.far).start()

        @pl.when(self.middle)
        def _():
            self._copy(own, own, send.at[2], recv.at[2], self.opposite).start()

    def gather_relay(self, region, send, recv):
        block = region(self.far)
        self._copy(block, block, send.at[1], recv.at[1], self.far).wait_recv()

        @pl.when(self.middle)
        def _():
            self._copy(block, block, send.at[3], recv.at[2], self.pair).start()

    def gather_take(self, region, send, recv, which=("pair", "opposite")):
        for i, name, j in ((0, "pair", self.pair), (2, "opposite", self.opposite)):
            if name in which:
                self._copy(region(j), region(j), send.at[i], recv.at[i], self.pair).wait_recv()

    def gather_finish(self, region, send, recv):
        own = region(self.me)
        for i in (0, 1):
            self._copy(own, own, send.at[i], recv.at[i], self.pair).wait_send()

        @pl.when(self.middle)
        def _():
            for i in (2, 3):
                self._copy(own, own, send.at[i], recv.at[2], self.pair).wait_send()

    def sum_start(self, region, slot, send, recv, which=("opposite", "far", "pair")):
        if "opposite" in which:
            block = region(self.opposite)

            @pl.when(self.middle)
            def _():
                self._copy(block, slot(2), send.at[2], recv.at[2], self.opposite).start()

            @pl.when(self.end)
            def _():
                self._copy(block, slot(3), send.at[2], recv.at[3], self.pair).start()

        if "far" in which:

            @pl.when(self.end)
            def _():
                self._copy(region(self.far), slot(1), send.at[1], recv.at[1], self.far).start()

        if "pair" in which:
            self._copy(region(self.pair), slot(0), send.at[0], recv.at[0], self.pair).start()

    def sum_relay(self, region, slot, send, recv, add):
        @pl.when(self.middle)
        def _():
            block = region(self.far)
            self._copy(block, slot(3), send.at[2], recv.at[3], self.pair).wait_recv()
            add(self.far)
            self._copy(block, slot(1), send.at[1], recv.at[1], self.far).start()

    def sum_take(self, region, slot, send, recv):
        for i in (0, 1):
            self._copy(region(self.me), slot(i), send.at[i], recv.at[i], self.pair).wait_recv()

        @pl.when(self.middle)
        def _():
            self._copy(region(self.me), slot(2), send.at[2], recv.at[2], self.pair).wait_recv()

    def sum_of(self, own, slots):
        total = own.astype(jnp.float32) + slots(0).astype(jnp.float32) + slots(1).astype(jnp.float32)
        return total + jnp.where(self.middle, slots(2).astype(jnp.float32), 0.0)

    def sum_finish(self, region, slot, send, recv):
        for i in (0, 1, 2):
            self._copy(region(self.me), slot(0), send.at[i], recv.at[0], self.pair).wait_send()


class Matrix:
    def __init__(self, name, rows, cols, by_rows, parts):
        self.name, self.rows, self.cols, self.by_rows = name, rows, cols, by_rows
        self.parts = parts if rows % (16 * parts) == 0 else 1

    def shape(self, n, seq_size):
        if self.by_rows:
            return (n, n, n, seq_size, self.rows, self.cols)
        return (n, n, n, self.rows, seq_size * self.cols)

    def tail(self, part, first, count):
        size = self.rows // self.parts
        rows = pl.ds(part * size, size)
        if self.by_rows:
            return (pl.ds(first, count), rows, slice(None))
        if isinstance(first, int):
            return (rows, pl.ds(first * self.cols, count * self.cols))
        return (rows, pl.ds(pl.multiple_of(first * self.cols, 128), count * self.cols))

    def tail_shape(self, count):
        size = self.rows // self.parts
        return (count, size, self.cols) if self.by_rows else (size, count * self.cols)


def small_stage(place, value, slots, send, recv, stage, axis):
    me = place.me(axis)
    slots[stage, me] = value
    copies = []
    for step in range(1, place.size(axis)):
        ref = slots.at[stage, me]
        copy = remote(
            ref, ref, send.at[stage, step - 1], recv.at[stage, step - 1], place.peer(axis, step)[1]
        )
        copy.start()
        copies.append(copy)

    def end():
        for copy in copies:
            copy.wait()
        total = slots[stage, 0]
        for other in range(1, place.size(axis)):
            total = total + slots[stage, other]
        return total

    return end


def small_sum(place, parts, between=None):
    values = [part[0] for part in parts]
    for stage, axis in enumerate((2, 1, 0, 3)):
        ends = [small_stage(place, v, *part[1:], stage, axis) for v, part in zip(values, parts)]
        if between is not None:
            between()
        values = [end() for end in ends]
    return values


class Gather:
    def __init__(self, place, matrices, refs, sems):
        self.place, self.refs, self.line = place, refs, Line(place)
        self.chunks = [(w, m, p) for w, m in enumerate(matrices) for p in range(m.parts)]
        self.seq_send, self.seq_recv, self.hop_send, self.hop_recv, self.far_send, self.far_recv = sems
        self.copies = {}

    def _send(self, key, axis, region, send, recv):
        made = []
        for step in range(1, self.place.size(axis)):
            copy = remote(region, region, send.at[step - 1], recv.at[step - 1], self.place.peer(axis, step)[1])
            copy.start()
            made.append(copy)
        self.copies[key] = made

    def _take(self, key):
        for copy in self.copies[key]:
            copy.wait_recv()

    def region(self, k, index, first, count):
        w, matrix, part = self.chunks[k]
        return self.refs[w].at[index + matrix.tail(part, first, count)]

    def _along(self, k):
        return lambda j: self.region(k, self.place.i, j, 1), self.seq_send.at[k], self.seq_recv.at[k]

    def along_seq(self, k):
        self.line.gather_start(*self._along(k))

    def relay(self, k):
        self.line.gather_relay(*self._along(k))

    def hop(self, k, number):
        p, half = self.place, self.place.seq_size // 2
        if number == 0:
            self.line.gather_take(*self._along(k))
        else:
            self._take((k, 1, 0))
            self._take((k, 1, 1))
        for h in (0, 1):
            axis = 1 - h if number == 0 else h
            index = [p.i[0], p.i[1], p.i[2]]
            if number == 1:
                index[1 - axis] = slice(None)
            at = 2 * number + h
            region = self.region(k, tuple(index), h * half, half)
            self._send((k, 1 + number, h), axis, region, self.hop_send.at[k, at], self.hop_recv.at[k, at])

    def third(self, k):
        p = self.place
        self._take((k, 2, 0))
        self._take((k, 2, 1))
        region = self.region(k, (slice(None), slice(None), p.i[2]), 0, p.seq_size)
        self._send((k, 3), 2, region, self.far_send.at[k], self.far_recv.at[k])

    def arrived(self, k):
        self._take((k, 3))

    def finish(self):
        for k in range(len(self.chunks)):
            self.line.gather_finish(*self._along(k))
        for made in self.copies.values():
            for copy in made:
                copy.wait_send()


def gather_sems(n, seq_size, chunks):
    sem = pltpu.SemaphoreType.DMA
    return [sem((chunks, 4)), sem((chunks, 3))] + [sem((chunks, 4, n - 1))] * 2 + [sem((chunks, n - 1))] * 2


def gelu_parts(x):
    cdf = 0.5 + 0.5 * lax.erf(x * (0.5**0.5))
    return x * cdf, cdf + x * (jnp.exp(-0.5 * x * x) * (2.0 * math.pi) ** -0.5)


def split_low(x):
    high = x.astype(jnp.bfloat16)
    return high, (x - high.astype(jnp.float32)).astype(jnp.bfloat16)


def texel_place(texel, seq_size, me):
    side, quarter = PRES * PATCH, PRES * PRES // seq_size
    row, col = texel // side, texel % side
    token = row // PATCH * PRES + col // PATCH
    a, b = row % PATCH, col % PATCH
    fold = PATCH // 2
    mine = token // quarter == me
    key = jnp.where(mine, a // 2 * quarter + token % quarter, -1)
    return key, a % 2 * PATCH + b, fold


def decode_both(
    place,
    grad_texels,
    tile,
    texels,
    index,
    w1,
    b1,
    w2,
    b2,
    d_density,
    d_color,
    density,
    color,
    grads,
    tables,
    grad_tables,
    features,
    part_out,
    part_in,
    own_part,
    grad_all,
    send_sem,
    recv_sem,
    back_send,
    back_recv,
):
    seq_size = place.seq_size
    bfloat, f32 = jnp.bfloat16, jnp.float32
    samples = index.shape[3]
    quarter = PRES * PRES // seq_size
    width = texels.shape[1]
    groups = 2 * PATCH
    cols = groups * CH
    depth = width // cols * quarter
    hidden, inputs = w1.shape
    line = Line(place)
    for p in range(3):
        own = texels[p * quarter : (p + 1) * quarter].astype(f32)
        stacked = jnp.concatenate([own[:, i * cols : (i + 1) * cols] for i in range(width // cols)], axis=0)
        tables[p] = stacked.T.astype(bfloat)
    w1_high, w1_low = split_low(w1[...])
    w1_stack = jnp.concatenate([w1_high, w1_low], axis=0)
    tiles = samples // tile // HALVES
    size = samples // HALVES

    def one_hot(source, at, p):
        texel = index[source, p, :, at]
        key, group, _ = texel_place(texel, seq_size, place.seq)
        rows = lax.broadcasted_iota(jnp.int32, (depth, tile), 0)
        return (rows == key).astype(f32).astype(bfloat), group

    def forward(source, h):
        @pl.loop(h * tiles, (h + 1) * tiles)
        def _(t):
            at = pl.ds(pl.multiple_of(t * tile, tile), tile)
            picked = []
            for p in range(3):
                hot, group = one_hot(source, at, p)
                spread = matmul(tables[p], hot)
                total = jnp.where(group == 0, spread[:CH], 0.0)
                for g in range(1, groups):
                    total = total + jnp.where(group == g, spread[g * CH : (g + 1) * CH], 0.0)
                picked.append(total)
            feature = jnp.concatenate(picked, axis=0).astype(bfloat)
            features[source, :, at] = feature
            both = matmul(w1_stack, feature)
            part = both[:hidden] + both[hidden:]
            own_part[:, at] = part
            part_out[source, :, at] = part.astype(bfloat)

    def forward_line(h):
        at = pl.ds(h * size, size)
        return lambda j: part_out.at[j, :, at], lambda i: part_in.at[i, :, at], send_sem.at[h], recv_sem.at[h]

    def back_line(h):
        at = pl.ds(h * size, size)
        return lambda j: grad_all.at[j, :, at], back_send.at[h], back_recv.at[h]

    for h in range(HALVES):
        for name, j in (("opposite", line.opposite), ("far", line.far), ("pair", line.pair)):
            forward(j, h)
            line.sum_start(*forward_line(h), which=(name,))
        forward(place.seq, h)
        at = pl.ds(h * size, size)

        def add(j, at=at):
            part_out[j, :, at] = (part_out[j, :, at].astype(f32) + part_in[3, :, at].astype(f32)).astype(bfloat)

        line.sum_relay(*forward_line(h), add)
    highest = lax.Precision.HIGHEST
    tn, nt = (((0,), (0,)), ((), ())), (((1,), (1,)), ((), ()))
    ones = jnp.ones((8, size), f32)

    def eight(x):
        return jnp.concatenate([x, jnp.zeros((8 - x.shape[0], x.shape[1]), f32)], axis=0)

    def dot(left, right, dims):
        return lax.dot_general(left, right, dims, precision=highest, preferred_element_type=f32)

    grads[...] = jnp.zeros(grads.shape, f32)
    grad_tables[...] = jnp.zeros(grad_tables.shape, f32)
    outs = w2.shape[0]
    me = place.seq
    for h in range(HALVES):
        at = pl.ds(h * size, size)
        line.sum_take(*forward_line(h))
        pre = line.sum_of(own_part[:, at], lambda i: part_in[i, :, at]) + dot(eight(b1[...]), ones, tn)
        act, slope = gelu_parts(pre)
        out = jnp.dot(w2[...], act, precision=highest, preferred_element_type=f32) + dot(eight(b2[...]), ones, tn)
        gate = 1.0 / (1.0 + jnp.exp(-out))
        first = out[:1]
        density[:, at] = jnp.maximum(first, 0.0) + jnp.log1p(jnp.exp(-jnp.abs(first)))
        rows = [d_density[:, at] * gate[:1]]
        for p in range(3):
            own = gate[p + 1 : p + 2]
            color[p, :, at] = own
            rows.append(d_color[p, :, at] * own * (1.0 - own))
        grad_out = jnp.concatenate(rows, axis=0)
        grad_pre = dot(eight(w2[...]), eight(grad_out), tn) * slope
        grad_all[me, :, at] = grad_pre.astype(bfloat)
        line.gather_start(*back_line(h))
        grads[hidden : hidden + outs, :hidden] += dot(grad_out, act, nt)
        grads[hidden + 8 : hidden + 9, :hidden] += dot(ones, grad_pre, nt)[:1]
        grads[hidden + 16 : hidden + 17, :outs] += dot(ones, grad_out, nt)[:1]

    def backward(source, h):
        @pl.loop(h * tiles, (h + 1) * tiles)
        def _(t):
            at = pl.ds(pl.multiple_of(t * tile, tile), tile)
            grad = grad_all[source, :, at]
            grads[:hidden, :inputs] += matmul_nt(grad, features[source, :, at])
            grad_feature = matmul_tn(w1_high, grad) + matmul_tn(w1_low, grad)
            for p in range(3):
                hot, group = one_hot(source, at, p)
                mine = grad_feature[p * CH : (p + 1) * CH]
                spread = jnp.concatenate(
                    [jnp.where(group == g, mine, 0.0) for g in range(groups)], axis=0
                ).astype(bfloat)
                grad_tables[p] += matmul_nt(spread, hot)

    for h in range(HALVES):
        backward(me, h)
        line.gather_relay(*back_line(h))
    for h in range(HALVES):
        backward(line.far, h)
        line.gather_take(*back_line(h), which=("pair",))
        backward(line.pair, h)
        line.gather_take(*back_line(h), which=("opposite",))
        backward(line.opposite, h)
    for p in range(3):
        back = grad_tables[p].T
        for i in range(width // cols):
            block = back[i * quarter : (i + 1) * quarter].astype(bfloat)
            grad_texels[p * quarter : (p + 1) * quarter, i * cols : (i + 1) * cols] = block
    for h in range(HALVES):
        line.sum_finish(*forward_line(h))
        line.gather_finish(*back_line(h))


def core_columns(ref, n, segment, to):
    width = ref.shape[1]
    parts = width // (n * segment)
    if segment % 128 == 0:
        places = [pl.multiple_of((q * n + to) * segment, 128) for q in range(parts)]
        return jnp.concatenate([ref[:, pl.ds(at, segment)] for at in places], axis=1).T
    place = lax.broadcasted_iota(jnp.int32, (width, width // n), 1)
    source = (lax.div(place, segment) * n + to) * segment + lax.rem(place, segment)
    pick = lax.broadcasted_iota(jnp.int32, (width, width // n), 0) == source
    return matmul(ref[...], pick.astype(jnp.float32).astype(jnp.bfloat16)).astype(jnp.bfloat16).T


class Exchange:
    def __init__(self, place, send, recv):
        self.place, self.send, self.recv = place, send, recv
        self.made, self.used = [], 0

    def _start(self, source_of, buf):
        copies, p = [], self.place
        for step in range(1, p.size(2)):
            to, device = p.peer(2, step)
            sems = (self.send.at[self.used, step - 1], self.recv.at[self.used, step - 1])
            copy = remote(source_of(step, to), buf.at[p.i[2]], *sems, device)
            copy.start()
            copies.append(copy)
        self.used += 1
        self.made += copies

        def wait():
            for copy in copies:
                copy.wait_recv()

        return wait

    def columns(self, ref, segment, split, buf):
        p = self.place
        for step in range(1, p.size(2)):
            split[step - 1] = core_columns(ref, p.n, segment, p.peer(2, step)[0])
        wait = self._start(lambda step, to: split.at[step - 1], buf)
        buf[p.i[2]] = core_columns(ref, p.n, segment, p.i[2])
        return wait

    def rows(self, buf):
        return self._start(lambda step, to: buf.at[self.place.i[2]], buf)

    def finish(self):
        for copy in self.made:
            copy.wait_send()


def weight_grad(left, right, grad, first=0, tile=512):
    shape, width = grad.shape[:-1], right.shape[-1]
    for at in range(0, width, tile):
        size = min(tile, width - at)
        block = matmul(left[0], right[0, :, at : at + size])
        for i in range(1, left.shape[0]):
            block = block + matmul(left[i], right[i, :, at : at + size])
        grad[..., first + at : first + at + size] = block.astype(jnp.bfloat16).reshape(shape + (size,))


def norm_back(grad, normed, inverse, gain):
    scaled = grad * gain
    inner = scaled - jnp.mean(scaled, axis=-1, keepdims=True)
    inner = inner - normed * jnp.mean(scaled * normed, axis=-1, keepdims=True)
    return inner * inverse


def feed_back(place, matrices, refs):
    (planes, hidden_two, inverse_two, gains, act_in, slope_in, normed_in, weights) = refs[:8]
    (grads_out, grad_after, norm_grads, bufs) = refs[8:12]
    (planes_split, planes_all, act_split, act_all, hidden_split, hidden_all) = refs[12:18]
    (texels_all, layer_all, pre_all, layer, act, slope, normed_two, load_sem, out_sem, send, recv) = refs[18:29]
    grads = [buf.at[0] for buf in bufs]
    n = place.n
    bfloat, f32 = jnp.bfloat16, jnp.float32
    up, down, unpatch = matrices
    w_up, w_down, w_unpatch = bufs
    exchange = Exchange(place, send, recv)
    me = place.i[2]
    loads, waits = [], []

    def start():
        pairs = [(act_in, act)] + [(weights[k], bufs[k]) for k in (2, 1, 0)] + [(slope_in, slope), (normed_in, normed_two)]
        for k, (source, target) in enumerate(pairs):
            copy = pltpu.make_async_copy(source, target, load_sem.at[k])
            copy.start()
            loads.append(copy)

    def start_remote():
        waits.append(exchange.columns(planes, unpatch.rows, planes_split, planes_all))
        loads[0].wait()
        waits.append(exchange.columns(act, place.seq_size * down.rows, act_split, act_all))
        waits.append(exchange.columns(hidden_two, up.rows, hidden_split, hidden_all))

    outs = []

    def put(k):
        copy = pltpu.make_async_copy(grads[k], grads_out[k], out_sem.at[k])
        copy.start()
        outs.append(copy)

    def end():
        got_texels = exchange.rows(texels_all)
        loads[1].wait()
        grad_texels = texels_all[me]
        step = layer.shape[1] // n
        for i in range(n):
            block = w_unpatch[i].reshape(step, -1)
            layer[:, i * step : (i + 1) * step] = matmul_nt(grad_texels, block)
        layer_all[me] = layer[...].astype(bfloat)
        got_layer = exchange.rows(layer_all)
        loads[2].wait()
        loads[4].wait()
        step = act.shape[1] // (n * n)
        for i in range(n):
            for j in range(n):
                block = w_down[i, j].reshape(step, -1)
                at = (i * n + j) * step
                value = matmul_nt(layer_all[me], block) * slope[:, at : at + step].astype(f32)
                pre_all[me, :, at : at + step] = value.astype(bfloat)
        got_pre = exchange.rows(pre_all)
        waits[0]()
        got_texels()
        weight_grad(planes_all, texels_all, grads[2])
        put(2)
        loads[3].wait()
        loads[5].wait()
        step = layer.shape[1] // n
        pieces = []
        for i in range(n):
            block = w_up[i].reshape(step, -1)
            pieces.append(matmul_nt(pre_all[me], block))
        grad = jnp.concatenate(pieces, axis=1)
        normed = normed_two[...]
        norm_grads[0:1] = jnp.sum(grad * normed, axis=0, keepdims=True)
        norm_grads[1:2] = jnp.sum(grad, axis=0, keepdims=True)
        grad_after[...] = layer[...] + norm_back(grad, normed, inverse_two[...], gains[2:3])
        waits[1]()
        got_layer()
        weight_grad(act_all, layer_all, grads[1])
        put(1)
        waits[2]()
        got_pre()
        weight_grad(hidden_all, pre_all, grads[0])
        put(0)
        exchange.finish()
        for copy in outs:
            copy.wait()

    return start, start_remote, end


def middle_kernel(n, seq_size, matrices, *refs):
    refs = list(refs)

    def take(k):
        taken = refs[:k]
        del refs[:k]
        return taken

    decode_in, feed_in, weights = take(8), take(7), take(3)
    density, color, decoder_grads, grad_after, norm_grads = take(5)
    grads_out, bufs, decode_scratch = take(3), take(3), take(11)
    place = Place(n, seq_size)
    feed = list(feed_in) + [weights, grads_out, grad_after, norm_grads, bufs] + refs
    texels_all = refs[6]
    start, start_remote, end = feed_back(place, matrices, feed)
    start()
    place.enter((2, 3))
    start_remote()
    tile = min(512, decode_in[1].shape[3])
    outs = (density, color, decoder_grads)
    decode_both(place, texels_all.at[place.i[2]], tile, *decode_in, *outs, *decode_scratch)
    end()


def middle(n, seq_size, matrices, decode_in, feed_in, weights):
    texels, index, w1, b1, w2, b2, d_density, d_color = decode_in
    planes, hidden_two, inverse_two, gains, act, slope, normed_two = feed_in
    bfloat, f32 = jnp.bfloat16, jnp.float32
    samples, hidden = index.shape[3], w1.shape[0]
    quarter = PRES * PRES // seq_size
    cols = 2 * PATCH * CH
    depth = texels.shape[1] // cols * quarter
    vmem, any_space = pl.BlockSpec(memory_space=pltpu.VMEM), pl.BlockSpec(memory_space=pl.ANY)
    sem = pltpu.SemaphoreType.DMA
    rows, width = normed_two.shape
    ff, core_ff = act.shape[1], act.shape[1] // n
    shapes = [m.shape(n, seq_size) for m in matrices]
    halves = [(n, n) + s[3:] for s in shapes]
    return pl.pallas_call(
        functools.partial(middle_kernel, n, seq_size, matrices),
        out_shape=[
            jax.ShapeDtypeStruct((1, samples), f32),
            jax.ShapeDtypeStruct((3, 1, samples), f32),
            jax.ShapeDtypeStruct((hidden + 24, 128), f32),
            jax.ShapeDtypeStruct((rows, width), f32),
            jax.ShapeDtypeStruct((2, width), f32),
        ]
        + [jax.ShapeDtypeStruct(s, bfloat) for s in halves],
        in_specs=[vmem] * 12 + [any_space] * 6,
        out_specs=[vmem] * 5 + [any_space] * 3,
        scratch_shapes=[pltpu.VMEM(s, bfloat) for s in shapes]
        + [
            pltpu.VMEM((3, cols, depth), bfloat),
            pltpu.VMEM((3, cols, depth), f32),
            pltpu.VMEM((seq_size, 3 * CH, samples), bfloat),
            pltpu.VMEM((seq_size, hidden, samples), bfloat),
            pltpu.VMEM((4, hidden, samples), bfloat),
            pltpu.VMEM((hidden, samples), f32),
            pltpu.VMEM((seq_size, hidden, samples), bfloat),
        ]
        + [sem((HALVES, 3)), sem((HALVES, 4)), sem((HALVES, 4)), sem((HALVES, 3))]
        + [
            pltpu.VMEM((n - 1, width // n, rows), bfloat),
            pltpu.VMEM((n, width // n, rows), bfloat),
            pltpu.VMEM((n - 1, core_ff, rows), bfloat),
            pltpu.VMEM((n, core_ff, rows), bfloat),
            pltpu.VMEM((n - 1, width // n, rows), bfloat),
            pltpu.VMEM((n, width // n, rows), bfloat),
            pltpu.VMEM((n,) + texels.shape, bfloat),
            pltpu.VMEM((n, rows, width), bfloat),
            pltpu.VMEM((n, rows, ff), bfloat),
            pltpu.VMEM((rows, width), f32),
            pltpu.VMEM((rows, ff), bfloat),
            pltpu.VMEM((rows, ff), bfloat),
            pltpu.VMEM((rows, width), f32),
            sem((6,)),
            sem((3,)),
        ]
        + [sem((8, n - 1))] * 2,
        compiler_params=pltpu.CompilerParams(
            collective_id=2, has_side_effects=True, vmem_limit_bytes=VMEM_LIMIT
        ),
    )(*decode_in, *feed_in, *weights)


class Scatter:
    def __init__(self, place, matrices, sources, kept, hops, near, outs, sems):
        self.place, self.sources, self.kept = place, sources, kept
        self.hops, self.near, self.outs, self.line = hops, near, outs, Line(place)
        self.chunks = [(w, m, p) for w, m in enumerate(matrices) for p in range(m.parts)]
        self.load_sem, self.seq_send, self.seq_recv, self.hop_send, self.hop_recv = sems
        self.copies, self.loads = {}, {}

    def _send(self, key, axis, region_to, slot, send, recv):
        made = []
        for step in range(1, self.place.size(axis)):
            to, device = self.place.peer(axis, step)
            copy = remote(region_to(to), slot(step - 1), send.at[step - 1], recv.at[step - 1], device)
            copy.start()
            made.append(copy)
        self.copies[key] = made

    def _take(self, key):
        for copy in self.copies[key]:
            copy.wait_recv()

    def hop(self, k, number):
        w, matrix, part = self.chunks[k]
        p, half, n = self.place, self.place.seq_size // 2, self.place.n
        kept, every = self.kept[w], slice(None)
        local = matrix.tail(part, 0, half)
        if number == 0:
            for h in (0, 1):
                index = (p.i[0], every) if h == 0 else (every, p.i[1])
                source = self.sources[w].at[index + matrix.tail(part, h * half, half)]
                copy = pltpu.make_async_copy(source, kept.at[(h, every) + local], self.load_sem.at[k, h])
                copy.start()
                self.loads[k, h] = copy
        else:
            for h in (0, 1):
                self.loads[k, h].wait()
                self._take((k, 1, h))
                for a in range(n):
                    value = kept[(h, a) + local].astype(jnp.float32)
                    for s in range(n - 1):
                        value = value + self.hops[w][(h, s, a) + local].astype(jnp.float32)
                    kept[(h, a) + local] = value.astype(jnp.bfloat16)
        for h in (0, 1):
            axis = h if number == 0 else 1 - h
            tail, at = matrix.tail(part, h * half, half), 2 * number + h

            def region_to(to, h=h, tail=tail):
                if number == 1:
                    return kept.at[(h, to) + local]
                return self.sources[w].at[((to, every) if h == 0 else (every, to)) + tail]

            def slot(s, h=h):
                return self.hops[w].at[(h, s, pl.ds(0, n) if number == 0 else n) + local]

            self._send((k, 1 + number, h), axis, region_to, slot, self.hop_send.at[k, at], self.hop_recv.at[k, at])

    def _block(self, matrix, part, j):
        p, half = self.place, self.place.seq_size // 2
        h = lax.div(j, half)
        return (h, p.i[1] + h * (p.i[0] - p.i[1])) + matrix.tail(part, lax.rem(j, half), 1)

    def along_seq(self, k):
        w, matrix, part = self.chunks[k]
        p, half, n = self.place, self.place.seq_size // 2, self.place.n
        kept = self.kept[w]
        local = matrix.tail(part, 0, half)
        for h in (0, 1):
            self._take((k, 2, h))
            value = kept[(h, p.i[1 - h]) + local].astype(jnp.float32)
            for s in range(n - 1):
                value = value + self.hops[w][(h, s, n) + local].astype(jnp.float32)
            kept[(h, p.i[1 - h]) + local] = value.astype(jnp.bfloat16)
        self.line.sum_start(*self._along(k))

    def _along(self, k):
        w, matrix, part = self.chunks[k]
        kept, near, own = self.kept[w], self.near[w], matrix.tail(part, 0, 1)
        region, slot = lambda j: kept.at[self._block(matrix, part, j)], lambda i: near.at[(i,) + own]
        return region, slot, self.seq_send.at[k], self.seq_recv.at[k]

    def relay(self, k):
        w, matrix, part = self.chunks[k]
        kept, own = self.kept[w], matrix.tail(part, 0, 1)

        def add(j):
            at = self._block(matrix, part, j)
            kept[at] = (kept[at].astype(jnp.float32) + self.near[w][(3,) + own].astype(jnp.float32)).astype(jnp.bfloat16)

        self.line.sum_relay(*self._along(k), add)

    def arrived(self, k):
        w, matrix, part = self.chunks[k]
        own = matrix.tail(part, 0, 1)
        self.line.sum_take(*self._along(k))
        value = self.kept[w][self._block(matrix, part, self.place.seq)]
        value = self.line.sum_of(value, lambda i: self.near[w][(i,) + own])
        size = matrix.rows // matrix.parts
        self.outs[w][pl.ds(part * size, size)] = value.reshape(size, matrix.cols)

    def finish(self):
        for k in range(len(self.chunks)):
            self.line.sum_finish(*self._along(k))
        for made in self.copies.values():
            for copy in made:
                copy.wait_send()


def backward_kernel(n, seq_size, matrices, *refs):
    count = len(matrices)
    refs = list(refs)

    def take(k):
        taken = refs[:k]
        del refs[:k]
        return taken

    grad_after, mixed, query, normed_one, inverse_one, gains, norm_grads, decoder_grads, scene_count = take(9)
    w_out_in, w_qkv_in, keys_in, values_in, hidden_all_in = take(5)
    early = take(count - 2)
    outs = take(count)
    g_tokens, *norm_outs = take(5)
    g_w1, g_b1, g_w2, g_b2 = take(4)
    w_out, w_qkv, work = take(3)
    g_out, g_qkv = w_out.at[0], w_qkv.at[0]
    kept, hops, near = take(count), take(count), take(count)
    mixed_split, mixed_all, after_all, hidden_split, hidden_core, own_split, own_core = take(7)
    query_all, grad_all, hidden_in = take(3)
    grad_mixed, load_sem, core_send, core_recv, hidden_send, hidden_recv = take(6)
    norm_part, decoder_part = take(3), take(3)
    sems = refs
    bfloat, f32 = jnp.bfloat16, jnp.float32
    place = Place(n, seq_size)
    me = place.i[2]
    loads = []
    rows, width = query.shape
    token_rows = normed_one.shape[0]
    keys, values = grad_all.at[me, :, pl.ds(0, width)], grad_all.at[me, :, pl.ds(width, width)]
    for k, (source, target) in enumerate(
        ((hidden_all_in, work), (w_out_in, w_out), (keys_in, keys), (values_in, values), (w_qkv_in, w_qkv))
    ):
        copy = pltpu.make_async_copy(source, target, load_sem.at[k])
        copy.start()
        loads.append(copy)
    place.enter()
    scatter = Scatter(place, matrices, list(early) + [g_out, g_qkv], kept, hops, near, outs, sems)
    total = len(scatter.chunks)
    state = [0]

    def advance():
        t = state[0]
        state[0] += 1
        if t < total:
            scatter.hop(t, 0)
        if 0 <= t - LAG < total:
            scatter.hop(t - LAG, 1)
        if 0 <= t - 2 * LAG < total:
            scatter.along_seq(t - 2 * LAG)
        if 0 <= t - 2 * LAG - 1 < total:
            scatter.relay(t - 2 * LAG - 1)
        if 0 <= t - 3 * LAG - 1 < total:
            scatter.arrived(t - 3 * LAG - 1)

    line = Line(place)
    advance()
    advance()
    exchange = Exchange(place, core_send, core_recv)
    out_matrix, qkv_matrix = matrices[-2:]
    got_mixed = exchange.columns(mixed, out_matrix.rows, mixed_split, mixed_all)
    after_all[me] = grad_after[...].astype(bfloat)
    got_after = exchange.rows(after_all)
    loads[0].wait()
    own = work.at[pl.ds(pl.multiple_of(place.seq * token_rows, 16), rows)]
    got_own = exchange.columns(own, qkv_matrix.rows, own_split, own_core)
    got_hidden = exchange.columns(work, qkv_matrix.rows, hidden_split, hidden_core)
    loads[1].wait()
    step = width // n
    for i in range(n):
        block = w_out[i].reshape(step, width)
        grad_mixed[:, i * step : (i + 1) * step] = matmul_nt(after_all[me], block).astype(bfloat)
    got_mixed()
    got_after()
    weight_grad(mixed_all, after_all, g_out)
    loads[2].wait()
    loads[3].wait()
    valid = key_valid(scene_count, seq_size, rows, token_rows, 0)
    pair = 2 * width // HEADS
    scale = (width // HEADS) ** (-0.5)
    first = lax.broadcasted_iota(jnp.int32, (rows, pair), 1) < pair // 2
    pairs, segments = HEADS // 2, 4
    for segment in range(segments):

        @pl.loop(segment * pairs // segments, (segment + 1) * pairs // segments)
        def _(p):
            at = pl.ds(pl.multiple_of(p * pair, pair), pair)
            query_two, grad_two = query[:, at].astype(f32) * scale, grad_mixed[:, at].astype(f32)
            later = pl.ds(pl.multiple_of(width + p * pair, pair), pair)
            key_two, value_two = grad_all[me, :, at], grad_all[me, :, later]
            key_turned = key_two.T
            grad_key, grad_value, turned = 0.0, 0.0, []
            for h, mine in enumerate((first, ~first)):
                query_h = jnp.where(mine, query_two, 0.0).astype(bfloat)
                grad_h = jnp.where(mine, grad_two, 0.0).astype(bfloat)
                scores = jnp.where(valid, matmul_nt(key_two, query_h), NEGATIVE)
                expo = jnp.exp(scores - jnp.max(scores, axis=0, keepdims=True))
                probs = expo * (1.0 / jnp.sum(expo, axis=0, keepdims=True))
                grad_value = grad_value + matmul(probs.astype(bfloat), grad_h)
                grad_probs = matmul_nt(value_two, grad_h)
                inner = jnp.sum(probs * grad_probs, axis=0, keepdims=True)
                grad_scores = (probs * (grad_probs - inner)).astype(bfloat)
                grad_key = grad_key + matmul(grad_scores, query_h)
                grad_query = matmul(key_turned, grad_scores)
                turned.append(grad_query[h * (pair // 2) : (h + 1) * (pair // 2)])
            query_all[me, :, at] = (jnp.concatenate(turned, axis=0) * scale).T.astype(bfloat)
            grad_all[me, :, at] = grad_key.astype(bfloat)
            grad_all[me, :, later] = grad_value.astype(bfloat)

        advance()
    got_grad = exchange.rows(grad_all)
    got_query = exchange.rows(query_all)
    loads[4].wait()
    for i in range(n):
        block = w_qkv[i].reshape(step, 3 * width)
        work[:, i * step : (i + 1) * step] = matmul_nt(grad_all[me], block[:, width:]).astype(bfloat)
    pieces = [matmul_nt(query_all[me], w_qkv[i].reshape(step, 3 * width)[:, :width]) for i in range(n)]
    from_query = jnp.concatenate(pieces, axis=1)
    hidden_line = (
        lambda j: work.at[pl.ds(pl.multiple_of(j * token_rows, 16), token_rows)],
        lambda i: hidden_in.at[i],
        hidden_send,
        hidden_recv,
    )
    line.sum_start(*hidden_line)
    advance()
    got_grad()
    got_query()
    got_hidden()
    got_own()
    weight_grad(own_core, query_all, g_qkv)

    def add(j):
        at = pl.ds(pl.multiple_of(j * token_rows, 16), token_rows)
        work[at] = (work[at].astype(f32) + hidden_in[3].astype(f32)).astype(bfloat)

    line.sum_relay(*hidden_line, add)
    weight_grad(hidden_core, grad_all, g_qkv, width)
    advance()
    advance()
    line.sum_take(*hidden_line)
    grad = line.sum_of(work[pl.ds(pl.multiple_of(place.seq * token_rows, 16), token_rows)], lambda i: hidden_in[i])
    rest = jnp.zeros((token_rows - rows, width), f32)
    grad = grad + jnp.concatenate([from_query, rest], axis=0)
    normed = normed_one[...]
    g_tokens[...] = norm_back(grad, normed, inverse_one[...], gains[0:1])
    g_tokens[0:rows] += grad_after[...]
    gain_row = jnp.sum(grad * normed, axis=0, keepdims=True)
    shift_row = jnp.sum(grad, axis=0, keepdims=True)
    norm_rows = jnp.concatenate([gain_row, shift_row, norm_grads[...], jnp.zeros((4, width), f32)], axis=0)
    parts = [(norm_rows, *norm_part), (decoder_grads[...], *decoder_part)]
    norm_sums, decoder_sums = small_sum(place, parts, advance)
    own = norm_outs[0].shape[1]
    spot = lax.broadcasted_iota(jnp.int32, (width, own), 0) - lax.broadcasted_iota(jnp.int32, (width, own), 1)
    pick = (spot == (place.dp * seq_size + place.seq) * own).astype(f32)
    picked = jnp.dot(norm_sums, pick, precision=lax.Precision.HIGHEST, preferred_element_type=f32)
    for i, ref in enumerate(norm_outs):
        ref[...] = picked[i : i + 1]
    hidden, inputs = g_w1.shape
    g_w1[...] = decoder_sums[:hidden, :inputs]
    g_w2[...] = decoder_sums[hidden : hidden + g_w2.shape[0], :hidden]
    g_b1[...] = decoder_sums[hidden + 8 : hidden + 9, :hidden]
    g_b2[...] = decoder_sums[hidden + 16 : hidden + 17, : g_b2.shape[1]]
    while state[0] < total + 3 * LAG + 1:
        advance()
    scatter.finish()
    exchange.finish()
    line.sum_finish(*hidden_line)


def finish(values):
    def kernel(*refs):
        for source, target in zip(refs[: len(values)], refs[len(values) :]):
            target[...] = source[...]

    vmem = [pl.BlockSpec(memory_space=pltpu.VMEM)] * len(values)
    return pl.pallas_call(
        kernel,
        out_shape=[jax.ShapeDtypeStruct(x.shape, x.dtype) for x in values],
        in_specs=vmem,
        out_specs=vmem,
    )(*values)


def half_tail(matrix, seq_size):
    half = seq_size // 2
    if matrix.by_rows:
        return (half, matrix.rows, matrix.cols)
    return (matrix.rows, half * matrix.cols)


def backward_attention(n, seq_size, matrices, inputs, loaded, early):
    grad_after, mixed, query, normed_one, inverse_one, gains, norm_grads, decoder_grads, scene_count = inputs
    own = query.shape[1] // (lax.axis_size("dp") * seq_size)
    hidden, features, outs = decoder_grads.shape[0] - 24, 3 * CH, 4
    bfloat, f32 = jnp.bfloat16, jnp.float32
    vmem, any_space = pl.BlockSpec(memory_space=pltpu.VMEM), pl.BlockSpec(memory_space=pl.ANY)
    shapes = [m.shape(n, seq_size) for m in matrices]
    chunks = sum(m.parts for m in matrices)
    rows, width = query.shape
    all_rows = loaded[2].shape[0]
    largest = max(n, seq_size)
    sem = pltpu.SemaphoreType.DMA
    return pl.pallas_call(
        functools.partial(backward_kernel, n, seq_size, matrices),
        out_shape=[jax.ShapeDtypeStruct((m.rows, m.cols), f32) for m in matrices]
        + [jax.ShapeDtypeStruct(normed_one.shape, f32)]
        + [jax.ShapeDtypeStruct((1, own), f32)] * 4
        + [jax.ShapeDtypeStruct(s, f32) for s in ((hidden, features), (1, hidden), (outs, hidden), (1, outs))],
        in_specs=[vmem] * (len(inputs) - 1) + [pl.BlockSpec(memory_space=pltpu.SMEM)] + [any_space] * (len(loaded) + len(early)),
        out_specs=[vmem] * (len(matrices) + 9),
        scratch_shapes=[pltpu.VMEM(x.shape, bfloat) for x in loaded[:3]]
        + [pltpu.VMEM((2, n) + half_tail(m, seq_size), bfloat) for m in matrices]
        + [pltpu.VMEM((2, n - 1, n + 1) + half_tail(m, seq_size), bfloat) for m in matrices]
        + [pltpu.VMEM((4,) + ((1, m.rows, m.cols) if m.by_rows else (m.rows, m.cols)), bfloat) for m in matrices]
        + [
            pltpu.VMEM((n - 1, width // n, rows), bfloat),
            pltpu.VMEM((n, width // n, rows), bfloat),
            pltpu.VMEM((n, rows, width), bfloat),
            pltpu.VMEM((n - 1, width // n, all_rows), bfloat),
            pltpu.VMEM((n, width // n, all_rows), bfloat),
            pltpu.VMEM((n - 1, width // n, rows), bfloat),
            pltpu.VMEM((n, width // n, rows), bfloat),
            pltpu.VMEM((n, rows, width), bfloat),
            pltpu.VMEM((n, all_rows, 2 * width), bfloat),
            pltpu.VMEM((4,) + normed_one.shape, bfloat),
            pltpu.VMEM((rows, width), bfloat),
            sem((len(loaded),)),
        ]
        + [sem((8, n - 1))] * 2
        + [sem((3,)), sem((4,))]
        + [pltpu.VMEM((4, largest, 8, width), f32)]
        + [sem((4, largest - 1))] * 2
        + [pltpu.VMEM((4, largest) + decoder_grads.shape, f32)]
        + [sem((4, largest - 1))] * 2
        + [sem((chunks, 2))]
        + [sem((chunks, 3)), sem((chunks, 4))]
        + [sem((chunks, 4, n - 1))] * 2,
        compiler_params=pltpu.CompilerParams(
            collective_id=1, has_side_effects=True, vmem_limit_bytes=VMEM_LIMIT
        ),
    )(*inputs, *loaded, *early)


def columns(ref, first, count):
    block = ref[..., pl.ds(first, count)]
    return block.reshape(-1, count)


def normalize(values):
    center = values - jnp.mean(values, axis=-1, keepdims=True)
    inverse = lax.rsqrt(jnp.mean(center * center, axis=-1, keepdims=True) + EPSILON)
    return center * inverse, inverse


def forward_kernel(n, seq_size, matrices, *refs):
    count = len(matrices)
    refs = list(refs)

    def take(k):
        taken = refs[:k]
        del refs[:k]
        return taken

    shards = take(count)
    tokens, gain_one, shift_one, gain_two, shift_two, index, scene_count = take(7)
    wholes = take(count)
    gains_out, index_out, inverse_one, inverse_two = take(4)
    kept = take(12)
    bufs = take(count)
    made = take(12)
    hidden_all, query, keys, values, mixed, normed_one, normed_two, hidden_two, act, slope, planes, texels = made
    after, index_send, index_recv, hidden_send, hidden_recv, slots, small_send, small_recv, out_sem, kept_sem = take(10)
    bfloat, f32 = jnp.bfloat16, jnp.float32
    place = Place(n, seq_size)
    line = Line(place)
    for matrix, shard, buf in zip(matrices, shards, bufs):
        if matrix.by_rows:
            buf[place.i + (place.seq,)] = shard[...].astype(bfloat)
        else:
            at = pl.ds(pl.multiple_of(place.seq * matrix.cols, 128), matrix.cols)
            buf[place.i + (slice(None), at)] = shard[...].astype(bfloat)
    index_out[place.seq] = index[...]
    rows_all, width = tokens.shape
    pieces = hidden_pieces(rows_all)
    rows = query.shape[0]
    own = gain_one.shape[1]
    first_own = (place.dp * seq_size + place.seq) * own
    spot = lax.broadcasted_iota(jnp.int32, (own, width), 1) - lax.broadcasted_iota(jnp.int32, (own, width), 0)
    spread_out = (spot == first_own).astype(f32).astype(bfloat)
    gains = [ref[...] for ref in (gain_one, shift_one, gain_two, shift_two)]
    gains = jnp.concatenate(gains + [jnp.zeros((4, own), f32)], axis=0).astype(bfloat)
    gains = matmul(gains, spread_out)
    place.enter()
    gather = Gather(place, matrices, bufs, refs)
    total = len(gather.chunks)
    outs = []
    state = [0]

    def put(*which):
        for k in which:
            copy = pltpu.make_async_copy(made[k], kept[k], kept_sem.at[k])
            copy.start()
            outs.append(copy)

    def advance():
        t = state[0]
        state[0] += 1
        k = t - 3 * LAG
        if 0 <= k < total:
            gather.arrived(k)
            w, matrix, part = gather.chunks[k]
            at = (slice(None),) * 3 + matrix.tail(part, 0, seq_size)
            copy = pltpu.make_async_copy(bufs[w].at[at], wholes[w].at[at], out_sem.at[k])
            copy.start()
            outs.append(copy)
        if 0 <= t - 2 * LAG < total:
            gather.third(t - 2 * LAG)
        if 0 <= t - LAG < total:
            gather.hop(t - LAG, 1)
        if t < total:
            gather.hop(t, 0)
        if t + 1 < total:
            gather.relay(t + 1)
        issue(t + AHEAD)
        hidden_step(t)

    def advance_to(weight):
        last = max(k for k, (w, _, _) in enumerate(gather.chunks) if w == weight)
        while state[0] <= last + 3 * LAG:
            advance()

    def issue(last):
        while issued[0] <= min(last, total - 1):
            gather.along_seq(issued[0])
            issued[0] += 1

    issued = [0]
    issue(FIRST)
    index_line = (lambda j: index_out.at[j], index_send, index_recv)

    def hidden_line(piece):
        size = rows_all // pieces
        at = pl.ds(piece * size, size)
        return lambda j: hidden_all.at[j, at], hidden_send.at[piece], hidden_recv.at[piece]

    def hidden_step(t):
        for piece in range(pieces):
            if t == HIDDEN_FIRST + piece * HIDDEN_EVERY + HIDDEN_LAG:
                line.gather_relay(*hidden_line(piece))
            if t == HIDDEN_FIRST + piece * HIDDEN_EVERY:
                line.gather_start(*hidden_line(piece))

    normed, inverse = normalize(tokens[...])
    hidden_all[place.seq] = normed.astype(bfloat)
    normed_one[...] = normed
    inverse_one[...] = inverse
    hidden_step(-1)
    gather.relay(0)
    for _ in range(SUM_AT):
        advance()
    (gains_out[...],) = small_sum(place, [(gains, slots, small_send, small_recv)], advance)
    put(5)
    line.gather_start(*index_line)
    advance()
    line.gather_relay(*index_line)
    w_qkv, w_out, w_up, w_down, w_unpatch = bufs
    tile = 512
    advance_to(0)
    while state[0] <= HIDDEN_FIRST + (pieces - 1) * HIDDEN_EVERY + HIDDEN_LAG:
        advance()
    for piece in range(pieces):
        line.gather_take(*hidden_line(piece))
        line.gather_finish(*hidden_line(piece))

    @pl.loop(0, seq_size)
    def _(j):
        spread_gain, spread_shift = gains_out[0:1], gains_out[1:2]
        hidden_all[j] = (hidden_all[j].astype(f32) * spread_gain + spread_shift).astype(bfloat)

    for at in range(0, width, tile):
        block = hidden_all[place.seq, pl.ds(0, rows)]
        query[:, at : at + tile] = matmul(block, columns(w_qkv, at, tile)).astype(bfloat)
    put(0, 1)

    @pl.loop(0, width // tile)
    def _(t):
        at = pl.multiple_of(t * tile, tile)
        hidden = hidden_all[...].reshape(-1, width)
        keys[:, pl.ds(at, tile)] = matmul(hidden, columns(w_qkv, at + width, tile)).astype(bfloat)
        values[:, pl.ds(at, tile)] = matmul(hidden, columns(w_qkv, at + 2 * width, tile)).astype(bfloat)

    put(2, 3)
    advance()
    valid = key_valid(scene_count, seq_size, rows, rows_all, 1)
    pair = 2 * width // HEADS
    scale = (width // HEADS) ** (-0.5)
    first = lax.broadcasted_iota(jnp.int32, (rows, pair), 1) < pair // 2
    pairs, segments = HEADS // 2, 4
    for segment in range(segments):

        @pl.loop(segment * pairs // segments, (segment + 1) * pairs // segments)
        def _(p):
            at = pl.ds(pl.multiple_of(p * pair, pair), pair)
            query_two, key_two, value_two = query[:, at].astype(f32) * scale, keys[:, at], values[:, at]
            both = []
            for mine in (first, ~first):
                scores = matmul_nt(jnp.where(mine, query_two, 0.0).astype(bfloat), key_two)
                scores = jnp.where(valid, scores, NEGATIVE)
                expo = jnp.exp(scores - jnp.max(scores, axis=-1, keepdims=True))
                probs = expo * (1.0 / jnp.sum(expo, axis=-1, keepdims=True))
                both.append(matmul(probs.astype(bfloat), value_two))
            mixed[:, at] = jnp.where(first, both[0], both[1]).astype(bfloat)

        advance()
    put(4)
    advance_to(1)
    for at in range(0, width, tile):
        after[:, at : at + tile] = tokens[:rows, at : at + tile] + matmul(mixed[...], columns(w_out, at, tile))
    normed, inverse = normalize(after[...])
    normed_two[...] = normed
    inverse_two[...] = inverse
    hidden_two[...] = (normed * gains_out[2:3] + gains_out[3:4]).astype(bfloat)
    put(6, 7)
    advance_to(2)

    @pl.loop(0, act.shape[1] // tile)
    def _(t):
        at = pl.multiple_of(t * tile, tile)
        value, rate = gelu_parts(matmul(hidden_two[...], columns(w_up, at, tile)))
        act[:, pl.ds(at, tile)] = value.astype(bfloat)
        slope[:, pl.ds(at, tile)] = rate.astype(bfloat)

    put(8, 9)
    advance_to(3)
    deep = act.shape[1] // n
    for i in range(n):
        block = w_down[i].reshape(deep, width)
        for at in range(0, width, tile):
            after[:, at : at + tile] += matmul(act[:, i * deep : (i + 1) * deep], block[:, at : at + tile])
    planes[...] = after[...].astype(bfloat)
    put(10)
    advance_to(4)
    for at in range(0, texels.shape[1], tile):
        texels[:, at : at + tile] = matmul(planes[...], columns(w_unpatch, at, tile)).astype(bfloat)
    put(11)
    gather.finish()
    line.gather_take(*index_line)
    line.gather_finish(*index_line)
    for copy in outs:
        copy.wait()


def hidden_pieces(rows):
    return rows // PIECE if rows % PIECE == 0 else 1


def key_valid(scene_count, seq_size, plane_rows, rows, axis):
    shape = (1, seq_size * rows) if axis == 1 else (seq_size * rows, 1)
    position = lax.broadcasted_iota(jnp.int32, shape, axis)
    owner = lax.div(position, rows)
    offset = position - owner * rows
    return (offset < plane_rows) | (owner * (rows - plane_rows) + offset - plane_rows < scene_count[0, 0])


def forward_layer(n, seq_size, matrices, shards, tokens, gains, index, scene_count):
    chunks = sum(m.parts for m in matrices)
    vmem, any_space = pl.BlockSpec(memory_space=pltpu.VMEM), pl.BlockSpec(memory_space=pl.ANY)
    shapes = [m.shape(n, seq_size) for m in matrices]
    largest = max(n, seq_size)
    bfloat, f32 = jnp.bfloat16, jnp.float32
    rows, width = tokens.shape
    pieces = hidden_pieces(rows)
    plane_rows = 3 * PRES * PRES // seq_size
    ff = matrices[2].cols * seq_size
    results = [
        ((8, width), f32),
        ((seq_size,) + index.shape, jnp.int32),
        ((rows, 1), f32),
        ((plane_rows, 1), f32),
    ]
    kept = [
        ((seq_size, rows, width), bfloat),
        ((plane_rows, width), bfloat),
        ((seq_size * rows, width), bfloat),
        ((seq_size * rows, width), bfloat),
        ((plane_rows, width), bfloat),
        ((rows, width), f32),
        ((plane_rows, width), f32),
        ((plane_rows, width), bfloat),
        ((plane_rows, ff), bfloat),
        ((plane_rows, ff), bfloat),
        ((plane_rows, width), bfloat),
        ((plane_rows, matrices[4].cols * seq_size), bfloat),
    ]
    sem = pltpu.SemaphoreType.DMA
    made = pl.pallas_call(
        functools.partial(forward_kernel, n, seq_size, matrices),
        out_shape=[jax.ShapeDtypeStruct(s, bfloat) for s in shapes]
        + [jax.ShapeDtypeStruct(s, t) for s, t in results + kept],
        in_specs=[vmem] * (len(matrices) + 6) + [pl.BlockSpec(memory_space=pltpu.SMEM)],
        out_specs=[any_space] * len(matrices) + [vmem] * len(results) + [any_space] * len(kept),
        scratch_shapes=[pltpu.VMEM(s, bfloat) for s in shapes]
        + [pltpu.VMEM(s, t) for s, t in kept]
        + [pltpu.VMEM((plane_rows, width), f32)]
        + [sem((4,)), sem((3,)), sem((pieces, 4)), sem((pieces, 3))]
        + [pltpu.VMEM((4, largest, 8, width), f32)]
        + [sem((4, largest - 1))] * 2
        + [sem((chunks,)), sem((len(kept),))]
        + gather_sems(n, seq_size, chunks),
        compiler_params=pltpu.CompilerParams(
            collective_id=0, has_side_effects=True, vmem_limit_bytes=VMEM_LIMIT
        ),
    )(*shards, tokens, *gains, index, scene_count)
    return made[: len(matrices)], made[len(matrices) :]


def weight_list(shards):
    names = ("qkv", "out", "up", "down", "unpatch")
    parts = (4, 1, 4, 4, 2)
    return tuple(
        Matrix(name, shard.shape[0], shard.shape[1], name == "down", part)
        for name, shard, part in zip(names, shards, parts)
    )


def matmul(left, right):
    return jnp.dot(left, right, preferred_element_type=jnp.float32)


def matmul_tn(left, right):
    return lax.dot_general(
        left, right, (((0,), (0,)), ((), ())), preferred_element_type=jnp.float32
    )


def matmul_nt(left, right):
    return lax.dot_general(
        left, right, (((1,), (1,)), ((), ())), preferred_element_type=jnp.float32
    )


def split_at(values, count):
    return values[:count], values[count:]


def shards(
    tokens,
    ln1_gain,
    ln1_bias,
    w_qkv,
    w_out,
    ln2_gain,
    ln2_bias,
    w_up,
    w_down,
    w_unpatch,
    dec_w1,
    dec_b1,
    dec_w2,
    dec_b2,
    counts,
    sample_texels,
    d_density,
    d_color,
):
    seq_size = lax.axis_size("seq")
    dp_size = lax.axis_size("dp")
    n = round(dp_size ** (1 / 3))
    shards_of = (w_qkv, w_out, w_up, w_down, w_unpatch)
    matrices = weight_list(shards_of)
    qkv, out, up, down, unpatch = matrices
    gains = [part[None] for part in (ln1_gain, ln1_bias, ln2_gain, ln2_bias)]
    scene_count = counts[None]
    index = sample_texels.transpose(1, 0, 2)
    wholes, made = forward_layer(n, seq_size, matrices, shards_of, tokens[0], gains, index, scene_count)
    gains_all, index_all, inverse_one, inverse_two = made[:4]
    hidden_all, query, keys, values, mixed, normed_one = made[4:10]
    normed_two, hidden_two, act, slope, planes, texels = made[10:]
    decoder = (dec_w1.T, dec_b1[None], dec_w2.T, dec_b2[None])
    (density, color, decoder_grads, grad_after, norm_grads), grads = split_at(
        middle(
            n,
            seq_size,
            (up, down, unpatch),
            (texels, index_all) + decoder + (d_density, d_color.transpose(1, 0, 2)),
            (planes, hidden_two, inverse_two, gains_all, act, slope, normed_two),
            wholes[2:],
        ),
        5,
    )
    block_sums, (g_tokens, *small_sums) = split_at(
        backward_attention(
            n,
            seq_size,
            (unpatch, down, up, out, qkv),
            (grad_after, mixed, query, normed_one, inverse_one, gains_all, norm_grads, decoder_grads, scene_count),
            (wholes[1], wholes[0], keys, values, hidden_all.reshape(-1, hidden_all.shape[2])),
            (grads[2], grads[1], grads[0]),
        ),
        5,
    )
    large, small = split_at(finish((*block_sums, g_tokens, density, color, *small_sums)), 6)
    g_unpatch, g_down, g_up, g_out, g_qkv, g_tokens = large
    density, color, gain_one, shift_one, gain_two, shift_two, g_w1, g_b1, g_w2, g_b2 = small
    return (
        density,
        color.transpose(1, 0, 2),
        g_tokens[None],
        gain_one[0],
        shift_one[0],
        g_qkv,
        g_out,
        gain_two[0],
        shift_two[0],
        g_up,
        g_down,
        g_unpatch,
        g_w1.T,
        g_b1[0],
        g_w2.T,
        g_b2[0],
    )


def solution(mesh):
    in_specs = (
        P("dp", "seq", None),
        P(("dp", "seq")),
        P(("dp", "seq")),
        P("dp", "seq"),
        P("dp", "seq"),
        P(("dp", "seq")),
        P(("dp", "seq")),
        P("dp", "seq"),
        P(("dp", "seq"), None),
        P("dp", "seq"),
        P(),
        P(),
        P(),
        P(),
        P("dp"),
        P("dp", None, "seq"),
        P("dp", "seq"),
        P("dp", None, "seq"),
    )
    out_specs = (
        P("dp", "seq"),
        P("dp", None, "seq"),
        P("dp", "seq", None),
        P(("dp", "seq")),
        P(("dp", "seq")),
        P("dp", "seq"),
        P("dp", "seq"),
        P(("dp", "seq")),
        P(("dp", "seq")),
        P("dp", "seq"),
        P(("dp", "seq"), None),
        P("dp", "seq"),
        P(),
        P(),
        P(),
        P(),
    )
    return jax.shard_map(shards, mesh=mesh, in_specs=in_specs, out_specs=out_specs, check_vma=False)
```

```python
import functools
import math

import jax
import jax.numpy as jnp
from jax import lax
from jax.experimental import pallas as pl
from jax.experimental.pallas import tpu as pltpu
from jax.sharding import PartitionSpec as P

HEADS = 16
PATCH = 8
CH = 32
PRES = 16


EPSILON = 1e-05
NEGATIVE = -1e30
VMEM_LIMIT = 58 * 2**20
AHEAD = 2
FIRST = 1
PIECE = 32
HIDDEN_LAG = 1
HIDDEN_FIRST = -1
HIDDEN_EVERY = 2
SUM_AT = 4
HALVES = 2
LATE = ((4, 1),)
LATE_SEQ = 12
FIRST_RELAY = 3
GATHER_CUTS = ((32,) * 4, (128,), (32,) * 4, (32,) * 4, (32, 96))
SUM_CUTS = ((32,) * 4, (128,), (32,) * 4, (32,) * 4, (64,) * 2)
LAG = 2


MESH = pl.DeviceIdType.MESH


class Place:
    def __init__(self, n, seq_size):
        dp = lax.axis_index("dp")
        self.n, self.seq_size = n, seq_size
        self.seq = lax.axis_index("seq")
        self.i = (lax.div(dp, n * n), lax.rem(lax.div(dp, n), n), lax.rem(dp, n))
        self.dp = dp

    def size(self, axis):
        return self.seq_size if axis == 3 else self.n

    def me(self, axis):
        return self.seq if axis == 3 else self.i[axis]

    def peer(self, axis, step):
        to = lax.rem(self.me(axis) + step, self.size(axis))
        if axis == 3:
            return to, (self.dp, to)
        where = [to if a == axis else self.i[a] for a in range(3)]
        return to, ((where[0] * self.n + where[1]) * self.n + where[2], self.seq)

    def source(self, axis, step):
        size = self.size(axis)
        return lax.rem(self.me(axis) + (size - step), size)

    def enter(self, axes=(0, 1, 2, 3)):
        barrier = pltpu.get_barrier_semaphore()
        count = 0
        for axis in axes:
            for step in range(1, self.size(axis)):
                pl.semaphore_signal(
                    barrier, inc=1, device_id=self.peer(axis, step)[1], device_id_type=MESH
                )
                count += 1
        pl.semaphore_wait(barrier, count)


def remote(src, dst, send, recv, device):
    return pltpu.make_async_remote_copy(
        src_ref=src, dst_ref=dst, send_sem=send, recv_sem=recv, device_id=device, device_id_type=MESH
    )


class Line:
    def __init__(self, place):
        z = place.seq
        assert place.seq_size == 4
        self.dp, self.me = place.dp, z
        self.pair, self.far, self.opposite = z + 1 - 2 * lax.rem(z, 2), lax.rem(z + 2, 4), 3 - z
        self.middle = z * (3 - z) == 2
        self.end = z * (3 - z) == 0

    def _copy(self, source, target, send, recv, to):
        return remote(source, target, send, recv, (self.dp, to))

    def gather_start(self, region, send, recv):
        own = region(self.me)
        self._copy(own, own, send.at[0], recv.at[0], self.pair).start()
        self._copy(own, own, send.at[1], recv.at[1], self.far).start()

        @pl.when(self.middle)
        def _():
            self._copy(own, own, send.at[2], recv.at[2], self.opposite).start()

    def gather_relay(self, region, send, recv):
        block = region(self.far)
        self._copy(block, block, send.at[1], recv.at[1], self.far).wait_recv()

        @pl.when(self.middle)
        def _():
            self._copy(block, block, send.at[3], recv.at[2], self.pair).start()

    def gather_take(self, region, send, recv, which=("pair", "opposite")):
        for i, name, j in ((0, "pair", self.pair), (2, "opposite", self.opposite)):
            if name in which:
                self._copy(region(j), region(j), send.at[i], recv.at[i], self.pair).wait_recv()

    def gather_finish(self, region, send, recv):
        own = region(self.me)
        for i in (0, 1):
            self._copy(own, own, send.at[i], recv.at[i], self.pair).wait_send()

        @pl.when(self.middle)
        def _():
            for i in (2, 3):
                self._copy(own, own, send.at[i], recv.at[2], self.pair).wait_send()

    def sum_start(self, region, slot, send, recv, which=("opposite", "far", "pair")):
        if "opposite" in which:
            block = region(self.opposite)

            @pl.when(self.middle)
            def _():
                self._copy(block, slot(2), send.at[2], recv.at[2], self.opposite).start()

            @pl.when(self.end)
            def _():
                self._copy(block, slot(3), send.at[2], recv.at[3], self.pair).start()

        if "far" in which:

            @pl.when(self.end)
            def _():
                self._copy(region(self.far), slot(1), send.at[1], recv.at[1], self.far).start()

        if "pair" in which:
            self._copy(region(self.pair), slot(0), send.at[0], recv.at[0], self.pair).start()

    def sum_relay(self, region, slot, send, recv, add):
        @pl.when(self.middle)
        def _():
            block = region(self.far)
            self._copy(block, slot(3), send.at[2], recv.at[3], self.pair).wait_recv()
            add(self.far)
            self._copy(block, slot(1), send.at[1], recv.at[1], self.far).start()

    def sum_take(self, region, slot, send, recv):
        for i in (0, 1):
            self._copy(region(self.me), slot(i), send.at[i], recv.at[i], self.pair).wait_recv()

        @pl.when(self.middle)
        def _():
            self._copy(region(self.me), slot(2), send.at[2], recv.at[2], self.pair).wait_recv()

    def sum_of(self, own, slots):
        total = own.astype(jnp.float32) + slots(0).astype(jnp.float32) + slots(1).astype(jnp.float32)
        return total + jnp.where(self.middle, slots(2).astype(jnp.float32), 0.0)

    def sum_finish(self, region, slot, send, recv):
        for i in (0, 1, 2):
            self._copy(region(self.me), slot(0), send.at[i], recv.at[0], self.pair).wait_send()


class Matrix:
    def __init__(self, rows, cols, by_rows, cuts):
        self.rows, self.cols, self.by_rows = rows, cols, by_rows
        self.cuts = cuts if sum(cuts) == rows else (rows,)
        self.parts = len(self.cuts)

    def cut(self, part):
        return pl.ds(sum(self.cuts[:part]), self.cuts[part])

    def half_tail(self, part, j, h):
        half = self.cols // 2
        return (self.cut(part), pl.ds(pl.multiple_of(j * self.cols + h * half, 128), half))

    def shape(self, n, seq_size):
        if self.by_rows:
            return (n, n, n, seq_size, self.rows, self.cols)
        return (n, n, n, self.rows, seq_size * self.cols)

    def tail(self, part, first, count):
        rows = self.cut(part)
        if self.by_rows:
            return (pl.ds(first, count), rows, slice(None))
        if isinstance(first, int):
            return (rows, pl.ds(first * self.cols, count * self.cols))
        return (rows, pl.ds(pl.multiple_of(first * self.cols, 128), count * self.cols))


def small_stage(place, value, slots, send, recv, stage, axis):
    me = place.me(axis)
    slots[stage, me] = value
    copies = []
    for step in range(1, place.size(axis)):
        ref = slots.at[stage, me]
        copy = remote(
            ref, ref, send.at[stage, step - 1], recv.at[stage, step - 1], place.peer(axis, step)[1]
        )
        copy.start()
        copies.append(copy)

    def end():
        for copy in copies:
            copy.wait()
        total = slots[stage, 0]
        for other in range(1, place.size(axis)):
            total = total + slots[stage, other]
        return total

    return end


def small_sum(place, parts, between=None):
    values = [part[0] for part in parts]
    for stage, axis in enumerate((2, 1, 0, 3)):
        ends = [small_stage(place, v, *part[1:], stage, axis) for v, part in zip(values, parts)]
        if between is not None:
            between()
        values = [end() for end in ends]
    return values


class Gather:
    def __init__(self, place, matrices, refs, sems, late=()):
        self.place, self.refs, self.line = place, refs, Line(place)
        self.chunks = [(w, m, p) for w, m in enumerate(matrices) for p in range(m.parts)]
        self.seq_send, self.seq_recv, self.hop_send, self.hop_recv, self.far_send, self.far_recv = sems
        self.late = [k for k, (w, _, p) in enumerate(self.chunks) if (w, p) in late]
        self.copies = {}

    def _send(self, key, axis, region, send, recv):
        made = []
        for step in range(1, self.place.size(axis)):
            copy = remote(region, region, send.at[step - 1], recv.at[step - 1], self.place.peer(axis, step)[1])
            copy.start()
            made.append(copy)
        self.copies[key] = made

    def _take(self, key):
        for copy in self.copies[key]:
            copy.wait_recv()

    def region(self, k, index, first, count):
        w, matrix, part = self.chunks[k]
        return self.refs[w].at[index + matrix.tail(part, first, count)]

    def _along(self, k):
        every = slice(None)
        index = (every, every, self.place.i[2]) if k in self.late else self.place.i
        return lambda j: self.region(k, index, j, 1), self.seq_send.at[k], self.seq_recv.at[k]

    def along_seq(self, k):
        if k in self.late:
            self._take((k, 2, 0))
            self._take((k, 2, 1))
        self.line.gather_start(*self._along(k))

    def relay(self, k):
        self.line.gather_relay(*self._along(k))

    def hop(self, k, number):
        p, half = self.place, self.place.seq_size // 2
        w, matrix, part = self.chunks[k]
        if number == 1:
            self._take((k, 1, 0))
            self._take((k, 1, 1))
        elif k not in self.late:
            self.line.gather_take(*self._along(k))
        for h in (0, 1):
            axis = 1 - h if number == 0 else h
            index = [p.i[0], p.i[1], p.i[2]]
            if number == 1:
                index[1 - axis] = slice(None)
            at = 2 * number + h
            tail = matrix.half_tail(part, p.seq, h) if k in self.late else matrix.tail(part, h * half, half)
            region = self.refs[w].at[tuple(index) + tail]
            self._send((k, 1 + number, h), axis, region, self.hop_send.at[k, at], self.hop_recv.at[k, at])

    def third(self, k):
        p = self.place
        if k in self.late:
            self.line.gather_take(*self._along(k))
        else:
            self._take((k, 2, 0))
            self._take((k, 2, 1))
        region = self.region(k, (slice(None), slice(None), p.i[2]), 0, p.seq_size)
        self._send((k, 3), 2, region, self.far_send.at[k], self.far_recv.at[k])

    def arrived(self, k):
        self._take((k, 3))

    def finish(self):
        for k in range(len(self.chunks)):
            self.line.gather_finish(*self._along(k))
        for made in self.copies.values():
            for copy in made:
                copy.wait_send()


def gather_sems(n, seq_size, chunks):
    sem = pltpu.SemaphoreType.DMA
    return [sem((chunks, 4)), sem((chunks, 3))] + [sem((chunks, 4, n - 1))] * 2 + [sem((chunks, n - 1))] * 2


def gelu_parts(x):
    cdf = 0.5 + 0.5 * lax.erf(x * (0.5**0.5))
    return x * cdf, cdf + x * (jnp.exp(-0.5 * x * x) * (2.0 * math.pi) ** -0.5)


def split_low(x):
    high = x.astype(jnp.bfloat16)
    return high, (x - high.astype(jnp.float32)).astype(jnp.bfloat16)


def texel_place(texel, seq_size, me):
    side, quarter = PRES * PATCH, PRES * PRES // seq_size
    row, col = texel // side, texel % side
    token = row // PATCH * PRES + col // PATCH
    a, b = row % PATCH, col % PATCH
    fold = PATCH // 2
    mine = token // quarter == me
    key = jnp.where(mine, a // 2 * quarter + token % quarter, -1)
    return key, a % 2 * PATCH + b, fold


def decode_both(
    place,
    grad_texels,
    tile,
    texels,
    index,
    w1,
    b1,
    w2,
    b2,
    d_density,
    d_color,
    density,
    color,
    grads,
    tables,
    grad_tables,
    features,
    part_out,
    part_in,
    own_part,
    grad_all,
    send_sem,
    recv_sem,
    back_send,
    back_recv,
):
    seq_size = place.seq_size
    bfloat, f32 = jnp.bfloat16, jnp.float32
    samples = index.shape[3]
    quarter = PRES * PRES // seq_size
    width = texels.shape[1]
    groups = 2 * PATCH
    cols = groups * CH
    depth = width // cols * quarter
    hidden, inputs = w1.shape
    line = Line(place)
    for p in range(3):
        own = texels[p * quarter : (p + 1) * quarter].astype(f32)
        stacked = jnp.concatenate([own[:, i * cols : (i + 1) * cols] for i in range(width // cols)], axis=0)
        tables[p] = stacked.T.astype(bfloat)
    w1_high, w1_low = split_low(w1[...])
    w1_stack = jnp.concatenate([w1_high, w1_low], axis=0)
    tiles = samples // tile // HALVES
    size = samples // HALVES

    def one_hot(source, at, p):
        texel = index[source, p, :, at]
        key, group, _ = texel_place(texel, seq_size, place.seq)
        rows = lax.broadcasted_iota(jnp.int32, (depth, tile), 0)
        return (rows == key).astype(f32).astype(bfloat), group

    def forward(source, h):
        @pl.loop(h * tiles, (h + 1) * tiles)
        def _(t):
            at = pl.ds(pl.multiple_of(t * tile, tile), tile)
            picked = []
            for p in range(3):
                hot, group = one_hot(source, at, p)
                spread = matmul(tables[p], hot)
                total = jnp.where(group == 0, spread[:CH], 0.0)
                for g in range(1, groups):
                    total = total + jnp.where(group == g, spread[g * CH : (g + 1) * CH], 0.0)
                picked.append(total)
            feature = jnp.concatenate(picked, axis=0).astype(bfloat)
            features[source, :, at] = feature
            both = matmul(w1_stack, feature)
            part = both[:hidden] + both[hidden:]
            own_part[:, at] = part
            part_out[source, :, at] = part.astype(bfloat)

    def forward_line(h):
        at = pl.ds(h * size, size)
        return lambda j: part_out.at[j, :, at], lambda i: part_in.at[i, :, at], send_sem.at[h], recv_sem.at[h]

    def back_line(h):
        at = pl.ds(h * size, size)
        return lambda j: grad_all.at[j, :, at], back_send.at[h], back_recv.at[h]

    for h in range(HALVES):
        for name, j in (("opposite", line.opposite), ("far", line.far), ("pair", line.pair)):
            forward(j, h)
            line.sum_start(*forward_line(h), which=(name,))
        forward(place.seq, h)
        at = pl.ds(h * size, size)

        def add(j, at=at):
            part_out[j, :, at] = (part_out[j, :, at].astype(f32) + part_in[3, :, at].astype(f32)).astype(bfloat)

        line.sum_relay(*forward_line(h), add)
    highest = lax.Precision.HIGHEST
    tn, nt = (((0,), (0,)), ((), ())), (((1,), (1,)), ((), ()))
    ones = jnp.ones((8, size), f32)

    def eight(x):
        return jnp.concatenate([x, jnp.zeros((8 - x.shape[0], x.shape[1]), f32)], axis=0)

    def dot(left, right, dims):
        return lax.dot_general(left, right, dims, precision=highest, preferred_element_type=f32)

    grads[...] = jnp.zeros(grads.shape, f32)
    grad_tables[...] = jnp.zeros(grad_tables.shape, f32)
    outs = w2.shape[0]
    me = place.seq
    for h in range(HALVES):
        at = pl.ds(h * size, size)
        line.sum_take(*forward_line(h))
        pre = line.sum_of(own_part[:, at], lambda i: part_in[i, :, at]) + dot(eight(b1[...]), ones, tn)
        act, slope = gelu_parts(pre)
        out = jnp.dot(w2[...], act, precision=highest, preferred_element_type=f32) + dot(eight(b2[...]), ones, tn)
        gate = 1.0 / (1.0 + jnp.exp(-out))
        first = out[:1]
        density[:, at] = jnp.maximum(first, 0.0) + jnp.log1p(jnp.exp(-jnp.abs(first)))
        rows = [d_density[:, at] * gate[:1]]
        for p in range(3):
            own = gate[p + 1 : p + 2]
            color[p, :, at] = own
            rows.append(d_color[p, :, at] * own * (1.0 - own))
        grad_out = jnp.concatenate(rows, axis=0)
        grad_pre = dot(eight(w2[...]), eight(grad_out), tn) * slope
        grad_all[me, :, at] = grad_pre.astype(bfloat)
        line.gather_start(*back_line(h))
        grads[hidden : hidden + outs, :hidden] += dot(grad_out, act, nt)
        grads[hidden + 8 : hidden + 9, :hidden] += dot(ones, grad_pre, nt)[:1]
        grads[hidden + 16 : hidden + 17, :outs] += dot(ones, grad_out, nt)[:1]

    def backward(source, h):
        @pl.loop(h * tiles, (h + 1) * tiles)
        def _(t):
            at = pl.ds(pl.multiple_of(t * tile, tile), tile)
            grad = grad_all[source, :, at]
            grads[:hidden, :inputs] += matmul_nt(grad, features[source, :, at])
            grad_feature = matmul_tn(w1_high, grad) + matmul_tn(w1_low, grad)
            for p in range(3):
                hot, group = one_hot(source, at, p)
                mine = grad_feature[p * CH : (p + 1) * CH]
                spread = jnp.concatenate(
                    [jnp.where(group == g, mine, 0.0) for g in range(groups)], axis=0
                ).astype(bfloat)
                grad_tables[p] += matmul_nt(spread, hot)

    for h in range(HALVES):
        backward(me, h)
        line.gather_relay(*back_line(h))
    for h in range(HALVES):
        backward(line.far, h)
        line.gather_take(*back_line(h), which=("pair",))
        backward(line.pair, h)
        line.gather_take(*back_line(h), which=("opposite",))
        backward(line.opposite, h)
    for p in range(3):
        back = grad_tables[p].T
        for i in range(width // cols):
            block = back[i * quarter : (i + 1) * quarter].astype(bfloat)
            grad_texels[p * quarter : (p + 1) * quarter, i * cols : (i + 1) * cols] = block
    for h in range(HALVES):
        line.sum_finish(*forward_line(h))
        line.gather_finish(*back_line(h))


def core_columns(ref, n, segment, to):
    width = ref.shape[1]
    parts = width // (n * segment)
    if segment % 128 == 0:
        places = [pl.multiple_of((q * n + to) * segment, 128) for q in range(parts)]
        return jnp.concatenate([ref[:, pl.ds(at, segment)] for at in places], axis=1).T
    place = lax.broadcasted_iota(jnp.int32, (width, width // n), 1)
    source = (lax.div(place, segment) * n + to) * segment + lax.rem(place, segment)
    pick = lax.broadcasted_iota(jnp.int32, (width, width // n), 0) == source
    return matmul(ref[...], pick.astype(jnp.float32).astype(jnp.bfloat16)).astype(jnp.bfloat16).T


class Exchange:
    def __init__(self, place, send, recv):
        self.place, self.send, self.recv = place, send, recv
        self.made, self.used = [], 0

    def _start(self, source_of, buf):
        copies, p = [], self.place
        for step in range(1, p.size(2)):
            to, device = p.peer(2, step)
            sems = (self.send.at[self.used, step - 1], self.recv.at[self.used, step - 1])
            copy = remote(source_of(step, to), buf.at[p.i[2]], *sems, device)
            copy.start()
            copies.append(copy)
        self.used += 1
        self.made += copies

        def wait():
            for copy in copies:
                copy.wait_recv()

        return wait

    def columns(self, ref, segment, split, buf):
        p = self.place
        for step in range(1, p.size(2)):
            split[step - 1] = core_columns(ref, p.n, segment, p.peer(2, step)[0])
        wait = self._start(lambda step, to: split.at[step - 1], buf)
        buf[p.i[2]] = core_columns(ref, p.n, segment, p.i[2])
        return wait

    def rows(self, buf):
        return self._start(lambda step, to: buf.at[self.place.i[2]], buf)

    def finish(self):
        for copy in self.made:
            copy.wait_send()


def weight_grad(left, right, grad, first=0, tile=512):
    shape, width = grad.shape[:-1], right.shape[-1]
    for at in range(0, width, tile):
        size = min(tile, width - at)
        block = matmul(left[0], right[0, :, at : at + size])
        for i in range(1, left.shape[0]):
            block = block + matmul(left[i], right[i, :, at : at + size])
        grad[..., first + at : first + at + size] = block.astype(jnp.bfloat16).reshape(shape + (size,))


def norm_back(grad, normed, inverse, gain):
    scaled = grad * gain
    inner = scaled - jnp.mean(scaled, axis=-1, keepdims=True)
    inner = inner - normed * jnp.mean(scaled * normed, axis=-1, keepdims=True)
    return inner * inverse


def feed_back(place, matrices, refs):
    (planes, hidden_two, inverse_two, gains, act_in, slope_in, normed_in, weights) = refs[:8]
    (grads_out, grad_after, norm_grads, bufs) = refs[8:12]
    (planes_split, planes_all, act_split, act_all, hidden_split, hidden_all) = refs[12:18]
    (texels_all, layer_all, pre_all, layer, act, slope, normed_two, load_sem, out_sem, send, recv) = refs[18:29]
    grads = [buf.at[0] for buf in bufs]
    n = place.n
    bfloat, f32 = jnp.bfloat16, jnp.float32
    up, down, unpatch = matrices
    w_up, w_down, w_unpatch = bufs
    exchange = Exchange(place, send, recv)
    me = place.i[2]
    loads, waits = [], []

    def start():
        pairs = [(act_in, act)] + [(weights[k], bufs[k]) for k in (2, 1, 0)] + [(slope_in, slope), (normed_in, normed_two)]
        for k, (source, target) in enumerate(pairs):
            copy = pltpu.make_async_copy(source, target, load_sem.at[k])
            copy.start()
            loads.append(copy)

    def start_remote():
        waits.append(exchange.columns(planes, unpatch.rows, planes_split, planes_all))
        loads[0].wait()
        waits.append(exchange.columns(act, place.seq_size * down.rows, act_split, act_all))
        waits.append(exchange.columns(hidden_two, up.rows, hidden_split, hidden_all))

    outs = []

    def put(k):
        copy = pltpu.make_async_copy(grads[k], grads_out[k], out_sem.at[k])
        copy.start()
        outs.append(copy)

    def end():
        got_texels = exchange.rows(texels_all)
        loads[1].wait()
        grad_texels = texels_all[me]
        step = layer.shape[1] // n
        for i in range(n):
            block = w_unpatch[i].reshape(step, -1)
            layer[:, i * step : (i + 1) * step] = matmul_nt(grad_texels, block)
        layer_all[me] = layer[...].astype(bfloat)
        got_layer = exchange.rows(layer_all)
        loads[2].wait()
        loads[4].wait()
        step = act.shape[1] // (n * n)
        for i in range(n):
            for j in range(n):
                block = w_down[i, j].reshape(step, -1)
                at = (i * n + j) * step
                value = matmul_nt(layer_all[me], block) * slope[:, at : at + step].astype(f32)
                pre_all[me, :, at : at + step] = value.astype(bfloat)
        got_pre = exchange.rows(pre_all)
        waits[0]()
        got_texels()
        weight_grad(planes_all, texels_all, grads[2])
        put(2)
        loads[3].wait()
        loads[5].wait()
        step = layer.shape[1] // n
        pieces = []
        for i in range(n):
            block = w_up[i].reshape(step, -1)
            pieces.append(matmul_nt(pre_all[me], block))
        grad = jnp.concatenate(pieces, axis=1)
        normed = normed_two[...]
        norm_grads[0:1] = jnp.sum(grad * normed, axis=0, keepdims=True)
        norm_grads[1:2] = jnp.sum(grad, axis=0, keepdims=True)
        grad_after[...] = layer[...] + norm_back(grad, normed, inverse_two[...], gains[2:3])
        waits[1]()
        got_layer()
        weight_grad(act_all, layer_all, grads[1])
        put(1)
        waits[2]()
        got_pre()
        weight_grad(hidden_all, pre_all, grads[0])
        put(0)
        exchange.finish()
        for copy in outs:
            copy.wait()

    return start, start_remote, end


def middle_kernel(n, seq_size, matrices, *refs):
    refs = list(refs)

    def take(k):
        taken = refs[:k]
        del refs[:k]
        return taken

    decode_in, feed_in, weights = take(8), take(7), take(3)
    density, color, decoder_grads, grad_after, norm_grads = take(5)
    grads_out, bufs, decode_scratch = take(3), take(3), take(11)
    place = Place(n, seq_size)
    feed = list(feed_in) + [weights, grads_out, grad_after, norm_grads, bufs] + refs
    texels_all = refs[6]
    start, start_remote, end = feed_back(place, matrices, feed)
    start()
    place.enter((2, 3))
    start_remote()
    tile = min(512, decode_in[1].shape[3])
    outs = (density, color, decoder_grads)
    decode_both(place, texels_all.at[place.i[2]], tile, *decode_in, *outs, *decode_scratch)
    end()


def middle(n, seq_size, matrices, decode_in, feed_in, weights):
    texels, index, w1, b1, w2, b2, d_density, d_color = decode_in
    planes, hidden_two, inverse_two, gains, act, slope, normed_two = feed_in
    bfloat, f32 = jnp.bfloat16, jnp.float32
    samples, hidden = index.shape[3], w1.shape[0]
    quarter = PRES * PRES // seq_size
    cols = 2 * PATCH * CH
    depth = texels.shape[1] // cols * quarter
    vmem, any_space = pl.BlockSpec(memory_space=pltpu.VMEM), pl.BlockSpec(memory_space=pl.ANY)
    sem = pltpu.SemaphoreType.DMA
    rows, width = normed_two.shape
    ff, core_ff = act.shape[1], act.shape[1] // n
    shapes = [m.shape(n, seq_size) for m in matrices]
    halves = [(n, n) + s[3:] for s in shapes]
    return pl.pallas_call(
        functools.partial(middle_kernel, n, seq_size, matrices),
        out_shape=[
            jax.ShapeDtypeStruct((1, samples), f32),
            jax.ShapeDtypeStruct((3, 1, samples), f32),
            jax.ShapeDtypeStruct((hidden + 24, 128), f32),
            jax.ShapeDtypeStruct((rows, width), f32),
            jax.ShapeDtypeStruct((2, width), f32),
        ]
        + [jax.ShapeDtypeStruct(s, bfloat) for s in halves],
        in_specs=[vmem] * 12 + [any_space] * 6,
        out_specs=[vmem] * 5 + [any_space] * 3,
        scratch_shapes=[pltpu.VMEM(s, bfloat) for s in shapes]
        + [
            pltpu.VMEM((3, cols, depth), bfloat),
            pltpu.VMEM((3, cols, depth), f32),
            pltpu.VMEM((seq_size, 3 * CH, samples), bfloat),
            pltpu.VMEM((seq_size, hidden, samples), bfloat),
            pltpu.VMEM((4, hidden, samples), bfloat),
            pltpu.VMEM((hidden, samples), f32),
            pltpu.VMEM((seq_size, hidden, samples), bfloat),
        ]
        + [sem((HALVES, 3)), sem((HALVES, 4)), sem((HALVES, 4)), sem((HALVES, 3))]
        + [
            pltpu.VMEM((n - 1, width // n, rows), bfloat),
            pltpu.VMEM((n, width // n, rows), bfloat),
            pltpu.VMEM((n - 1, core_ff, rows), bfloat),
            pltpu.VMEM((n, core_ff, rows), bfloat),
            pltpu.VMEM((n - 1, width // n, rows), bfloat),
            pltpu.VMEM((n, width // n, rows), bfloat),
            pltpu.VMEM((n,) + texels.shape, bfloat),
            pltpu.VMEM((n, rows, width), bfloat),
            pltpu.VMEM((n, rows, ff), bfloat),
            pltpu.VMEM((rows, width), f32),
            pltpu.VMEM((rows, ff), bfloat),
            pltpu.VMEM((rows, ff), bfloat),
            pltpu.VMEM((rows, width), f32),
            sem((6,)),
            sem((3,)),
        ]
        + [sem((8, n - 1))] * 2,
        compiler_params=pltpu.CompilerParams(
            collective_id=2, has_side_effects=True, vmem_limit_bytes=VMEM_LIMIT
        ),
    )(*decode_in, *feed_in, *weights)


class Scatter:
    def __init__(self, place, matrices, sources, kept, hops, near, outs, sems):
        self.place, self.sources, self.kept = place, sources, kept
        self.hops, self.near, self.outs, self.line = hops, near, outs, Line(place)
        self.chunks = [(w, m, p) for w, m in enumerate(matrices) for p in range(m.parts)]
        self.load_sem, self.seq_send, self.seq_recv, self.hop_send, self.hop_recv = sems
        self.copies, self.loads = {}, {}
        self.first = [k for k, (w, _, _) in enumerate(self.chunks) if w == len(matrices) - 1]

    def _send(self, key, axis, region_to, slot, send, recv):
        made = []
        for step in range(1, self.place.size(axis)):
            to, device = self.place.peer(axis, step)
            copy = remote(region_to(to), slot(step - 1), send.at[step - 1], recv.at[step - 1], device)
            copy.start()
            made.append(copy)
        self.copies[key] = made

    def _take(self, key):
        for copy in self.copies[key]:
            copy.wait_recv()

    def hop(self, k, number):
        w, matrix, part = self.chunks[k]
        p, half, n = self.place, self.place.seq_size // 2, self.place.n
        kept, every = self.kept[w], slice(None)
        local = matrix.tail(part, 0, half)
        if number == 0:
            for h in (0, 1):
                index = (p.i[0], every) if h == 0 else (every, p.i[1])
                source = self.sources[w].at[index + matrix.tail(part, h * half, half)]
                copy = pltpu.make_async_copy(source, kept.at[(h, every) + local], self.load_sem.at[k, h])
                copy.start()
                self.loads[k, h] = copy
        else:
            for h in (0, 1):
                self.loads[k, h].wait()
                self._take((k, 1, h))
                for a in range(n):
                    value = kept[(h, a) + local].astype(jnp.float32)
                    for s in range(n - 1):
                        value = value + self.hops[w][(h, s, a) + local].astype(jnp.float32)
                    kept[(h, a) + local] = value.astype(jnp.bfloat16)
        for h in (0, 1):
            axis = h if number == 0 else 1 - h
            tail, at = matrix.tail(part, h * half, half), 2 * number + h

            def region_to(to, h=h, tail=tail):
                if number == 1:
                    return kept.at[(h, to) + local]
                return self.sources[w].at[((to, every) if h == 0 else (every, to)) + tail]

            def slot(s, h=h):
                return self.hops[w].at[(h, s, pl.ds(0, n) if number == 0 else n) + local]

            self._send((k, 1 + number, h), axis, region_to, slot, self.hop_send.at[k, at], self.hop_recv.at[k, at])

    def _block(self, matrix, part, j):
        p, half = self.place, self.place.seq_size // 2
        h = lax.div(j, half)
        return (h, p.i[1] + h * (p.i[0] - p.i[1])) + matrix.tail(part, lax.rem(j, half), 1)

    def along_seq(self, k):
        w, matrix, part = self.chunks[k]
        p, half, n = self.place, self.place.seq_size // 2, self.place.n
        kept = self.kept[w]
        local = matrix.tail(part, 0, half)
        for h in (0, 1):
            self._take((k, 2, h))
            value = kept[(h, p.i[1 - h]) + local].astype(jnp.float32)
            for s in range(n - 1):
                value = value + self.hops[w][(h, s, n) + local].astype(jnp.float32)
            kept[(h, p.i[1 - h]) + local] = value.astype(jnp.bfloat16)
        self.line.sum_start(*self._along(k))

    def _along(self, k):
        w, matrix, part = self.chunks[k]
        kept, near, own = self.kept[w], self.near[w], matrix.tail(part, 0, 1)
        region, slot = lambda j: kept.at[self._block(matrix, part, j)], lambda i: near.at[(i,) + own]
        return region, slot, self.seq_send.at[k], self.seq_recv.at[k]

    def relay(self, k):
        w, matrix, part = self.chunks[k]
        kept, own = self.kept[w], matrix.tail(part, 0, 1)

        def add(j):
            at = self._block(matrix, part, j)
            kept[at] = (kept[at].astype(jnp.float32) + self.near[w][(3,) + own].astype(jnp.float32)).astype(jnp.bfloat16)

        self.line.sum_relay(*self._along(k), add)

    def arrived(self, k):
        w, matrix, part = self.chunks[k]
        own = matrix.tail(part, 0, 1)
        self.line.sum_take(*self._along(k))
        value = self.kept[w][self._block(matrix, part, self.place.seq)]
        value = self.line.sum_of(value, lambda i: self.near[w][(i,) + own])
        self.outs[w][matrix.cut(part)] = value.reshape(-1, matrix.cols)


    def _first(self, k):
        w, matrix, part = self.chunks[k]
        every = (slice(None),) * 2
        region = lambda j: self.sources[w].at[every + matrix.tail(part, j, 1)]
        slot = lambda i: self.near[w].at[(i,) + every + (matrix.cut(part),)]
        return region, slot, self.seq_send.at[k], self.seq_recv.at[k]

    def first_seq(self, k):
        self.line.sum_start(*self._first(k))

    def first_relay(self, k):
        region, slot, send, recv = self._first(k)

        def add(j):
            block = region(j)
            block[...] = (block[...].astype(jnp.float32) + slot(3)[...].astype(jnp.float32)).astype(jnp.bfloat16)

        self.line.sum_relay(region, slot, send, recv, add)

    def first_hop(self, k, number):
        w, matrix, part = self.chunks[k]
        p, n, every, f32 = self.place, self.place.n, slice(None), jnp.float32
        source, hops, rows = self.sources[w], self.hops[w], matrix.cut(part)
        if number == 0:
            region, slot, send, recv = self._first(k)
            self.line.sum_take(region, slot, send, recv)
            own = region(p.seq)
            own[...] = self.line.sum_of(own[...], lambda i: slot(i)[...]).astype(jnp.bfloat16)
        half = matrix.cols // 2
        for h in (0, 1):
            tail = matrix.half_tail(part, p.seq, h)
            if number > 0:
                self._take((k, number, h))
            for a in range(n) if number == 1 else ():
                at = ((p.i[0], a) if h == 0 else (a, p.i[1])) + tail
                value = source[at].astype(f32)
                for s in range(n - 1):
                    value = value + hops[h, s, a, rows].astype(f32)
                source[at] = value.astype(jnp.bfloat16)
            if number == 2:
                value = source[p.i[:2] + tail].astype(f32)
                for s in range(n - 1):
                    value = value + hops[h, s, n, rows].astype(f32)
                self.outs[w][rows, h * half : (h + 1) * half] = value
                continue
            axis, at = (h if number == 0 else 1 - h), 2 * number + h

            def region_to(to, h=h, tail=tail):
                if number == 1:
                    return source.at[((p.i[0], to) if h == 0 else (to, p.i[1])) + tail]
                return source.at[((to, every) if h == 0 else (every, to)) + tail]

            def slot_of(s, h=h):
                return hops.at[h, s, pl.ds(0, n) if number == 0 else n, rows]

            self._send((k, 1 + number, h), axis, region_to, slot_of, self.hop_send.at[k, at], self.hop_recv.at[k, at])

    def finish(self):
        for k in range(len(self.chunks)):
            self.line.sum_finish(*(self._first(k) if k in self.first else self._along(k)))
        for made in self.copies.values():
            for copy in made:
                copy.wait_send()


def backward_kernel(n, seq_size, matrices, *refs):
    count = len(matrices)
    refs = list(refs)

    def take(k):
        taken = refs[:k]
        del refs[:k]
        return taken

    grad_after, mixed, query, normed_one, inverse_one, gains, norm_grads, decoder_grads, scene_count = take(9)
    w_out_in, w_qkv_in, keys_in, values_in, hidden_all_in = take(5)
    early = take(count - 2)
    outs = take(count)
    g_tokens, *norm_outs = take(5)
    g_w1, g_b1, g_w2, g_b2 = take(4)
    w_out, w_qkv, work = take(3)
    g_out, g_qkv = w_out.at[0], w_qkv.at[0]
    kept, hops, near = take(count), take(count), take(count)
    mixed_split, mixed_all, after_all, hidden_split, hidden_core, own_split, own_core = take(7)
    query_all, grad_all, hidden_in = take(3)
    grad_mixed, load_sem, core_send, core_recv, hidden_send, hidden_recv = take(6)
    norm_part, decoder_part = take(3), take(3)
    sems = refs
    bfloat, f32 = jnp.bfloat16, jnp.float32
    place = Place(n, seq_size)
    me = place.i[2]
    loads = []
    rows, width = query.shape
    token_rows = normed_one.shape[0]
    keys, values = grad_all.at[me, :, pl.ds(0, width)], grad_all.at[me, :, pl.ds(width, width)]
    for k, (source, target) in enumerate(
        ((hidden_all_in, work), (w_out_in, w_out), (keys_in, keys), (values_in, values), (w_qkv_in, w_qkv))
    ):
        copy = pltpu.make_async_copy(source, target, load_sem.at[k])
        copy.start()
        loads.append(copy)
    place.enter()
    scatter = Scatter(place, matrices, list(early) + [g_qkv, g_out], kept, hops, near, outs, sems)
    order = [k for k in range(len(scatter.chunks)) if k not in scatter.first]
    total = len(order)
    state = [0]
    first_steps = {
        FIRST_RELAY: scatter.first_relay,
        FIRST_RELAY + 2: lambda k: scatter.first_hop(k, 0),
        FIRST_RELAY + 4: lambda k: scatter.first_hop(k, 1),
        FIRST_RELAY + 6: lambda k: scatter.first_hop(k, 2),
    }

    def advance():
        t = state[0]
        state[0] += 1
        if t < total:
            scatter.hop(order[t], 0)
        if 0 <= t - LAG < total:
            scatter.hop(order[t - LAG], 1)
        if 0 <= t - 2 * LAG < total:
            scatter.along_seq(order[t - 2 * LAG])
        if 0 <= t - 2 * LAG - 1 < total:
            scatter.relay(order[t - 2 * LAG - 1])
        if 0 <= t - 3 * LAG - 1 < total:
            scatter.arrived(order[t - 3 * LAG - 1])
        for k in scatter.first:
            if t in first_steps:
                first_steps[t](k)

    line = Line(place)
    advance()
    advance()
    exchange = Exchange(place, core_send, core_recv)
    qkv_matrix, out_matrix = matrices[-2:]
    got_mixed = exchange.columns(mixed, out_matrix.rows, mixed_split, mixed_all)
    after_all[me] = grad_after[...].astype(bfloat)
    got_after = exchange.rows(after_all)
    loads[0].wait()
    own = work.at[pl.ds(pl.multiple_of(place.seq * token_rows, 16), rows)]
    got_own = exchange.columns(own, qkv_matrix.rows, own_split, own_core)
    got_hidden = exchange.columns(work, qkv_matrix.rows, hidden_split, hidden_core)
    loads[1].wait()
    step = width // n
    for i in range(n):
        block = w_out[i].reshape(step, width)
        grad_mixed[:, i * step : (i + 1) * step] = matmul_nt(after_all[me], block).astype(bfloat)
    got_mixed()
    got_after()
    weight_grad(mixed_all, after_all, g_out)
    for k in scatter.first:
        scatter.first_seq(k)
    loads[2].wait()
    loads[3].wait()
    valid = key_valid(scene_count, seq_size, rows, token_rows, 0)
    pair = 2 * width // HEADS
    scale = (width // HEADS) ** (-0.5)
    first = lax.broadcasted_iota(jnp.int32, (rows, pair), 1) < pair // 2
    pairs, segments = HEADS // 2, 4
    for segment in range(segments):

        @pl.loop(segment * pairs // segments, (segment + 1) * pairs // segments)
        def _(p):
            at = pl.ds(pl.multiple_of(p * pair, pair), pair)
            query_two, grad_two = query[:, at].astype(f32) * scale, grad_mixed[:, at].astype(f32)
            later = pl.ds(pl.multiple_of(width + p * pair, pair), pair)
            key_two, value_two = grad_all[me, :, at], grad_all[me, :, later]
            key_turned = key_two.T
            grad_key, grad_value, turned = 0.0, 0.0, []
            for h, mine in enumerate((first, ~first)):
                query_h = jnp.where(mine, query_two, 0.0).astype(bfloat)
                grad_h = jnp.where(mine, grad_two, 0.0).astype(bfloat)
                scores = jnp.where(valid, matmul_nt(key_two, query_h), NEGATIVE)
                expo = jnp.exp(scores - jnp.max(scores, axis=0, keepdims=True))
                probs = expo * (1.0 / jnp.sum(expo, axis=0, keepdims=True))
                grad_value = grad_value + matmul(probs.astype(bfloat), grad_h)
                grad_probs = matmul_nt(value_two, grad_h)
                inner = jnp.sum(probs * grad_probs, axis=0, keepdims=True)
                grad_scores = (probs * (grad_probs - inner)).astype(bfloat)
                grad_key = grad_key + matmul(grad_scores, query_h)
                grad_query = matmul(key_turned, grad_scores)
                turned.append(grad_query[h * (pair // 2) : (h + 1) * (pair // 2)])
            query_all[me, :, at] = (jnp.concatenate(turned, axis=0) * scale).T.astype(bfloat)
            grad_all[me, :, at] = grad_key.astype(bfloat)
            grad_all[me, :, later] = grad_value.astype(bfloat)

        advance()
    got_grad = exchange.rows(grad_all)
    got_query = exchange.rows(query_all)
    loads[4].wait()
    for i in range(n):
        block = w_qkv[i].reshape(step, 3 * width)
        work[:, i * step : (i + 1) * step] = matmul_nt(grad_all[me], block[:, width:]).astype(bfloat)
    pieces = [matmul_nt(query_all[me], w_qkv[i].reshape(step, 3 * width)[:, :width]) for i in range(n)]
    from_query = jnp.concatenate(pieces, axis=1)
    hidden_line = (
        lambda j: work.at[pl.ds(pl.multiple_of(j * token_rows, 16), token_rows)],
        lambda i: hidden_in.at[i],
        hidden_send,
        hidden_recv,
    )
    line.sum_start(*hidden_line)
    advance()
    got_grad()
    got_query()
    got_hidden()
    got_own()
    weight_grad(own_core, query_all, g_qkv)

    def add(j):
        at = pl.ds(pl.multiple_of(j * token_rows, 16), token_rows)
        work[at] = (work[at].astype(f32) + hidden_in[3].astype(f32)).astype(bfloat)

    line.sum_relay(*hidden_line, add)
    weight_grad(hidden_core, grad_all, g_qkv, width)
    advance()
    advance()
    line.sum_take(*hidden_line)
    grad = line.sum_of(work[pl.ds(pl.multiple_of(place.seq * token_rows, 16), token_rows)], lambda i: hidden_in[i])
    rest = jnp.zeros((token_rows - rows, width), f32)
    grad = grad + jnp.concatenate([from_query, rest], axis=0)
    normed = normed_one[...]
    g_tokens[...] = norm_back(grad, normed, inverse_one[...], gains[0:1])
    g_tokens[0:rows] += grad_after[...]
    gain_row = jnp.sum(grad * normed, axis=0, keepdims=True)
    shift_row = jnp.sum(grad, axis=0, keepdims=True)
    norm_rows = jnp.concatenate([gain_row, shift_row, norm_grads[...], jnp.zeros((4, width), f32)], axis=0)
    parts = [(norm_rows, *norm_part), (decoder_grads[...], *decoder_part)]
    norm_sums, decoder_sums = small_sum(place, parts, advance)
    own = norm_outs[0].shape[1]
    spot = lax.broadcasted_iota(jnp.int32, (width, own), 0) - lax.broadcasted_iota(jnp.int32, (width, own), 1)
    pick = (spot == (place.dp * seq_size + place.seq) * own).astype(f32)
    picked = jnp.dot(norm_sums, pick, precision=lax.Precision.HIGHEST, preferred_element_type=f32)
    for i, ref in enumerate(norm_outs):
        ref[...] = picked[i : i + 1]
    hidden, inputs = g_w1.shape
    g_w1[...] = decoder_sums[:hidden, :inputs]
    g_w2[...] = decoder_sums[hidden : hidden + g_w2.shape[0], :hidden]
    g_b1[...] = decoder_sums[hidden + 8 : hidden + 9, :hidden]
    g_b2[...] = decoder_sums[hidden + 16 : hidden + 17, : g_b2.shape[1]]
    while state[0] < total + 3 * LAG + 1:
        advance()
    scatter.finish()
    exchange.finish()
    line.sum_finish(*hidden_line)


def finish(values):
    def kernel(*refs):
        for source, target in zip(refs[: len(values)], refs[len(values) :]):
            target[...] = source[...]

    vmem = [pl.BlockSpec(memory_space=pltpu.VMEM)] * len(values)
    return pl.pallas_call(
        kernel,
        out_shape=[jax.ShapeDtypeStruct(x.shape, x.dtype) for x in values],
        in_specs=vmem,
        out_specs=vmem,
    )(*values)


def half_tail(matrix, seq_size):
    half = seq_size // 2
    if matrix.by_rows:
        return (half, matrix.rows, matrix.cols)
    return (matrix.rows, half * matrix.cols)


def backward_attention(n, seq_size, matrices, inputs, loaded, early):
    grad_after, mixed, query, normed_one, inverse_one, gains, norm_grads, decoder_grads, scene_count = inputs
    own = query.shape[1] // (lax.axis_size("dp") * seq_size)
    hidden, features, outs = decoder_grads.shape[0] - 24, 3 * CH, 4
    bfloat, f32 = jnp.bfloat16, jnp.float32
    vmem, any_space = pl.BlockSpec(memory_space=pltpu.VMEM), pl.BlockSpec(memory_space=pl.ANY)
    shapes = [m.shape(n, seq_size) for m in matrices]
    chunks = sum(m.parts for m in matrices)
    rows, width = query.shape
    all_rows = loaded[2].shape[0]
    largest = max(n, seq_size)
    sem = pltpu.SemaphoreType.DMA
    return pl.pallas_call(
        functools.partial(backward_kernel, n, seq_size, matrices),
        out_shape=[jax.ShapeDtypeStruct((m.rows, m.cols), f32) for m in matrices]
        + [jax.ShapeDtypeStruct(normed_one.shape, f32)]
        + [jax.ShapeDtypeStruct((1, own), f32)] * 4
        + [jax.ShapeDtypeStruct(s, f32) for s in ((hidden, features), (1, hidden), (outs, hidden), (1, outs))],
        in_specs=[vmem] * (len(inputs) - 1) + [pl.BlockSpec(memory_space=pltpu.SMEM)] + [any_space] * (len(loaded) + len(early)),
        out_specs=[vmem] * (len(matrices) + 9),
        scratch_shapes=[pltpu.VMEM(x.shape, bfloat) for x in loaded[:3]]
        + [pltpu.VMEM((2, n) + half_tail(m, seq_size), bfloat) for m in matrices[:-1]]
        + [pltpu.VMEM((16, 128), bfloat)]
        + [pltpu.VMEM((2, n - 1, n + 1) + half_tail(m, seq_size), bfloat) for m in matrices[:-1]]
        + [pltpu.VMEM((2, n - 1, n + 1, matrices[-1].rows, matrices[-1].cols // 2), bfloat)]
        + [pltpu.VMEM((4,) + ((1, m.rows, m.cols) if m.by_rows else (m.rows, m.cols)), bfloat) for m in matrices[:-1]]
        + [pltpu.VMEM((4, n, n, matrices[-1].rows, matrices[-1].cols), bfloat)]
        + [
            pltpu.VMEM((n - 1, width // n, rows), bfloat),
            pltpu.VMEM((n, width // n, rows), bfloat),
            pltpu.VMEM((n, rows, width), bfloat),
            pltpu.VMEM((n - 1, width // n, all_rows), bfloat),
            pltpu.VMEM((n, width // n, all_rows), bfloat),
            pltpu.VMEM((n - 1, width // n, rows), bfloat),
            pltpu.VMEM((n, width // n, rows), bfloat),
            pltpu.VMEM((n, rows, width), bfloat),
            pltpu.VMEM((n, all_rows, 2 * width), bfloat),
            pltpu.VMEM((4,) + normed_one.shape, bfloat),
            pltpu.VMEM((rows, width), bfloat),
            sem((len(loaded),)),
        ]
        + [sem((8, n - 1))] * 2
        + [sem((3,)), sem((4,))]
        + [pltpu.VMEM((4, largest, 8, width), f32)]
        + [sem((4, largest - 1))] * 2
        + [pltpu.VMEM((4, largest) + decoder_grads.shape, f32)]
        + [sem((4, largest - 1))] * 2
        + [sem((chunks, 2))]
        + [sem((chunks, 3)), sem((chunks, 4))]
        + [sem((chunks, 4, n - 1))] * 2,
        compiler_params=pltpu.CompilerParams(
            collective_id=1, has_side_effects=True, vmem_limit_bytes=VMEM_LIMIT
        ),
    )(*inputs, *loaded, *early)


def columns(ref, first, count):
    block = ref[..., pl.ds(first, count)]
    return block.reshape(-1, count)


def normalize(values):
    center = values - jnp.mean(values, axis=-1, keepdims=True)
    inverse = lax.rsqrt(jnp.mean(center * center, axis=-1, keepdims=True) + EPSILON)
    return center * inverse, inverse


def forward_kernel(n, seq_size, matrices, *refs):
    count = len(matrices)
    refs = list(refs)

    def take(k):
        taken = refs[:k]
        del refs[:k]
        return taken

    shards = take(count)
    tokens, gain_one, shift_one, gain_two, shift_two, index, scene_count = take(7)
    wholes = take(count)
    gains_out, index_out, inverse_one, inverse_two = take(4)
    kept = take(12)
    bufs = take(count)
    made = take(12)
    hidden_all, query, keys, values, mixed, normed_one, normed_two, hidden_two, act, slope, planes, texels = made
    after, index_send, index_recv, hidden_send, hidden_recv, slots, small_send, small_recv, out_sem, kept_sem = take(10)
    bfloat, f32 = jnp.bfloat16, jnp.float32
    place = Place(n, seq_size)
    line = Line(place)
    for matrix, shard, buf in zip(matrices, shards, bufs):
        if matrix.by_rows:
            buf[place.i + (place.seq,)] = shard[...].astype(bfloat)
        else:
            at = pl.ds(pl.multiple_of(place.seq * matrix.cols, 128), matrix.cols)
            buf[place.i + (slice(None), at)] = shard[...].astype(bfloat)
    index_out[place.seq] = index[...]
    rows_all, width = tokens.shape
    pieces = hidden_pieces(rows_all)
    rows = query.shape[0]
    own = gain_one.shape[1]
    first_own = (place.dp * seq_size + place.seq) * own
    spot = lax.broadcasted_iota(jnp.int32, (own, width), 1) - lax.broadcasted_iota(jnp.int32, (own, width), 0)
    spread_out = (spot == first_own).astype(f32).astype(bfloat)
    gains = [ref[...] for ref in (gain_one, shift_one, gain_two, shift_two)]
    gains = jnp.concatenate(gains + [jnp.zeros((4, own), f32)], axis=0).astype(bfloat)
    gains = matmul(gains, spread_out)
    place.enter()
    gather = Gather(place, matrices, bufs, refs, LATE)
    order = [k for k in range(len(gather.chunks)) if k not in gather.late]
    total = len(order)
    outs = []
    state = [0]

    def put(*which):
        for k in which:
            copy = pltpu.make_async_copy(made[k], kept[k], kept_sem.at[k])
            copy.start()
            outs.append(copy)

    def land(k):
        gather.arrived(k)
        w, matrix, part = gather.chunks[k]
        at = (slice(None),) * 3 + matrix.tail(part, 0, seq_size)
        copy = pltpu.make_async_copy(bufs[w].at[at], wholes[w].at[at], out_sem.at[k])
        copy.start()
        outs.append(copy)

    late_steps = {
        0: lambda k: gather.hop(k, 1),
        LATE_SEQ: gather.along_seq,
        LATE_SEQ + 2: gather.relay,
        LATE_SEQ + 3: gather.third,
        LATE_SEQ + 5: land,
    }

    def advance():
        t = state[0]
        state[0] += 1
        if 0 <= t - 3 * LAG < total:
            land(order[t - 3 * LAG])
        if 0 <= t - 2 * LAG < total:
            gather.third(order[t - 2 * LAG])
        if 0 <= t - LAG < total:
            gather.hop(order[t - LAG], 1)
        if t < total:
            gather.hop(order[t], 0)
        if t + 1 < total:
            gather.relay(order[t + 1])
        issue(t + AHEAD)
        hidden_step(t)
        for i, k in enumerate(gather.late):
            if t - i in late_steps:
                late_steps[t - i](k)

    def advance_to(weight):
        last = max([at for at, k in enumerate(order) if gather.chunks[k][0] == weight] + [-1]) + 3 * LAG
        for i, k in enumerate(gather.late):
            if gather.chunks[k][0] == weight:
                last = max(last, LATE_SEQ + 5 + i)
        while state[0] <= last:
            advance()

    def issue(last):
        while issued[0] <= min(last, total - 1):
            gather.along_seq(order[issued[0]])
            issued[0] += 1

    issued = [0]
    issue(FIRST)
    for k in gather.late:
        gather.hop(k, 0)
    index_line = (lambda j: index_out.at[j], index_send, index_recv)

    def hidden_line(piece):
        size = rows_all // pieces
        at = pl.ds(piece * size, size)
        return lambda j: hidden_all.at[j, at], hidden_send.at[piece], hidden_recv.at[piece]

    def hidden_step(t):
        for piece in range(pieces):
            if t == HIDDEN_FIRST + piece * HIDDEN_EVERY + HIDDEN_LAG:
                line.gather_relay(*hidden_line(piece))
            if t == HIDDEN_FIRST + piece * HIDDEN_EVERY:
                line.gather_start(*hidden_line(piece))

    normed, inverse = normalize(tokens[...])
    hidden_all[place.seq] = normed.astype(bfloat)
    normed_one[...] = normed
    inverse_one[...] = inverse
    hidden_step(-1)
    gather.relay(order[0])
    for _ in range(SUM_AT):
        advance()
    (gains_out[...],) = small_sum(place, [(gains, slots, small_send, small_recv)], advance)
    put(5)
    line.gather_start(*index_line)
    advance()
    line.gather_relay(*index_line)
    w_qkv, w_out, w_up, w_down, w_unpatch = bufs
    tile = 512
    advance_to(0)
    while state[0] <= HIDDEN_FIRST + (pieces - 1) * HIDDEN_EVERY + HIDDEN_LAG:
        advance()
    for piece in range(pieces):
        line.gather_take(*hidden_line(piece))
        line.gather_finish(*hidden_line(piece))

    @pl.loop(0, seq_size)
    def _(j):
        spread_gain, spread_shift = gains_out[0:1], gains_out[1:2]
        hidden_all[j] = (hidden_all[j].astype(f32) * spread_gain + spread_shift).astype(bfloat)

    for at in range(0, width, tile):
        block = hidden_all[place.seq, pl.ds(0, rows)]
        query[:, at : at + tile] = matmul(block, columns(w_qkv, at, tile)).astype(bfloat)
    put(0, 1)

    @pl.loop(0, width // tile)
    def _(t):
        at = pl.multiple_of(t * tile, tile)
        hidden = hidden_all[...].reshape(-1, width)
        keys[:, pl.ds(at, tile)] = matmul(hidden, columns(w_qkv, at + width, tile)).astype(bfloat)
        values[:, pl.ds(at, tile)] = matmul(hidden, columns(w_qkv, at + 2 * width, tile)).astype(bfloat)

    put(2, 3)
    advance()
    valid = key_valid(scene_count, seq_size, rows, rows_all, 1)
    pair = 2 * width // HEADS
    scale = (width // HEADS) ** (-0.5)
    first = lax.broadcasted_iota(jnp.int32, (rows, pair), 1) < pair // 2
    pairs, segments = HEADS // 2, 4
    for segment in range(segments):

        @pl.loop(segment * pairs // segments, (segment + 1) * pairs // segments)
        def _(p):
            at = pl.ds(pl.multiple_of(p * pair, pair), pair)
            query_two, key_two, value_two = query[:, at].astype(f32) * scale, keys[:, at], values[:, at]
            both = []
            for mine in (first, ~first):
                scores = matmul_nt(jnp.where(mine, query_two, 0.0).astype(bfloat), key_two)
                scores = jnp.where(valid, scores, NEGATIVE)
                expo = jnp.exp(scores - jnp.max(scores, axis=-1, keepdims=True))
                probs = expo * (1.0 / jnp.sum(expo, axis=-1, keepdims=True))
                both.append(matmul(probs.astype(bfloat), value_two))
            mixed[:, at] = jnp.where(first, both[0], both[1]).astype(bfloat)

        advance()
    put(4)
    advance_to(1)
    for at in range(0, width, tile):
        after[:, at : at + tile] = tokens[:rows, at : at + tile] + matmul(mixed[...], columns(w_out, at, tile))
    normed, inverse = normalize(after[...])
    normed_two[...] = normed
    inverse_two[...] = inverse
    hidden_two[...] = (normed * gains_out[2:3] + gains_out[3:4]).astype(bfloat)
    put(6, 7)
    advance_to(2)

    @pl.loop(0, act.shape[1] // tile)
    def _(t):
        at = pl.multiple_of(t * tile, tile)
        value, rate = gelu_parts(matmul(hidden_two[...], columns(w_up, at, tile)))
        act[:, pl.ds(at, tile)] = value.astype(bfloat)
        slope[:, pl.ds(at, tile)] = rate.astype(bfloat)

    put(8, 9)
    advance_to(3)
    deep = act.shape[1] // n
    for i in range(n):
        block = w_down[i].reshape(deep, width)
        for at in range(0, width, tile):
            after[:, at : at + tile] += matmul(act[:, i * deep : (i + 1) * deep], block[:, at : at + tile])
    planes[...] = after[...].astype(bfloat)
    put(10)
    advance_to(4)
    for at in range(0, texels.shape[1], tile):
        texels[:, at : at + tile] = matmul(planes[...], columns(w_unpatch, at, tile)).astype(bfloat)
    put(11)
    gather.finish()
    line.gather_take(*index_line)
    line.gather_finish(*index_line)
    for copy in outs:
        copy.wait()


def hidden_pieces(rows):
    return rows // PIECE if rows % PIECE == 0 else 1


def key_valid(scene_count, seq_size, plane_rows, rows, axis):
    shape = (1, seq_size * rows) if axis == 1 else (seq_size * rows, 1)
    position = lax.broadcasted_iota(jnp.int32, shape, axis)
    owner = lax.div(position, rows)
    offset = position - owner * rows
    return (offset < plane_rows) | (owner * (rows - plane_rows) + offset - plane_rows < scene_count[0, 0])


def forward_layer(n, seq_size, matrices, shards, tokens, gains, index, scene_count):
    chunks = sum(m.parts for m in matrices)
    vmem, any_space = pl.BlockSpec(memory_space=pltpu.VMEM), pl.BlockSpec(memory_space=pl.ANY)
    shapes = [m.shape(n, seq_size) for m in matrices]
    largest = max(n, seq_size)
    bfloat, f32 = jnp.bfloat16, jnp.float32
    rows, width = tokens.shape
    pieces = hidden_pieces(rows)
    plane_rows = 3 * PRES * PRES // seq_size
    ff = matrices[2].cols * seq_size
    results = [
        ((8, width), f32),
        ((seq_size,) + index.shape, jnp.int32),
        ((rows, 1), f32),
        ((plane_rows, 1), f32),
    ]
    kept = [
        ((seq_size, rows, width), bfloat),
        ((plane_rows, width), bfloat),
        ((seq_size * rows, width), bfloat),
        ((seq_size * rows, width), bfloat),
        ((plane_rows, width), bfloat),
        ((rows, width), f32),
        ((plane_rows, width), f32),
        ((plane_rows, width), bfloat),
        ((plane_rows, ff), bfloat),
        ((plane_rows, ff), bfloat),
        ((plane_rows, width), bfloat),
        ((plane_rows, matrices[4].cols * seq_size), bfloat),
    ]
    sem = pltpu.SemaphoreType.DMA
    made = pl.pallas_call(
        functools.partial(forward_kernel, n, seq_size, matrices),
        out_shape=[jax.ShapeDtypeStruct(s, bfloat) for s in shapes]
        + [jax.ShapeDtypeStruct(s, t) for s, t in results + kept],
        in_specs=[vmem] * (len(matrices) + 6) + [pl.BlockSpec(memory_space=pltpu.SMEM)],
        out_specs=[any_space] * len(matrices) + [vmem] * len(results) + [any_space] * len(kept),
        scratch_shapes=[pltpu.VMEM(s, bfloat) for s in shapes]
        + [pltpu.VMEM(s, t) for s, t in kept]
        + [pltpu.VMEM((plane_rows, width), f32)]
        + [sem((4,)), sem((3,)), sem((pieces, 4)), sem((pieces, 3))]
        + [pltpu.VMEM((4, largest, 8, width), f32)]
        + [sem((4, largest - 1))] * 2
        + [sem((chunks,)), sem((len(kept),))]
        + gather_sems(n, seq_size, chunks),
        compiler_params=pltpu.CompilerParams(
            collective_id=0, has_side_effects=True, vmem_limit_bytes=VMEM_LIMIT
        ),
    )(*shards, tokens, *gains, index, scene_count)
    return made[: len(matrices)], made[len(matrices) :]


def weight_list(shards, cuts):
    return tuple(
        Matrix(shard.shape[0], shard.shape[1], k == 3, rows) for k, (shard, rows) in enumerate(zip(shards, cuts))
    )


def matmul(left, right):
    return jnp.dot(left, right, preferred_element_type=jnp.float32)


def matmul_tn(left, right):
    return lax.dot_general(
        left, right, (((0,), (0,)), ((), ())), preferred_element_type=jnp.float32
    )


def matmul_nt(left, right):
    return lax.dot_general(
        left, right, (((1,), (1,)), ((), ())), preferred_element_type=jnp.float32
    )


def split_at(values, count):
    return values[:count], values[count:]


def shards(
    tokens,
    ln1_gain,
    ln1_bias,
    w_qkv,
    w_out,
    ln2_gain,
    ln2_bias,
    w_up,
    w_down,
    w_unpatch,
    dec_w1,
    dec_b1,
    dec_w2,
    dec_b2,
    counts,
    sample_texels,
    d_density,
    d_color,
):
    seq_size = lax.axis_size("seq")
    dp_size = lax.axis_size("dp")
    n = round(dp_size ** (1 / 3))
    shards_of = (w_qkv, w_out, w_up, w_down, w_unpatch)
    matrices = weight_list(shards_of, GATHER_CUTS)
    qkv, out, up, down, unpatch = weight_list(shards_of, SUM_CUTS)
    gains = [part[None] for part in (ln1_gain, ln1_bias, ln2_gain, ln2_bias)]
    scene_count = counts[None]
    index = sample_texels.transpose(1, 0, 2)
    wholes, made = forward_layer(n, seq_size, matrices, shards_of, tokens[0], gains, index, scene_count)
    gains_all, index_all, inverse_one, inverse_two = made[:4]
    hidden_all, query, keys, values, mixed, normed_one = made[4:10]
    normed_two, hidden_two, act, slope, planes, texels = made[10:]
    decoder = (dec_w1.T, dec_b1[None], dec_w2.T, dec_b2[None])
    (density, color, decoder_grads, grad_after, norm_grads), grads = split_at(
        middle(
            n,
            seq_size,
            (up, down, unpatch),
            (texels, index_all) + decoder + (d_density, d_color.transpose(1, 0, 2)),
            (planes, hidden_two, inverse_two, gains_all, act, slope, normed_two),
            wholes[2:],
        ),
        5,
    )
    block_sums, (g_tokens, *small_sums) = split_at(
        backward_attention(
            n,
            seq_size,
            (unpatch, down, up, qkv, out),
            (grad_after, mixed, query, normed_one, inverse_one, gains_all, norm_grads, decoder_grads, scene_count),
            (wholes[1], wholes[0], keys, values, hidden_all.reshape(-1, hidden_all.shape[2])),
            (grads[2], grads[1], grads[0]),
        ),
        5,
    )
    large, small = split_at(finish((*block_sums, g_tokens, density, color, *small_sums)), 6)
    g_unpatch, g_down, g_up, g_qkv, g_out, g_tokens = large
    density, color, gain_one, shift_one, gain_two, shift_two, g_w1, g_b1, g_w2, g_b2 = small
    return (
        density,
        color.transpose(1, 0, 2),
        g_tokens[None],
        gain_one[0],
        shift_one[0],
        g_qkv,
        g_out,
        gain_two[0],
        shift_two[0],
        g_up,
        g_down,
        g_unpatch,
        g_w1.T,
        g_b1[0],
        g_w2.T,
        g_b2[0],
    )


def solution(mesh):
    in_specs = (
        P("dp", "seq", None),
        P(("dp", "seq")),
        P(("dp", "seq")),
        P("dp", "seq"),
        P("dp", "seq"),
        P(("dp", "seq")),
        P(("dp", "seq")),
        P("dp", "seq"),
        P(("dp", "seq"), None),
        P("dp", "seq"),
        P(),
        P(),
        P(),
        P(),
        P("dp"),
        P("dp", None, "seq"),
        P("dp", "seq"),
        P("dp", None, "seq"),
    )
    out_specs = (
        P("dp", "seq"),
        P("dp", None, "seq"),
        P("dp", "seq", None),
        P(("dp", "seq")),
        P(("dp", "seq")),
        P("dp", "seq"),
        P("dp", "seq"),
        P(("dp", "seq")),
        P(("dp", "seq")),
        P("dp", "seq"),
        P(("dp", "seq"), None),
        P("dp", "seq"),
        P(),
        P(),
        P(),
        P(),
    )
    return jax.shard_map(shards, mesh=mesh, in_specs=in_specs, out_specs=out_specs, check_vma=False)
```

```python
import functools
import math

import jax
import jax.numpy as jnp
from jax import lax
from jax.experimental import pallas as pl
from jax.experimental.pallas import tpu as pltpu
from jax.sharding import PartitionSpec as P

HEADS = 16
PATCH = 8
CH = 32
PRES = 16


EPSILON = 1e-05
NEGATIVE = -1e30
VMEM_LIMIT = 58 * 2**20
AHEAD = 2
FIRST = 1
PIECE = 32
HIDDEN_LAG = 1
HIDDEN_FIRST = -1
HIDDEN_EVERY = 2
SUM_AT = 4
HALVES = 2
LATE = ((4, 1),)
LATE_SEQ = 12
FIRST_RELAY = 3
GATHER_CUTS = ((32,) * 4, (128,), (32,) * 4, (32,) * 4, (32, 96))
SUM_CUTS = ((32,) * 4, (128,), (32,) * 4, (32,) * 4, (64,) * 2)
LAG = 2


MESH = pl.DeviceIdType.MESH


class Place:
    def __init__(self, n, seq_size):
        dp = lax.axis_index("dp")
        self.n, self.seq_size = n, seq_size
        self.seq = lax.axis_index("seq")
        self.i = (lax.div(dp, n * n), lax.rem(lax.div(dp, n), n), lax.rem(dp, n))
        self.dp = dp

    def size(self, axis):
        return self.seq_size if axis == 3 else self.n

    def me(self, axis):
        return self.seq if axis == 3 else self.i[axis]

    def peer(self, axis, step):
        to = lax.rem(self.me(axis) + step, self.size(axis))
        if axis == 3:
            return to, (self.dp, to)
        where = [to if a == axis else self.i[a] for a in range(3)]
        return to, ((where[0] * self.n + where[1]) * self.n + where[2], self.seq)

    def source(self, axis, step):
        size = self.size(axis)
        return lax.rem(self.me(axis) + (size - step), size)

    def enter(self, axes=(0, 1, 2, 3)):
        self.greet(axes)
        self.meet(axes)

    def greet(self, axes=(0, 1, 2, 3)):
        barrier = pltpu.get_barrier_semaphore()
        for axis in axes:
            for step in range(1, self.size(axis)):
                pl.semaphore_signal(
                    barrier, inc=1, device_id=self.peer(axis, step)[1], device_id_type=MESH
                )

    def meet(self, axes=(0, 1, 2, 3)):
        pl.semaphore_wait(pltpu.get_barrier_semaphore(), sum(self.size(axis) - 1 for axis in axes))


def remote(src, dst, send, recv, device):
    return pltpu.make_async_remote_copy(
        src_ref=src, dst_ref=dst, send_sem=send, recv_sem=recv, device_id=device, device_id_type=MESH
    )


class Line:
    def __init__(self, place):
        z = place.seq
        assert place.seq_size == 4
        self.dp, self.me = place.dp, z
        self.pair, self.far, self.opposite = z + 1 - 2 * lax.rem(z, 2), lax.rem(z + 2, 4), 3 - z
        self.middle = z * (3 - z) == 2
        self.end = z * (3 - z) == 0

    def _copy(self, source, target, send, recv, to):
        return remote(source, target, send, recv, (self.dp, to))

    def gather_start(self, region, send, recv):
        own = region(self.me)
        self._copy(own, own, send.at[0], recv.at[0], self.pair).start()
        self._copy(own, own, send.at[1], recv.at[1], self.far).start()

        @pl.when(self.middle)
        def _():
            self._copy(own, own, send.at[2], recv.at[2], self.opposite).start()

    def gather_relay(self, region, send, recv):
        block = region(self.far)
        self._copy(block, block, send.at[1], recv.at[1], self.far).wait_recv()

        @pl.when(self.middle)
        def _():
            self._copy(block, block, send.at[3], recv.at[2], self.pair).start()

    def gather_take(self, region, send, recv, which=("pair", "opposite")):
        for i, name, j in ((0, "pair", self.pair), (2, "opposite", self.opposite)):
            if name in which:
                self._copy(region(j), region(j), send.at[i], recv.at[i], self.pair).wait_recv()

    def gather_finish(self, region, send, recv):
        own = region(self.me)
        for i in (0, 1):
            self._copy(own, own, send.at[i], recv.at[i], self.pair).wait_send()

        @pl.when(self.middle)
        def _():
            for i in (2, 3):
                self._copy(own, own, send.at[i], recv.at[2], self.pair).wait_send()

    def sum_start(self, region, slot, send, recv, which=("opposite", "far", "pair")):
        if "opposite" in which:
            block = region(self.opposite)

            @pl.when(self.middle)
            def _():
                self._copy(block, slot(2), send.at[2], recv.at[2], self.opposite).start()

            @pl.when(self.end)
            def _():
                self._copy(block, slot(3), send.at[2], recv.at[3], self.pair).start()

        if "far" in which:

            @pl.when(self.end)
            def _():
                self._copy(region(self.far), slot(1), send.at[1], recv.at[1], self.far).start()

        if "pair" in which:
            self._copy(region(self.pair), slot(0), send.at[0], recv.at[0], self.pair).start()

    def sum_relay(self, region, slot, send, recv, add):
        @pl.when(self.middle)
        def _():
            block = region(self.far)
            self._copy(block, slot(3), send.at[2], recv.at[3], self.pair).wait_recv()
            add(self.far)
            self._copy(block, slot(1), send.at[1], recv.at[1], self.far).start()

    def sum_take(self, region, slot, send, recv):
        for i in (0, 1):
            self._copy(region(self.me), slot(i), send.at[i], recv.at[i], self.pair).wait_recv()

        @pl.when(self.middle)
        def _():
            self._copy(region(self.me), slot(2), send.at[2], recv.at[2], self.pair).wait_recv()

    def sum_of(self, own, slots):
        total = own.astype(jnp.float32) + slots(0).astype(jnp.float32) + slots(1).astype(jnp.float32)
        return total + jnp.where(self.middle, slots(2).astype(jnp.float32), 0.0)

    def sum_finish(self, region, slot, send, recv):
        for i in (0, 1, 2):
            self._copy(region(self.me), slot(0), send.at[i], recv.at[0], self.pair).wait_send()


class Matrix:
    def __init__(self, rows, cols, by_rows, cuts):
        self.rows, self.cols, self.by_rows = rows, cols, by_rows
        self.cuts = cuts if sum(cuts) == rows else (rows,)
        self.parts = len(self.cuts)

    def cut(self, part):
        return pl.ds(sum(self.cuts[:part]), self.cuts[part])

    def half_tail(self, part, j, h):
        half = self.cols // 2
        return (self.cut(part), pl.ds(pl.multiple_of(j * self.cols + h * half, 128), half))

    def shape(self, n, seq_size):
        if self.by_rows:
            return (n, n, n, seq_size, self.rows, self.cols)
        return (n, n, n, self.rows, seq_size * self.cols)

    def tail(self, part, first, count):
        rows = self.cut(part)
        if self.by_rows:
            return (pl.ds(first, count), rows, slice(None))
        if isinstance(first, int):
            return (rows, pl.ds(first * self.cols, count * self.cols))
        return (rows, pl.ds(pl.multiple_of(first * self.cols, 128), count * self.cols))


def small_stage(place, value, slots, send, recv, stage, axis):
    me = place.me(axis)
    slots[stage, me] = value
    copies = []
    for step in range(1, place.size(axis)):
        ref = slots.at[stage, me]
        copy = remote(
            ref, ref, send.at[stage, step - 1], recv.at[stage, step - 1], place.peer(axis, step)[1]
        )
        copy.start()
        copies.append(copy)

    def end():
        for copy in copies:
            copy.wait()
        total = slots[stage, 0]
        for other in range(1, place.size(axis)):
            total = total + slots[stage, other]
        return total

    return end


def small_sum(place, parts, between=None):
    values = [part[0] for part in parts]
    for stage, axis in enumerate((2, 1, 0, 3)):
        ends = [small_stage(place, v, *part[1:], stage, axis) for v, part in zip(values, parts)]
        if between is not None:
            between()
        values = [end() for end in ends]
    return values


class Gather:
    def __init__(self, place, matrices, refs, sems, late=()):
        self.place, self.refs, self.line = place, refs, Line(place)
        self.chunks = [(w, m, p) for w, m in enumerate(matrices) for p in range(m.parts)]
        self.seq_send, self.seq_recv, self.hop_send, self.hop_recv, self.far_send, self.far_recv = sems
        self.late = [k for k, (w, _, p) in enumerate(self.chunks) if (w, p) in late]
        self.copies = {}

    def _send(self, key, axis, region, send, recv):
        made = []
        for step in range(1, self.place.size(axis)):
            copy = remote(region, region, send.at[step - 1], recv.at[step - 1], self.place.peer(axis, step)[1])
            copy.start()
            made.append(copy)
        self.copies[key] = made

    def _take(self, key):
        for copy in self.copies[key]:
            copy.wait_recv()

    def region(self, k, index, first, count):
        w, matrix, part = self.chunks[k]
        return self.refs[w].at[index + matrix.tail(part, first, count)]

    def _along(self, k):
        every = slice(None)
        index = (every, every, self.place.i[2]) if k in self.late else self.place.i
        return lambda j: self.region(k, index, j, 1), self.seq_send.at[k], self.seq_recv.at[k]

    def along_seq(self, k):
        if k in self.late:
            self._take((k, 2, 0))
            self._take((k, 2, 1))
        self.line.gather_start(*self._along(k))

    def relay(self, k):
        self.line.gather_relay(*self._along(k))

    def hop(self, k, number):
        p, half = self.place, self.place.seq_size // 2
        w, matrix, part = self.chunks[k]
        if number == 1:
            self._take((k, 1, 0))
            self._take((k, 1, 1))
        elif k not in self.late:
            self.line.gather_take(*self._along(k))
        for h in (0, 1):
            axis = 1 - h if number == 0 else h
            index = [p.i[0], p.i[1], p.i[2]]
            if number == 1:
                index[1 - axis] = slice(None)
            at = 2 * number + h
            tail = matrix.half_tail(part, p.seq, h) if k in self.late else matrix.tail(part, h * half, half)
            region = self.refs[w].at[tuple(index) + tail]
            self._send((k, 1 + number, h), axis, region, self.hop_send.at[k, at], self.hop_recv.at[k, at])

    def third(self, k):
        p = self.place
        if k in self.late:
            self.line.gather_take(*self._along(k))
        else:
            self._take((k, 2, 0))
            self._take((k, 2, 1))
        region = self.region(k, (slice(None), slice(None), p.i[2]), 0, p.seq_size)
        self._send((k, 3), 2, region, self.far_send.at[k], self.far_recv.at[k])

    def arrived(self, k):
        self._take((k, 3))

    def finish(self):
        for k in range(len(self.chunks)):
            self.line.gather_finish(*self._along(k))
        for made in self.copies.values():
            for copy in made:
                copy.wait_send()


def gather_sems(n, seq_size, chunks):
    sem = pltpu.SemaphoreType.DMA
    return [sem((chunks, 4)), sem((chunks, 3))] + [sem((chunks, 4, n - 1))] * 2 + [sem((chunks, n - 1))] * 2


def gelu_parts(x):
    cdf = 0.5 + 0.5 * lax.erf(x * (0.5**0.5))
    return x * cdf, cdf + x * (jnp.exp(-0.5 * x * x) * (2.0 * math.pi) ** -0.5)


def split_low(x):
    high = x.astype(jnp.bfloat16)
    return high, (x - high.astype(jnp.float32)).astype(jnp.bfloat16)


def texel_place(texel, seq_size, me):
    side, quarter = PRES * PATCH, PRES * PRES // seq_size
    row, col = texel // side, texel % side
    token = row // PATCH * PRES + col // PATCH
    a, b = row % PATCH, col % PATCH
    fold = PATCH // 2
    mine = token // quarter == me
    key = jnp.where(mine, a // 2 * quarter + token % quarter, -1)
    return key, a % 2 * PATCH + b, fold


def decode_both(
    place,
    grad_texels,
    between,
    tile,
    texels,
    index,
    w1,
    b1,
    w2,
    b2,
    d_density,
    d_color,
    density,
    color,
    grads,
    tables,
    grad_tables,
    features,
    part_out,
    part_in,
    own_part,
    grad_all,
    send_sem,
    recv_sem,
    back_send,
    back_recv,
):
    seq_size = place.seq_size
    bfloat, f32 = jnp.bfloat16, jnp.float32
    samples = index.shape[3]
    quarter = PRES * PRES // seq_size
    width = texels.shape[1]
    groups = 2 * PATCH
    cols = groups * CH
    depth = width // cols * quarter
    hidden, inputs = w1.shape
    line = Line(place)
    for p in range(3):
        own = texels[p * quarter : (p + 1) * quarter].astype(f32)
        stacked = jnp.concatenate([own[:, i * cols : (i + 1) * cols] for i in range(width // cols)], axis=0)
        tables[p] = stacked.T.astype(bfloat)
    place.meet((2, 3))
    w1_high, w1_low = split_low(w1[...])
    w1_stack = jnp.concatenate([w1_high, w1_low], axis=0)
    tiles = samples // tile // HALVES
    size = samples // HALVES

    def one_hot(source, at, p):
        texel = index[source, p, :, at]
        key, group, _ = texel_place(texel, seq_size, place.seq)
        rows = lax.broadcasted_iota(jnp.int32, (depth, tile), 0)
        return (rows == key).astype(f32).astype(bfloat), group

    def forward(source, h):
        @pl.loop(h * tiles, (h + 1) * tiles)
        def _(t):
            at = pl.ds(pl.multiple_of(t * tile, tile), tile)
            picked = []
            for p in range(3):
                hot, group = one_hot(source, at, p)
                spread = matmul(tables[p], hot)
                total = jnp.where(group == 0, spread[:CH], 0.0)
                for g in range(1, groups):
                    total = total + jnp.where(group == g, spread[g * CH : (g + 1) * CH], 0.0)
                picked.append(total)
            feature = jnp.concatenate(picked, axis=0).astype(bfloat)
            features[source, :, at] = feature
            both = matmul(w1_stack, feature)
            part = both[:hidden] + both[hidden:]
            own_part[:, at] = part
            part_out[source, :, at] = part.astype(bfloat)

    def forward_line(h):
        at = pl.ds(h * size, size)
        return lambda j: part_out.at[j, :, at], lambda i: part_in.at[i, :, at], send_sem.at[h], recv_sem.at[h]

    def back_line(h):
        at = pl.ds(h * size, size)
        return lambda j: grad_all.at[j, :, at], back_send.at[h], back_recv.at[h]

    for h in range(HALVES):
        for name, j in (("opposite", line.opposite), ("far", line.far), ("pair", line.pair)):
            forward(j, h)
            line.sum_start(*forward_line(h), which=(name,))
        forward(place.seq, h)
        at = pl.ds(h * size, size)

        def add(j, at=at):
            part_out[j, :, at] = (part_out[j, :, at].astype(f32) + part_in[3, :, at].astype(f32)).astype(bfloat)

        line.sum_relay(*forward_line(h), add)
    between()
    highest = lax.Precision.HIGHEST
    tn, nt = (((0,), (0,)), ((), ())), (((1,), (1,)), ((), ()))
    ones = jnp.ones((8, size), f32)

    def eight(x):
        return jnp.concatenate([x, jnp.zeros((8 - x.shape[0], x.shape[1]), f32)], axis=0)

    def dot(left, right, dims):
        return lax.dot_general(left, right, dims, precision=highest, preferred_element_type=f32)

    grads[...] = jnp.zeros(grads.shape, f32)
    grad_tables[...] = jnp.zeros(grad_tables.shape, f32)
    outs = w2.shape[0]
    me = place.seq
    for h in range(HALVES):
        at = pl.ds(h * size, size)
        line.sum_take(*forward_line(h))
        pre = line.sum_of(own_part[:, at], lambda i: part_in[i, :, at]) + dot(eight(b1[...]), ones, tn)
        act, slope = gelu_parts(pre)
        out = jnp.dot(w2[...], act, precision=highest, preferred_element_type=f32) + dot(eight(b2[...]), ones, tn)
        gate = 1.0 / (1.0 + jnp.exp(-out))
        first = out[:1]
        density[:, at] = jnp.maximum(first, 0.0) + jnp.log1p(jnp.exp(-jnp.abs(first)))
        rows = [d_density[:, at] * gate[:1]]
        for p in range(3):
            own = gate[p + 1 : p + 2]
            color[p, :, at] = own
            rows.append(d_color[p, :, at] * own * (1.0 - own))
        grad_out = jnp.concatenate(rows, axis=0)
        grad_pre = dot(eight(w2[...]), eight(grad_out), tn) * slope
        grad_all[me, :, at] = grad_pre.astype(bfloat)
        line.gather_start(*back_line(h))
        grads[hidden : hidden + outs, :hidden] += dot(grad_out, act, nt)
        grads[hidden + 8 : hidden + 9, :hidden] += dot(ones, grad_pre, nt)[:1]
        grads[hidden + 16 : hidden + 17, :outs] += dot(ones, grad_out, nt)[:1]

    def backward(source, h):
        @pl.loop(h * tiles, (h + 1) * tiles)
        def _(t):
            at = pl.ds(pl.multiple_of(t * tile, tile), tile)
            grad = grad_all[source, :, at]
            grads[:hidden, :inputs] += matmul_nt(grad, features[source, :, at])
            grad_feature = matmul_tn(w1_high, grad) + matmul_tn(w1_low, grad)
            for p in range(3):
                hot, group = one_hot(source, at, p)
                mine = grad_feature[p * CH : (p + 1) * CH]
                spread = jnp.concatenate(
                    [jnp.where(group == g, mine, 0.0) for g in range(groups)], axis=0
                ).astype(bfloat)
                grad_tables[p] += matmul_nt(spread, hot)

    for h in range(HALVES):
        backward(me, h)
        line.gather_relay(*back_line(h))
    for h in range(HALVES):
        backward(line.far, h)
        line.gather_take(*back_line(h), which=("pair",))
        backward(line.pair, h)
        line.gather_take(*back_line(h), which=("opposite",))
        backward(line.opposite, h)
    for p in range(3):
        back = grad_tables[p].T
        for i in range(width // cols):
            block = back[i * quarter : (i + 1) * quarter].astype(bfloat)
            grad_texels[p * quarter : (p + 1) * quarter, i * cols : (i + 1) * cols] = block
    for h in range(HALVES):
        line.sum_finish(*forward_line(h))
        line.gather_finish(*back_line(h))


def core_columns(ref, n, segment, to):
    width = ref.shape[1]
    parts = width // (n * segment)
    if segment % 128 == 0:
        places = [pl.multiple_of((q * n + to) * segment, 128) for q in range(parts)]
        return jnp.concatenate([ref[:, pl.ds(at, segment)] for at in places], axis=1).T
    place = lax.broadcasted_iota(jnp.int32, (width, width // n), 1)
    source = (lax.div(place, segment) * n + to) * segment + lax.rem(place, segment)
    pick = lax.broadcasted_iota(jnp.int32, (width, width // n), 0) == source
    return matmul(ref[...], pick.astype(jnp.float32).astype(jnp.bfloat16)).astype(jnp.bfloat16).T


class Exchange:
    def __init__(self, place, send, recv):
        self.place, self.send, self.recv = place, send, recv
        self.made, self.used = [], 0

    def _start(self, source_of, buf):
        copies, p = [], self.place
        for step in range(1, p.size(2)):
            to, device = p.peer(2, step)
            sems = (self.send.at[self.used, step - 1], self.recv.at[self.used, step - 1])
            copy = remote(source_of(step, to), buf.at[p.i[2]], *sems, device)
            copy.start()
            copies.append(copy)
        self.used += 1
        self.made += copies

        def wait():
            for copy in copies:
                copy.wait_recv()

        return wait

    def columns(self, ref, segment, split, buf):
        p = self.place
        for step in range(1, p.size(2)):
            split[step - 1] = core_columns(ref, p.n, segment, p.peer(2, step)[0])
        wait = self._start(lambda step, to: split.at[step - 1], buf)
        buf[p.i[2]] = core_columns(ref, p.n, segment, p.i[2])
        return wait

    def rows(self, buf):
        return self._start(lambda step, to: buf.at[self.place.i[2]], buf)

    def finish(self):
        for copy in self.made:
            copy.wait_send()


def weight_grad(left, right, grad, first=0, tile=512):
    shape, width = grad.shape[:-1], right.shape[-1]
    for at in range(0, width, tile):
        size = min(tile, width - at)
        block = matmul(left[0], right[0, :, at : at + size])
        for i in range(1, left.shape[0]):
            block = block + matmul(left[i], right[i, :, at : at + size])
        grad[..., first + at : first + at + size] = block.astype(jnp.bfloat16).reshape(shape + (size,))


def norm_back(grad, normed, inverse, gain):
    scaled = grad * gain
    inner = scaled - jnp.mean(scaled, axis=-1, keepdims=True)
    inner = inner - normed * jnp.mean(scaled * normed, axis=-1, keepdims=True)
    return inner * inverse


def feed_back(place, matrices, refs):
    (planes, hidden_two, inverse_two, gains, act_in, slope_in, normed_in, weights) = refs[:8]
    (grads_out, grad_after, norm_grads, bufs) = refs[8:12]
    (planes_split, planes_all, act_split, act_all, hidden_split, hidden_all) = refs[12:18]
    (texels_all, layer_all, pre_all, layer, act, slope, normed_two, load_sem, out_sem, send, recv) = refs[18:29]
    grads = [buf.at[0] for buf in bufs]
    n = place.n
    bfloat, f32 = jnp.bfloat16, jnp.float32
    up, down, unpatch = matrices
    w_up, w_down, w_unpatch = bufs
    exchange = Exchange(place, send, recv)
    me = place.i[2]
    loads, waits = [], []

    def start():
        pairs = [(act_in, act)] + [(weights[k], bufs[k]) for k in (2, 1, 0)] + [(slope_in, slope), (normed_in, normed_two)]
        for k, (source, target) in enumerate(pairs):
            copy = pltpu.make_async_copy(source, target, load_sem.at[k])
            copy.start()
            loads.append(copy)

    def start_remote():
        waits.append(exchange.columns(planes, unpatch.rows, planes_split, planes_all))
        loads[0].wait()
        waits.append(exchange.columns(act, place.seq_size * down.rows, act_split, act_all))
        waits.append(exchange.columns(hidden_two, up.rows, hidden_split, hidden_all))

    outs = []

    def put(k):
        copy = pltpu.make_async_copy(grads[k], grads_out[k], out_sem.at[k])
        copy.start()
        outs.append(copy)

    def end():
        got_texels = exchange.rows(texels_all)
        loads[1].wait()
        grad_texels = texels_all[me]
        step = layer.shape[1] // n
        for i in range(n):
            block = w_unpatch[i].reshape(step, -1)
            layer[:, i * step : (i + 1) * step] = matmul_nt(grad_texels, block)
        layer_all[me] = layer[...].astype(bfloat)
        got_layer = exchange.rows(layer_all)
        loads[2].wait()
        loads[4].wait()
        step = act.shape[1] // (n * n)
        for i in range(n):
            for j in range(n):
                block = w_down[i, j].reshape(step, -1)
                at = (i * n + j) * step
                value = matmul_nt(layer_all[me], block) * slope[:, at : at + step].astype(f32)
                pre_all[me, :, at : at + step] = value.astype(bfloat)
        got_pre = exchange.rows(pre_all)
        loads[3].wait()
        loads[5].wait()
        step = layer.shape[1] // n
        pieces = []
        for i in range(n):
            block = w_up[i].reshape(step, -1)
            pieces.append(matmul_nt(pre_all[me], block))
        grad = jnp.concatenate(pieces, axis=1)
        grad_after[...] = grad
        waits[1]()
        got_layer()
        weight_grad(act_all, layer_all, grads[1])
        put(1)
        waits[2]()
        got_pre()
        weight_grad(hidden_all, pre_all, grads[0])
        put(0)
        waits[0]()
        got_texels()
        weight_grad(planes_all, texels_all, grads[2])
        put(2)
        grad, normed = grad_after[...], normed_two[...]
        norm_grads[0:1] = jnp.sum(grad * normed, axis=0, keepdims=True)
        norm_grads[1:2] = jnp.sum(grad, axis=0, keepdims=True)
        grad_after[...] = layer[...] + norm_back(grad, normed, inverse_two[...], gains[2:3])
        exchange.finish()
        for copy in outs:
            copy.wait()

    return start, start_remote, end


def middle_kernel(n, seq_size, matrices, *refs):
    refs = list(refs)

    def take(k):
        taken = refs[:k]
        del refs[:k]
        return taken

    decode_in, feed_in, weights = take(8), take(7), take(3)
    density, color, decoder_grads, grad_after, norm_grads = take(5)
    grads_out, bufs, decode_scratch = take(3), take(3), take(11)
    place = Place(n, seq_size)
    feed = list(feed_in) + [weights, grads_out, grad_after, norm_grads, bufs] + refs
    texels_all = refs[6]
    start, start_remote, end = feed_back(place, matrices, feed)
    start()
    place.greet((2, 3))
    tile = min(512, decode_in[1].shape[3])
    outs = (density, color, decoder_grads)
    decode_both(place, texels_all.at[place.i[2]], start_remote, tile, *decode_in, *outs, *decode_scratch)
    end()


def middle(n, seq_size, matrices, decode_in, feed_in, weights):
    texels, index, w1, b1, w2, b2, d_density, d_color = decode_in
    planes, hidden_two, inverse_two, gains, act, slope, normed_two = feed_in
    bfloat, f32 = jnp.bfloat16, jnp.float32
    samples, hidden = index.shape[3], w1.shape[0]
    quarter = PRES * PRES // seq_size
    cols = 2 * PATCH * CH
    depth = texels.shape[1] // cols * quarter
    vmem, any_space = pl.BlockSpec(memory_space=pltpu.VMEM), pl.BlockSpec(memory_space=pl.ANY)
    sem = pltpu.SemaphoreType.DMA
    rows, width = normed_two.shape
    ff, core_ff = act.shape[1], act.shape[1] // n
    shapes = [m.shape(n, seq_size) for m in matrices]
    halves = [(n, n) + s[3:] for s in shapes]
    return pl.pallas_call(
        functools.partial(middle_kernel, n, seq_size, matrices),
        out_shape=[
            jax.ShapeDtypeStruct((1, samples), f32),
            jax.ShapeDtypeStruct((3, 1, samples), f32),
            jax.ShapeDtypeStruct((hidden + 24, 128), f32),
            jax.ShapeDtypeStruct((rows, width), f32),
            jax.ShapeDtypeStruct((2, width), f32),
        ]
        + [jax.ShapeDtypeStruct(s, bfloat) for s in halves],
        in_specs=[vmem] * 12 + [any_space] * 6,
        out_specs=[vmem] * 5 + [any_space] * 3,
        scratch_shapes=[pltpu.VMEM(s, bfloat) for s in shapes]
        + [
            pltpu.VMEM((3, cols, depth), bfloat),
            pltpu.VMEM((3, cols, depth), f32),
            pltpu.VMEM((seq_size, 3 * CH, samples), bfloat),
            pltpu.VMEM((seq_size, hidden, samples), bfloat),
            pltpu.VMEM((4, hidden, samples), bfloat),
            pltpu.VMEM((hidden, samples), f32),
            pltpu.VMEM((seq_size, hidden, samples), bfloat),
        ]
        + [sem((HALVES, 3)), sem((HALVES, 4)), sem((HALVES, 4)), sem((HALVES, 3))]
        + [
            pltpu.VMEM((n - 1, width // n, rows), bfloat),
            pltpu.VMEM((n, width // n, rows), bfloat),
            pltpu.VMEM((n - 1, core_ff, rows), bfloat),
            pltpu.VMEM((n, core_ff, rows), bfloat),
            pltpu.VMEM((n - 1, width // n, rows), bfloat),
            pltpu.VMEM((n, width // n, rows), bfloat),
            pltpu.VMEM((n,) + texels.shape, bfloat),
            pltpu.VMEM((n, rows, width), bfloat),
            pltpu.VMEM((n, rows, ff), bfloat),
            pltpu.VMEM((rows, width), f32),
            pltpu.VMEM((rows, ff), bfloat),
            pltpu.VMEM((rows, ff), bfloat),
            pltpu.VMEM((rows, width), f32),
            sem((6,)),
            sem((3,)),
        ]
        + [sem((8, n - 1))] * 2,
        compiler_params=pltpu.CompilerParams(
            collective_id=2, has_side_effects=True, vmem_limit_bytes=VMEM_LIMIT
        ),
    )(*decode_in, *feed_in, *weights)


class Scatter:
    def __init__(self, place, matrices, sources, kept, hops, near, outs, sems):
        self.place, self.sources, self.kept = place, sources, kept
        self.hops, self.near, self.outs, self.line = hops, near, outs, Line(place)
        self.chunks = [(w, m, p) for w, m in enumerate(matrices) for p in range(m.parts)]
        self.load_sem, self.seq_send, self.seq_recv, self.hop_send, self.hop_recv = sems
        self.copies, self.loads = {}, {}
        self.first = [k for k, (w, _, _) in enumerate(self.chunks) if w == len(matrices) - 1]

    def _send(self, key, axis, region_to, slot, send, recv):
        made = []
        for step in range(1, self.place.size(axis)):
            to, device = self.place.peer(axis, step)
            copy = remote(region_to(to), slot(step - 1), send.at[step - 1], recv.at[step - 1], device)
            copy.start()
            made.append(copy)
        self.copies[key] = made

    def _take(self, key):
        for copy in self.copies[key]:
            copy.wait_recv()

    def hop(self, k, number):
        w, matrix, part = self.chunks[k]
        p, half, n = self.place, self.place.seq_size // 2, self.place.n
        kept, every = self.kept[w], slice(None)
        local = matrix.tail(part, 0, half)
        if number == 0:
            for h in (0, 1):
                index = (p.i[0], every) if h == 0 else (every, p.i[1])
                source = self.sources[w].at[index + matrix.tail(part, h * half, half)]
                copy = pltpu.make_async_copy(source, kept.at[(h, every) + local], self.load_sem.at[k, h])
                copy.start()
                self.loads[k, h] = copy
        else:
            for h in (0, 1):
                self.loads[k, h].wait()
                self._take((k, 1, h))
                for a in range(n):
                    value = kept[(h, a) + local].astype(jnp.float32)
                    for s in range(n - 1):
                        value = value + self.hops[w][(h, s, a) + local].astype(jnp.float32)
                    kept[(h, a) + local] = value.astype(jnp.bfloat16)
        for h in (0, 1):
            axis = h if number == 0 else 1 - h
            tail, at = matrix.tail(part, h * half, half), 2 * number + h

            def region_to(to, h=h, tail=tail):
                if number == 1:
                    return kept.at[(h, to) + local]
                return self.sources[w].at[((to, every) if h == 0 else (every, to)) + tail]

            def slot(s, h=h):
                return self.hops[w].at[(h, s, pl.ds(0, n) if number == 0 else n) + local]

            self._send((k, 1 + number, h), axis, region_to, slot, self.hop_send.at[k, at], self.hop_recv.at[k, at])

    def _block(self, matrix, part, j):
        p, half = self.place, self.place.seq_size // 2
        h = lax.div(j, half)
        return (h, p.i[1] + h * (p.i[0] - p.i[1])) + matrix.tail(part, lax.rem(j, half), 1)

    def along_seq(self, k):
        w, matrix, part = self.chunks[k]
        p, half, n = self.place, self.place.seq_size // 2, self.place.n
        kept = self.kept[w]
        local = matrix.tail(part, 0, half)
        for h in (0, 1):
            self._take((k, 2, h))
            value = kept[(h, p.i[1 - h]) + local].astype(jnp.float32)
            for s in range(n - 1):
                value = value + self.hops[w][(h, s, n) + local].astype(jnp.float32)
            kept[(h, p.i[1 - h]) + local] = value.astype(jnp.bfloat16)
        self.line.sum_start(*self._along(k))

    def _along(self, k):
        w, matrix, part = self.chunks[k]
        kept, near, own = self.kept[w], self.near[w], matrix.tail(part, 0, 1)
        region, slot = lambda j: kept.at[self._block(matrix, part, j)], lambda i: near.at[(i,) + own]
        return region, slot, self.seq_send.at[k], self.seq_recv.at[k]

    def relay(self, k):
        w, matrix, part = self.chunks[k]
        kept, own = self.kept[w], matrix.tail(part, 0, 1)

        def add(j):
            at = self._block(matrix, part, j)
            kept[at] = (kept[at].astype(jnp.float32) + self.near[w][(3,) + own].astype(jnp.float32)).astype(jnp.bfloat16)

        self.line.sum_relay(*self._along(k), add)

    def arrived(self, k):
        w, matrix, part = self.chunks[k]
        own = matrix.tail(part, 0, 1)
        self.line.sum_take(*self._along(k))
        value = self.kept[w][self._block(matrix, part, self.place.seq)]
        value = self.line.sum_of(value, lambda i: self.near[w][(i,) + own])
        self.outs[w][matrix.cut(part)] = value.reshape(-1, matrix.cols)


    def _first(self, k):
        w, matrix, part = self.chunks[k]
        every = (slice(None),) * 2
        region = lambda j: self.sources[w].at[every + matrix.tail(part, j, 1)]
        slot = lambda i: self.near[w].at[(i,) + every + (matrix.cut(part),)]
        return region, slot, self.seq_send.at[k], self.seq_recv.at[k]

    def first_seq(self, k):
        self.line.sum_start(*self._first(k))

    def first_relay(self, k):
        region, slot, send, recv = self._first(k)

        def add(j):
            block = region(j)
            block[...] = (block[...].astype(jnp.float32) + slot(3)[...].astype(jnp.float32)).astype(jnp.bfloat16)

        self.line.sum_relay(region, slot, send, recv, add)

    def first_hop(self, k, number):
        w, matrix, part = self.chunks[k]
        p, n, every, f32 = self.place, self.place.n, slice(None), jnp.float32
        source, hops, rows = self.sources[w], self.hops[w], matrix.cut(part)
        if number == 0:
            region, slot, send, recv = self._first(k)
            self.line.sum_take(region, slot, send, recv)
            own = region(p.seq)
            own[...] = self.line.sum_of(own[...], lambda i: slot(i)[...]).astype(jnp.bfloat16)
        half = matrix.cols // 2
        for h in (0, 1):
            tail = matrix.half_tail(part, p.seq, h)
            if number > 0:
                self._take((k, number, h))
            for a in range(n) if number == 1 else ():
                at = ((p.i[0], a) if h == 0 else (a, p.i[1])) + tail
                value = source[at].astype(f32)
                for s in range(n - 1):
                    value = value + hops[h, s, a, rows].astype(f32)
                source[at] = value.astype(jnp.bfloat16)
            if number == 2:
                value = source[p.i[:2] + tail].astype(f32)
                for s in range(n - 1):
                    value = value + hops[h, s, n, rows].astype(f32)
                self.outs[w][rows, h * half : (h + 1) * half] = value
                continue
            axis, at = (h if number == 0 else 1 - h), 2 * number + h

            def region_to(to, h=h, tail=tail):
                if number == 1:
                    return source.at[((p.i[0], to) if h == 0 else (to, p.i[1])) + tail]
                return source.at[((to, every) if h == 0 else (every, to)) + tail]

            def slot_of(s, h=h):
                return hops.at[h, s, pl.ds(0, n) if number == 0 else n, rows]

            self._send((k, 1 + number, h), axis, region_to, slot_of, self.hop_send.at[k, at], self.hop_recv.at[k, at])

    def finish(self):
        for k in range(len(self.chunks)):
            self.line.sum_finish(*(self._first(k) if k in self.first else self._along(k)))
        for made in self.copies.values():
            for copy in made:
                copy.wait_send()


def backward_kernel(n, seq_size, matrices, *refs):
    count = len(matrices)
    refs = list(refs)

    def take(k):
        taken = refs[:k]
        del refs[:k]
        return taken

    grad_after, mixed, query, normed_one, inverse_one, gains, norm_grads, decoder_grads, scene_count = take(9)
    w_out_in, w_qkv_in, keys_in, values_in, hidden_all_in = take(5)
    early = take(count - 2)
    outs = take(count)
    g_tokens, *norm_outs = take(5)
    g_w1, g_b1, g_w2, g_b2 = take(4)
    w_out, w_qkv, work = take(3)
    g_out, g_qkv = w_out.at[0], w_qkv.at[0]
    kept, hops, near = take(count), take(count), take(count)
    mixed_split, mixed_all, after_all, hidden_split, hidden_core, own_split, own_core = take(7)
    query_all, grad_all, hidden_in = take(3)
    grad_mixed, load_sem, core_send, core_recv, hidden_send, hidden_recv = take(6)
    norm_part, decoder_part = take(3), take(3)
    sems = refs
    bfloat, f32 = jnp.bfloat16, jnp.float32
    place = Place(n, seq_size)
    me = place.i[2]
    loads = []
    rows, width = query.shape
    token_rows = normed_one.shape[0]
    keys, values = grad_all.at[me, :, pl.ds(0, width)], grad_all.at[me, :, pl.ds(width, width)]
    for k, (source, target) in enumerate(
        ((hidden_all_in, work), (w_out_in, w_out), (keys_in, keys), (values_in, values), (w_qkv_in, w_qkv))
    ):
        copy = pltpu.make_async_copy(source, target, load_sem.at[k])
        copy.start()
        loads.append(copy)
    place.enter()
    scatter = Scatter(place, matrices, list(early) + [g_qkv, g_out], kept, hops, near, outs, sems)
    order = [k for k in range(len(scatter.chunks)) if k not in scatter.first]
    total = len(order)
    state = [0]
    first_steps = {
        FIRST_RELAY: scatter.first_relay,
        FIRST_RELAY + 2: lambda k: scatter.first_hop(k, 0),
        FIRST_RELAY + 4: lambda k: scatter.first_hop(k, 1),
        FIRST_RELAY + 6: lambda k: scatter.first_hop(k, 2),
    }

    def advance():
        t = state[0]
        state[0] += 1
        if t < total:
            scatter.hop(order[t], 0)
        if 0 <= t - LAG < total:
            scatter.hop(order[t - LAG], 1)
        if 0 <= t - 2 * LAG < total:
            scatter.along_seq(order[t - 2 * LAG])
        if 0 <= t - 2 * LAG - 1 < total:
            scatter.relay(order[t - 2 * LAG - 1])
        if 0 <= t - 3 * LAG - 1 < total:
            scatter.arrived(order[t - 3 * LAG - 1])
        for k in scatter.first:
            if t in first_steps:
                first_steps[t](k)

    line = Line(place)
    advance()
    advance()
    exchange = Exchange(place, core_send, core_recv)
    qkv_matrix, out_matrix = matrices[-2:]
    got_mixed = exchange.columns(mixed, out_matrix.rows, mixed_split, mixed_all)
    after_all[me] = grad_after[...].astype(bfloat)
    got_after = exchange.rows(after_all)
    loads[0].wait()
    own = work.at[pl.ds(pl.multiple_of(place.seq * token_rows, 16), rows)]
    got_own = exchange.columns(own, qkv_matrix.rows, own_split, own_core)
    got_hidden = exchange.columns(work, qkv_matrix.rows, hidden_split, hidden_core)
    loads[1].wait()
    step = width // n
    for i in range(n):
        block = w_out[i].reshape(step, width)
        grad_mixed[:, i * step : (i + 1) * step] = matmul_nt(after_all[me], block).astype(bfloat)
    got_mixed()
    got_after()
    weight_grad(mixed_all, after_all, g_out)
    for k in scatter.first:
        scatter.first_seq(k)
    loads[2].wait()
    loads[3].wait()
    valid = key_valid(scene_count, seq_size, rows, token_rows, 0)
    pair = 2 * width // HEADS
    scale = (width // HEADS) ** (-0.5)
    first = lax.broadcasted_iota(jnp.int32, (rows, pair), 1) < pair // 2
    pairs, segments = HEADS // 2, 4
    for segment in range(segments):

        @pl.loop(segment * pairs // segments, (segment + 1) * pairs // segments)
        def _(p):
            at = pl.ds(pl.multiple_of(p * pair, pair), pair)
            query_two, grad_two = query[:, at].astype(f32) * scale, grad_mixed[:, at].astype(f32)
            later = pl.ds(pl.multiple_of(width + p * pair, pair), pair)
            key_two, value_two = grad_all[me, :, at], grad_all[me, :, later]
            key_turned = key_two.T
            grad_key, grad_value, turned = 0.0, 0.0, []
            for h, mine in enumerate((first, ~first)):
                query_h = jnp.where(mine, query_two, 0.0).astype(bfloat)
                grad_h = jnp.where(mine, grad_two, 0.0).astype(bfloat)
                scores = jnp.where(valid, matmul_nt(key_two, query_h), NEGATIVE)
                expo = jnp.exp(scores - jnp.max(scores, axis=0, keepdims=True))
                probs = expo * (1.0 / jnp.sum(expo, axis=0, keepdims=True))
                grad_value = grad_value + matmul(probs.astype(bfloat), grad_h)
                grad_probs = matmul_nt(value_two, grad_h)
                inner = jnp.sum(probs * grad_probs, axis=0, keepdims=True)
                grad_scores = (probs * (grad_probs - inner)).astype(bfloat)
                grad_key = grad_key + matmul(grad_scores, query_h)
                grad_query = matmul(key_turned, grad_scores)
                turned.append(grad_query[h * (pair // 2) : (h + 1) * (pair // 2)])
            query_all[me, :, at] = (jnp.concatenate(turned, axis=0) * scale).T.astype(bfloat)
            grad_all[me, :, at] = grad_key.astype(bfloat)
            grad_all[me, :, later] = grad_value.astype(bfloat)

        advance()
    got_grad = exchange.rows(grad_all)
    got_query = exchange.rows(query_all)
    loads[4].wait()
    for i in range(n):
        block = w_qkv[i].reshape(step, 3 * width)
        work[:, i * step : (i + 1) * step] = matmul_nt(grad_all[me], block[:, width:]).astype(bfloat)
    pieces = [matmul_nt(query_all[me], w_qkv[i].reshape(step, 3 * width)[:, :width]) for i in range(n)]
    from_query = jnp.concatenate(pieces, axis=1)
    hidden_line = (
        lambda j: work.at[pl.ds(pl.multiple_of(j * token_rows, 16), token_rows)],
        lambda i: hidden_in.at[i],
        hidden_send,
        hidden_recv,
    )
    line.sum_start(*hidden_line)
    advance()
    got_grad()
    got_query()
    got_hidden()
    got_own()
    weight_grad(own_core, query_all, g_qkv)

    def add(j):
        at = pl.ds(pl.multiple_of(j * token_rows, 16), token_rows)
        work[at] = (work[at].astype(f32) + hidden_in[3].astype(f32)).astype(bfloat)

    line.sum_relay(*hidden_line, add)
    weight_grad(hidden_core, grad_all, g_qkv, width)
    advance()
    advance()
    line.sum_take(*hidden_line)
    grad = line.sum_of(work[pl.ds(pl.multiple_of(place.seq * token_rows, 16), token_rows)], lambda i: hidden_in[i])
    rest = jnp.zeros((token_rows - rows, width), f32)
    grad = grad + jnp.concatenate([from_query, rest], axis=0)
    normed = normed_one[...]
    g_tokens[...] = norm_back(grad, normed, inverse_one[...], gains[0:1])
    g_tokens[0:rows] += grad_after[...]
    gain_row = jnp.sum(grad * normed, axis=0, keepdims=True)
    shift_row = jnp.sum(grad, axis=0, keepdims=True)
    norm_rows = jnp.concatenate([gain_row, shift_row, norm_grads[...], jnp.zeros((4, width), f32)], axis=0)
    parts = [(norm_rows, *norm_part), (decoder_grads[...], *decoder_part)]
    norm_sums, decoder_sums = small_sum(place, parts, advance)
    own = norm_outs[0].shape[1]
    spot = lax.broadcasted_iota(jnp.int32, (width, own), 0) - lax.broadcasted_iota(jnp.int32, (width, own), 1)
    pick = (spot == (place.dp * seq_size + place.seq) * own).astype(f32)
    picked = jnp.dot(norm_sums, pick, precision=lax.Precision.HIGHEST, preferred_element_type=f32)
    for i, ref in enumerate(norm_outs):
        ref[...] = picked[i : i + 1]
    hidden, inputs = g_w1.shape
    g_w1[...] = decoder_sums[:hidden, :inputs]
    g_w2[...] = decoder_sums[hidden : hidden + g_w2.shape[0], :hidden]
    g_b1[...] = decoder_sums[hidden + 8 : hidden + 9, :hidden]
    g_b2[...] = decoder_sums[hidden + 16 : hidden + 17, : g_b2.shape[1]]
    while state[0] < total + 3 * LAG + 1:
        advance()
    scatter.finish()
    exchange.finish()
    line.sum_finish(*hidden_line)


def finish(values):
    def kernel(*refs):
        for source, target in zip(refs[: len(values)], refs[len(values) :]):
            target[...] = source[...]

    vmem = [pl.BlockSpec(memory_space=pltpu.VMEM)] * len(values)
    return pl.pallas_call(
        kernel,
        out_shape=[jax.ShapeDtypeStruct(x.shape, x.dtype) for x in values],
        in_specs=vmem,
        out_specs=vmem,
    )(*values)


def half_tail(matrix, seq_size):
    half = seq_size // 2
    if matrix.by_rows:
        return (half, matrix.rows, matrix.cols)
    return (matrix.rows, half * matrix.cols)


def backward_attention(n, seq_size, matrices, inputs, loaded, early):
    grad_after, mixed, query, normed_one, inverse_one, gains, norm_grads, decoder_grads, scene_count = inputs
    own = query.shape[1] // (lax.axis_size("dp") * seq_size)
    hidden, features, outs = decoder_grads.shape[0] - 24, 3 * CH, 4
    bfloat, f32 = jnp.bfloat16, jnp.float32
    vmem, any_space = pl.BlockSpec(memory_space=pltpu.VMEM), pl.BlockSpec(memory_space=pl.ANY)
    shapes = [m.shape(n, seq_size) for m in matrices]
    chunks = sum(m.parts for m in matrices)
    rows, width = query.shape
    all_rows = loaded[2].shape[0]
    largest = max(n, seq_size)
    sem = pltpu.SemaphoreType.DMA
    return pl.pallas_call(
        functools.partial(backward_kernel, n, seq_size, matrices),
        out_shape=[jax.ShapeDtypeStruct((m.rows, m.cols), f32) for m in matrices]
        + [jax.ShapeDtypeStruct(normed_one.shape, f32)]
        + [jax.ShapeDtypeStruct((1, own), f32)] * 4
        + [jax.ShapeDtypeStruct(s, f32) for s in ((hidden, features), (1, hidden), (outs, hidden), (1, outs))],
        in_specs=[vmem] * (len(inputs) - 1) + [pl.BlockSpec(memory_space=pltpu.SMEM)] + [any_space] * (len(loaded) + len(early)),
        out_specs=[vmem] * (len(matrices) + 9),
        scratch_shapes=[pltpu.VMEM(x.shape, bfloat) for x in loaded[:3]]
        + [pltpu.VMEM((2, n) + half_tail(m, seq_size), bfloat) for m in matrices[:-1]]
        + [pltpu.VMEM((16, 128), bfloat)]
        + [pltpu.VMEM((2, n - 1, n + 1) + half_tail(m, seq_size), bfloat) for m in matrices[:-1]]
        + [pltpu.VMEM((2, n - 1, n + 1, matrices[-1].rows, matrices[-1].cols // 2), bfloat)]
        + [pltpu.VMEM((4,) + ((1, m.rows, m.cols) if m.by_rows else (m.rows, m.cols)), bfloat) for m in matrices[:-1]]
        + [pltpu.VMEM((4, n, n, matrices[-1].rows, matrices[-1].cols), bfloat)]
        + [
            pltpu.VMEM((n - 1, width // n, rows), bfloat),
            pltpu.VMEM((n, width // n, rows), bfloat),
            pltpu.VMEM((n, rows, width), bfloat),
            pltpu.VMEM((n - 1, width // n, all_rows), bfloat),
            pltpu.VMEM((n, width // n, all_rows), bfloat),
            pltpu.VMEM((n - 1, width // n, rows), bfloat),
            pltpu.VMEM((n, width // n, rows), bfloat),
            pltpu.VMEM((n, rows, width), bfloat),
            pltpu.VMEM((n, all_rows, 2 * width), bfloat),
            pltpu.VMEM((4,) + normed_one.shape, bfloat),
            pltpu.VMEM((rows, width), bfloat),
            sem((len(loaded),)),
        ]
        + [sem((8, n - 1))] * 2
        + [sem((3,)), sem((4,))]
        + [pltpu.VMEM((4, largest, 8, width), f32)]
        + [sem((4, largest - 1))] * 2
        + [pltpu.VMEM((4, largest) + decoder_grads.shape, f32)]
        + [sem((4, largest - 1))] * 2
        + [sem((chunks, 2))]
        + [sem((chunks, 3)), sem((chunks, 4))]
        + [sem((chunks, 4, n - 1))] * 2,
        compiler_params=pltpu.CompilerParams(
            collective_id=1, has_side_effects=True, vmem_limit_bytes=VMEM_LIMIT
        ),
    )(*inputs, *loaded, *early)


def columns(ref, first, count):
    block = ref[..., pl.ds(first, count)]
    return block.reshape(-1, count)


def normalize(values):
    center = values - jnp.mean(values, axis=-1, keepdims=True)
    inverse = lax.rsqrt(jnp.mean(center * center, axis=-1, keepdims=True) + EPSILON)
    return center * inverse, inverse


def forward_kernel(n, seq_size, matrices, *refs):
    count = len(matrices)
    refs = list(refs)

    def take(k):
        taken = refs[:k]
        del refs[:k]
        return taken

    shards = take(count)
    tokens, gain_one, shift_one, gain_two, shift_two, index, scene_count = take(7)
    wholes = take(count)
    gains_out, index_out, inverse_one, inverse_two = take(4)
    kept = take(12)
    bufs = take(count)
    made = take(12)
    hidden_all, query, keys, values, mixed, normed_one, normed_two, hidden_two, act, slope, planes, texels = made
    after, index_send, index_recv, hidden_send, hidden_recv, slots, small_send, small_recv, out_sem, kept_sem = take(10)
    bfloat, f32 = jnp.bfloat16, jnp.float32
    place = Place(n, seq_size)
    line = Line(place)
    place.greet()
    for matrix, shard, buf in zip(matrices, shards, bufs):
        if matrix.by_rows:
            buf[place.i + (place.seq,)] = shard[...].astype(bfloat)
        else:
            at = pl.ds(pl.multiple_of(place.seq * matrix.cols, 128), matrix.cols)
            buf[place.i + (slice(None), at)] = shard[...].astype(bfloat)
    index_out[place.seq] = index[...]
    rows_all, width = tokens.shape
    pieces = hidden_pieces(rows_all)
    rows = query.shape[0]
    own = gain_one.shape[1]
    first_own = (place.dp * seq_size + place.seq) * own
    spot = lax.broadcasted_iota(jnp.int32, (own, width), 1) - lax.broadcasted_iota(jnp.int32, (own, width), 0)
    spread_out = (spot == first_own).astype(f32).astype(bfloat)
    gains = [ref[...] for ref in (gain_one, shift_one, gain_two, shift_two)]
    gains = jnp.concatenate(gains + [jnp.zeros((4, own), f32)], axis=0).astype(bfloat)
    gains = matmul(gains, spread_out)
    place.meet()
    gather = Gather(place, matrices, bufs, refs, LATE)
    order = [k for k in range(len(gather.chunks)) if k not in gather.late]
    total = len(order)
    outs = []
    state = [0]

    def put(*which):
        for k in which:
            copy = pltpu.make_async_copy(made[k], kept[k], kept_sem.at[k])
            copy.start()
            outs.append(copy)

    def land(k):
        gather.arrived(k)
        w, matrix, part = gather.chunks[k]
        at = (slice(None),) * 3 + matrix.tail(part, 0, seq_size)
        copy = pltpu.make_async_copy(bufs[w].at[at], wholes[w].at[at], out_sem.at[k])
        copy.start()
        outs.append(copy)

    late_steps = {
        0: lambda k: gather.hop(k, 1),
        LATE_SEQ: gather.along_seq,
        LATE_SEQ + 2: gather.relay,
        LATE_SEQ + 3: gather.third,
        LATE_SEQ + 5: land,
    }

    def advance():
        t = state[0]
        state[0] += 1
        if 0 <= t - 3 * LAG < total:
            land(order[t - 3 * LAG])
        if 0 <= t - 2 * LAG < total:
            gather.third(order[t - 2 * LAG])
        if 0 <= t - LAG < total:
            gather.hop(order[t - LAG], 1)
        if t < total:
            gather.hop(order[t], 0)
        if t + 1 < total:
            gather.relay(order[t + 1])
        issue(t + AHEAD)
        hidden_step(t)
        for i, k in enumerate(gather.late):
            if t - i in late_steps:
                late_steps[t - i](k)

    def advance_to(weight):
        last = max([at for at, k in enumerate(order) if gather.chunks[k][0] == weight] + [-1]) + 3 * LAG
        for i, k in enumerate(gather.late):
            if gather.chunks[k][0] == weight:
                last = max(last, LATE_SEQ + 5 + i)
        while state[0] <= last:
            advance()

    def issue(last):
        while issued[0] <= min(last, total - 1):
            gather.along_seq(order[issued[0]])
            issued[0] += 1

    issued = [0]
    issue(FIRST)
    for k in gather.late:
        gather.hop(k, 0)
    index_line = (lambda j: index_out.at[j], index_send, index_recv)

    def hidden_line(piece):
        size = rows_all // pieces
        at = pl.ds(piece * size, size)
        return lambda j: hidden_all.at[j, at], hidden_send.at[piece], hidden_recv.at[piece]

    def hidden_step(t):
        for piece in range(pieces):
            if t == HIDDEN_FIRST + piece * HIDDEN_EVERY + HIDDEN_LAG:
                line.gather_relay(*hidden_line(piece))
            if t == HIDDEN_FIRST + piece * HIDDEN_EVERY:
                line.gather_start(*hidden_line(piece))

    normed, inverse = normalize(tokens[...])
    hidden_all[place.seq] = normed.astype(bfloat)
    normed_one[...] = normed
    inverse_one[...] = inverse
    hidden_step(-1)
    gather.relay(order[0])
    for _ in range(SUM_AT):
        advance()
    (gains_out[...],) = small_sum(place, [(gains, slots, small_send, small_recv)], advance)
    put(5)
    line.gather_start(*index_line)
    advance()
    line.gather_relay(*index_line)
    w_qkv, w_out, w_up, w_down, w_unpatch = bufs
    tile = 512
    advance_to(0)
    while state[0] <= HIDDEN_FIRST + (pieces - 1) * HIDDEN_EVERY + HIDDEN_LAG:
        advance()
    for piece in range(pieces):
        line.gather_take(*hidden_line(piece))
        line.gather_finish(*hidden_line(piece))

    @pl.loop(0, seq_size)
    def _(j):
        spread_gain, spread_shift = gains_out[0:1], gains_out[1:2]
        hidden_all[j] = (hidden_all[j].astype(f32) * spread_gain + spread_shift).astype(bfloat)

    for at in range(0, width, tile):
        block = hidden_all[place.seq, pl.ds(0, rows)]
        query[:, at : at + tile] = matmul(block, columns(w_qkv, at, tile)).astype(bfloat)
    put(0, 1)

    @pl.loop(0, width // tile)
    def _(t):
        at = pl.multiple_of(t * tile, tile)
        hidden = hidden_all[...].reshape(-1, width)
        keys[:, pl.ds(at, tile)] = matmul(hidden, columns(w_qkv, at + width, tile)).astype(bfloat)
        values[:, pl.ds(at, tile)] = matmul(hidden, columns(w_qkv, at + 2 * width, tile)).astype(bfloat)

    put(2, 3)
    advance()
    valid = key_valid(scene_count, seq_size, rows, rows_all, 1)
    pair = 2 * width // HEADS
    scale = (width // HEADS) ** (-0.5)
    first = lax.broadcasted_iota(jnp.int32, (rows, pair), 1) < pair // 2
    pairs, segments = HEADS // 2, 4
    for segment in range(segments):

        @pl.loop(segment * pairs // segments, (segment + 1) * pairs // segments)
        def _(p):
            at = pl.ds(pl.multiple_of(p * pair, pair), pair)
            query_two, key_two, value_two = query[:, at].astype(f32) * scale, keys[:, at], values[:, at]
            both = []
            for mine in (first, ~first):
                scores = matmul_nt(jnp.where(mine, query_two, 0.0).astype(bfloat), key_two)
                scores = jnp.where(valid, scores, NEGATIVE)
                expo = jnp.exp(scores - jnp.max(scores, axis=-1, keepdims=True))
                probs = expo * (1.0 / jnp.sum(expo, axis=-1, keepdims=True))
                both.append(matmul(probs.astype(bfloat), value_two))
            mixed[:, at] = jnp.where(first, both[0], both[1]).astype(bfloat)

        advance()
    put(4)
    advance_to(1)
    for at in range(0, width, tile):
        after[:, at : at + tile] = tokens[:rows, at : at + tile] + matmul(mixed[...], columns(w_out, at, tile))
    normed, inverse = normalize(after[...])
    normed_two[...] = normed
    inverse_two[...] = inverse
    hidden_two[...] = (normed * gains_out[2:3] + gains_out[3:4]).astype(bfloat)
    put(6, 7)
    advance_to(2)

    @pl.loop(0, act.shape[1] // tile)
    def _(t):
        at = pl.multiple_of(t * tile, tile)
        value, rate = gelu_parts(matmul(hidden_two[...], columns(w_up, at, tile)))
        act[:, pl.ds(at, tile)] = value.astype(bfloat)
        slope[:, pl.ds(at, tile)] = rate.astype(bfloat)

    put(8, 9)
    advance_to(3)
    deep = act.shape[1] // n
    for i in range(n):
        block = w_down[i].reshape(deep, width)
        for at in range(0, width, tile):
            after[:, at : at + tile] += matmul(act[:, i * deep : (i + 1) * deep], block[:, at : at + tile])
    planes[...] = after[...].astype(bfloat)
    put(10)
    advance_to(4)
    for at in range(0, texels.shape[1], tile):
        texels[:, at : at + tile] = matmul(planes[...], columns(w_unpatch, at, tile)).astype(bfloat)
    put(11)
    gather.finish()
    line.gather_take(*index_line)
    line.gather_finish(*index_line)
    for copy in outs:
        copy.wait()


def hidden_pieces(rows):
    return rows // PIECE if rows % PIECE == 0 else 1


def key_valid(scene_count, seq_size, plane_rows, rows, axis):
    shape = (1, seq_size * rows) if axis == 1 else (seq_size * rows, 1)
    position = lax.broadcasted_iota(jnp.int32, shape, axis)
    owner = lax.div(position, rows)
    offset = position - owner * rows
    return (offset < plane_rows) | (owner * (rows - plane_rows) + offset - plane_rows < scene_count[0, 0])


def forward_layer(n, seq_size, matrices, shards, tokens, gains, index, scene_count):
    chunks = sum(m.parts for m in matrices)
    vmem, any_space = pl.BlockSpec(memory_space=pltpu.VMEM), pl.BlockSpec(memory_space=pl.ANY)
    shapes = [m.shape(n, seq_size) for m in matrices]
    largest = max(n, seq_size)
    bfloat, f32 = jnp.bfloat16, jnp.float32
    rows, width = tokens.shape
    pieces = hidden_pieces(rows)
    plane_rows = 3 * PRES * PRES // seq_size
    ff = matrices[2].cols * seq_size
    results = [
        ((8, width), f32),
        ((seq_size,) + index.shape, jnp.int32),
        ((rows, 1), f32),
        ((plane_rows, 1), f32),
    ]
    kept = [
        ((seq_size, rows, width), bfloat),
        ((plane_rows, width), bfloat),
        ((seq_size * rows, width), bfloat),
        ((seq_size * rows, width), bfloat),
        ((plane_rows, width), bfloat),
        ((rows, width), f32),
        ((plane_rows, width), f32),
        ((plane_rows, width), bfloat),
        ((plane_rows, ff), bfloat),
        ((plane_rows, ff), bfloat),
        ((plane_rows, width), bfloat),
        ((plane_rows, matrices[4].cols * seq_size), bfloat),
    ]
    sem = pltpu.SemaphoreType.DMA
    made = pl.pallas_call(
        functools.partial(forward_kernel, n, seq_size, matrices),
        out_shape=[jax.ShapeDtypeStruct(s, bfloat) for s in shapes]
        + [jax.ShapeDtypeStruct(s, t) for s, t in results + kept],
        in_specs=[vmem] * (len(matrices) + 6) + [pl.BlockSpec(memory_space=pltpu.SMEM)],
        out_specs=[any_space] * len(matrices) + [vmem] * len(results) + [any_space] * len(kept),
        scratch_shapes=[pltpu.VMEM(s, bfloat) for s in shapes]
        + [pltpu.VMEM(s, t) for s, t in kept]
        + [pltpu.VMEM((plane_rows, width), f32)]
        + [sem((4,)), sem((3,)), sem((pieces, 4)), sem((pieces, 3))]
        + [pltpu.VMEM((4, largest, 8, width), f32)]
        + [sem((4, largest - 1))] * 2
        + [sem((chunks,)), sem((len(kept),))]
        + gather_sems(n, seq_size, chunks),
        compiler_params=pltpu.CompilerParams(
            collective_id=0, has_side_effects=True, vmem_limit_bytes=VMEM_LIMIT
        ),
    )(*shards, tokens, *gains, index, scene_count)
    return made[: len(matrices)], made[len(matrices) :]


def weight_list(shards, cuts):
    return tuple(
        Matrix(shard.shape[0], shard.shape[1], k == 3, rows) for k, (shard, rows) in enumerate(zip(shards, cuts))
    )


def matmul(left, right):
    return jnp.dot(left, right, preferred_element_type=jnp.float32)


def matmul_tn(left, right):
    return lax.dot_general(
        left, right, (((0,), (0,)), ((), ())), preferred_element_type=jnp.float32
    )


def matmul_nt(left, right):
    return lax.dot_general(
        left, right, (((1,), (1,)), ((), ())), preferred_element_type=jnp.float32
    )


def split_at(values, count):
    return values[:count], values[count:]


def shards(
    tokens,
    ln1_gain,
    ln1_bias,
    w_qkv,
    w_out,
    ln2_gain,
    ln2_bias,
    w_up,
    w_down,
    w_unpatch,
    dec_w1,
    dec_b1,
    dec_w2,
    dec_b2,
    counts,
    sample_texels,
    d_density,
    d_color,
):
    seq_size = lax.axis_size("seq")
    dp_size = lax.axis_size("dp")
    n = round(dp_size ** (1 / 3))
    shards_of = (w_qkv, w_out, w_up, w_down, w_unpatch)
    matrices = weight_list(shards_of, GATHER_CUTS)
    qkv, out, up, down, unpatch = weight_list(shards_of, SUM_CUTS)
    gains = [part[None] for part in (ln1_gain, ln1_bias, ln2_gain, ln2_bias)]
    scene_count = counts[None]
    index = sample_texels.transpose(1, 0, 2)
    wholes, made = forward_layer(n, seq_size, matrices, shards_of, tokens[0], gains, index, scene_count)
    gains_all, index_all, inverse_one, inverse_two = made[:4]
    hidden_all, query, keys, values, mixed, normed_one = made[4:10]
    normed_two, hidden_two, act, slope, planes, texels = made[10:]
    decoder = (dec_w1.T, dec_b1[None], dec_w2.T, dec_b2[None])
    (density, color, decoder_grads, grad_after, norm_grads), grads = split_at(
        middle(
            n,
            seq_size,
            (up, down, unpatch),
            (texels, index_all) + decoder + (d_density, d_color.transpose(1, 0, 2)),
            (planes, hidden_two, inverse_two, gains_all, act, slope, normed_two),
            wholes[2:],
        ),
        5,
    )
    block_sums, (g_tokens, *small_sums) = split_at(
        backward_attention(
            n,
            seq_size,
            (unpatch, down, up, qkv, out),
            (grad_after, mixed, query, normed_one, inverse_one, gains_all, norm_grads, decoder_grads, scene_count),
            (wholes[1], wholes[0], keys, values, hidden_all.reshape(-1, hidden_all.shape[2])),
            (grads[2], grads[1], grads[0]),
        ),
        5,
    )
    large, small = split_at(finish((*block_sums, g_tokens, density, color, *small_sums)), 6)
    g_unpatch, g_down, g_up, g_qkv, g_out, g_tokens = large
    density, color, gain_one, shift_one, gain_two, shift_two, g_w1, g_b1, g_w2, g_b2 = small
    return (
        density,
        color.transpose(1, 0, 2),
        g_tokens[None],
        gain_one[0],
        shift_one[0],
        g_qkv,
        g_out,
        gain_two[0],
        shift_two[0],
        g_up,
        g_down,
        g_unpatch,
        g_w1.T,
        g_b1[0],
        g_w2.T,
        g_b2[0],
    )


def solution(mesh):
    in_specs = (
        P("dp", "seq", None),
        P(("dp", "seq")),
        P(("dp", "seq")),
        P("dp", "seq"),
        P("dp", "seq"),
        P(("dp", "seq")),
        P(("dp", "seq")),
        P("dp", "seq"),
        P(("dp", "seq"), None),
        P("dp", "seq"),
        P(),
        P(),
        P(),
        P(),
        P("dp"),
        P("dp", None, "seq"),
        P("dp", "seq"),
        P("dp", None, "seq"),
    )
    out_specs = (
        P("dp", "seq"),
        P("dp", None, "seq"),
        P("dp", "seq", None),
        P(("dp", "seq")),
        P(("dp", "seq")),
        P("dp", "seq"),
        P("dp", "seq"),
        P(("dp", "seq")),
        P(("dp", "seq")),
        P("dp", "seq"),
        P(("dp", "seq"), None),
        P("dp", "seq"),
        P(),
        P(),
        P(),
        P(),
    )
    return jax.shard_map(shards, mesh=mesh, in_specs=in_specs, out_specs=out_specs, check_vma=False)
```

```python
import functools
import math

import jax
import jax.numpy as jnp
from jax import lax
from jax.experimental import pallas as pl
from jax.experimental.pallas import tpu as pltpu
from jax.sharding import PartitionSpec as P

HEADS = 16
PATCH = 8
CH = 32
PRES = 16


EPSILON = 1e-05
NEGATIVE = -1e30
VMEM_LIMIT = 58 * 2**20
AHEAD = 2
FIRST = 1
PIECE = 32
HIDDEN_LAG = 1
HIDDEN_FIRST = -1
HIDDEN_EVERY = 2
SUM_AT = 4
HALVES = 2
LATE = ((4, 1),)
LATE_SEQ = 12
FIRST_RELAY = 3
GATHER_CUTS = ((32,) * 4, (128,), (32,) * 4, (32,) * 4, (32, 96))
SUM_CUTS = ((32,) * 4, (128,), (32,) * 4, (32,) * 4, (64,) * 2)
LAG = 2


MESH = pl.DeviceIdType.MESH


class Place:
    def __init__(self, n, seq_size):
        dp = lax.axis_index("dp")
        self.n, self.seq_size = n, seq_size
        self.seq = lax.axis_index("seq")
        self.i = (lax.div(dp, n * n), lax.rem(lax.div(dp, n), n), lax.rem(dp, n))
        self.dp = dp

    def size(self, axis):
        return self.seq_size if axis == 3 else self.n

    def me(self, axis):
        return self.seq if axis == 3 else self.i[axis]

    def peer(self, axis, step):
        to = lax.rem(self.me(axis) + step, self.size(axis))
        if axis == 3:
            return to, (self.dp, to)
        where = [to if a == axis else self.i[a] for a in range(3)]
        return to, ((where[0] * self.n + where[1]) * self.n + where[2], self.seq)

    def source(self, axis, step):
        size = self.size(axis)
        return lax.rem(self.me(axis) + (size - step), size)

    def enter(self, axes=(0, 1, 2, 3)):
        self.greet(axes)
        self.meet(axes)

    def greet(self, axes=(0, 1, 2, 3)):
        barrier = pltpu.get_barrier_semaphore()
        for axis in axes:
            for step in range(1, self.size(axis)):
                pl.semaphore_signal(
                    barrier, inc=1, device_id=self.peer(axis, step)[1], device_id_type=MESH
                )

    def meet(self, axes=(0, 1, 2, 3)):
        pl.semaphore_wait(pltpu.get_barrier_semaphore(), sum(self.size(axis) - 1 for axis in axes))


def remote(src, dst, send, recv, device):
    return pltpu.make_async_remote_copy(
        src_ref=src, dst_ref=dst, send_sem=send, recv_sem=recv, device_id=device, device_id_type=MESH
    )


class Line:
    def __init__(self, place):
        z = place.seq
        assert place.seq_size == 4
        self.dp, self.me = place.dp, z
        self.pair, self.far, self.opposite = z + 1 - 2 * lax.rem(z, 2), lax.rem(z + 2, 4), 3 - z
        self.middle = z * (3 - z) == 2
        self.end = z * (3 - z) == 0

    def _copy(self, source, target, send, recv, to):
        return remote(source, target, send, recv, (self.dp, to))

    def gather_start(self, region, send, recv):
        own = region(self.me)
        self._copy(own, own, send.at[0], recv.at[0], self.pair).start()
        self._copy(own, own, send.at[1], recv.at[1], self.far).start()

        @pl.when(self.middle)
        def _():
            self._copy(own, own, send.at[2], recv.at[2], self.opposite).start()

    def gather_relay(self, region, send, recv):
        block = region(self.far)
        self._copy(block, block, send.at[1], recv.at[1], self.far).wait_recv()

        @pl.when(self.middle)
        def _():
            self._copy(block, block, send.at[3], recv.at[2], self.pair).start()

    def gather_take(self, region, send, recv, which=("pair", "opposite")):
        for i, name, j in ((0, "pair", self.pair), (2, "opposite", self.opposite)):
            if name in which:
                self._copy(region(j), region(j), send.at[i], recv.at[i], self.pair).wait_recv()

    def gather_finish(self, region, send, recv):
        own = region(self.me)
        for i in (0, 1):
            self._copy(own, own, send.at[i], recv.at[i], self.pair).wait_send()

        @pl.when(self.middle)
        def _():
            for i in (2, 3):
                self._copy(own, own, send.at[i], recv.at[2], self.pair).wait_send()

    def sum_start(self, region, slot, send, recv, which=("opposite", "far", "pair")):
        if "opposite" in which:
            block = region(self.opposite)

            @pl.when(self.middle)
            def _():
                self._copy(block, slot(2), send.at[2], recv.at[2], self.opposite).start()

            @pl.when(self.end)
            def _():
                self._copy(block, slot(3), send.at[2], recv.at[3], self.pair).start()

        if "far" in which:

            @pl.when(self.end)
            def _():
                self._copy(region(self.far), slot(1), send.at[1], recv.at[1], self.far).start()

        if "pair" in which:
            self._copy(region(self.pair), slot(0), send.at[0], recv.at[0], self.pair).start()

    def sum_relay(self, region, slot, send, recv, add):
        @pl.when(self.middle)
        def _():
            block = region(self.far)
            self._copy(block, slot(3), send.at[2], recv.at[3], self.pair).wait_recv()
            add(self.far)
            self._copy(block, slot(1), send.at[1], recv.at[1], self.far).start()

    def sum_take(self, region, slot, send, recv):
        for i in (0, 1):
            self._copy(region(self.me), slot(i), send.at[i], recv.at[i], self.pair).wait_recv()

        @pl.when(self.middle)
        def _():
            self._copy(region(self.me), slot(2), send.at[2], recv.at[2], self.pair).wait_recv()

    def sum_of(self, own, slots):
        total = own.astype(jnp.float32) + slots(0).astype(jnp.float32) + slots(1).astype(jnp.float32)
        return total + jnp.where(self.middle, slots(2).astype(jnp.float32), 0.0)

    def sum_finish(self, region, slot, send, recv):
        for i in (0, 1, 2):
            self._copy(region(self.me), slot(0), send.at[i], recv.at[0], self.pair).wait_send()


class Matrix:
    def __init__(self, rows, cols, by_rows, cuts):
        self.rows, self.cols, self.by_rows = rows, cols, by_rows
        self.cuts = cuts if sum(cuts) == rows else (rows,)
        self.parts = len(self.cuts)

    def cut(self, part):
        return pl.ds(sum(self.cuts[:part]), self.cuts[part])

    def half_tail(self, part, j, h):
        half = self.cols // 2
        return (self.cut(part), pl.ds(pl.multiple_of(j * self.cols + h * half, 128), half))

    def shape(self, n, seq_size):
        if self.by_rows:
            return (n, n, n, seq_size, self.rows, self.cols)
        return (n, n, n, self.rows, seq_size * self.cols)

    def tail(self, part, first, count):
        rows = self.cut(part)
        if self.by_rows:
            return (pl.ds(first, count), rows, slice(None))
        if isinstance(first, int):
            return (rows, pl.ds(first * self.cols, count * self.cols))
        return (rows, pl.ds(pl.multiple_of(first * self.cols, 128), count * self.cols))


def small_stage(place, value, slots, send, recv, stage, axis):
    me = place.me(axis)
    slots[stage, me] = value
    copies = []
    for step in range(1, place.size(axis)):
        ref = slots.at[stage, me]
        copy = remote(
            ref, ref, send.at[stage, step - 1], recv.at[stage, step - 1], place.peer(axis, step)[1]
        )
        copy.start()
        copies.append(copy)

    def end():
        for copy in copies:
            copy.wait()
        total = slots[stage, 0]
        for other in range(1, place.size(axis)):
            total = total + slots[stage, other]
        return total

    return end


def small_sum(place, parts, between=None):
    values = [part[0] for part in parts]
    for stage, axis in enumerate((2, 1, 0, 3)):
        ends = [small_stage(place, v, *part[1:], stage, axis) for v, part in zip(values, parts)]
        if between is not None:
            between()
        values = [end() for end in ends]
    return values


class Gather:
    def __init__(self, place, matrices, refs, sems, late=()):
        self.place, self.refs, self.line = place, refs, Line(place)
        self.chunks = [(w, m, p) for w, m in enumerate(matrices) for p in range(m.parts)]
        self.seq_send, self.seq_recv, self.hop_send, self.hop_recv, self.far_send, self.far_recv = sems
        self.late = [k for k, (w, _, p) in enumerate(self.chunks) if (w, p) in late]
        self.copies = {}

    def _send(self, key, axis, region, send, recv):
        made = []
        for step in range(1, self.place.size(axis)):
            copy = remote(region, region, send.at[step - 1], recv.at[step - 1], self.place.peer(axis, step)[1])
            copy.start()
            made.append(copy)
        self.copies[key] = made

    def _take(self, key):
        for copy in self.copies[key]:
            copy.wait_recv()

    def region(self, k, index, first, count):
        w, matrix, part = self.chunks[k]
        return self.refs[w].at[index + matrix.tail(part, first, count)]

    def _along(self, k):
        every = slice(None)
        index = (every, every, self.place.i[2]) if k in self.late else self.place.i
        return lambda j: self.region(k, index, j, 1), self.seq_send.at[k], self.seq_recv.at[k]

    def along_seq(self, k):
        if k in self.late:
            self._take((k, 2, 0))
            self._take((k, 2, 1))
        self.line.gather_start(*self._along(k))

    def relay(self, k):
        self.line.gather_relay(*self._along(k))

    def hop(self, k, number):
        p, half = self.place, self.place.seq_size // 2
        w, matrix, part = self.chunks[k]
        if number == 1:
            self._take((k, 1, 0))
            self._take((k, 1, 1))
        elif k not in self.late:
            self.line.gather_take(*self._along(k))
        for h in (0, 1):
            axis = 1 - h if number == 0 else h
            index = [p.i[0], p.i[1], p.i[2]]
            if number == 1:
                index[1 - axis] = slice(None)
            at = 2 * number + h
            tail = matrix.half_tail(part, p.seq, h) if k in self.late else matrix.tail(part, h * half, half)
            region = self.refs[w].at[tuple(index) + tail]
            self._send((k, 1 + number, h), axis, region, self.hop_send.at[k, at], self.hop_recv.at[k, at])

    def third(self, k):
        p = self.place
        if k in self.late:
            self.line.gather_take(*self._along(k))
        else:
            self._take((k, 2, 0))
            self._take((k, 2, 1))
        region = self.region(k, (slice(None), slice(None), p.i[2]), 0, p.seq_size)
        self._send((k, 3), 2, region, self.far_send.at[k], self.far_recv.at[k])

    def arrived(self, k):
        self._take((k, 3))

    def finish(self):
        for k in range(len(self.chunks)):
            self.line.gather_finish(*self._along(k))
        for made in self.copies.values():
            for copy in made:
                copy.wait_send()


def gather_sems(n, seq_size, chunks):
    sem = pltpu.SemaphoreType.DMA
    return [sem((chunks, 4)), sem((chunks, 3))] + [sem((chunks, 4, n - 1))] * 2 + [sem((chunks, n - 1))] * 2


def gelu_parts(x):
    cdf = 0.5 + 0.5 * lax.erf(x * (0.5**0.5))
    return x * cdf, cdf + x * (jnp.exp(-0.5 * x * x) * (2.0 * math.pi) ** -0.5)


def split_low(x):
    high = x.astype(jnp.bfloat16)
    return high, (x - high.astype(jnp.float32)).astype(jnp.bfloat16)


def texel_place(texel, seq_size, me):
    side, quarter = PRES * PATCH, PRES * PRES // seq_size
    row, col = texel // side, texel % side
    token = row // PATCH * PRES + col // PATCH
    a, b = row % PATCH, col % PATCH
    fold = PATCH // 2
    mine = token // quarter == me
    key = jnp.where(mine, a // 2 * quarter + token % quarter, -1)
    return key, a % 2 * PATCH + b, fold


def decode_both(
    place,
    grad_texels,
    between,
    tile,
    texels,
    index,
    w1,
    b1,
    w2,
    b2,
    d_density,
    d_color,
    density,
    color,
    grads,
    tables,
    grad_tables,
    features,
    part_out,
    part_in,
    own_part,
    grad_all,
    send_sem,
    recv_sem,
    back_send,
    back_recv,
):
    seq_size = place.seq_size
    bfloat, f32 = jnp.bfloat16, jnp.float32
    samples = index.shape[3]
    quarter = PRES * PRES // seq_size
    width = texels.shape[1]
    groups = 2 * PATCH
    cols = groups * CH
    depth = width // cols * quarter
    hidden, inputs = w1.shape
    line = Line(place)
    for p in range(3):
        own = texels[p * quarter : (p + 1) * quarter].astype(f32)
        stacked = jnp.concatenate([own[:, i * cols : (i + 1) * cols] for i in range(width // cols)], axis=0)
        tables[p] = stacked.T.astype(bfloat)
    place.meet((2, 3))
    w1_high, w1_low = split_low(w1[...])
    w1_stack = jnp.concatenate([w1_high, w1_low], axis=0)
    tiles = samples // tile // HALVES
    size = samples // HALVES

    def one_hot(source, at, p):
        texel = index[source, p, :, at]
        key, group, _ = texel_place(texel, seq_size, place.seq)
        rows = lax.broadcasted_iota(jnp.int32, (depth, tile), 0)
        return (rows == key).astype(f32).astype(bfloat), group

    def forward(source, h):
        @pl.loop(h * tiles, (h + 1) * tiles)
        def _(t):
            at = pl.ds(pl.multiple_of(t * tile, tile), tile)
            picked = []
            for p in range(3):
                hot, group = one_hot(source, at, p)
                spread = matmul(tables[p], hot)
                total = jnp.where(group == 0, spread[:CH], 0.0)
                for g in range(1, groups):
                    total = total + jnp.where(group == g, spread[g * CH : (g + 1) * CH], 0.0)
                picked.append(total)
            feature = jnp.concatenate(picked, axis=0).astype(bfloat)
            features[source, :, at] = feature
            both = matmul(w1_stack, feature)
            part = both[:hidden] + both[hidden:]
            own_part[:, at] = part
            part_out[source, :, at] = part.astype(bfloat)

    def forward_line(h):
        at = pl.ds(h * size, size)
        return lambda j: part_out.at[j, :, at], lambda i: part_in.at[i, :, at], send_sem.at[h], recv_sem.at[h]

    def back_line(h):
        at = pl.ds(h * size, size)
        return lambda j: grad_all.at[j, :, at], back_send.at[h], back_recv.at[h]

    for h in range(HALVES):
        for name, j in (("opposite", line.opposite), ("far", line.far), ("pair", line.pair)):
            forward(j, h)
            line.sum_start(*forward_line(h), which=(name,))
        forward(place.seq, h)
        at = pl.ds(h * size, size)

        def add(j, at=at):
            part_out[j, :, at] = (part_out[j, :, at].astype(f32) + part_in[3, :, at].astype(f32)).astype(bfloat)

        line.sum_relay(*forward_line(h), add)
    between()
    highest = lax.Precision.HIGHEST
    tn, nt = (((0,), (0,)), ((), ())), (((1,), (1,)), ((), ()))
    ones = jnp.ones((8, size), f32)

    def eight(x):
        return jnp.concatenate([x, jnp.zeros((8 - x.shape[0], x.shape[1]), f32)], axis=0)

    def dot(left, right, dims):
        return lax.dot_general(left, right, dims, precision=highest, preferred_element_type=f32)

    grads[...] = jnp.zeros(grads.shape, f32)
    grad_tables[...] = jnp.zeros(grad_tables.shape, f32)
    outs = w2.shape[0]
    me = place.seq
    lanes = lax.broadcasted_iota(jnp.int32, (8, 128), 1)
    same = (lanes == lax.broadcasted_iota(jnp.int32, (8, 128), 0)).astype(f32)
    b1_column = dot(eight(b1[...]), same, tn)[:, :1]
    b2_column = dot(eight(b2[...]), same, tn)[:, :1]
    w2_columns = dot(eight(w2[...]), same, tn)
    w2_columns = [w2_columns[:, i : i + 1] for i in range(outs)]
    for h in range(HALVES):
        at = pl.ds(h * size, size)
        line.sum_take(*forward_line(h))
        pre = line.sum_of(own_part[:, at], lambda i: part_in[i, :, at]) + b1_column
        act, slope = gelu_parts(pre)
        out = jnp.concatenate([jnp.sum(column * act, axis=0, keepdims=True) for column in w2_columns], axis=0)
        out = out + b2_column
        gate = 1.0 / (1.0 + jnp.exp(-out))
        first = out[:1]
        density[:, at] = jnp.maximum(first, 0.0) + jnp.log1p(jnp.exp(-jnp.abs(first)))
        rows = [d_density[:, at] * gate[:1]]
        for p in range(3):
            own = gate[p + 1 : p + 2]
            color[p, :, at] = own
            rows.append(d_color[p, :, at] * own * (1.0 - own))
        grad_out = jnp.concatenate(rows, axis=0)
        grad_pre = sum(column * grad_out[i : i + 1] for i, column in enumerate(w2_columns)) * slope
        grad_all[me, :, at] = grad_pre.astype(bfloat)
        line.gather_start(*back_line(h))
        grads[hidden : hidden + outs, :hidden] += dot(grad_out, act, nt)
        grads[hidden + 8 : hidden + 9, :hidden] += dot(ones, grad_pre, nt)[:1]
        grads[hidden + 16 : hidden + 17, :outs] += dot(ones, grad_out, nt)[:1]

    def backward(source, h):
        @pl.loop(h * tiles, (h + 1) * tiles)
        def _(t):
            at = pl.ds(pl.multiple_of(t * tile, tile), tile)
            grad = grad_all[source, :, at]
            grads[:hidden, :inputs] += matmul_nt(grad, features[source, :, at])
            grad_feature = matmul_tn(w1_high, grad) + matmul_tn(w1_low, grad)
            for p in range(3):
                hot, group = one_hot(source, at, p)
                mine = grad_feature[p * CH : (p + 1) * CH]
                spread = jnp.concatenate(
                    [jnp.where(group == g, mine, 0.0) for g in range(groups)], axis=0
                ).astype(bfloat)
                grad_tables[p] += matmul_nt(spread, hot)

    for h in range(HALVES):
        backward(me, h)
        line.gather_relay(*back_line(h))
    for h in range(HALVES):
        backward(line.far, h)
        line.gather_take(*back_line(h), which=("pair",))
        backward(line.pair, h)
        line.gather_take(*back_line(h), which=("opposite",))
        backward(line.opposite, h)
    for p in range(3):
        back = grad_tables[p].T
        for i in range(width // cols):
            block = back[i * quarter : (i + 1) * quarter].astype(bfloat)
            grad_texels[p * quarter : (p + 1) * quarter, i * cols : (i + 1) * cols] = block
    for h in range(HALVES):
        line.sum_finish(*forward_line(h))
        line.gather_finish(*back_line(h))


def core_columns(ref, n, segment, to):
    width = ref.shape[1]
    parts = width // (n * segment)
    if segment % 128 == 0:
        places = [pl.multiple_of((q * n + to) * segment, 128) for q in range(parts)]
        return jnp.concatenate([ref[:, pl.ds(at, segment)] for at in places], axis=1).T
    place = lax.broadcasted_iota(jnp.int32, (width, width // n), 1)
    source = (lax.div(place, segment) * n + to) * segment + lax.rem(place, segment)
    pick = lax.broadcasted_iota(jnp.int32, (width, width // n), 0) == source
    return matmul(ref[...], pick.astype(jnp.float32).astype(jnp.bfloat16)).astype(jnp.bfloat16).T


class Exchange:
    def __init__(self, place, send, recv):
        self.place, self.send, self.recv = place, send, recv
        self.made, self.used = [], 0

    def _start(self, source_of, buf):
        copies, p = [], self.place
        for step in range(1, p.size(2)):
            to, device = p.peer(2, step)
            sems = (self.send.at[self.used, step - 1], self.recv.at[self.used, step - 1])
            copy = remote(source_of(step, to), buf.at[p.i[2]], *sems, device)
            copy.start()
            copies.append(copy)
        self.used += 1
        self.made += copies

        def wait():
            for copy in copies:
                copy.wait_recv()

        return wait

    def columns(self, ref, segment, split, buf):
        p = self.place
        for step in range(1, p.size(2)):
            split[step - 1] = core_columns(ref, p.n, segment, p.peer(2, step)[0])
        wait = self._start(lambda step, to: split.at[step - 1], buf)
        buf[p.i[2]] = core_columns(ref, p.n, segment, p.i[2])
        return wait

    def rows(self, buf):
        return self._start(lambda step, to: buf.at[self.place.i[2]], buf)

    def finish(self):
        for copy in self.made:
            copy.wait_send()


def weight_grad(left, right, grad, first=0, tile=512):
    shape, width = grad.shape[:-1], right.shape[-1]
    for at in range(0, width, tile):
        size = min(tile, width - at)
        block = matmul(left[0], right[0, :, at : at + size])
        for i in range(1, left.shape[0]):
            block = block + matmul(left[i], right[i, :, at : at + size])
        grad[..., first + at : first + at + size] = block.astype(jnp.bfloat16).reshape(shape + (size,))


def norm_back(grad, normed, inverse, gain):
    scaled = grad * gain
    inner = scaled - jnp.mean(scaled, axis=-1, keepdims=True)
    inner = inner - normed * jnp.mean(scaled * normed, axis=-1, keepdims=True)
    return inner * inverse


def feed_back(place, matrices, refs):
    (planes, hidden_two, inverse_two, gains, act_in, slope_in, normed_in, weights) = refs[:8]
    (grads_out, grad_after, norm_grads, bufs) = refs[8:12]
    (planes_split, planes_all, act_split, act_all, hidden_split, hidden_all) = refs[12:18]
    (texels_all, layer_all, pre_all, layer, act, slope, normed_two, load_sem, out_sem, send, recv) = refs[18:29]
    grads = [buf.at[0] for buf in bufs]
    n = place.n
    bfloat, f32 = jnp.bfloat16, jnp.float32
    up, down, unpatch = matrices
    w_up, w_down, w_unpatch = bufs
    exchange = Exchange(place, send, recv)
    me = place.i[2]
    loads, waits = [], []

    def start():
        pairs = [(act_in, act)] + [(weights[k], bufs[k]) for k in (2, 1, 0)] + [(slope_in, slope), (normed_in, normed_two)]
        for k, (source, target) in enumerate(pairs):
            copy = pltpu.make_async_copy(source, target, load_sem.at[k])
            copy.start()
            loads.append(copy)

    def start_remote():
        waits.append(exchange.columns(planes, unpatch.rows, planes_split, planes_all))
        loads[0].wait()
        waits.append(exchange.columns(act, place.seq_size * down.rows, act_split, act_all))
        waits.append(exchange.columns(hidden_two, up.rows, hidden_split, hidden_all))

    outs = []

    def put(k):
        copy = pltpu.make_async_copy(grads[k], grads_out[k], out_sem.at[k])
        copy.start()
        outs.append(copy)

    def end():
        got_texels = exchange.rows(texels_all)
        loads[1].wait()
        grad_texels = texels_all[me]
        step = layer.shape[1] // n
        for i in range(n):
            block = w_unpatch[i].reshape(step, -1)
            layer[:, i * step : (i + 1) * step] = matmul_nt(grad_texels, block)
        layer_all[me] = layer[...].astype(bfloat)
        got_layer = exchange.rows(layer_all)
        loads[2].wait()
        loads[4].wait()
        step = act.shape[1] // (n * n)
        for i in range(n):
            for j in range(n):
                block = w_down[i, j].reshape(step, -1)
                at = (i * n + j) * step
                value = matmul_nt(layer_all[me], block) * slope[:, at : at + step].astype(f32)
                pre_all[me, :, at : at + step] = value.astype(bfloat)
        got_pre = exchange.rows(pre_all)
        loads[3].wait()
        loads[5].wait()
        step = layer.shape[1] // n
        pieces = []
        for i in range(n):
            block = w_up[i].reshape(step, -1)
            pieces.append(matmul_nt(pre_all[me], block))
        grad = jnp.concatenate(pieces, axis=1)
        grad_after[...] = grad
        waits[1]()
        got_layer()
        weight_grad(act_all, layer_all, grads[1])
        put(1)
        waits[2]()
        got_pre()
        weight_grad(hidden_all, pre_all, grads[0])
        put(0)
        waits[0]()
        got_texels()
        weight_grad(planes_all, texels_all, grads[2])
        put(2)
        grad, normed = grad_after[...], normed_two[...]
        norm_grads[0:1] = jnp.sum(grad * normed, axis=0, keepdims=True)
        norm_grads[1:2] = jnp.sum(grad, axis=0, keepdims=True)
        grad_after[...] = layer[...] + norm_back(grad, normed, inverse_two[...], gains[2:3])
        exchange.finish()
        for copy in outs:
            copy.wait()

    return start, start_remote, end


def middle_kernel(n, seq_size, matrices, *refs):
    refs = list(refs)

    def take(k):
        taken = refs[:k]
        del refs[:k]
        return taken

    decode_in, feed_in, weights = take(8), take(7), take(3)
    density, color, decoder_grads, grad_after, norm_grads = take(5)
    grads_out, bufs, decode_scratch = take(3), take(3), take(11)
    place = Place(n, seq_size)
    feed = list(feed_in) + [weights, grads_out, grad_after, norm_grads, bufs] + refs
    texels_all = refs[6]
    start, start_remote, end = feed_back(place, matrices, feed)
    start()
    place.greet((2, 3))
    tile = min(512, decode_in[1].shape[3])
    outs = (density, color, decoder_grads)
    decode_both(place, texels_all.at[place.i[2]], start_remote, tile, *decode_in, *outs, *decode_scratch)
    end()


def middle(n, seq_size, matrices, decode_in, feed_in, weights):
    texels, index, w1, b1, w2, b2, d_density, d_color = decode_in
    planes, hidden_two, inverse_two, gains, act, slope, normed_two = feed_in
    bfloat, f32 = jnp.bfloat16, jnp.float32
    samples, hidden = index.shape[3], w1.shape[0]
    quarter = PRES * PRES // seq_size
    cols = 2 * PATCH * CH
    depth = texels.shape[1] // cols * quarter
    vmem, any_space = pl.BlockSpec(memory_space=pltpu.VMEM), pl.BlockSpec(memory_space=pl.ANY)
    sem = pltpu.SemaphoreType.DMA
    rows, width = normed_two.shape
    ff, core_ff = act.shape[1], act.shape[1] // n
    shapes = [m.shape(n, seq_size) for m in matrices]
    halves = [(n, n) + s[3:] for s in shapes]
    return pl.pallas_call(
        functools.partial(middle_kernel, n, seq_size, matrices),
        out_shape=[
            jax.ShapeDtypeStruct((1, samples), f32),
            jax.ShapeDtypeStruct((3, 1, samples), f32),
            jax.ShapeDtypeStruct((hidden + 24, 128), f32),
            jax.ShapeDtypeStruct((rows, width), f32),
            jax.ShapeDtypeStruct((2, width), f32),
        ]
        + [jax.ShapeDtypeStruct(s, bfloat) for s in halves],
        in_specs=[vmem] * 12 + [any_space] * 6,
        out_specs=[vmem] * 5 + [any_space] * 3,
        scratch_shapes=[pltpu.VMEM(s, bfloat) for s in shapes]
        + [
            pltpu.VMEM((3, cols, depth), bfloat),
            pltpu.VMEM((3, cols, depth), f32),
            pltpu.VMEM((seq_size, 3 * CH, samples), bfloat),
            pltpu.VMEM((seq_size, hidden, samples), bfloat),
            pltpu.VMEM((4, hidden, samples), bfloat),
            pltpu.VMEM((hidden, samples), f32),
            pltpu.VMEM((seq_size, hidden, samples), bfloat),
        ]
        + [sem((HALVES, 3)), sem((HALVES, 4)), sem((HALVES, 4)), sem((HALVES, 3))]
        + [
            pltpu.VMEM((n - 1, width // n, rows), bfloat),
            pltpu.VMEM((n, width // n, rows), bfloat),
            pltpu.VMEM((n - 1, core_ff, rows), bfloat),
            pltpu.VMEM((n, core_ff, rows), bfloat),
            pltpu.VMEM((n - 1, width // n, rows), bfloat),
            pltpu.VMEM((n, width // n, rows), bfloat),
            pltpu.VMEM((n,) + texels.shape, bfloat),
            pltpu.VMEM((n, rows, width), bfloat),
            pltpu.VMEM((n, rows, ff), bfloat),
            pltpu.VMEM((rows, width), f32),
            pltpu.VMEM((rows, ff), bfloat),
            pltpu.VMEM((rows, ff), bfloat),
            pltpu.VMEM((rows, width), f32),
            sem((6,)),
            sem((3,)),
        ]
        + [sem((8, n - 1))] * 2,
        compiler_params=pltpu.CompilerParams(
            collective_id=2, has_side_effects=True, vmem_limit_bytes=VMEM_LIMIT
        ),
    )(*decode_in, *feed_in, *weights)


class Scatter:
    def __init__(self, place, matrices, sources, kept, hops, near, outs, sems):
        self.place, self.sources, self.kept = place, sources, kept
        self.hops, self.near, self.outs, self.line = hops, near, outs, Line(place)
        self.chunks = [(w, m, p) for w, m in enumerate(matrices) for p in range(m.parts)]
        self.load_sem, self.seq_send, self.seq_recv, self.hop_send, self.hop_recv = sems
        self.copies, self.loads = {}, {}
        self.first = [k for k, (w, _, _) in enumerate(self.chunks) if w == len(matrices) - 1]

    def _send(self, key, axis, region_to, slot, send, recv):
        made = []
        for step in range(1, self.place.size(axis)):
            to, device = self.place.peer(axis, step)
            copy = remote(region_to(to), slot(step - 1), send.at[step - 1], recv.at[step - 1], device)
            copy.start()
            made.append(copy)
        self.copies[key] = made

    def _take(self, key):
        for copy in self.copies[key]:
            copy.wait_recv()

    def hop(self, k, number):
        w, matrix, part = self.chunks[k]
        p, half, n = self.place, self.place.seq_size // 2, self.place.n
        kept, every = self.kept[w], slice(None)
        local = matrix.tail(part, 0, half)
        if number == 0:
            for h in (0, 1):
                index = (p.i[0], every) if h == 0 else (every, p.i[1])
                source = self.sources[w].at[index + matrix.tail(part, h * half, half)]
                copy = pltpu.make_async_copy(source, kept.at[(h, every) + local], self.load_sem.at[k, h])
                copy.start()
                self.loads[k, h] = copy
        else:
            for h in (0, 1):
                self.loads[k, h].wait()
                self._take((k, 1, h))
                for a in range(n):
                    value = kept[(h, a) + local].astype(jnp.float32)
                    for s in range(n - 1):
                        value = value + self.hops[w][(h, s, a) + local].astype(jnp.float32)
                    kept[(h, a) + local] = value.astype(jnp.bfloat16)
        for h in (0, 1):
            axis = h if number == 0 else 1 - h
            tail, at = matrix.tail(part, h * half, half), 2 * number + h

            def region_to(to, h=h, tail=tail):
                if number == 1:
                    return kept.at[(h, to) + local]
                return self.sources[w].at[((to, every) if h == 0 else (every, to)) + tail]

            def slot(s, h=h):
                return self.hops[w].at[(h, s, pl.ds(0, n) if number == 0 else n) + local]

            self._send((k, 1 + number, h), axis, region_to, slot, self.hop_send.at[k, at], self.hop_recv.at[k, at])

    def _block(self, matrix, part, j):
        p, half = self.place, self.place.seq_size // 2
        h = lax.div(j, half)
        return (h, p.i[1] + h * (p.i[0] - p.i[1])) + matrix.tail(part, lax.rem(j, half), 1)

    def along_seq(self, k):
        w, matrix, part = self.chunks[k]
        p, half, n = self.place, self.place.seq_size // 2, self.place.n
        kept = self.kept[w]
        local = matrix.tail(part, 0, half)
        for h in (0, 1):
            self._take((k, 2, h))
            value = kept[(h, p.i[1 - h]) + local].astype(jnp.float32)
            for s in range(n - 1):
                value = value + self.hops[w][(h, s, n) + local].astype(jnp.float32)
            kept[(h, p.i[1 - h]) + local] = value.astype(jnp.bfloat16)
        self.line.sum_start(*self._along(k))

    def _along(self, k):
        w, matrix, part = self.chunks[k]
        kept, near, own = self.kept[w], self.near[w], matrix.tail(part, 0, 1)
        region, slot = lambda j: kept.at[self._block(matrix, part, j)], lambda i: near.at[(i,) + own]
        return region, slot, self.seq_send.at[k], self.seq_recv.at[k]

    def relay(self, k):
        w, matrix, part = self.chunks[k]
        kept, own = self.kept[w], matrix.tail(part, 0, 1)

        def add(j):
            at = self._block(matrix, part, j)
            kept[at] = (kept[at].astype(jnp.float32) + self.near[w][(3,) + own].astype(jnp.float32)).astype(jnp.bfloat16)

        self.line.sum_relay(*self._along(k), add)

    def arrived(self, k):
        w, matrix, part = self.chunks[k]
        own = matrix.tail(part, 0, 1)
        self.line.sum_take(*self._along(k))
        value = self.kept[w][self._block(matrix, part, self.place.seq)]
        value = self.line.sum_of(value, lambda i: self.near[w][(i,) + own])
        self.outs[w][matrix.cut(part)] = value.reshape(-1, matrix.cols)


    def _first(self, k):
        w, matrix, part = self.chunks[k]
        every = (slice(None),) * 2
        region = lambda j: self.sources[w].at[every + matrix.tail(part, j, 1)]
        slot = lambda i: self.near[w].at[(i,) + every + (matrix.cut(part),)]
        return region, slot, self.seq_send.at[k], self.seq_recv.at[k]

    def first_seq(self, k):
        self.line.sum_start(*self._first(k))

    def first_relay(self, k):
        region, slot, send, recv = self._first(k)

        def add(j):
            block = region(j)
            block[...] = (block[...].astype(jnp.float32) + slot(3)[...].astype(jnp.float32)).astype(jnp.bfloat16)

        self.line.sum_relay(region, slot, send, recv, add)

    def first_hop(self, k, number):
        w, matrix, part = self.chunks[k]
        p, n, every, f32 = self.place, self.place.n, slice(None), jnp.float32
        source, hops, rows = self.sources[w], self.hops[w], matrix.cut(part)
        if number == 0:
            region, slot, send, recv = self._first(k)
            self.line.sum_take(region, slot, send, recv)
            own = region(p.seq)
            own[...] = self.line.sum_of(own[...], lambda i: slot(i)[...]).astype(jnp.bfloat16)
        half = matrix.cols // 2
        for h in (0, 1):
            tail = matrix.half_tail(part, p.seq, h)
            if number > 0:
                self._take((k, number, h))
            for a in range(n) if number == 1 else ():
                at = ((p.i[0], a) if h == 0 else (a, p.i[1])) + tail
                value = source[at].astype(f32)
                for s in range(n - 1):
                    value = value + hops[h, s, a, rows].astype(f32)
                source[at] = value.astype(jnp.bfloat16)
            if number == 2:
                value = source[p.i[:2] + tail].astype(f32)
                for s in range(n - 1):
                    value = value + hops[h, s, n, rows].astype(f32)
                self.outs[w][rows, h * half : (h + 1) * half] = value
                continue
            axis, at = (h if number == 0 else 1 - h), 2 * number + h

            def region_to(to, h=h, tail=tail):
                if number == 1:
                    return source.at[((p.i[0], to) if h == 0 else (to, p.i[1])) + tail]
                return source.at[((to, every) if h == 0 else (every, to)) + tail]

            def slot_of(s, h=h):
                return hops.at[h, s, pl.ds(0, n) if number == 0 else n, rows]

            self._send((k, 1 + number, h), axis, region_to, slot_of, self.hop_send.at[k, at], self.hop_recv.at[k, at])

    def finish(self):
        for k in range(len(self.chunks)):
            self.line.sum_finish(*(self._first(k) if k in self.first else self._along(k)))
        for made in self.copies.values():
            for copy in made:
                copy.wait_send()


def backward_kernel(n, seq_size, matrices, *refs):
    count = len(matrices)
    refs = list(refs)

    def take(k):
        taken = refs[:k]
        del refs[:k]
        return taken

    grad_after, mixed, query, normed_one, inverse_one, gains, norm_grads, decoder_grads, scene_count = take(9)
    w_out_in, w_qkv_in, keys_in, values_in, hidden_all_in = take(5)
    early = take(count - 2)
    outs = take(count)
    g_tokens, *norm_outs = take(5)
    g_w1, g_b1, g_w2, g_b2 = take(4)
    w_out, w_qkv, work = take(3)
    g_out, g_qkv = w_out.at[0], w_qkv.at[0]
    kept, hops, near = take(count), take(count), take(count)
    mixed_split, mixed_all, after_all, hidden_split, hidden_core, own_split, own_core = take(7)
    query_all, grad_all, hidden_in = take(3)
    grad_mixed, load_sem, core_send, core_recv, hidden_send, hidden_recv = take(6)
    norm_part, decoder_part = take(3), take(3)
    sems = refs
    bfloat, f32 = jnp.bfloat16, jnp.float32
    place = Place(n, seq_size)
    me = place.i[2]
    loads = []
    rows, width = query.shape
    token_rows = normed_one.shape[0]
    keys, values = grad_all.at[me, :, pl.ds(0, width)], grad_all.at[me, :, pl.ds(width, width)]
    for k, (source, target) in enumerate(
        ((hidden_all_in, work), (w_out_in, w_out), (keys_in, keys), (values_in, values), (w_qkv_in, w_qkv))
    ):
        copy = pltpu.make_async_copy(source, target, load_sem.at[k])
        copy.start()
        loads.append(copy)
    place.enter()
    scatter = Scatter(place, matrices, list(early) + [g_qkv, g_out], kept, hops, near, outs, sems)
    order = [k for k in range(len(scatter.chunks)) if k not in scatter.first]
    total = len(order)
    state = [0]
    first_steps = {
        FIRST_RELAY: scatter.first_relay,
        FIRST_RELAY + 2: lambda k: scatter.first_hop(k, 0),
        FIRST_RELAY + 4: lambda k: scatter.first_hop(k, 1),
        FIRST_RELAY + 6: lambda k: scatter.first_hop(k, 2),
    }

    def advance():
        t = state[0]
        state[0] += 1
        if t < total:
            scatter.hop(order[t], 0)
        if 0 <= t - LAG < total:
            scatter.hop(order[t - LAG], 1)
        if 0 <= t - 2 * LAG < total:
            scatter.along_seq(order[t - 2 * LAG])
        if 0 <= t - 2 * LAG - 1 < total:
            scatter.relay(order[t - 2 * LAG - 1])
        if 0 <= t - 3 * LAG - 1 < total:
            scatter.arrived(order[t - 3 * LAG - 1])
        for k in scatter.first:
            if t in first_steps:
                first_steps[t](k)

    line = Line(place)
    advance()
    advance()
    exchange = Exchange(place, core_send, core_recv)
    qkv_matrix, out_matrix = matrices[-2:]
    got_mixed = exchange.columns(mixed, out_matrix.rows, mixed_split, mixed_all)
    after_all[me] = grad_after[...].astype(bfloat)
    got_after = exchange.rows(after_all)
    loads[0].wait()
    own = work.at[pl.ds(pl.multiple_of(place.seq * token_rows, 16), rows)]
    got_own = exchange.columns(own, qkv_matrix.rows, own_split, own_core)
    got_hidden = exchange.columns(work, qkv_matrix.rows, hidden_split, hidden_core)
    loads[1].wait()
    step = width // n
    for i in range(n):
        block = w_out[i].reshape(step, width)
        grad_mixed[:, i * step : (i + 1) * step] = matmul_nt(after_all[me], block).astype(bfloat)
    got_mixed()
    got_after()
    weight_grad(mixed_all, after_all, g_out)
    for k in scatter.first:
        scatter.first_seq(k)
    loads[2].wait()
    loads[3].wait()
    valid = key_valid(scene_count, seq_size, rows, token_rows, 0)
    pair = 2 * width // HEADS
    scale = (width // HEADS) ** (-0.5)
    first = lax.broadcasted_iota(jnp.int32, (rows, pair), 1) < pair // 2
    pairs, segments = HEADS // 2, 4
    for segment in range(segments):

        @pl.loop(segment * pairs // segments, (segment + 1) * pairs // segments)
        def _(p):
            at = pl.ds(pl.multiple_of(p * pair, pair), pair)
            query_two, grad_two = query[:, at].astype(f32) * scale, grad_mixed[:, at].astype(f32)
            later = pl.ds(pl.multiple_of(width + p * pair, pair), pair)
            key_two, value_two = grad_all[me, :, at], grad_all[me, :, later]
            key_turned = key_two.T
            grad_key, grad_value, turned = 0.0, 0.0, []
            for h, mine in enumerate((first, ~first)):
                query_h = jnp.where(mine, query_two, 0.0).astype(bfloat)
                grad_h = jnp.where(mine, grad_two, 0.0).astype(bfloat)
                scores = jnp.where(valid, matmul_nt(key_two, query_h), NEGATIVE)
                expo = jnp.exp(scores - jnp.max(scores, axis=0, keepdims=True))
                probs = expo * (1.0 / jnp.sum(expo, axis=0, keepdims=True))
                grad_value = grad_value + matmul(probs.astype(bfloat), grad_h)
                grad_probs = matmul_nt(value_two, grad_h)
                inner = jnp.sum(probs * grad_probs, axis=0, keepdims=True)
                grad_scores = (probs * (grad_probs - inner)).astype(bfloat)
                grad_key = grad_key + matmul(grad_scores, query_h)
                grad_query = matmul(key_turned, grad_scores)
                turned.append(grad_query[h * (pair // 2) : (h + 1) * (pair // 2)])
            query_all[me, :, at] = (jnp.concatenate(turned, axis=0) * scale).T.astype(bfloat)
            grad_all[me, :, at] = grad_key.astype(bfloat)
            grad_all[me, :, later] = grad_value.astype(bfloat)

        advance()
    got_grad = exchange.rows(grad_all)
    got_query = exchange.rows(query_all)
    loads[4].wait()
    for i in range(n):
        block = w_qkv[i].reshape(step, 3 * width)
        work[:, i * step : (i + 1) * step] = matmul_nt(grad_all[me], block[:, width:]).astype(bfloat)
    pieces = [matmul_nt(query_all[me], w_qkv[i].reshape(step, 3 * width)[:, :width]) for i in range(n)]
    from_query = jnp.concatenate(pieces, axis=1)
    hidden_line = (
        lambda j: work.at[pl.ds(pl.multiple_of(j * token_rows, 16), token_rows)],
        lambda i: hidden_in.at[i],
        hidden_send,
        hidden_recv,
    )
    line.sum_start(*hidden_line)
    advance()
    got_grad()
    got_query()
    got_hidden()
    got_own()
    weight_grad(own_core, query_all, g_qkv)

    def add(j):
        at = pl.ds(pl.multiple_of(j * token_rows, 16), token_rows)
        work[at] = (work[at].astype(f32) + hidden_in[3].astype(f32)).astype(bfloat)

    line.sum_relay(*hidden_line, add)
    weight_grad(hidden_core, grad_all, g_qkv, width)
    advance()
    advance()
    line.sum_take(*hidden_line)
    grad = line.sum_of(work[pl.ds(pl.multiple_of(place.seq * token_rows, 16), token_rows)], lambda i: hidden_in[i])
    rest = jnp.zeros((token_rows - rows, width), f32)
    grad = grad + jnp.concatenate([from_query, rest], axis=0)
    normed = normed_one[...]
    g_tokens[...] = norm_back(grad, normed, inverse_one[...], gains[0:1])
    g_tokens[0:rows] += grad_after[...]
    gain_row = jnp.sum(grad * normed, axis=0, keepdims=True)
    shift_row = jnp.sum(grad, axis=0, keepdims=True)
    norm_rows = jnp.concatenate([gain_row, shift_row, norm_grads[...], jnp.zeros((4, width), f32)], axis=0)
    parts = [(norm_rows, *norm_part), (decoder_grads[...], *decoder_part)]
    norm_sums, decoder_sums = small_sum(place, parts, advance)
    own = norm_outs[0].shape[1]
    spot = lax.broadcasted_iota(jnp.int32, (width, own), 0) - lax.broadcasted_iota(jnp.int32, (width, own), 1)
    pick = (spot == (place.dp * seq_size + place.seq) * own).astype(f32)
    picked = jnp.dot(norm_sums, pick, precision=lax.Precision.HIGHEST, preferred_element_type=f32)
    for i, ref in enumerate(norm_outs):
        ref[...] = picked[i : i + 1]
    hidden, inputs = g_w1.shape
    g_w1[...] = decoder_sums[:hidden, :inputs]
    g_w2[...] = decoder_sums[hidden : hidden + g_w2.shape[0], :hidden]
    g_b1[...] = decoder_sums[hidden + 8 : hidden + 9, :hidden]
    g_b2[...] = decoder_sums[hidden + 16 : hidden + 17, : g_b2.shape[1]]
    while state[0] < total + 3 * LAG + 1:
        advance()
    scatter.finish()
    exchange.finish()
    line.sum_finish(*hidden_line)


def finish(values):
    def kernel(*refs):
        for source, target in zip(refs[: len(values)], refs[len(values) :]):
            target[...] = source[...]

    vmem = [pl.BlockSpec(memory_space=pltpu.VMEM)] * len(values)
    return pl.pallas_call(
        kernel,
        out_shape=[jax.ShapeDtypeStruct(x.shape, x.dtype) for x in values],
        in_specs=vmem,
        out_specs=vmem,
    )(*values)


def half_tail(matrix, seq_size):
    half = seq_size // 2
    if matrix.by_rows:
        return (half, matrix.rows, matrix.cols)
    return (matrix.rows, half * matrix.cols)


def backward_attention(n, seq_size, matrices, inputs, loaded, early):
    grad_after, mixed, query, normed_one, inverse_one, gains, norm_grads, decoder_grads, scene_count = inputs
    own = query.shape[1] // (lax.axis_size("dp") * seq_size)
    hidden, features, outs = decoder_grads.shape[0] - 24, 3 * CH, 4
    bfloat, f32 = jnp.bfloat16, jnp.float32
    vmem, any_space = pl.BlockSpec(memory_space=pltpu.VMEM), pl.BlockSpec(memory_space=pl.ANY)
    shapes = [m.shape(n, seq_size) for m in matrices]
    chunks = sum(m.parts for m in matrices)
    rows, width = query.shape
    all_rows = loaded[2].shape[0]
    largest = max(n, seq_size)
    sem = pltpu.SemaphoreType.DMA
    return pl.pallas_call(
        functools.partial(backward_kernel, n, seq_size, matrices),
        out_shape=[jax.ShapeDtypeStruct((m.rows, m.cols), f32) for m in matrices]
        + [jax.ShapeDtypeStruct(normed_one.shape, f32)]
        + [jax.ShapeDtypeStruct((1, own), f32)] * 4
        + [jax.ShapeDtypeStruct(s, f32) for s in ((hidden, features), (1, hidden), (outs, hidden), (1, outs))],
        in_specs=[vmem] * (len(inputs) - 1) + [pl.BlockSpec(memory_space=pltpu.SMEM)] + [any_space] * (len(loaded) + len(early)),
        out_specs=[vmem] * (len(matrices) + 9),
        scratch_shapes=[pltpu.VMEM(x.shape, bfloat) for x in loaded[:3]]
        + [pltpu.VMEM((2, n) + half_tail(m, seq_size), bfloat) for m in matrices[:-1]]
        + [pltpu.VMEM((16, 128), bfloat)]
        + [pltpu.VMEM((2, n - 1, n + 1) + half_tail(m, seq_size), bfloat) for m in matrices[:-1]]
        + [pltpu.VMEM((2, n - 1, n + 1, matrices[-1].rows, matrices[-1].cols // 2), bfloat)]
        + [pltpu.VMEM((4,) + ((1, m.rows, m.cols) if m.by_rows else (m.rows, m.cols)), bfloat) for m in matrices[:-1]]
        + [pltpu.VMEM((4, n, n, matrices[-1].rows, matrices[-1].cols), bfloat)]
        + [
            pltpu.VMEM((n - 1, width // n, rows), bfloat),
            pltpu.VMEM((n, width // n, rows), bfloat),
            pltpu.VMEM((n, rows, width), bfloat),
            pltpu.VMEM((n - 1, width // n, all_rows), bfloat),
            pltpu.VMEM((n, width // n, all_rows), bfloat),
            pltpu.VMEM((n - 1, width // n, rows), bfloat),
            pltpu.VMEM((n, width // n, rows), bfloat),
            pltpu.VMEM((n, rows, width), bfloat),
            pltpu.VMEM((n, all_rows, 2 * width), bfloat),
            pltpu.VMEM((4,) + normed_one.shape, bfloat),
            pltpu.VMEM((rows, width), bfloat),
            sem((len(loaded),)),
        ]
        + [sem((8, n - 1))] * 2
        + [sem((3,)), sem((4,))]
        + [pltpu.VMEM((4, largest, 8, width), f32)]
        + [sem((4, largest - 1))] * 2
        + [pltpu.VMEM((4, largest) + decoder_grads.shape, f32)]
        + [sem((4, largest - 1))] * 2
        + [sem((chunks, 2))]
        + [sem((chunks, 3)), sem((chunks, 4))]
        + [sem((chunks, 4, n - 1))] * 2,
        compiler_params=pltpu.CompilerParams(
            collective_id=1, has_side_effects=True, vmem_limit_bytes=VMEM_LIMIT
        ),
    )(*inputs, *loaded, *early)


def columns(ref, first, count):
    block = ref[..., pl.ds(first, count)]
    return block.reshape(-1, count)


def normalize(values):
    center = values - jnp.mean(values, axis=-1, keepdims=True)
    inverse = lax.rsqrt(jnp.mean(center * center, axis=-1, keepdims=True) + EPSILON)
    return center * inverse, inverse


def forward_kernel(n, seq_size, matrices, *refs):
    count = len(matrices)
    refs = list(refs)

    def take(k):
        taken = refs[:k]
        del refs[:k]
        return taken

    shards = take(count)
    tokens, gain_one, shift_one, gain_two, shift_two, index, scene_count = take(7)
    wholes = take(count)
    gains_out, index_out, inverse_one, inverse_two = take(4)
    kept = take(12)
    bufs = take(count)
    made = take(12)
    hidden_all, query, keys, values, mixed, normed_one, normed_two, hidden_two, act, slope, planes, texels = made
    after, index_send, index_recv, hidden_send, hidden_recv, slots, small_send, small_recv, out_sem, kept_sem = take(10)
    bfloat, f32 = jnp.bfloat16, jnp.float32
    place = Place(n, seq_size)
    line = Line(place)
    place.greet()

    def cast(first, last):
        for matrix, shard, buf in list(zip(matrices, shards, bufs))[first:last]:
            if matrix.by_rows:
                buf[place.i + (place.seq,)] = shard[...].astype(bfloat)
            else:
                at = pl.ds(pl.multiple_of(place.seq * matrix.cols, 128), matrix.cols)
                buf[place.i + (slice(None), at)] = shard[...].astype(bfloat)

    cast(0, 1)
    rows_all, width = tokens.shape
    pieces = hidden_pieces(rows_all)
    rows = query.shape[0]
    place.meet()
    gather = Gather(place, matrices, bufs, refs, LATE)
    order = [k for k in range(len(gather.chunks)) if k not in gather.late]
    total = len(order)
    outs = []
    state = [0]

    def put(*which):
        for k in which:
            copy = pltpu.make_async_copy(made[k], kept[k], kept_sem.at[k])
            copy.start()
            outs.append(copy)

    def land(k):
        gather.arrived(k)
        w, matrix, part = gather.chunks[k]
        at = (slice(None),) * 3 + matrix.tail(part, 0, seq_size)
        copy = pltpu.make_async_copy(bufs[w].at[at], wholes[w].at[at], out_sem.at[k])
        copy.start()
        outs.append(copy)

    late_steps = {
        0: lambda k: gather.hop(k, 1),
        LATE_SEQ: gather.along_seq,
        LATE_SEQ + 2: gather.relay,
        LATE_SEQ + 3: gather.third,
        LATE_SEQ + 5: land,
    }

    def advance():
        t = state[0]
        state[0] += 1
        if 0 <= t - 3 * LAG < total:
            land(order[t - 3 * LAG])
        if 0 <= t - 2 * LAG < total:
            gather.third(order[t - 2 * LAG])
        if 0 <= t - LAG < total:
            gather.hop(order[t - LAG], 1)
        if t < total:
            gather.hop(order[t], 0)
        if t + 1 < total:
            gather.relay(order[t + 1])
        issue(t + AHEAD)
        hidden_step(t)
        for i, k in enumerate(gather.late):
            if t - i in late_steps:
                late_steps[t - i](k)

    def advance_to(weight):
        last = max([at for at, k in enumerate(order) if gather.chunks[k][0] == weight] + [-1]) + 3 * LAG
        for i, k in enumerate(gather.late):
            if gather.chunks[k][0] == weight:
                last = max(last, LATE_SEQ + 5 + i)
        while state[0] <= last:
            advance()

    def issue(last):
        while issued[0] <= min(last, total - 1):
            gather.along_seq(order[issued[0]])
            issued[0] += 1

    issued = [0]
    issue(FIRST)
    cast(1, count)
    index_out[place.seq] = index[...]
    own = gain_one.shape[1]
    first_own = (place.dp * seq_size + place.seq) * own
    spot = lax.broadcasted_iota(jnp.int32, (own, width), 1) - lax.broadcasted_iota(jnp.int32, (own, width), 0)
    spread_out = (spot == first_own).astype(f32).astype(bfloat)
    gains = [ref[...] for ref in (gain_one, shift_one, gain_two, shift_two)]
    gains = jnp.concatenate(gains + [jnp.zeros((4, own), f32)], axis=0).astype(bfloat)
    gains = matmul(gains, spread_out)
    for k in gather.late:
        gather.hop(k, 0)
    index_line = (lambda j: index_out.at[j], index_send, index_recv)

    def hidden_line(piece):
        size = rows_all // pieces
        at = pl.ds(piece * size, size)
        return lambda j: hidden_all.at[j, at], hidden_send.at[piece], hidden_recv.at[piece]

    def hidden_step(t):
        for piece in range(pieces):
            if t == HIDDEN_FIRST + piece * HIDDEN_EVERY + HIDDEN_LAG:
                line.gather_relay(*hidden_line(piece))
            if t == HIDDEN_FIRST + piece * HIDDEN_EVERY:
                line.gather_start(*hidden_line(piece))

    normed, inverse = normalize(tokens[...])
    hidden_all[place.seq] = normed.astype(bfloat)
    normed_one[...] = normed
    inverse_one[...] = inverse
    hidden_step(-1)
    gather.relay(order[0])
    for _ in range(SUM_AT):
        advance()
    (gains_out[...],) = small_sum(place, [(gains, slots, small_send, small_recv)], advance)
    put(5)
    line.gather_start(*index_line)
    advance()
    line.gather_relay(*index_line)
    w_qkv, w_out, w_up, w_down, w_unpatch = bufs
    tile = 512
    advance_to(0)
    while state[0] <= HIDDEN_FIRST + (pieces - 1) * HIDDEN_EVERY + HIDDEN_LAG:
        advance()
    for piece in range(pieces):
        line.gather_take(*hidden_line(piece))
        line.gather_finish(*hidden_line(piece))

    @pl.loop(0, seq_size)
    def _(j):
        spread_gain, spread_shift = gains_out[0:1], gains_out[1:2]
        hidden_all[j] = (hidden_all[j].astype(f32) * spread_gain + spread_shift).astype(bfloat)

    for at in range(0, width, tile):
        block = hidden_all[place.seq, pl.ds(0, rows)]
        query[:, at : at + tile] = matmul(block, columns(w_qkv, at, tile)).astype(bfloat)
    put(0, 1)

    @pl.loop(0, width // tile)
    def _(t):
        at = pl.multiple_of(t * tile, tile)
        hidden = hidden_all[...].reshape(-1, width)
        keys[:, pl.ds(at, tile)] = matmul(hidden, columns(w_qkv, at + width, tile)).astype(bfloat)
        values[:, pl.ds(at, tile)] = matmul(hidden, columns(w_qkv, at + 2 * width, tile)).astype(bfloat)

    put(2, 3)
    advance()
    valid = key_valid(scene_count, seq_size, rows, rows_all, 1)
    pair = 2 * width // HEADS
    scale = (width // HEADS) ** (-0.5)
    first = lax.broadcasted_iota(jnp.int32, (rows, pair), 1) < pair // 2
    pairs, segments = HEADS // 2, 4
    for segment in range(segments):

        @pl.loop(segment * pairs // segments, (segment + 1) * pairs // segments)
        def _(p):
            at = pl.ds(pl.multiple_of(p * pair, pair), pair)
            query_two, key_two, value_two = query[:, at].astype(f32) * scale, keys[:, at], values[:, at]
            both = []
            for mine in (first, ~first):
                scores = matmul_nt(jnp.where(mine, query_two, 0.0).astype(bfloat), key_two)
                scores = jnp.where(valid, scores, NEGATIVE)
                expo = jnp.exp(scores - jnp.max(scores, axis=-1, keepdims=True))
                probs = expo * (1.0 / jnp.sum(expo, axis=-1, keepdims=True))
                both.append(matmul(probs.astype(bfloat), value_two))
            mixed[:, at] = jnp.where(first, both[0], both[1]).astype(bfloat)

        advance()
    put(4)
    advance_to(1)
    for at in range(0, width, tile):
        after[:, at : at + tile] = tokens[:rows, at : at + tile] + matmul(mixed[...], columns(w_out, at, tile))
    normed, inverse = normalize(after[...])
    normed_two[...] = normed
    inverse_two[...] = inverse
    hidden_two[...] = (normed * gains_out[2:3] + gains_out[3:4]).astype(bfloat)
    put(6, 7)
    advance_to(2)

    @pl.loop(0, act.shape[1] // tile)
    def _(t):
        at = pl.multiple_of(t * tile, tile)
        value, rate = gelu_parts(matmul(hidden_two[...], columns(w_up, at, tile)))
        act[:, pl.ds(at, tile)] = value.astype(bfloat)
        slope[:, pl.ds(at, tile)] = rate.astype(bfloat)

    put(8, 9)
    advance_to(3)
    deep = act.shape[1] // n
    for i in range(n):
        block = w_down[i].reshape(deep, width)
        for at in range(0, width, tile):
            after[:, at : at + tile] += matmul(act[:, i * deep : (i + 1) * deep], block[:, at : at + tile])
    planes[...] = after[...].astype(bfloat)
    put(10)
    advance_to(4)
    for at in range(0, texels.shape[1], tile):
        texels[:, at : at + tile] = matmul(planes[...], columns(w_unpatch, at, tile)).astype(bfloat)
    put(11)
    gather.finish()
    line.gather_take(*index_line)
    line.gather_finish(*index_line)
    for copy in outs:
        copy.wait()


def hidden_pieces(rows):
    return rows // PIECE if rows % PIECE == 0 else 1


def key_valid(scene_count, seq_size, plane_rows, rows, axis):
    shape = (1, seq_size * rows) if axis == 1 else (seq_size * rows, 1)
    position = lax.broadcasted_iota(jnp.int32, shape, axis)
    owner = lax.div(position, rows)
    offset = position - owner * rows
    return (offset < plane_rows) | (owner * (rows - plane_rows) + offset - plane_rows < scene_count[0, 0])


def forward_layer(n, seq_size, matrices, shards, tokens, gains, index, scene_count):
    chunks = sum(m.parts for m in matrices)
    vmem, any_space = pl.BlockSpec(memory_space=pltpu.VMEM), pl.BlockSpec(memory_space=pl.ANY)
    shapes = [m.shape(n, seq_size) for m in matrices]
    largest = max(n, seq_size)
    bfloat, f32 = jnp.bfloat16, jnp.float32
    rows, width = tokens.shape
    pieces = hidden_pieces(rows)
    plane_rows = 3 * PRES * PRES // seq_size
    ff = matrices[2].cols * seq_size
    results = [
        ((8, width), f32),
        ((seq_size,) + index.shape, jnp.int32),
        ((rows, 1), f32),
        ((plane_rows, 1), f32),
    ]
    kept = [
        ((seq_size, rows, width), bfloat),
        ((plane_rows, width), bfloat),
        ((seq_size * rows, width), bfloat),
        ((seq_size * rows, width), bfloat),
        ((plane_rows, width), bfloat),
        ((rows, width), f32),
        ((plane_rows, width), f32),
        ((plane_rows, width), bfloat),
        ((plane_rows, ff), bfloat),
        ((plane_rows, ff), bfloat),
        ((plane_rows, width), bfloat),
        ((plane_rows, matrices[4].cols * seq_size), bfloat),
    ]
    sem = pltpu.SemaphoreType.DMA
    made = pl.pallas_call(
        functools.partial(forward_kernel, n, seq_size, matrices),
        out_shape=[jax.ShapeDtypeStruct(s, bfloat) for s in shapes]
        + [jax.ShapeDtypeStruct(s, t) for s, t in results + kept],
        in_specs=[vmem] * (len(matrices) + 6) + [pl.BlockSpec(memory_space=pltpu.SMEM)],
        out_specs=[any_space] * len(matrices) + [vmem] * len(results) + [any_space] * len(kept),
        scratch_shapes=[pltpu.VMEM(s, bfloat) for s in shapes]
        + [pltpu.VMEM(s, t) for s, t in kept]
        + [pltpu.VMEM((plane_rows, width), f32)]
        + [sem((4,)), sem((3,)), sem((pieces, 4)), sem((pieces, 3))]
        + [pltpu.VMEM((4, largest, 8, width), f32)]
        + [sem((4, largest - 1))] * 2
        + [sem((chunks,)), sem((len(kept),))]
        + gather_sems(n, seq_size, chunks),
        compiler_params=pltpu.CompilerParams(
            collective_id=0, has_side_effects=True, vmem_limit_bytes=VMEM_LIMIT
        ),
    )(*shards, tokens, *gains, index, scene_count)
    return made[: len(matrices)], made[len(matrices) :]


def weight_list(shards, cuts):
    return tuple(
        Matrix(shard.shape[0], shard.shape[1], k == 3, rows) for k, (shard, rows) in enumerate(zip(shards, cuts))
    )


def matmul(left, right):
    return jnp.dot(left, right, preferred_element_type=jnp.float32)


def matmul_tn(left, right):
    return lax.dot_general(
        left, right, (((0,), (0,)), ((), ())), preferred_element_type=jnp.float32
    )


def matmul_nt(left, right):
    return lax.dot_general(
        left, right, (((1,), (1,)), ((), ())), preferred_element_type=jnp.float32
    )


def split_at(values, count):
    return values[:count], values[count:]


def shards(
    tokens,
    ln1_gain,
    ln1_bias,
    w_qkv,
    w_out,
    ln2_gain,
    ln2_bias,
    w_up,
    w_down,
    w_unpatch,
    dec_w1,
    dec_b1,
    dec_w2,
    dec_b2,
    counts,
    sample_texels,
    d_density,
    d_color,
):
    seq_size = lax.axis_size("seq")
    dp_size = lax.axis_size("dp")
    n = round(dp_size ** (1 / 3))
    shards_of = (w_qkv, w_out, w_up, w_down, w_unpatch)
    matrices = weight_list(shards_of, GATHER_CUTS)
    qkv, out, up, down, unpatch = weight_list(shards_of, SUM_CUTS)
    gains = [part[None] for part in (ln1_gain, ln1_bias, ln2_gain, ln2_bias)]
    scene_count = counts[None]
    index = sample_texels.transpose(1, 0, 2)
    wholes, made = forward_layer(n, seq_size, matrices, shards_of, tokens[0], gains, index, scene_count)
    gains_all, index_all, inverse_one, inverse_two = made[:4]
    hidden_all, query, keys, values, mixed, normed_one = made[4:10]
    normed_two, hidden_two, act, slope, planes, texels = made[10:]
    decoder = (dec_w1.T, dec_b1[None], dec_w2.T, dec_b2[None])
    (density, color, decoder_grads, grad_after, norm_grads), grads = split_at(
        middle(
            n,
            seq_size,
            (up, down, unpatch),
            (texels, index_all) + decoder + (d_density, d_color.transpose(1, 0, 2)),
            (planes, hidden_two, inverse_two, gains_all, act, slope, normed_two),
            wholes[2:],
        ),
        5,
    )
    block_sums, (g_tokens, *small_sums) = split_at(
        backward_attention(
            n,
            seq_size,
            (unpatch, down, up, qkv, out),
            (grad_after, mixed, query, normed_one, inverse_one, gains_all, norm_grads, decoder_grads, scene_count),
            (wholes[1], wholes[0], keys, values, hidden_all.reshape(-1, hidden_all.shape[2])),
            (grads[2], grads[1], grads[0]),
        ),
        5,
    )
    large, small = split_at(finish((*block_sums, g_tokens, density, color, *small_sums)), 6)
    g_unpatch, g_down, g_up, g_qkv, g_out, g_tokens = large
    density, color, gain_one, shift_one, gain_two, shift_two, g_w1, g_b1, g_w2, g_b2 = small
    return (
        density,
        color.transpose(1, 0, 2),
        g_tokens[None],
        gain_one[0],
        shift_one[0],
        g_qkv,
        g_out,
        gain_two[0],
        shift_two[0],
        g_up,
        g_down,
        g_unpatch,
        g_w1.T,
        g_b1[0],
        g_w2.T,
        g_b2[0],
    )


def solution(mesh):
    in_specs = (
        P("dp", "seq", None),
        P(("dp", "seq")),
        P(("dp", "seq")),
        P("dp", "seq"),
        P("dp", "seq"),
        P(("dp", "seq")),
        P(("dp", "seq")),
        P("dp", "seq"),
        P(("dp", "seq"), None),
        P("dp", "seq"),
        P(),
        P(),
        P(),
        P(),
        P("dp"),
        P("dp", None, "seq"),
        P("dp", "seq"),
        P("dp", None, "seq"),
    )
    out_specs = (
        P("dp", "seq"),
        P("dp", None, "seq"),
        P("dp", "seq", None),
        P(("dp", "seq")),
        P(("dp", "seq")),
        P("dp", "seq"),
        P("dp", "seq"),
        P(("dp", "seq")),
        P(("dp", "seq")),
        P("dp", "seq"),
        P(("dp", "seq"), None),
        P("dp", "seq"),
        P(),
        P(),
        P(),
        P(),
    )
    return jax.shard_map(shards, mesh=mesh, in_specs=in_specs, out_specs=out_specs, check_vma=False)
```
